32 devices in a mesh: dp: 4 (over y, x), fsdp: 8 (over z, core).
Axes of the slice: x: 2, y: 2, z: 4, core: 2. Of those that a mesh axis runs over, the one named last changes fastest.
Arguments:
- tokens: bfloat16 [8, 1024, 4, 512], P('dp', 'fsdp'), may hold values from -6 to 6
- sample_counts: int32 [8], P('dp'), may hold values from 1 to 1024, as said below
- feature_counts: int32 [8], P('dp'), may hold values from 1 to 4, as said below
- norms: bfloat16 [6, 512], P(None, ('dp', 'fsdp')), may hold values from -1.2 to 1.4, as said below
- sample_qkv: bfloat16 [3, 512, 512], P(None, ('dp', 'fsdp')), may hold values from -0.25 to 0.25
- sample_out: bfloat16 [512, 512], P(('dp', 'fsdp')), may hold values from -2 to 2
- feature_qkv: bfloat16 [3, 512, 512], P(None, ('dp', 'fsdp')), may hold values from -0.25 to 0.25
- feature_out: bfloat16 [512, 512], P(('dp', 'fsdp')), may hold values from -0.375 to 0.375
- mlp_in: bfloat16 [512, 2048], P(('dp', 'fsdp')), may hold values from -0.25 to 0.25
- mlp_in_bias: bfloat16 [2048], P(('dp', 'fsdp')), may hold values from -3 to 3
- mlp_out: bfloat16 [2048, 512], P(('dp', 'fsdp')), may hold values from -0.125 to 0.125
- mlp_out_bias: bfloat16 [512], P(('dp', 'fsdp')), may hold values from -2 to 2
- cotangent: bfloat16 [8, 1024, 4, 512], P('dp', 'fsdp'), may hold values from -6 to 6
Outputs:
- layer_output: bfloat16 [8, 1024, 4, 512], P('dp', 'fsdp')
- tokens_grad: float32 [8, 1024, 4, 512], P('dp', 'fsdp')
- norms_grad: float32 [6, 512], P(None, ('dp', 'fsdp'))
- sample_qkv_grad: float32 [3, 512, 512], P(None, ('dp', 'fsdp'))
- sample_out_grad: float32 [512, 512], P(('dp', 'fsdp'))
- feature_qkv_grad: float32 [3, 512, 512], P(None, ('dp', 'fsdp'))
- feature_out_grad: float32 [512, 512], P(('dp', 'fsdp'))
- mlp_in_grad: float32 [512, 2048], P(('dp', 'fsdp'))
- mlp_in_bias_grad: float32 [2048], P(('dp', 'fsdp'))
- mlp_out_grad: float32 [2048, 512], P(('dp', 'fsdp'))
- mlp_out_bias_grad: float32 [512], P(('dp', 'fsdp'))
The draws below stay inside these ranges and needn't reach their ends.
Inputs may be any that keep to these rules, and one draw needn't show every extreme that they name: `sample_counts`: in each group of 2 tasks on one dp index, one task, drawn from the seed, holds all 1024 samples; the others are heavy-tailed. `feature_counts`: some task holds all 4 features. `norms`: gains lie in 0.7 to 1.4, biases in -1.2 to 1.2.
All inputs are finite; a program needn't handle non-finite values.
Results may differ from the reference program's by a relative error of at most 0.015.
Values may be sent and summed in bfloat16 or wider, within the bound.
A program may use at most 320 MiB of HBM per device.

```python
import jax
import jax.numpy as jnp
from jax import lax

D = 512
HEADS = 8
FF = 2048
FEAT = 4
TASK_DEV = 2
TASKS = 8
SAMPLES = 1024


def draw_sample_counts(key, part):
    key = jax.random.fold_in(key, 11)
    base_key, halve_key, pick_key = jax.random.split(key, 3)
    drawn_base = jax.random.randint(base_key, (TASKS,), 1, SAMPLES + 1)
    halvings = jax.random.randint(halve_key, (TASKS,), 0, 5)
    ragged = jnp.maximum(jnp.right_shift(drawn_base, halvings), 1)
    chosen = jax.random.randint(pick_key, (TASKS // TASK_DEV,), 0, TASK_DEV)
    slot_index = jnp.arange(TASKS) % TASK_DEV
    full_task = slot_index == jnp.repeat(chosen, TASK_DEV, total_repeat_length=TASKS)
    return jnp.where(full_task, SAMPLES, ragged).astype(jnp.int32)


def draw_feature_counts(key, part):
    key = jax.random.fold_in(key, 7)
    pick_key, value_key = jax.random.split(key)
    drawn = jax.random.randint(value_key, (TASKS,), 1, FEAT + 1)
    widest = jax.random.randint(pick_key, (), 0, TASKS)
    return jnp.where(jnp.arange(TASKS) == widest, FEAT, drawn).astype(jnp.int32)


def draw_norms(key, part):
    key = jax.random.fold_in(key, 5)
    gain_key, bias_key = jax.random.split(key)
    gain_rows = 1.0 + 0.1 * jax.random.normal(gain_key, (3, D), jnp.float32)
    biases = 0.3 * jax.random.normal(bias_key, (3, D), jnp.float32)
    gain_rows = jnp.clip(gain_rows, 0.7, 1.4)
    biases = jnp.clip(biases, -1.2, 1.2)
    return jnp.stack([gain_rows, biases], 1).reshape(6, D).astype(jnp.bfloat16)


def shard_levels(own_key, shape, cuts, low, high):
    gain = 1.0
    for dim, blocks in cuts:
        draws = jax.random.uniform(jax.random.fold_in(jax.random.fold_in(own_key, 6), dim), (blocks,), jnp.float32, low / len(cuts), high / len(cuts))
        gain = gain * jnp.repeat(jnp.exp(draws), shape[dim] // blocks).reshape((-1,) + (1,) * (len(shape) - 1 - dim))
    return gain


def gaussian(rng, dims, spread, most, shards=(), kind=jnp.bfloat16):
    values = jax.random.normal(rng, dims, jnp.float32) * spread
    if len(shards) > 0:
        values = shard_levels(rng, dims, shards, -0.22, 0.18) * values
    return jnp.clip(values, min=-most, max=most).astype(kind)


def setup_inputs(seed: int = 0) -> dict:
    streams_of = jax.random.split(jax.random.key(seed), 14)
    tokens = gaussian(streams_of[0], (TASKS, SAMPLES, FEAT, D), 1.0, 6.0, ((0, 4), (1, 8)))
    sample_counts = draw_sample_counts(jax.random.fold_in(streams_of[13], 71), 0)
    feature_counts = draw_feature_counts(jax.random.fold_in(streams_of[13], 71), 0)
    norms = draw_norms(jax.random.fold_in(streams_of[13], 71), 0)
    sample_qkv = gaussian(streams_of[4], (3, D, D), D ** -0.5, 0.25, ((1, 32),))
    sample_out = gaussian(streams_of[5], (D, D), (D // 64) ** -0.5, 2.0, ((0, 32),))
    feature_qkv = gaussian(streams_of[6], (3, D, D), D ** -0.5, 0.25, ((1, 32),))
    feature_out = gaussian(streams_of[7], (D, D), (D // 2) ** -0.5, 0.375, ((0, 32),))
    mlp_in = gaussian(streams_of[8], (D, FF), D ** -0.5, 0.25, ((0, 32),))
    mlp_in_bias = gaussian(streams_of[9], (FF,), 0.5, 3.0, ((0, 32),))
    mlp_out = gaussian(streams_of[10], (FF, D), FF ** -0.5, 0.125, ((0, 32),))
    mlp_out_bias = gaussian(streams_of[11], (D,), 0.3, 2.0, ((0, 32),))
    cotangent = gaussian(streams_of[12], (TASKS, SAMPLES, FEAT, D), 1.0, 6.0, ((0, 4), (1, 8)))
    return {"tokens": tokens, "sample_counts": sample_counts, "feature_counts": feature_counts, "norms": norms, "sample_qkv": sample_qkv, "sample_out": sample_out, "feature_qkv": feature_qkv, "feature_out": feature_out, "mlp_in": mlp_in, "mlp_in_bias": mlp_in_bias, "mlp_out": mlp_out, "mlp_out_bias": mlp_out_bias, "cotangent": cotangent}


epsilon = 1e-05
highest = lax.Precision.HIGHEST
masked_score = -1e+30

@jax.custom_vjp
def low(v):
    return lax.optimization_barrier(v.astype(jnp.bfloat16)).astype(jnp.float32)

@jax.custom_vjp
def low_back(v):
    return v

def low_keep(v):
    return (low(v), None)

def low_pass(kept, grad):
    return (grad,)

def back_keep(v):
    return (v, None)

def back_low(kept, grad):
    return (low(grad),)
low.defvjp(low_keep, low_pass)
low_back.defvjp(back_keep, back_low)

def layer_norm(inputs, gain_row, bias_row):
    average = lax.optimization_barrier(jnp.mean(inputs, -1, keepdims=True))
    centred = inputs - average
    variance = lax.optimization_barrier(jnp.mean(centred * centred, -1, keepdims=True))
    return centred * lax.rsqrt(variance + epsilon) * gain_row + bias_row

def project(inputs, weight):
    return jnp.einsum('tsfd,de->tsfe', inputs, weight, precision=highest)

def split_heads(inputs):
    return inputs.reshape(inputs.shape[:-1] + (HEADS, D // HEADS))

def sample_mix(normed, qkv_weight, counts):
    score_scale = (D // HEADS) ** (-0.5)

    def per_task(task_item):
        task_rows, task_count = task_item
        queries = split_heads(low(low_back(jnp.einsum('sfd,de->sfe', task_rows, qkv_weight[0], precision=highest))))
        key_rows = split_heads(low(low_back(jnp.einsum('sfd,de->sfe', task_rows, qkv_weight[1], precision=highest))))
        value_rows = split_heads(low(low_back(jnp.einsum('sfd,de->sfe', task_rows, qkv_weight[2], precision=highest))))
        scores = low_back(jnp.einsum('sfhe,kfhe->fhsk', queries, key_rows, precision=highest) * score_scale)
        allowed = jnp.arange(SAMPLES) < task_count
        scores = jnp.where(allowed, scores, masked_score)
        weights = jax.nn.softmax(scores, axis=-1)
        mixture = jnp.einsum('fhsk,kfhe->sfhe', weights, value_rows, precision=highest)
        return mixture.reshape(task_rows.shape)
    return lax.map(jax.checkpoint(per_task), (normed, counts))

def feature_mix(normed, qkv_weight, counts):
    score_scale = (D // HEADS) ** (-0.5)
    queries = split_heads(low(low_back(project(normed, qkv_weight[0]))))
    key_rows = split_heads(low(low_back(project(normed, qkv_weight[1]))))
    value_rows = split_heads(low(low_back(project(normed, qkv_weight[2]))))
    scores = low_back(jnp.einsum('tsfhe,tsghe->tshfg', queries, key_rows, precision=highest) * score_scale)
    allowed = jnp.arange(FEAT)[None, :] < counts[:, None]
    scores = jnp.where(allowed[:, None, None, None, :], scores, masked_score)
    weights = jax.nn.softmax(scores, axis=-1)
    mixture = jnp.einsum('tshfg,tsghe->tsfhe', weights, value_rows, precision=highest)
    return mixture.reshape(normed.shape)

def forward(tokens, norms, sample_qkv, sample_out, feature_qkv, feature_out, mlp_in, mlp_in_bias, mlp_out, mlp_out_bias, sample_counts, feature_counts):
    normed = low(layer_norm(tokens, norms[0], norms[1]))
    mixture = low(low_back(sample_mix(normed, sample_qkv, sample_counts)))
    first_sum = tokens + low_back(project(mixture, sample_out))
    normed = low(layer_norm(first_sum, norms[2], norms[3]))
    mixture = low(low_back(feature_mix(normed, feature_qkv, feature_counts)))
    second_sum = first_sum + low_back(project(mixture, feature_out))
    normed = low(layer_norm(second_sum, norms[4], norms[5]))
    hidden = low_back(project(normed, mlp_in) + mlp_in_bias)
    activated = low(jax.nn.gelu(hidden, approximate=False))
    return second_sum + low_back(project(activated, mlp_out) + mlp_out_bias)

def reference(tokens, sample_counts, feature_counts, norms, sample_qkv, sample_out, feature_qkv, feature_out, mlp_in, mlp_in_bias, mlp_out, mlp_out_bias, cotangent):

    def layer_run(inputs, norm_rows, s_qkv, s_out, f_qkv, f_out, first_matrix, first_bias, second_matrix, second_bias):
        return forward(inputs, norm_rows, s_qkv, s_out, f_qkv, f_out, first_matrix, first_bias, second_matrix, second_bias, sample_counts, feature_counts)
    output, pullback = jax.vjp(layer_run, tokens.astype(jnp.float32), norms.astype(jnp.float32), sample_qkv.astype(jnp.float32), sample_out.astype(jnp.float32), feature_qkv.astype(jnp.float32), feature_out.astype(jnp.float32), mlp_in.astype(jnp.float32), mlp_in_bias.astype(jnp.float32), mlp_out.astype(jnp.float32), mlp_out_bias.astype(jnp.float32))
    gradients = pullback(cotangent.astype(jnp.float32))
    return (output.astype(jnp.bfloat16), gradients[0], gradients[1], gradients[2], gradients[3], gradients[4], gradients[5], gradients[6], gradients[7], gradients[8], gradients[9])
```

```python
import functools
import jax
import jax.numpy as jnp
from jax import lax
from jax.experimental import pallas as pl
from jax.experimental.pallas import tpu as pltpu
from jax.sharding import PartitionSpec as P

MESH = pl.DeviceIdType.MESH
f32, bf16 = jnp.float32, jnp.bfloat16


def mod(a, n):
    return lax.rem(a, n)


def greet(dp_n, fs_n, with_dp=True):
    me_d, me_f = lax.axis_index("dp"), lax.axis_index("fsdp")
    barrier = pltpu.get_barrier_semaphore()
    n = 0
    for k in range(1, fs_n):
        pl.semaphore_signal(barrier, inc=1, device_id=(me_d, mod(me_f + k, fs_n)), device_id_type=MESH)
        n += 1
    if with_dp:
        for k in range(1, dp_n):
            pl.semaphore_signal(barrier, inc=1, device_id=(mod(me_d + k, dp_n), me_f), device_id_type=MESH)
            n += 1
    pl.semaphore_wait(barrier, n)


def rcopy(src, dst, ss, rs, dev):
    return pltpu.make_async_remote_copy(src_ref=src, dst_ref=dst, send_sem=ss, recv_sem=rs, device_id=dev, device_id_type=MESH)


class Swap:
    def __init__(self, fs_n, src, dst, local_sem, ss, rs):
        me_d, me_f = lax.axis_index("dp"), lax.axis_index("fsdp")
        self.own = pltpu.make_async_copy(src.at[me_f], dst.at[me_f], local_sem)
        self.copies = []
        for k in range(1, fs_n):
            to = mod(me_f + k, fs_n)
            self.copies.append(rcopy(src.at[to], dst.at[me_f], ss.at[k - 1], rs.at[k - 1], (me_d, to)))

    def start(self):
        for c in self.copies:
            c.start()
        self.own.start()

    def wait(self):
        self.own.wait()
        for c in self.copies:
            c.wait()


class Gather:
    def __init__(self, dp_n, fs_n, src, dst, local_sem, zs, zr, ds, dr, cs, cr):
        me_d, me_f = lax.axis_index("dp"), lax.axis_index("fsdp")
        z_n = fs_n // 2
        me_z, me_c = me_f // 2, mod(me_f, 2)
        self.z_n, self.dp_n = z_n, dp_n
        partner = (me_d, me_z * 2 + 1 - me_c)
        self.own = pltpu.make_async_copy(src, dst.at[me_d, me_z, me_c], local_sem)
        self.z = []
        for k in range(1, z_n):
            to = mod(me_z + k, z_n) * 2 + me_c
            self.z.append(rcopy(src, dst.at[me_d, me_z, me_c], zs.at[k - 1], zr.at[k - 1], (me_d, to)))
        self.d = {}
        self.c = {}
        for k in range(z_n):
            z = mod(me_z - k + z_n, z_n)
            for j in range(dp_n):
                d = mod(me_d - j + dp_n, dp_n)
                here = src if (k == 0 and j == 0) else dst.at[d, z, me_c]
                self.c[k, j] = rcopy(here, dst.at[d, z, me_c], cs.at[k * dp_n + j], cr.at[k * dp_n + j], partner)
                if j > 0:
                    here = src if k == 0 else dst.at[me_d, z, me_c]
                    i = k * (dp_n - 1) + j - 1
                    self.d[k, j] = rcopy(here, dst.at[me_d, z, me_c], ds.at[i], dr.at[i], (mod(me_d + j, dp_n), me_f))

    def start(self):
        for c in self.z:
            c.start()
        self.own.start()
        for j in range(1, self.dp_n):
            self.d[0, j].start()
        self.c[0, 0].start()

    def forward_z(self):
        for k in range(1, self.z_n):
            self.z[k - 1].wait_recv()
            for j in range(1, self.dp_n):
                self.d[k, j].start()
            self.c[k, 0].start()

    def forward_d(self):
        for k in range(self.z_n):
            for j in range(1, self.dp_n):
                self.d[k, j].wait_recv()
                self.c[k, j].start()

    def wait(self):
        self.own.wait()
        for c in self.z:
            c.wait_send()
        for c in self.d.values():
            c.wait_send()
        for c in self.c.values():
            c.wait()


def gather_sems(dp_n, fs_n):
    z = fs_n // 2
    D = pltpu.SemaphoreType.DMA
    return [D, D((z - 1,)), D((z - 1,)), D((z * (dp_n - 1),)), D((z * (dp_n - 1),)), D((z * dp_n,)), D((z * dp_n,))]


def swap_sems(fs_n):
    D = pltpu.SemaphoreType.DMA
    return [D, D((fs_n - 1,)), D((fs_n - 1,))]


ANY = pl.BlockSpec(memory_space=pl.ANY)
VM = pl.BlockSpec(memory_space=pltpu.VMEM)


def swap_call(x, dp_n, fs_n, cid, space=ANY):
    def body(x_ref, o_ref, *sems):
        greet(dp_n, fs_n, False)
        s = Swap(fs_n, x_ref, o_ref, *sems)
        s.start()
        s.wait()

    return pl.pallas_call(
        body, out_shape=jax.ShapeDtypeStruct(x.shape, x.dtype), in_specs=[space], out_specs=space,
        scratch_shapes=swap_sems(fs_n),
        compiler_params=pltpu.CompilerParams(collective_id=cid, has_side_effects=True, vmem_limit_bytes=60 << 20),
        name="swap%d" % cid,
    )(x)


def gather_call(packs, dp_n, fs_n, cid, space=ANY):
    n = len(packs)

    def body(*refs):
        ins, outs, sems = refs[:n], refs[n:2 * n], refs[2 * n:]
        greet(dp_n, fs_n)
        gs = [Gather(dp_n, fs_n, ins[i], outs[i], *sems[7 * i:7 * i + 7]) for i in range(n)]
        for g in gs:
            g.start()
        for g in gs:
            g.forward_z()
        for g in gs:
            g.forward_d()
        for g in gs:
            g.wait()

    return pl.pallas_call(
        body,
        out_shape=[jax.ShapeDtypeStruct((dp_n, fs_n // 2, 2) + p.shape, p.dtype) for p in packs],
        in_specs=[space] * n, out_specs=[space] * n,
        scratch_shapes=gather_sems(dp_n, fs_n) * n,
        compiler_params=pltpu.CompilerParams(collective_id=cid, has_side_effects=True, vmem_limit_bytes=60 << 20),
        name="gather%d" % cid,
    )(*packs)


def scatter_call(g, dp_n, fs_n, cid):
    z_n = fs_n // 2
    rows, width = g.shape[3:]
    step = 16

    def body(g_ref, o_ref, from_c, half, from_d, quarter, from_z, cs, cr, ds, dr, zs, zr):
        me_d, me_f = lax.axis_index("dp"), lax.axis_index("fsdp")
        me_z, me_c = me_f // 2, mod(me_f, 2)
        greet(dp_n, fs_n)
        partner = (me_d, me_z * 2 + 1 - me_c)

        def add(out, parts):
            def one(i, _):
                at = pl.ds(pl.multiple_of(i * step, step), step)
                total = parts[0][at, :].astype(f32)
                for p in parts[1:]:
                    total = total + p[at, :].astype(f32)
                out[at, :] = total.astype(out.dtype)
                return 0
            lax.fori_loop(0, rows // step, one, 0, unroll=True if rows // step <= 4 else 4)

        order = [(j, k) for j in list(range(1, dp_n)) + [0] for k in list(range(1, z_n)) + [0]]
        cc, dd, zz = {}, {}, {}
        for i, (j, k) in enumerate(order):
            d, z = mod(me_d + j, dp_n), mod(me_z + k, z_n)
            cc[j, k] = rcopy(g_ref.at[d, z, 1 - me_c], from_c.at[i], cs.at[i], cr.at[i], partner)
            cc[j, k].start()
        for i, (j, k) in enumerate(order):
            d, z = mod(me_d + j, dp_n), mod(me_z + k, z_n)
            cc[j, k].wait_recv()
            add(half.at[j, k], [g_ref.at[d, z, me_c], from_c.at[i]])
            if j:
                n = (j - 1) * z_n + k
                dd[j, k] = rcopy(half.at[j, k], from_d.at[j - 1, k], ds.at[n], dr.at[n], (d, me_f))
                dd[j, k].start()
        for k in list(range(1, z_n)) + [0]:
            for j in range(1, dp_n):
                dd[j, k].wait_recv()
            if k:
                add(quarter.at[k], [half.at[0, k]] + [from_d.at[j - 1, k] for j in range(1, dp_n)])
                to = mod(me_z + k, z_n) * 2 + me_c
                zz[k] = rcopy(quarter.at[k], from_z.at[k - 1], zs.at[k - 1], zr.at[k - 1], (me_d, to))
                zz[k].start()
        for k in range(1, z_n):
            zz[k].wait_recv()
        add(o_ref, [half.at[0, 0]] + [from_d.at[j - 1, 0] for j in range(1, dp_n)] + [from_z.at[k - 1] for k in range(1, z_n)])
        for c in list(cc.values()) + list(dd.values()) + list(zz.values()):
            c.wait_send()

    D = pltpu.SemaphoreType.DMA
    n = dp_n * z_n
    return pl.pallas_call(
        body, out_shape=jax.ShapeDtypeStruct((rows, width), f32), in_specs=[VM], out_specs=VM,
        scratch_shapes=[
            pltpu.VMEM((n, rows, width), bf16), pltpu.VMEM((dp_n, z_n, rows, width), bf16),
            pltpu.VMEM((dp_n - 1, z_n, rows, width), bf16), pltpu.VMEM((z_n, rows, width), bf16),
            pltpu.VMEM((z_n - 1, rows, width), bf16),
            D((n,)), D((n,)), D((n - z_n,)), D((n - z_n,)), D((z_n - 1,)), D((z_n - 1,)),
        ],
        compiler_params=pltpu.CompilerParams(collective_id=cid, has_side_effects=True, vmem_limit_bytes=60 << 20),
        name="scatter%d" % cid,
    )(g)
HEADS = 8
EPS = 1e-05
MASKED = -1e30
NN = (((1,), (0,)), ((), ()))
NT = (((1,), (1,)), ((), ()))
TN = (((0,), (0,)), ((), ()))


def dot(a, b, dims=NN):
    return lax.dot_general(a, b, dims, preferred_element_type=f32)


def unit(x):
    c = x - jnp.mean(x, -1, keepdims=True)
    r = lax.rsqrt(jnp.mean(c * c, -1, keepdims=True) + EPS)
    return c * r, r


def unit_back(y, u, r, gain):
    yg = y * gain
    return r * (yg - jnp.mean(yg, -1, keepdims=True) - u * jnp.mean(yg * u, -1, keepdims=True))


def blocks(total, size, body):
    lax.fori_loop(0, total // size, lambda i, c: (body(pl.ds(pl.multiple_of(i * size, size), size)), c)[1], 0)


def gelu_parts(v):
    z = jnp.abs(v) * 0.7071067811865476
    t = 1.0 / (1.0 + 0.3275911 * z)
    e = jnp.exp(-0.5 * (v * v))
    tail = t * (0.127414796 + t * (-0.142248368 + t * (0.7107068705 + t * (-0.7265760135 + t * 0.5307027145)))) * e
    return jnp.where(v >= 0, 1.0 - tail, tail), v * e * 0.3989422804014327


def head_mask(rows, second, width=128):
    lane = lax.broadcasted_iota(jnp.int32, (rows, width), 1)
    return (lane >= width // 2) if second else (lane < width // 2)


def params(cid=None):
    if cid is None:
        return pltpu.CompilerParams(vmem_limit_bytes=62 << 20)
    return pltpu.CompilerParams(collective_id=cid, has_side_effects=True, vmem_limit_bytes=62 << 20)


BQ = 256


def sample_forward_call(xg, w, smalls, keybias):
    rows, d = xg.shape
    dh = w.shape[2]
    heads = dh // 64

    def body(x_ref, w_ref, n_ref, kb_ref, o_ref, qkv_ref, l_ref, vt, ot):
        gain, bias = n_ref[0:1, :], n_ref[1:2, :]

        def project(at):
            u, _ = unit(x_ref[at, :].astype(f32))
            a = (u * gain + bias).astype(bf16)
            for i in range(3):
                y = dot(a, w_ref[i]).astype(bf16)
                qkv_ref[i, at, :] = y * 0.125 if i == 0 else y

        blocks(rows, 256, project)

        def pair(p, _):
            at = pl.ds(pl.multiple_of(p * 128, 128), 128)
            vt[...] = qkv_ref[2, :, at].astype(f32).T.astype(bf16)
            for h in range(2):
                def part(i, _):
                    qa = pl.ds(pl.multiple_of(i * BQ, BQ), BQ)
                    q = qkv_ref[0, qa, at]
                    q = jnp.where(head_mask(BQ, h), q, jnp.zeros_like(q))
                    s = dot(qkv_ref[1, :, at], q, NT) + kb_ref[:, 0:1]
                    m = jnp.max(s, 0, keepdims=True)
                    e = jnp.exp(s - m)
                    tot = jnp.sum(e, 0, keepdims=True)
                    o = dot(vt[h * 64:h * 64 + 64, :], e.astype(bf16))
                    ot[h * 64:h * 64 + 64, qa] = o * (1.0 / tot)
                    l_ref[pl.ds(p * 2 + h, 1), qa] = m + jnp.log(tot)
                    return 0
                lax.fori_loop(0, rows // BQ, part, 0)
            o_ref[:, at] = ot[...].T.astype(bf16)
            return 0

        lax.fori_loop(0, heads // 2, pair, 0)

    return pl.pallas_call(
        body,
        out_shape=[jax.ShapeDtypeStruct((rows, dh), bf16), jax.ShapeDtypeStruct((3, rows, dh), bf16), jax.ShapeDtypeStruct((heads, rows), f32)],
        in_specs=[VM] * 4, out_specs=[VM] * 3,
        scratch_shapes=[pltpu.VMEM((128, rows), bf16), pltpu.VMEM((128, rows), f32)],
        compiler_params=params(), name="sample_forward",
    )(xg, w, smalls, keybias)


def sample_backward_call(xg, qkv, o, do, lse, w, smalls, keybias):
    rows, d = xg.shape
    dh = w.shape[2]
    heads = dh // 64

    def body(x_ref, qkv_ref, o_ref, do_ref, l_ref, w_ref, n_ref, kb_ref, dx_ref, gw_ref, gn_ref, delta, kt, dqt, dk, dv, dqkv, acted, gn):
        gain, bias = n_ref[0:1, :], n_ref[1:2, :]
        lane = lax.broadcasted_iota(jnp.int32, (heads, dh), 1) // 64
        pick = (lane == lax.broadcasted_iota(jnp.int32, (heads, dh), 0)).astype(f32)

        def deltas(at):
            prod = do_ref[at, :].astype(f32) * o_ref[at, :].astype(f32)
            delta[:, at] = lax.dot_general(pick, prod, NT, precision=lax.Precision.HIGHEST, preferred_element_type=f32)

        blocks(rows, 256, deltas)

        def pair(p, _):
            at = pl.ds(pl.multiple_of(p * 128, 128), 128)
            kt[...] = qkv_ref[1, :, at].astype(f32).T.astype(bf16)
            dk[...] = jnp.zeros_like(dk)
            dv[...] = jnp.zeros_like(dv)
            for h in range(2):
                def part(i, _):
                    qa = pl.ds(pl.multiple_of(i * BQ, BQ), BQ)
                    mask = head_mask(BQ, h)
                    q = qkv_ref[0, qa, at]
                    q = jnp.where(mask, q, jnp.zeros_like(q))
                    g = do_ref[qa, at]
                    g = jnp.where(mask, g, jnp.zeros_like(g))
                    row = pl.ds(p * 2 + h, 1)
                    s = dot(qkv_ref[1, :, at], q, NT) + kb_ref[:, 0:1]
                    e = jnp.exp(s - l_ref[row, qa])
                    ds = (e * (dot(qkv_ref[2, :, at], g, NT) - delta[row, qa])).astype(bf16)
                    dv[...] += dot(e.astype(bf16), g)
                    dk[...] += dot(ds, q)
                    dqt[h * 64:h * 64 + 64, qa] = dot(kt[h * 64:h * 64 + 64, :], ds) * 0.125
                    return 0
                lax.fori_loop(0, rows // BQ, part, 0)
            dqkv[0, :, at] = dqt[...].T.astype(bf16)
            dqkv[1, :, at] = dk[...].astype(bf16)
            dqkv[2, :, at] = dv[...].astype(bf16)
            return 0

        lax.fori_loop(0, heads // 2, pair, 0)
        gn[...] = jnp.zeros_like(gn)

        def back(at):
            u, r = unit(x_ref[at, :].astype(f32))
            acted[at, :] = (u * gain + bias).astype(bf16)
            y = dot(dqkv[0, at, :], w_ref[0], NT) + dot(dqkv[1, at, :], w_ref[1], NT) + dot(dqkv[2, at, :], w_ref[2], NT)
            gn[0:1, :] += jnp.sum(y * u, 0, keepdims=True)
            gn[1:2, :] += jnp.sum(y, 0, keepdims=True)
            dx_ref[at, :] = unit_back(y, u, r, gain).astype(bf16)

        blocks(rows, 256, back)
        for i in range(3):
            def weight(at):
                gw_ref[i, at, :] = dot(acted[:, at], dqkv[i], TN).astype(bf16)
            blocks(d, 256, weight)
        gn_ref[...] = gn[...]

    V = pltpu.VMEM
    return pl.pallas_call(
        body,
        out_shape=[jax.ShapeDtypeStruct((rows, d), bf16), jax.ShapeDtypeStruct((3, d, dh), bf16), jax.ShapeDtypeStruct((8, d), f32)],
        in_specs=[VM] * 8, out_specs=[VM] * 3,
        scratch_shapes=[V((heads, rows), f32), V((128, rows), bf16), V((128, rows), f32), V((rows, 128), f32), V((rows, 128), f32),
                        V((3, rows, dh), bf16), V((rows, d), bf16), V((8, d), f32)],
        compiler_params=params(), name="sample_backward",
    )(xg, qkv, o, do, lse, w, smalls, keybias)


def middle_call(x, o1, cot, smalls, fbias, w_so, w_f, w_fo, w_in, w_out):
    pairs, samples, d = x.shape
    tasks, n = fbias.shape[0], fbias.shape[1]
    feats = pairs // tasks
    sb = n // feats
    rows = pairs * samples
    chunks = w_in.shape[0]
    hh = d // 64
    x, o1, cot = (v.reshape(rows, d) for v in (x, o1, cot))
    RB = 256

    def body(x_ref, o1_ref, cot_ref, n_ref, fb_ref, wso, wf, wfo, win, wout,
             lo_ref, g1_ref, do1_ref, gso, gf, gfo, gin, gout, gn_ref,
             x1, a, qkv, p2, o2, acc, dacc, act, gh, dqkv, do2):
        gn_ref[...] = jnp.zeros_like(gn_ref)

        def norm(i):
            return n_ref[2 * i:2 * i + 1, :], n_ref[2 * i + 1:2 * i + 2, :]

        def first(at):
            y = x_ref[at, :].astype(f32) + dot(o1_ref[at, :], wso[...])
            x1[at, :] = y
            u, _ = unit(y)
            g, b = norm(1)
            v = (u * g + b).astype(bf16)
            a[at, :] = v
            for i in range(3):
                z = dot(v, wf[i]).astype(bf16)
                qkv[i, at, :] = z * 0.125 if i == 0 else z

        blocks(rows, RB, first)

        def group(ref, i, t, s, lanes):
            parts = [ref[i, pl.ds(pl.multiple_of((t * feats + f) * samples + s * sb, sb), sb), lanes] for f in range(feats)]
            return jnp.concatenate(parts, 0)

        def ungroup(ref, i, t, s, lanes, value):
            for f in range(feats):
                at = pl.ds(pl.multiple_of((t * feats + f) * samples + s * sb, sb), sb)
                part = value[f * sb:f * sb + sb]
                if i is None:
                    ref[at, lanes] = part
                else:
                    ref[i, at, lanes] = part

        nb = samples // sb

        def mix(i, _):
            t, s = i // nb, lax.rem(i, nb)
            for p in range(hh // 2):
                lanes = pl.ds(p * 128, 128)
                q, k, v = (group(qkv, j, t, s, lanes) for j in range(3))
                outs = []
                for h in range(2):
                    qm = jnp.where(head_mask(n, h), q, jnp.zeros_like(q))
                    sc = dot(qm, k, NT) + fb_ref[t]
                    e = jnp.exp(sc - jnp.max(sc, -1, keepdims=True))
                    e = e * (1.0 / jnp.sum(e, -1, keepdims=True))
                    p2[i, p * 2 + h] = e
                    outs.append(dot(e.astype(bf16), v))
                ungroup(o2, None, t, s, lanes, jnp.where(head_mask(n, 0), outs[0], outs[1]).astype(bf16))
            return 0

        lax.fori_loop(0, tasks * nb, mix, 0)

        def second(at):
            y = x1[at, :] + dot(o2[at, :], wfo[...])
            acc[at, :] = y
            u, _ = unit(y)
            g, b = norm(2)
            do2[at, :] = (u * g + b).astype(bf16)
            dacc[at, :] = jnp.zeros((RB, d), f32)

        blocks(rows, RB, second)

        def chunk(c, _):
            def part(at):
                hid = dot(do2[at, :], win[c]) + n_ref[pl.ds(7 + c, 1), :]
                cdf, pdf = gelu_parts(hid)
                al = (hid * cdf).astype(bf16)
                act[at, :] = al
                gl = ((cdf + pdf) * dot(cot_ref[at, :], wout[c], NT)).astype(bf16)
                gh[at, :] = gl
                gn_ref[pl.ds(7 + c, 1), :] += jnp.sum(gl.astype(f32), 0, keepdims=True)
                acc[at, :] += dot(al, wout[c])
                dacc[at, :] += dot(gl, win[c], NT)

            blocks(rows, RB, part)

            def weight(at):
                gout[c, at, :] = dot(act[:, at], cot_ref[...], TN).astype(bf16)
                gin[c, at, :] = dot(do2[:, at], gh[...], TN).astype(bf16)

            blocks(d, 256, weight)
            return 0

        lax.fori_loop(0, chunks, chunk, 0)

        def third(at):
            lo_ref[at, :] = (acc[at, :] + n_ref[6:7, :]).astype(bf16)
            u, r = unit(x1[at, :] + dot(o2[at, :], wfo[...]))
            y = dacc[at, :]
            gn_ref[4:5, :] += jnp.sum(y * u, 0, keepdims=True)
            gn_ref[5:6, :] += jnp.sum(y, 0, keepdims=True)
            cf = cot_ref[at, :].astype(f32)
            gn_ref[6:7, :] += jnp.sum(cf, 0, keepdims=True)
            g2 = cf + unit_back(y, u, r, norm(2)[0])
            dacc[at, :] = g2
            e2 = g2.astype(bf16)
            act[at, :] = e2
            do2[at, :] = dot(e2, wfo[...], NT).astype(bf16)

        blocks(rows, RB, third)

        def weight2(at):
            gfo[at, :] = dot(o2[:, at], act[...], TN).astype(bf16)

        blocks(d, 256, weight2)

        def unmix(i, _):
            t, s = i // nb, lax.rem(i, nb)
            for p in range(hh // 2):
                lanes = pl.ds(p * 128, 128)
                q, k, v = (group(qkv, j, t, s, lanes) for j in range(3))
                parts = [do2[pl.ds(pl.multiple_of((t * feats + f) * samples + s * sb, sb), sb), lanes] for f in range(feats)]
                g = jnp.concatenate(parts, 0)
                dq = []
                dk = dv = 0.0
                for h in range(2):
                    mask = head_mask(n, h)
                    qm = jnp.where(mask, q, jnp.zeros_like(q))
                    gm = jnp.where(mask, g, jnp.zeros_like(g))
                    e = p2[i, p * 2 + h]
                    dp = dot(gm, v, NT)
                    ds = (e * (dp - jnp.sum(e * dp, -1, keepdims=True))).astype(bf16)
                    dq.append(dot(ds, k))
                    dk += dot(ds, qm, TN)
                    dv += dot(e.astype(bf16), gm, TN)
                ungroup(dqkv, 0, t, s, lanes, (jnp.where(head_mask(n, 0), dq[0], dq[1]) * 0.125).astype(bf16))
                ungroup(dqkv, 1, t, s, lanes, dk.astype(bf16))
                ungroup(dqkv, 2, t, s, lanes, dv.astype(bf16))
            return 0

        lax.fori_loop(0, tasks * nb, unmix, 0)

        def fourth(at):
            u, r = unit(x1[at, :])
            y = dot(dqkv[0, at, :], wf[0], NT) + dot(dqkv[1, at, :], wf[1], NT) + dot(dqkv[2, at, :], wf[2], NT)
            gn_ref[2:3, :] += jnp.sum(y * u, 0, keepdims=True)
            gn_ref[3:4, :] += jnp.sum(y, 0, keepdims=True)
            g1 = dacc[at, :] + unit_back(y, u, r, norm(1)[0])
            g1_ref[at, :] = g1
            e1 = g1.astype(bf16)
            act[at, :] = e1
            do1_ref[at, :] = dot(e1, wso[...], NT).astype(bf16)

        blocks(rows, RB, fourth)

        def weight3(at):
            gso[at, :] = dot(o1_ref[:, at], act[...], TN).astype(bf16)
            for i in range(3):
                gf[i, at, :] = dot(a[:, at], dqkv[i], TN).astype(bf16)

        blocks(d, 256, weight3)

    V = pltpu.VMEM
    S = jax.ShapeDtypeStruct
    nblk = tasks * samples // sb
    return pl.pallas_call(
        body,
        out_shape=[S((rows, d), bf16), S((rows, d), f32), S((rows, d), bf16), S((d, d), bf16), S((3, d, d), bf16), S((d, d), bf16),
                   S((chunks, d, d), bf16), S((chunks, d, d), bf16), S((16, d), f32)],
        in_specs=[VM] * 10, out_specs=[VM] * 9,
        scratch_shapes=[V((rows, d), f32), V((rows, d), bf16), V((3, rows, d), bf16), V((nblk, hh, n, n), f32), V((rows, d), bf16),
                        V((rows, d), f32), V((rows, d), f32), V((rows, d), bf16), V((rows, d), bf16), V((3, rows, d), bf16), V((rows, d), bf16)],
        compiler_params=params(), name="middle",
    )(x, o1, cot, smalls, fbias, w_so, w_f, w_fo, w_in, w_out)
def up16(a):
    rows = a.shape[-2]
    extra = (-rows) % 16
    return a if extra == 0 else jnp.pad(a, [(0, 0)] * (a.ndim - 2) + [(0, extra), (0, 0)])


def local(tokens, sample_counts, feature_counts, norms, sample_qkv, sample_out, feature_qkv, feature_out, mlp_in, mlp_in_bias,
          mlp_out, mlp_out_bias, cotangent):
    dp_n, fs_n = lax.axis_size("dp"), lax.axis_size("fsdp")
    nd = dp_n * fs_n
    me_d, me_f = lax.axis_index("dp"), lax.axis_index("fsdp")
    me = me_d * fs_n + me_f
    tasks, samples, feats, d = tokens.shape
    pairs = tasks * feats
    rep = fs_n // pairs
    dh = d // rep
    rl = sample_out.shape[0]
    ff = rl * nd * mlp_in.shape[1] // d
    chunks = mlp_in.shape[1] // d
    fl = mlp_out.shape[0]
    total = samples * fs_n

    small = jnp.zeros((16, d), bf16)
    small = lax.dynamic_update_slice(small, norms, (0, me * rl))
    small = lax.dynamic_update_slice(small, mlp_out_bias[None, :], (6, me * rl))
    small = lax.dynamic_update_slice(small, mlp_in_bias[None, :], (7 + (me * fl) // d, lax.rem(me * fl, d)))
    split_in = mlp_in.reshape(rl, chunks, d).transpose(1, 0, 2).reshape(chunks * rl, d)
    pack_a = up16(jnp.concatenate([small, sample_qkv.reshape(3 * rl, d)], 0))
    pack_b = up16(jnp.concatenate([sample_out, feature_qkv.reshape(3 * rl, d), feature_out, split_in, mlp_out], 0))

    xp = tokens.transpose(0, 2, 1, 3).reshape(pairs, samples, d)
    cp = cotangent.transpose(0, 2, 1, 3).reshape(pairs, samples, d)
    xg = swap_call(jnp.repeat(xp, rep, 0) if rep > 1 else xp, dp_n, fs_n, 1)
    ga, gb = gather_call([pack_a, pack_b], dp_n, fs_n, 2)
    ga, gb = ga.reshape((nd,) + ga.shape[3:]), gb.reshape((nd,) + gb.shape[3:])

    def take(g, start, parts, size):
        v = g[:, start:start + parts * size].reshape(nd, parts, size, d).transpose(1, 0, 2, 3)
        return v.reshape(parts, nd * size, d)

    smalls = jnp.sum(ga[:, :16].astype(f32), 0)
    w_s = take(ga, 16, 3, rl)
    w_so = take(gb, 0, 1, rl)[0]
    w_f = take(gb, rl, 3, rl)
    w_fo = take(gb, 4 * rl, 1, rl)[0]
    w_in = take(gb, 5 * rl, chunks, rl)
    w_out = take(gb, (5 + chunks) * rl, 1, fl).reshape(chunks, d, d)
    first = lax.rem(me_f, rep) * dh
    w_mine = lax.dynamic_slice_in_dim(w_s, first, dh, 2) if rep > 1 else w_s
    my_task = me_f // rep // feats
    count = lax.dynamic_index_in_dim(sample_counts, my_task, keepdims=False)
    keybias = jnp.broadcast_to(jnp.where(jnp.arange(total) < count, 0.0, MASKED).astype(f32)[:, None], (total, 128))
    sb = 32
    place = jnp.arange(feats * sb)
    same = (place[:, None] % sb) == (place[None, :] % sb)
    shown = (place[None, :] // sb) < feature_counts[:, None]
    fbias = jnp.where(same[None] & shown[:, None, :], 0.0, MASKED).astype(f32)

    xg = xg.reshape(total, d)
    o1, qkv, lse = sample_forward_call(xg, w_mine, smalls, keybias)
    back = swap_call(o1.reshape(fs_n, samples, dh), dp_n, fs_n, 3)
    o1r = back.reshape(pairs, rep, samples, dh).transpose(0, 2, 1, 3).reshape(pairs, samples, d)
    lo, g1, do1, gso, gf, gfo, gin, gout, gn_m = middle_call(xp, o1r, cp, smalls, fbias, w_so, w_f, w_fo, w_in, w_out)
    do1 = do1.reshape(pairs, samples, rep, dh).transpose(0, 2, 1, 3).reshape(fs_n, samples, dh)
    dog = swap_call(do1, dp_n, fs_n, 4).reshape(total, dh)
    dx, gs, gn_s = sample_backward_call(xg, qkv, o1, dog, lse, w_mine, smalls, keybias)
    dxr = swap_call(dx.reshape(fs_n, samples, d), dp_n, fs_n, 5)
    dxr = jnp.sum(dxr.reshape(pairs, rep, samples, d).astype(f32), 1)
    tokens_grad = (g1.reshape(pairs, samples, d) + dxr).reshape(tasks, feats, samples, d).transpose(0, 2, 1, 3)
    layer_output = lo.reshape(tasks, feats, samples, d).transpose(0, 2, 1, 3)
    if rep > 1:
        gs = lax.dynamic_update_slice_in_dim(jnp.zeros((3, d, d), bf16), gs, first, 2)
    gn = jnp.concatenate([gn_s[0:2], gn_m[2:]], 0).astype(bf16)

    def give(g, parts, size):
        return g.reshape(parts, nd, size, d).transpose(1, 0, 2, 3).reshape(nd, parts * size, d)

    grads = up16(jnp.concatenate([
        jnp.broadcast_to(gn[None], (nd, 16, d)), give(gs, 3, rl), give(gso, 1, rl), give(gf, 3, rl), give(gfo, 1, rl),
        give(gin, chunks, rl), give(gout.reshape(1, -1, d), 1, fl)], 1))
    s = scatter_call(grads.reshape((dp_n, fs_n // 2, 2) + grads.shape[1:]), dp_n, fs_n, 6)
    at = 16
    outs = []
    for parts, size in ((3, rl), (1, rl), (3, rl), (1, rl), (chunks, rl), (1, fl)):
        outs.append(s[at:at + parts * size].reshape(parts, size, d))
        at += parts * size
    sg = s[:16]
    return (
        layer_output,
        tokens_grad,
        lax.dynamic_slice(sg, (0, me * rl), (6, rl)),
        outs[0], outs[1][0], outs[2], outs[3][0],
        outs[4].transpose(1, 0, 2).reshape(rl, chunks * d),
        lax.dynamic_slice(sg[7:7 + chunks].reshape(-1), (me * fl,), (fl,)),
        outs[5][0],
        lax.dynamic_slice(sg[6], (me * rl,), (rl,)),
    )


def solution(mesh):
    rows, whole = ("dp", "fsdp"), P("dp", "fsdp", None, None)
    weights = (P(None, rows), P(None, rows, None), P(rows, None), P(None, rows, None), P(rows, None), P(rows, None), P(rows),
               P(rows, None), P(rows))
    return jax.shard_map(local, mesh=mesh, in_specs=(whole, P("dp"), P("dp")) + weights + (whole,),
                         out_specs=(whole, whole) + weights, check_vma=False)
```

```python
import functools
import jax
import jax.numpy as jnp
from jax import lax
from jax.experimental import pallas as pl
from jax.experimental.pallas import tpu as pltpu
from jax.sharding import PartitionSpec as P

MESH = pl.DeviceIdType.MESH
f32, bf16 = jnp.float32, jnp.bfloat16


def mod(a, n):
    return lax.rem(a, n)


def greet(dp_n, fs_n, with_dp=True):
    me_d, me_f = lax.axis_index("dp"), lax.axis_index("fsdp")
    barrier = pltpu.get_barrier_semaphore()
    n = 0
    for k in range(1, fs_n):
        pl.semaphore_signal(barrier, inc=1, device_id=(me_d, mod(me_f + k, fs_n)), device_id_type=MESH)
        n += 1
    if with_dp:
        for k in range(1, dp_n):
            pl.semaphore_signal(barrier, inc=1, device_id=(mod(me_d + k, dp_n), me_f), device_id_type=MESH)
            n += 1
    pl.semaphore_wait(barrier, n)


def rcopy(src, dst, ss, rs, dev):
    return pltpu.make_async_remote_copy(src_ref=src, dst_ref=dst, send_sem=ss, recv_sem=rs, device_id=dev, device_id_type=MESH)


class Swap:
    def __init__(self, fs_n, src, dst, local_sem, ss, rs):
        me_d, me_f = lax.axis_index("dp"), lax.axis_index("fsdp")
        self.own = pltpu.make_async_copy(src.at[me_f], dst.at[me_f], local_sem)
        self.copies = []
        for k in range(1, fs_n):
            to = mod(me_f + k, fs_n)
            self.copies.append(rcopy(src.at[to], dst.at[me_f], ss.at[k - 1], rs.at[k - 1], (me_d, to)))

    def start(self):
        for c in self.copies:
            c.start()
        self.own.start()

    def wait(self):
        self.own.wait()
        for c in self.copies:
            c.wait()


class Gather:
    def __init__(self, dp_n, fs_n, src, dst, local_sem, zs, zr, ds, dr, cs, cr):
        me_d, me_f = lax.axis_index("dp"), lax.axis_index("fsdp")
        z_n = fs_n // 2
        me_z, me_c = me_f // 2, mod(me_f, 2)
        self.z_n, self.dp_n = z_n, dp_n
        partner = (me_d, me_z * 2 + 1 - me_c)
        self.own = pltpu.make_async_copy(src, dst.at[me_d, me_z, me_c], local_sem)
        self.z = []
        for k in range(1, z_n):
            to = mod(me_z + k, z_n) * 2 + me_c
            self.z.append(rcopy(src, dst.at[me_d, me_z, me_c], zs.at[k - 1], zr.at[k - 1], (me_d, to)))
        self.d = {}
        self.c = {}
        for k in range(z_n):
            z = mod(me_z - k + z_n, z_n)
            for j in range(dp_n):
                d = mod(me_d - j + dp_n, dp_n)
                here = src if (k == 0 and j == 0) else dst.at[d, z, me_c]
                self.c[k, j] = rcopy(here, dst.at[d, z, me_c], cs.at[k * dp_n + j], cr.at[k * dp_n + j], partner)
                if j > 0:
                    here = src if k == 0 else dst.at[me_d, z, me_c]
                    i = k * (dp_n - 1) + j - 1
                    self.d[k, j] = rcopy(here, dst.at[me_d, z, me_c], ds.at[i], dr.at[i], (mod(me_d + j, dp_n), me_f))

    def start(self):
        for c in self.z:
            c.start()
        self.own.start()
        for j in range(1, self.dp_n):
            self.d[0, j].start()
        self.c[0, 0].start()

    def forward_z(self):
        for k in range(1, self.z_n):
            self.z[k - 1].wait_recv()
            for j in range(1, self.dp_n):
                self.d[k, j].start()
            self.c[k, 0].start()

    def forward_d(self):
        for k in range(self.z_n):
            for j in range(1, self.dp_n):
                self.d[k, j].wait_recv()
                self.c[k, j].start()

    def wait(self):
        self.own.wait()
        for c in self.z:
            c.wait_send()
        for c in self.d.values():
            c.wait_send()
        for c in self.c.values():
            c.wait()


def gather_sems(dp_n, fs_n):
    z = fs_n // 2
    D = pltpu.SemaphoreType.DMA
    return [D, D((z - 1,)), D((z - 1,)), D((z * (dp_n - 1),)), D((z * (dp_n - 1),)), D((z * dp_n,)), D((z * dp_n,))]


def swap_sems(fs_n):
    D = pltpu.SemaphoreType.DMA
    return [D, D((fs_n - 1,)), D((fs_n - 1,))]


ANY = pl.BlockSpec(memory_space=pl.ANY)
VM = pl.BlockSpec(memory_space=pltpu.VMEM)


def swap_call(x, dp_n, fs_n, cid, space=ANY):
    def body(x_ref, o_ref, *sems):
        greet(dp_n, fs_n, False)
        s = Swap(fs_n, x_ref, o_ref, *sems)
        s.start()
        s.wait()

    return pl.pallas_call(
        body, out_shape=jax.ShapeDtypeStruct(x.shape, x.dtype), in_specs=[space], out_specs=space,
        scratch_shapes=swap_sems(fs_n),
        compiler_params=pltpu.CompilerParams(collective_id=cid, has_side_effects=True, vmem_limit_bytes=60 << 20),
        name="swap%d" % cid,
    )(x)


def gather_call(packs, dp_n, fs_n, cid, space=ANY):
    n = len(packs)

    def body(*refs):
        ins, outs, sems = refs[:n], refs[n:2 * n], refs[2 * n:]
        greet(dp_n, fs_n)
        gs = [Gather(dp_n, fs_n, ins[i], outs[i], *sems[7 * i:7 * i + 7]) for i in range(n)]
        for g in gs:
            g.start()
        for g in gs:
            g.forward_z()
        for g in gs:
            g.forward_d()
        for g in gs:
            g.wait()

    return pl.pallas_call(
        body,
        out_shape=[jax.ShapeDtypeStruct((dp_n, fs_n // 2, 2) + p.shape, p.dtype) for p in packs],
        in_specs=[space] * n, out_specs=[space] * n,
        scratch_shapes=gather_sems(dp_n, fs_n) * n,
        compiler_params=pltpu.CompilerParams(collective_id=cid, has_side_effects=True, vmem_limit_bytes=60 << 20),
        name="gather%d" % cid,
    )(*packs)


def scatter_call(g, dp_n, fs_n, cid):
    z_n = fs_n // 2
    rows, width = g.shape[3:]
    step = 16

    def body(g_ref, o_ref, from_c, half, from_d, quarter, from_z, cs, cr, ds, dr, zs, zr):
        me_d, me_f = lax.axis_index("dp"), lax.axis_index("fsdp")
        me_z, me_c = me_f // 2, mod(me_f, 2)
        greet(dp_n, fs_n)
        partner = (me_d, me_z * 2 + 1 - me_c)

        def add(out, parts):
            def one(i, _):
                at = pl.ds(pl.multiple_of(i * step, step), step)
                total = parts[0][at, :].astype(f32)
                for p in parts[1:]:
                    total = total + p[at, :].astype(f32)
                out[at, :] = total.astype(out.dtype)
                return 0
            lax.fori_loop(0, rows // step, one, 0, unroll=True if rows // step <= 4 else 4)

        order = [(j, k) for j in list(range(1, dp_n)) + [0] for k in list(range(1, z_n)) + [0]]
        cc, dd, zz = {}, {}, {}
        for i, (j, k) in enumerate(order):
            d, z = mod(me_d + j, dp_n), mod(me_z + k, z_n)
            cc[j, k] = rcopy(g_ref.at[d, z, 1 - me_c], from_c.at[i], cs.at[i], cr.at[i], partner)
            cc[j, k].start()
        for i, (j, k) in enumerate(order):
            d, z = mod(me_d + j, dp_n), mod(me_z + k, z_n)
            cc[j, k].wait_recv()
            add(half.at[j, k], [g_ref.at[d, z, me_c], from_c.at[i]])
            if j:
                n = (j - 1) * z_n + k
                dd[j, k] = rcopy(half.at[j, k], from_d.at[j - 1, k], ds.at[n], dr.at[n], (d, me_f))
                dd[j, k].start()
        for k in list(range(1, z_n)) + [0]:
            for j in range(1, dp_n):
                dd[j, k].wait_recv()
            if k:
                add(quarter.at[k], [half.at[0, k]] + [from_d.at[j - 1, k] for j in range(1, dp_n)])
                to = mod(me_z + k, z_n) * 2 + me_c
                zz[k] = rcopy(quarter.at[k], from_z.at[k - 1], zs.at[k - 1], zr.at[k - 1], (me_d, to))
                zz[k].start()
        for k in range(1, z_n):
            zz[k].wait_recv()
        add(o_ref, [half.at[0, 0]] + [from_d.at[j - 1, 0] for j in range(1, dp_n)] + [from_z.at[k - 1] for k in range(1, z_n)])
        for c in list(cc.values()) + list(dd.values()) + list(zz.values()):
            c.wait_send()

    D = pltpu.SemaphoreType.DMA
    n = dp_n * z_n
    return pl.pallas_call(
        body, out_shape=jax.ShapeDtypeStruct((rows, width), f32), in_specs=[VM], out_specs=VM,
        scratch_shapes=[
            pltpu.VMEM((n, rows, width), bf16), pltpu.VMEM((dp_n, z_n, rows, width), bf16),
            pltpu.VMEM((dp_n - 1, z_n, rows, width), bf16), pltpu.VMEM((z_n, rows, width), bf16),
            pltpu.VMEM((z_n - 1, rows, width), bf16),
            D((n,)), D((n,)), D((n - z_n,)), D((n - z_n,)), D((z_n - 1,)), D((z_n - 1,)),
        ],
        compiler_params=pltpu.CompilerParams(collective_id=cid, has_side_effects=True, vmem_limit_bytes=60 << 20),
        name="scatter%d" % cid,
    )(g)
HEADS = 8
EPS = 1e-05
MASKED = -1e30
NN = (((1,), (0,)), ((), ()))
NT = (((1,), (1,)), ((), ()))
TN = (((0,), (0,)), ((), ()))


def dot(a, b, dims=NN):
    return lax.dot_general(a, b, dims, preferred_element_type=f32)


def unit(x):
    c = x - jnp.mean(x, -1, keepdims=True)
    r = lax.rsqrt(jnp.mean(c * c, -1, keepdims=True) + EPS)
    return c * r, r


def unit_back(y, u, r, gain):
    yg = y * gain
    return r * (yg - jnp.mean(yg, -1, keepdims=True) - u * jnp.mean(yg * u, -1, keepdims=True))


def blocks(total, size, body):
    lax.fori_loop(0, total // size, lambda i, c: (body(pl.ds(pl.multiple_of(i * size, size), size)), c)[1], 0)


def gelu_parts(v):
    z = jnp.abs(v) * 0.7071067811865476
    t = 1.0 / (1.0 + 0.3275911 * z)
    e = jnp.exp(-0.5 * (v * v))
    tail = t * (0.127414796 + t * (-0.142248368 + t * (0.7107068705 + t * (-0.7265760135 + t * 0.5307027145)))) * e
    return jnp.where(v >= 0, 1.0 - tail, tail), v * e * 0.3989422804014327


def head_mask(rows, second, width=128):
    lane = lax.broadcasted_iota(jnp.int32, (rows, width), 1)
    return (lane >= width // 2) if second else (lane < width // 2)


def params(cid=None):
    if cid is None:
        return pltpu.CompilerParams(vmem_limit_bytes=62 << 20)
    return pltpu.CompilerParams(collective_id=cid, has_side_effects=True, vmem_limit_bytes=62 << 20)


BQ = 256


def middle_call(x, o1, cot, smalls, fbias, w, chunks, unit_rows):
    pairs, samples, d = x.shape
    tasks, n = fbias.shape[0], fbias.shape[1]
    feats = pairs // tasks
    sb = n // feats
    rows = pairs * samples
    hh = d // 64
    nd = w.shape[0]
    U = unit_rows
    OUT = (5 + chunks) * U
    fl = chunks * d // nd
    x, cot = x.reshape(rows, d), cot.reshape(rows, d)
    RB = 256
    per = RB // samples

    def body(x_ref, back_ref, cot_ref, n_ref, fb_ref, w_ref,
             lo_ref, g1_ref, do1_ref, g_ref,
             x1, a, qkv, p2, o2, acc, dacc, act, gh, dqkv, do2, o1_ref, gn_ref):
        gn_ref[...] = jnp.zeros_like(gn_ref)

        def at_unit(k):
            return pl.ds(pl.multiple_of(k * U, 16), U) if not isinstance(k, int) else slice(k * U, k * U + U)

        def mat(k):
            return w_ref[:, at_unit(k), :].reshape(d, d)

        def out_mat(c):
            if nd == 1:
                return w_ref[0, pl.ds(pl.multiple_of(OUT + c * d, 16), d), :]
            m = nd // chunks
            return w_ref[pl.ds(c * m, m), OUT:OUT + fl, :].reshape(d, d)

        def put(k, at, i, value):
            if nd == 1:
                g_ref[0, pl.ds(pl.multiple_of(16 + k * U + i * 256, 16), 256), :] = value
            else:
                m = 256 // U
                g_ref[pl.ds(i * m, m), pl.ds(pl.multiple_of(16 + k * U, 16), U), :] = value.reshape(m, U, d)

        def put_out(c, i, value):
            if nd == 1:
                g_ref[0, pl.ds(pl.multiple_of(16 + OUT + c * d + i * 256, 16), 256), :] = value
            else:
                m = 256 // fl
                g_ref[pl.ds(c * (nd // chunks) + i * m, m), 16 + OUT:16 + OUT + fl, :] = value.reshape(m, fl, d)

        def tiles(body):
            for i in range(d // 256):
                body(slice(i * 256, i * 256 + 256), i)

        def norm(i):
            return n_ref[2 * i:2 * i + 1, :], n_ref[2 * i + 1:2 * i + 2, :]

        def collect(i, _):
            at = pl.ds(pl.multiple_of(i * RB, RB), RB)
            for p in range(hh // 2):
                o1_ref[at, p * 128:p * 128 + 128] = back_ref[pl.ds(i * per, per), p].reshape(RB, 128)
            return 0

        lax.fori_loop(0, rows // RB, collect, 0)

        def first(at):
            y = x_ref[at, :].astype(f32) + dot(o1_ref[at, :], mat(0))
            x1[at, :] = y
            u, _ = unit(y)
            g, b = norm(1)
            v = (u * g + b).astype(bf16)
            a[at, :] = v
            for i in range(3):
                z = dot(v, mat(1 + i)).astype(bf16)
                qkv[i, at, :] = z * 0.125 if i == 0 else z

        blocks(rows, RB, first)

        def group(ref, i, t, s, lanes):
            parts = [ref[i, pl.ds(pl.multiple_of((t * feats + f) * samples + s * sb, sb), sb), lanes] for f in range(feats)]
            return jnp.concatenate(parts, 0)

        def ungroup(ref, i, t, s, lanes, value):
            for f in range(feats):
                at = pl.ds(pl.multiple_of((t * feats + f) * samples + s * sb, sb), sb)
                part = value[f * sb:f * sb + sb]
                if i is None:
                    ref[at, lanes] = part
                else:
                    ref[i, at, lanes] = part

        nb = samples // sb

        def mix(i, _):
            t, s = i // nb, lax.rem(i, nb)
            for p in range(hh // 2):
                lanes = pl.ds(p * 128, 128)
                q, k, v = (group(qkv, j, t, s, lanes) for j in range(3))
                outs = []
                for h in range(2):
                    qm = jnp.where(head_mask(n, h), q, jnp.zeros_like(q))
                    sc = dot(qm, k, NT) + fb_ref[t]
                    e = jnp.exp(sc - jnp.max(sc, -1, keepdims=True))
                    e = e * (1.0 / jnp.sum(e, -1, keepdims=True))
                    p2[i, p * 2 + h] = e
                    outs.append(dot(e.astype(bf16), v))
                ungroup(o2, None, t, s, lanes, jnp.where(head_mask(n, 0), outs[0], outs[1]).astype(bf16))
            return 0

        lax.fori_loop(0, tasks * nb, mix, 0)

        def second(at):
            y = x1[at, :] + dot(o2[at, :], mat(4))
            acc[at, :] = y
            u, _ = unit(y)
            g, b = norm(2)
            do2[at, :] = (u * g + b).astype(bf16)
            dacc[at, :] = jnp.zeros((RB, d), f32)

        blocks(rows, RB, second)

        def chunk(c, _):
            def part(at):
                hid = dot(do2[at, :], mat(5 + c)) + n_ref[pl.ds(7 + c, 1), :]
                cdf, pdf = gelu_parts(hid)
                al = (hid * cdf).astype(bf16)
                act[at, :] = al
                gl = ((cdf + pdf) * dot(cot_ref[at, :], out_mat(c), NT)).astype(bf16)
                gh[at, :] = gl
                gn_ref[pl.ds(7 + c, 1), :] += jnp.sum(gl.astype(f32), 0, keepdims=True)
                acc[at, :] += dot(al, out_mat(c))
                dacc[at, :] += dot(gl, mat(5 + c), NT)

            blocks(rows, RB, part)

            def weight(at, i):
                put_out(c, i, dot(act[:, at], cot_ref[...], TN).astype(bf16))
                put(5 + c, at, i, dot(do2[:, at], gh[...], TN).astype(bf16))

            tiles(weight)
            return 0

        lax.fori_loop(0, chunks, chunk, 0)

        def third(at):
            lo_ref[at, :] = (acc[at, :] + n_ref[6:7, :]).astype(bf16)
            u, r = unit(x1[at, :] + dot(o2[at, :], mat(4)))
            y = dacc[at, :]
            gn_ref[4:5, :] += jnp.sum(y * u, 0, keepdims=True)
            gn_ref[5:6, :] += jnp.sum(y, 0, keepdims=True)
            cf = cot_ref[at, :].astype(f32)
            gn_ref[6:7, :] += jnp.sum(cf, 0, keepdims=True)
            g2 = cf + unit_back(y, u, r, norm(2)[0])
            dacc[at, :] = g2
            e2 = g2.astype(bf16)
            act[at, :] = e2
            do2[at, :] = dot(e2, mat(4), NT).astype(bf16)

        blocks(rows, RB, third)

        def weight2(at, i):
            put(4, at, i, dot(o2[:, at], act[...], TN).astype(bf16))

        tiles(weight2)

        def unmix(i, _):
            t, s = i // nb, lax.rem(i, nb)
            for p in range(hh // 2):
                lanes = pl.ds(p * 128, 128)
                q, k, v = (group(qkv, j, t, s, lanes) for j in range(3))
                parts = [do2[pl.ds(pl.multiple_of((t * feats + f) * samples + s * sb, sb), sb), lanes] for f in range(feats)]
                g = jnp.concatenate(parts, 0)
                dq = []
                dk = dv = 0.0
                for h in range(2):
                    mask = head_mask(n, h)
                    qm = jnp.where(mask, q, jnp.zeros_like(q))
                    gm = jnp.where(mask, g, jnp.zeros_like(g))
                    e = p2[i, p * 2 + h]
                    dp = dot(gm, v, NT)
                    ds = (e * (dp - jnp.sum(e * dp, -1, keepdims=True))).astype(bf16)
                    dq.append(dot(ds, k))
                    dk += dot(ds, qm, TN)
                    dv += dot(e.astype(bf16), gm, TN)
                ungroup(dqkv, 0, t, s, lanes, (jnp.where(head_mask(n, 0), dq[0], dq[1]) * 0.125).astype(bf16))
                ungroup(dqkv, 1, t, s, lanes, dk.astype(bf16))
                ungroup(dqkv, 2, t, s, lanes, dv.astype(bf16))
            return 0

        lax.fori_loop(0, tasks * nb, unmix, 0)

        def fourth(i, _):
            at = pl.ds(pl.multiple_of(i * RB, RB), RB)
            u, r = unit(x1[at, :])
            y = dot(dqkv[0, at, :], mat(1), NT) + dot(dqkv[1, at, :], mat(2), NT) + dot(dqkv[2, at, :], mat(3), NT)
            gn_ref[2:3, :] += jnp.sum(y * u, 0, keepdims=True)
            gn_ref[3:4, :] += jnp.sum(y, 0, keepdims=True)
            g1 = dacc[at, :] + unit_back(y, u, r, norm(1)[0])
            g1_ref[at, :] = g1
            e1 = g1.astype(bf16)
            act[at, :] = e1
            do = dot(e1, mat(0), NT).astype(bf16)
            for p in range(hh // 2):
                do1_ref[pl.ds(i * per, per), p] = do[:, p * 128:p * 128 + 128].reshape(per, samples, 128)
            return 0

        lax.fori_loop(0, rows // RB, fourth, 0)

        def weight3(at, i):
            put(0, at, i, dot(o1_ref[:, at], act[...], TN).astype(bf16))
            for j in range(3):
                put(1 + j, at, i, dot(a[:, at], dqkv[j], TN).astype(bf16))

        tiles(weight3)
        g_ref[:, 0:16, :] = jnp.broadcast_to(gn_ref[...].astype(bf16), (nd, 16, d))

    V = pltpu.VMEM
    S = jax.ShapeDtypeStruct
    nblk = tasks * samples // sb
    return pl.pallas_call(
        body,
        out_shape=[S((rows, d), bf16), S((rows, d), f32), S((pairs, hh // 2, samples, 128), bf16),
                   S((nd, 16 + OUT + fl, d), bf16)],
        in_specs=[VM] * 6, out_specs=[VM] * 4,
        scratch_shapes=[V((rows, d), f32), V((rows, d), bf16), V((3, rows, d), bf16), V((nblk, hh, n, n), f32), V((rows, d), bf16),
                        V((rows, d), f32), V((rows, d), f32), V((rows, d), bf16), V((rows, d), bf16), V((3, rows, d), bf16),
                        V((rows, d), bf16), V((rows, d), bf16), V((16, d), f32)],
        compiler_params=params(), name="middle",
    )(x, o1, cot, smalls, fbias, w)
class Turns:
    def __init__(self, fs_n, parts, src, dst, local_sem, ss, rs):
        me_d, me_f = lax.axis_index("dp"), lax.axis_index("fsdp")
        self.sets = []
        for p in range(parts):
            own = pltpu.make_async_copy(src(p, me_f), dst(p, me_f), local_sem.at[p])
            far = []
            for k in range(1, fs_n):
                to = mod(me_f + k, fs_n)
                i = p * (fs_n - 1) + k - 1
                far.append(rcopy(src(p, to), dst(p, me_f), ss.at[i], rs.at[i], (me_d, to)))
            self.sets.append((own, far))

    def start(self, p):
        own, far = self.sets[p]
        for c in far:
            c.start()
        own.start()

    def wait_recv(self, p):
        own, far = self.sets[p]
        own.wait()
        for c in far:
            c.wait_recv()

    def wait_send(self):
        for _, far in self.sets:
            for c in far:
                c.wait_send()


def turn_sems(fs_n, parts):
    D = pltpu.SemaphoreType.DMA
    return [D((parts,)), D((parts * (fs_n - 1),)), D((parts * (fs_n - 1),))]


class Reduce:
    def __init__(self, dp_n, fs_n, g, bufs, sems):
        me_d, me_f = lax.axis_index("dp"), lax.axis_index("fsdp")
        z_n = fs_n // 2
        me_z, me_c = me_f // 2, mod(me_f, 2)
        self.dp_n, self.z_n, self.g = dp_n, z_n, g
        self.from_c, self.half, self.from_d, self.quarter, self.from_z = bufs
        cs, cr, ds, dr, zs, zr = sems
        self.rows = g.shape[3]
        self.at = lambda j, k, c: g.at[mod(me_d + j, dp_n), mod(me_z + k, z_n), c]
        self.me_c = me_c
        partner = (me_d, me_z * 2 + 1 - me_c)
        self.js = list(range(1, dp_n)) + [0]
        self.ks = list(range(1, z_n)) + [0]
        self.c, self.d, self.z = {}, {}, {}
        for j in self.js:
            for k in self.ks:
                i = j * z_n + k
                self.c[j, k] = rcopy(self.at(j, k, 1 - me_c), self.from_c.at[j, k], cs.at[i], cr.at[i], partner)
            if j:
                self.d[j] = rcopy(self.half.at[j], self.from_d.at[j - 1], ds.at[j - 1], dr.at[j - 1], (mod(me_d + j, dp_n), me_f))
        for k in range(1, z_n):
            to = mod(me_z + k, z_n) * 2 + me_c
            self.z[k] = rcopy(self.quarter.at[k], self.from_z.at[k - 1], zs.at[k - 1], zr.at[k - 1], (me_d, to))

    def add(self, out, parts):
        step = 16

        def one(i, _):
            at = pl.ds(pl.multiple_of(i * step, step), step)
            total = parts[0][at, :].astype(f32)
            for p in parts[1:]:
                total = total + p[at, :].astype(f32)
            out[at, :] = total.astype(out.dtype)
            return 0

        n = self.rows // step
        lax.fori_loop(0, n, one, 0, unroll=2 if n % 2 == 0 else 1)

    def core(self):
        for j in self.js:
            for k in self.ks:
                self.c[j, k].start()

    def halve(self, js=None):
        for j in self.js if js is None else js:
            for k in self.ks:
                self.c[j, k].wait_recv()
                self.add(self.half.at[j, k], [self.at(j, k, self.me_c), self.from_c.at[j, k]])
            if j:
                self.d[j].start()

    def plane(self):
        for j in range(1, self.dp_n):
            self.d[j].wait_recv()
        for k in self.ks:
            if k:
                self.add(self.quarter.at[k], [self.half.at[0, k]] + [self.from_d.at[j - 1, k] for j in range(1, self.dp_n)])
                self.z[k].start()

    def finish(self, out):
        for k in range(1, self.z_n):
            self.z[k].wait_recv()
        self.add(out, [self.half.at[0, 0]] + [self.from_d.at[j - 1, 0] for j in range(1, self.dp_n)]
                 + [self.from_z.at[k - 1] for k in range(1, self.z_n)])
        for c in list(self.c.values()) + list(self.d.values()) + list(self.z.values()):
            c.wait_send()


def reduce_scratch(dp_n, fs_n, rows, width):
    z_n = fs_n // 2
    V, D = pltpu.VMEM, pltpu.SemaphoreType.DMA
    return [V((dp_n, z_n, rows, width), bf16), V((dp_n, z_n, rows, width), bf16), V((dp_n - 1, z_n, rows, width), bf16),
            V((z_n, rows, width), bf16), V((z_n - 1, rows, width), bf16),
            D((dp_n * z_n,)), D((dp_n * z_n,)), D((dp_n - 1,)), D((dp_n - 1,)), D((z_n - 1,)), D((z_n - 1,))]


def units(ref, start, size):
    v = ref[..., start:start + size, :]
    return v.reshape(-1, v.shape[-1])


def head_pair(p):
    return slice(p * 128, p * 128 + 128)


def forward_kernel(x, packs, plain, keybias, dp_n, fs_n, rl, dh):
    slots, samples, d = x.shape
    rows = slots * samples
    heads = dh // 64
    hp = heads // 2
    np_ = len(packs)

    def body(*refs):
        it = iter(refs)
        x_ref, kb_ref = next(it), next(it)
        pack_refs = [next(it) for _ in range(np_)]
        w_ref, sm_ref = (None, None) if np_ else (next(it), next(it))
        back_ref, xg_ref, o_ref, qkv_ref, l_ref = (next(it) for _ in range(5))
        g_refs = [next(it) for _ in range(np_)]
        if np_:
            sm_ref = next(it)
        acted, vt, ot = next(it), next(it), next(it)
        swap_s = [next(it) for _ in range(3)]
        turn_s = [next(it) for _ in range(3)]
        gat_s = [[next(it) for _ in range(7)] for _ in range(np_)]

        greet(dp_n, fs_n, np_ > 0)
        gathers = [Gather(dp_n, fs_n, pack_refs[i], g_refs[i], *gat_s[i]) for i in range(np_)]
        swap = Swap(fs_n, x_ref, xg_ref, *swap_s)
        if np_:
            gathers[0].start()
        swap.start()
        if np_:
            gathers[1].start()
            gathers[0].forward_z()
            gathers[0].forward_d()
        swap.wait()
        if np_:
            gathers[0].wait()
            sm_ref[...] = jnp.sum(units3(g_refs[0], 0, 16).astype(f32), 0)
        gain, bias = sm_ref[0:1, :], sm_ref[1:2, :]
        per = 256 // samples if samples < 256 else 1
        for s in range(slots // per):
            at = slice(s * per * samples, (s + 1) * per * samples)
            u, _ = unit(xg_ref[s * per:(s + 1) * per].reshape(per * samples, d).astype(f32))
            acted[at, :] = (u * gain + bias).astype(bf16)
        if np_:
            gathers[1].forward_z()
        for i in range(3):
            w = units(g_refs[0], 16 + i * rl, rl) if np_ else w_ref[i]

            def project(at):
                y = dot(acted[at, :], w).astype(bf16)
                qkv_ref[i, at, :] = y * 0.125 if i == 0 else y

            blocks(rows, 256, project)

        turns = Turns(fs_n, hp, lambda p, j: o_ref.at[p, pl.ds(pl.multiple_of(j * samples, samples), samples)],
                      lambda p, j: back_ref.at[j, p], *turn_s)
        for p in range(hp):
            at = head_pair(p)
            vt[...] = qkv_ref[2, :, at].astype(f32).T.astype(bf16)
            for h in range(2):
                def part(i, _):
                    qa = pl.ds(pl.multiple_of(i * BQ, BQ), BQ)
                    q = qkv_ref[0, qa, at]
                    q = jnp.where(head_mask(BQ, h), q, jnp.zeros_like(q))
                    s = dot(qkv_ref[1, :, at], q, NT) + kb_ref[:, 0:1]
                    m = jnp.max(s, 0, keepdims=True)
                    e = jnp.exp(s - m)
                    tot = jnp.sum(e, 0, keepdims=True)
                    o = dot(vt[h * 64:h * 64 + 64, :], e.astype(bf16))
                    ot[h * 64:h * 64 + 64, qa] = o * (1.0 / tot)
                    l_ref[p * 2 + h:p * 2 + h + 1, qa] = m + jnp.log(tot)
                    return 0
                lax.fori_loop(0, rows // BQ, part, 0)
            o_ref[p, :, :] = ot[...].T.astype(bf16)
            turns.start(p)
            if np_ and p == 0:
                gathers[1].forward_d()
        for p in range(hp):
            turns.wait_recv(p)
        turns.wait_send()
        if np_:
            gathers[1].wait()

    def units3(ref, start, size):
        v = ref[..., start:start + size, :]
        return v.reshape(-1, size, v.shape[-1])

    S, V = jax.ShapeDtypeStruct, pltpu.VMEM
    outs = [S((slots, hp, samples, 128), bf16), S((slots, samples, d), bf16), S((hp, rows, 128), bf16), S((3, rows, dh), bf16),
            S((heads, rows), f32)]
    outs += [S((dp_n, fs_n // 2, 2) + p.shape, bf16) for p in packs]
    args = [x, keybias] + list(packs)
    if np_:
        outs.append(S((16, d), f32))
    else:
        args += list(plain)
    return pl.pallas_call(
        body, out_shape=outs, in_specs=[VM] * len(args), out_specs=[VM] * len(outs),
        scratch_shapes=[V((rows, d), bf16), V((128, rows), bf16), V((128, rows), f32)] + swap_sems(fs_n) + turn_sems(fs_n, hp)
        + gather_sems(dp_n, fs_n) * np_,
        compiler_params=params(1), name="forward",
    )(*args)


def backward_kernel(do1, xg, qkv, o, lse, w, smalls, keybias, g1, gm, dp_n, fs_n, rl, dh, tasks, packed):
    slots, samples, d = xg.shape
    rows = slots * samples
    heads = dh // 64
    hp = heads // 2

    def body(*refs):
        it = iter(refs)
        do_in, xg_ref, qkv_ref, o_ref, l_ref, w_ref, n_ref, kb_ref = (next(it) for _ in range(8))
        g1_ref, gm_ref = (next(it), next(it)) if packed else (None, None)
        if packed:
            tg_ref, sm_ref, ss_ref = (next(it) for _ in range(3))
        else:
            dr_ref, gw_ref, gn_ref = (next(it) for _ in range(3))
        do, delta, kt, dqt, dk, dv, dqkv, acted, gn, dx = (next(it) for _ in range(10))
        turn_s = [next(it) for _ in range(3)]
        back_s = [next(it) for _ in range(3)]
        if packed:
            gs, dr_ref = next(it), next(it)
            rm = [next(it) for _ in range(11)]
            rs = [next(it) for _ in range(11)]

        greet(dp_n, fs_n, packed)
        turns = Turns(fs_n, hp, lambda p, j: do_in.at[j, p], lambda p, j: do.at[j, p], *turn_s)
        for p in range(hp):
            turns.start(p)
        if packed:
            red = Reduce(dp_n, fs_n, gm_ref, rm[:5], rm[5:])
            red_s = Reduce(dp_n, fs_n, gs, rs[:5], rs[5:])
            red.core()
        gain, bias = n_ref[0:1, :], n_ref[1:2, :]
        lane = lax.broadcasted_iota(jnp.int32, (8, 128), 1) // 64
        pick = (lane == lax.broadcasted_iota(jnp.int32, (8, 128), 0)).astype(f32)
        per = BQ // samples if samples < BQ else 1

        def grad_rows(i, p):
            return do[pl.ds(i * per, per), p].reshape(per * samples, 128)

        n = per * samples
        for p in range(hp):
            at = head_pair(p)
            kt[...] = qkv_ref[1, :, at].astype(f32).T.astype(bf16)
            dk[...] = jnp.zeros_like(dk)
            dv[...] = jnp.zeros_like(dv)
            turns.wait_recv(p)

            def deltas(i, _):
                qa = pl.ds(pl.multiple_of(i * n, n), n)
                prod = grad_rows(i, p).astype(f32) * o_ref[p, qa, :].astype(f32)
                delta[:, qa] = lax.dot_general(pick, prod, NT, precision=lax.Precision.HIGHEST, preferred_element_type=f32)
                return 0

            lax.fori_loop(0, rows // n, deltas, 0)
            for h in range(2):
                def part(i, _):
                    qa = pl.ds(pl.multiple_of(i * n, n), n)
                    mask = head_mask(n, h)
                    q = qkv_ref[0, qa, at]
                    q = jnp.where(mask, q, jnp.zeros_like(q))
                    g = grad_rows(i, p)
                    g = jnp.where(mask, g, jnp.zeros_like(g))
                    s = dot(qkv_ref[1, :, at], q, NT) + kb_ref[:, 0:1]
                    e = jnp.exp(s - l_ref[p * 2 + h:p * 2 + h + 1, qa])
                    ds = (e * (dot(qkv_ref[2, :, at], g, NT) - delta[h:h + 1, qa])).astype(bf16)
                    dv[...] += dot(e.astype(bf16), g)
                    dk[...] += dot(ds, q)
                    dqt[h * 64:h * 64 + 64, qa] = dot(kt[h * 64:h * 64 + 64, :], ds) * 0.125
                    return 0
                lax.fori_loop(0, rows // n, part, 0)
            dqkv[0, :, at] = dqt[...].T.astype(bf16)
            dqkv[1, :, at] = dk[...].astype(bf16)
            dqkv[2, :, at] = dv[...].astype(bf16)
            if packed:
                if p == 0:
                    red.halve()
                if p == hp - 2:
                    red.plane()

        def mats(i):
            return units(w_ref, 16 + i * rl, rl) if packed else w_ref[i]

        per2 = 256 // samples if samples < 256 else 1
        n2 = per2 * samples
        gn[...] = jnp.zeros_like(gn)

        def act_rows(i):
            at = pl.ds(pl.multiple_of(i * n2, n2), n2)
            u, r = unit(xg_ref[pl.ds(i * per2, per2)].reshape(n2, d).astype(f32))
            return at, u, r

        def first(i, _):
            at, u, r = act_rows(i)
            acted[at, :] = (u * gain + bias).astype(bf16)
            return 0

        lax.fori_loop(0, rows // n2, first, 0)
        for i in range(3):
            if packed:
                y = dot(acted[...], dqkv[i], TN).astype(bf16)
                gs[:, :, :, 16 + i * rl:16 + (i + 1) * rl, :] = y.reshape(gs.shape[:3] + (rl, d))
            else:
                gw_ref[i] = dot(acted[...], dqkv[i], TN).astype(bf16)

        def sums(i, _):
            at, u, r = act_rows(i)
            y = dot(dqkv[0, at, :], mats(0), NT) + dot(dqkv[1, at, :], mats(1), NT) + dot(dqkv[2, at, :], mats(2), NT)
            gn[0:1, :] += jnp.sum(y * u, 0, keepdims=True)
            gn[1:2, :] += jnp.sum(y, 0, keepdims=True)
            dx[pl.ds(i * per2, per2)] = unit_back(y, u, r, gain).astype(bf16).reshape(per2, samples, d)
            return 0

        lax.fori_loop(0, rows // n2, sums, 0)
        back = Turns(fs_n, 1, lambda p, j: dx.at[j], lambda p, j: dr_ref.at[j], *back_s)
        back.start(0)
        if packed:
            small = jnp.concatenate([gn[...].astype(bf16), jnp.zeros_like(gn).astype(bf16)], 0)
            gs[:, :, :, 0:16, :] = jnp.broadcast_to(small, gs.shape[:3] + (16, d))
            red_s.core()
            red.finish(sm_ref)
            red_s.halve()
            red_s.plane()
            back.wait_recv(0)
            feats = slots // tasks
            for s in range(slots):
                t, f = s // feats, s % feats
                for i in range(d // 128):
                    at = pl.ds(((t * samples * (d // 128)) + i) * feats + f, samples, stride=feats * (d // 128))
                    tg_ref[at, :] = g1_ref[s * samples:(s + 1) * samples, head_pair(i)] + dr_ref[s, :, head_pair(i)].astype(f32)
            red_s.finish(ss_ref)
        else:
            gn_ref[...] = gn[...]
            back.wait_recv(0)
        back.wait_send()
        turns.wait_send()

    S, V = jax.ShapeDtypeStruct, pltpu.VMEM
    args = [do1, xg, qkv, o, lse, w, smalls, keybias]
    scratch = [V((slots, hp, samples, 128), bf16), V((8, rows), f32), V((128, rows), bf16), V((128, rows), f32), V((rows, 128), f32),
               V((rows, 128), f32), V((3, rows, dh), bf16), V((rows, d), bf16), V((8, d), f32), V((slots, samples, d), bf16)]
    scratch += turn_sems(fs_n, hp) + turn_sems(fs_n, 1)
    if packed:
        args += [g1, gm]
        mrows, srows = gm.shape[3], 16 + 3 * rl
        outs = [S((rows * d // 128, 128), f32), S((mrows, d), f32), S((srows, d), f32)]
        scratch += [V((dp_n, fs_n // 2, 2, srows, d), bf16), V((slots, samples, d), bf16)]
        scratch += reduce_scratch(dp_n, fs_n, mrows, d) + reduce_scratch(dp_n, fs_n, srows, d)
    else:
        outs = [S((slots, samples, d), bf16), S((3, d, dh), bf16), S((8, d), f32)]
    return pl.pallas_call(
        body, out_shape=outs, in_specs=[VM] * len(args), out_specs=[VM] * len(outs), scratch_shapes=scratch,
        compiler_params=params(2), name="backward",
    )(*args)
def up16(a):
    rows = a.shape[-2]
    extra = (-rows) % 16
    return a if extra == 0 else jnp.pad(a, [(0, 0)] * (a.ndim - 2) + [(0, extra), (0, 0)])


def local(tokens, sample_counts, feature_counts, norms, sample_qkv, sample_out, feature_qkv, feature_out, mlp_in, mlp_in_bias,
          mlp_out, mlp_out_bias, cotangent):
    dp_n, fs_n = lax.axis_size("dp"), lax.axis_size("fsdp")
    nd = dp_n * fs_n
    me_d, me_f = lax.axis_index("dp"), lax.axis_index("fsdp")
    me = me_d * fs_n + me_f
    tasks, samples, feats, d = tokens.shape
    pairs = tasks * feats
    rep = fs_n // pairs
    dh = d // rep
    hp = dh // 128
    rl = sample_out.shape[0]
    chunks = mlp_in.shape[1] // d
    fl = mlp_out.shape[0]
    total = samples * fs_n
    packed = rep == 1 and rl % 16 == 0 and 256 % fl == 0

    small = jnp.zeros((16, d), bf16)
    small = lax.dynamic_update_slice(small, norms, (0, me * rl))
    small = lax.dynamic_update_slice(small, mlp_out_bias[None, :], (6, me * rl))
    small = lax.dynamic_update_slice(small, mlp_in_bias[None, :], (7 + (me * fl) // d, lax.rem(me * fl, d)))
    split_in = mlp_in.reshape(rl, chunks, d).transpose(1, 0, 2).reshape(chunks * rl, d)
    pack_a = up16(jnp.concatenate([small, sample_qkv.reshape(3 * rl, d)], 0))
    pack_b = up16(jnp.concatenate([sample_out, feature_qkv.reshape(3 * rl, d), feature_out, split_in, mlp_out], 0))

    xp = tokens.transpose(0, 2, 1, 3).reshape(pairs, samples, d)
    cp = cotangent.transpose(0, 2, 1, 3).reshape(pairs, samples, d)
    my_task = me_f // rep // feats
    count = lax.dynamic_index_in_dim(sample_counts, my_task, keepdims=False)
    keybias = jnp.broadcast_to(jnp.where(jnp.arange(total) < count, 0.0, MASKED).astype(f32)[:, None], (total, 128))
    sb = 128 // feats
    place = jnp.arange(feats * sb)
    same = (place[:, None] % sb) == (place[None, :] % sb)
    shown = (place[None, :] // sb) < feature_counts[:, None]
    fbias = jnp.where(same[None] & shown[:, None, :], 0.0, MASKED).astype(f32)

    if packed:
        back, xg, o, qkv, lse, ga, gb, smalls = forward_kernel(xp, [pack_a, pack_b], None, keybias, dp_n, fs_n, rl, dh)
        w_mine, w_mid, size = ga, gb.reshape(nd, gb.shape[3], d), rl
    else:
        ga, gb = gather_call([pack_a, pack_b], dp_n, fs_n, 3)
        ga, gb = ga.reshape((nd,) + ga.shape[3:]), gb.reshape((nd,) + gb.shape[3:])

        def take(g, start, rows):
            return g[:, start:start + rows].reshape(nd * rows, d)

        smalls = jnp.sum(ga[:, :16].astype(f32), 0)
        w_s = jnp.stack([take(ga, 16 + i * rl, rl) for i in range(3)])
        first = lax.rem(me_f, rep) * dh
        w_mine = lax.dynamic_slice_in_dim(w_s, first, dh, 2)
        w_mid = jnp.concatenate([take(gb, i * rl, rl) for i in range(5 + chunks)] + [take(gb, (5 + chunks) * rl, fl)])[None]
        size = d
        back, xg, o, qkv, lse = forward_kernel(jnp.repeat(xp, rep, 0), [], [w_mine, smalls], keybias, dp_n, fs_n, rl, dh)

    lo, g1, do1, gm = middle_call(xp, back.reshape(pairs, rep * hp, samples, 128), cp, smalls, fbias, w_mid, chunks, size)
    do1 = do1.reshape(fs_n, hp, samples, 128)
    if packed:
        gm = gm.reshape((dp_n, fs_n // 2, 2) + gm.shape[1:])
        tokens_grad, sm, ss = backward_kernel(do1, xg, qkv, o, lse, w_mine, smalls, keybias, g1, gm, dp_n, fs_n, rl, dh, tasks, True)
        tokens_grad = tokens_grad.reshape(tasks, samples, d // 128, feats, 128).transpose(0, 1, 3, 2, 4).reshape(tokens.shape)
        gn, outs, s = ss[0:2], [ss[16:]], sm
    else:
        dxr, gs, gn_s = backward_kernel(do1, xg, qkv, o, lse, w_mine, smalls, keybias, None, None, dp_n, fs_n, rl, dh, tasks, False)
        dxr = jnp.sum(dxr.reshape(pairs, rep, samples, d).astype(f32), 1)
        tokens_grad = (g1.reshape(pairs, samples, d) + dxr).reshape(tasks, feats, samples, d).transpose(0, 2, 1, 3)
        gs = lax.dynamic_update_slice_in_dim(jnp.zeros((3, d, d), bf16), gs, first, 2)

        def give(g, parts):
            return g.reshape(parts, nd, -1, d).transpose(1, 0, 2, 3).reshape(nd, -1, d)

        gm = gm[0]
        mix = jnp.concatenate([gn_s[0:2].astype(bf16), gm[2:16]], 0)
        grads = up16(jnp.concatenate([jnp.broadcast_to(mix[None], (nd, 16, d)), give(gm[16:16 + (5 + chunks) * d], 5 + chunks),
                                      give(gm[16 + (5 + chunks) * d:], 1), give(gs, 3)], 1))
        s = scatter_call(grads.reshape((dp_n, fs_n // 2, 2) + grads.shape[1:]), dp_n, fs_n, 6)
        outs = [s[16 + (5 + chunks) * rl + fl:][:3 * rl]]
        gn = s[0:2]
    gn = jnp.concatenate([gn, s[2:16]], 0)
    layer_output = lo.reshape(tasks, feats, samples, d).transpose(0, 2, 1, 3)

    def piece(start, rows):
        return s[16 + start * rl:16 + start * rl + rows]

    return (
        layer_output,
        tokens_grad,
        lax.dynamic_slice(gn, (0, me * rl), (6, rl)),
        outs[0].reshape(3, rl, d), piece(0, rl), piece(1, 3 * rl).reshape(3, rl, d), piece(4, rl),
        piece(5, chunks * rl).reshape(chunks, rl, d).transpose(1, 0, 2).reshape(rl, chunks * d),
        lax.dynamic_slice(gn[7:7 + chunks].reshape(-1), (me * fl,), (fl,)),
        piece(5 + chunks, fl),
        lax.dynamic_slice(gn[6], (me * rl,), (rl,)),
    )


def solution(mesh):
    rows, whole = ("dp", "fsdp"), P("dp", "fsdp", None, None)
    weights = (P(None, rows), P(None, rows, None), P(rows, None), P(None, rows, None), P(rows, None), P(rows, None), P(rows),
               P(rows, None), P(rows))
    return jax.shard_map(local, mesh=mesh, in_specs=(whole, P("dp"), P("dp")) + weights + (whole,),
                         out_specs=(whole, whole) + weights, check_vma=False)
```

```python
import functools
import jax
import jax.numpy as jnp
from jax import lax
from jax.experimental import pallas as pl
from jax.experimental.pallas import tpu as pltpu
from jax.sharding import PartitionSpec as P

MESH = pl.DeviceIdType.MESH
f32, bf16 = jnp.float32, jnp.bfloat16


def mod(a, n):
    return lax.rem(a, n)


def greet(dp_n, fs_n, with_dp=True):
    me_d, me_f = lax.axis_index("dp"), lax.axis_index("fsdp")
    barrier = pltpu.get_barrier_semaphore()
    n = 0
    for k in range(1, fs_n):
        pl.semaphore_signal(barrier, inc=1, device_id=(me_d, mod(me_f + k, fs_n)), device_id_type=MESH)
        n += 1
    if with_dp:
        for k in range(1, dp_n):
            pl.semaphore_signal(barrier, inc=1, device_id=(mod(me_d + k, dp_n), me_f), device_id_type=MESH)
            n += 1
    pl.semaphore_wait(barrier, n)


def rcopy(src, dst, ss, rs, dev):
    return pltpu.make_async_remote_copy(src_ref=src, dst_ref=dst, send_sem=ss, recv_sem=rs, device_id=dev, device_id_type=MESH)


class Swap:
    def __init__(self, fs_n, src, dst, local_sem, ss, rs):
        me_d, me_f = lax.axis_index("dp"), lax.axis_index("fsdp")
        self.own = pltpu.make_async_copy(src.at[me_f], dst.at[me_f], local_sem)
        self.copies = []
        for k in range(1, fs_n):
            to = mod(me_f + k, fs_n)
            self.copies.append(rcopy(src.at[to], dst.at[me_f], ss.at[k - 1], rs.at[k - 1], (me_d, to)))

    def start(self):
        for c in self.copies:
            c.start()
        self.own.start()

    def wait(self):
        self.own.wait()
        for c in self.copies:
            c.wait()


class Gather:
    def __init__(self, dp_n, fs_n, src, dst, local_sem, zs, zr, ds, dr, cs, cr):
        me_d, me_f = lax.axis_index("dp"), lax.axis_index("fsdp")
        z_n = fs_n // 2
        me_z, me_c = me_f // 2, mod(me_f, 2)
        self.z_n, self.dp_n = z_n, dp_n
        partner = (me_d, me_z * 2 + 1 - me_c)
        self.own = pltpu.make_async_copy(src, dst.at[me_d, me_z, me_c], local_sem)
        self.z = []
        for k in range(1, z_n):
            to = mod(me_z + k, z_n) * 2 + me_c
            self.z.append(rcopy(src, dst.at[me_d, me_z, me_c], zs.at[k - 1], zr.at[k - 1], (me_d, to)))
        self.d = {}
        self.c = {}
        for k in range(z_n):
            z = mod(me_z - k + z_n, z_n)
            for j in range(dp_n):
                d = mod(me_d - j + dp_n, dp_n)
                here = src if (k == 0 and j == 0) else dst.at[d, z, me_c]
                self.c[k, j] = rcopy(here, dst.at[d, z, me_c], cs.at[k * dp_n + j], cr.at[k * dp_n + j], partner)
                if j > 0:
                    here = src if k == 0 else dst.at[me_d, z, me_c]
                    i = k * (dp_n - 1) + j - 1
                    self.d[k, j] = rcopy(here, dst.at[me_d, z, me_c], ds.at[i], dr.at[i], (mod(me_d + j, dp_n), me_f))

    def start(self):
        for c in self.z:
            c.start()
        self.own.start()
        for j in range(1, self.dp_n):
            self.d[0, j].start()
        self.c[0, 0].start()

    def forward_z(self):
        for k in range(1, self.z_n):
            self.z[k - 1].wait_recv()
            for j in range(1, self.dp_n):
                self.d[k, j].start()
            self.c[k, 0].start()

    def forward_d(self):
        for k in range(self.z_n):
            for j in range(1, self.dp_n):
                self.d[k, j].wait_recv()
                self.c[k, j].start()

    def wait(self):
        self.own.wait()
        for c in self.z:
            c.wait_send()
        for c in self.d.values():
            c.wait_send()
        for c in self.c.values():
            c.wait()


def gather_sems(dp_n, fs_n):
    z = fs_n // 2
    D = pltpu.SemaphoreType.DMA
    return [D, D((z - 1,)), D((z - 1,)), D((z * (dp_n - 1),)), D((z * (dp_n - 1),)), D((z * dp_n,)), D((z * dp_n,))]


def swap_sems(fs_n):
    D = pltpu.SemaphoreType.DMA
    return [D, D((fs_n - 1,)), D((fs_n - 1,))]


ANY = pl.BlockSpec(memory_space=pl.ANY)
VM = pl.BlockSpec(memory_space=pltpu.VMEM)


def swap_call(x, dp_n, fs_n, cid, space=ANY):
    def body(x_ref, o_ref, *sems):
        greet(dp_n, fs_n, False)
        s = Swap(fs_n, x_ref, o_ref, *sems)
        s.start()
        s.wait()

    return pl.pallas_call(
        body, out_shape=jax.ShapeDtypeStruct(x.shape, x.dtype), in_specs=[space], out_specs=space,
        scratch_shapes=swap_sems(fs_n),
        compiler_params=pltpu.CompilerParams(collective_id=cid, has_side_effects=True, vmem_limit_bytes=60 << 20),
        name="swap%d" % cid,
    )(x)


def gather_call(packs, dp_n, fs_n, cid, space=ANY):
    n = len(packs)

    def body(*refs):
        ins, outs, sems = refs[:n], refs[n:2 * n], refs[2 * n:]
        greet(dp_n, fs_n)
        gs = [Gather(dp_n, fs_n, ins[i], outs[i], *sems[7 * i:7 * i + 7]) for i in range(n)]
        for g in gs:
            g.start()
        for g in gs:
            g.forward_z()
        for g in gs:
            g.forward_d()
        for g in gs:
            g.wait()

    return pl.pallas_call(
        body,
        out_shape=[jax.ShapeDtypeStruct((dp_n, fs_n // 2, 2) + p.shape, p.dtype) for p in packs],
        in_specs=[space] * n, out_specs=[space] * n,
        scratch_shapes=gather_sems(dp_n, fs_n) * n,
        compiler_params=pltpu.CompilerParams(collective_id=cid, has_side_effects=True, vmem_limit_bytes=60 << 20),
        name="gather%d" % cid,
    )(*packs)


def scatter_call(g, dp_n, fs_n, cid):
    z_n = fs_n // 2
    rows, width = g.shape[3:]
    step = 16

    def body(g_ref, o_ref, from_c, half, from_d, quarter, from_z, cs, cr, ds, dr, zs, zr):
        me_d, me_f = lax.axis_index("dp"), lax.axis_index("fsdp")
        me_z, me_c = me_f // 2, mod(me_f, 2)
        greet(dp_n, fs_n)
        partner = (me_d, me_z * 2 + 1 - me_c)

        def add(out, parts):
            def one(i, _):
                at = pl.ds(pl.multiple_of(i * step, step), step)
                total = parts[0][at, :].astype(f32)
                for p in parts[1:]:
                    total = total + p[at, :].astype(f32)
                out[at, :] = total.astype(out.dtype)
                return 0
            lax.fori_loop(0, rows // step, one, 0, unroll=True if rows // step <= 4 else 4)

        order = [(j, k) for j in list(range(1, dp_n)) + [0] for k in list(range(1, z_n)) + [0]]
        cc, dd, zz = {}, {}, {}
        for i, (j, k) in enumerate(order):
            d, z = mod(me_d + j, dp_n), mod(me_z + k, z_n)
            cc[j, k] = rcopy(g_ref.at[d, z, 1 - me_c], from_c.at[i], cs.at[i], cr.at[i], partner)
            cc[j, k].start()
        for i, (j, k) in enumerate(order):
            d, z = mod(me_d + j, dp_n), mod(me_z + k, z_n)
            cc[j, k].wait_recv()
            add(half.at[j, k], [g_ref.at[d, z, me_c], from_c.at[i]])
            if j:
                n = (j - 1) * z_n + k
                dd[j, k] = rcopy(half.at[j, k], from_d.at[j - 1, k], ds.at[n], dr.at[n], (d, me_f))
                dd[j, k].start()
        for k in list(range(1, z_n)) + [0]:
            for j in range(1, dp_n):
                dd[j, k].wait_recv()
            if k:
                add(quarter.at[k], [half.at[0, k]] + [from_d.at[j - 1, k] for j in range(1, dp_n)])
                to = mod(me_z + k, z_n) * 2 + me_c
                zz[k] = rcopy(quarter.at[k], from_z.at[k - 1], zs.at[k - 1], zr.at[k - 1], (me_d, to))
                zz[k].start()
        for k in range(1, z_n):
            zz[k].wait_recv()
        add(o_ref, [half.at[0, 0]] + [from_d.at[j - 1, 0] for j in range(1, dp_n)] + [from_z.at[k - 1] for k in range(1, z_n)])
        for c in list(cc.values()) + list(dd.values()) + list(zz.values()):
            c.wait_send()

    D = pltpu.SemaphoreType.DMA
    n = dp_n * z_n
    return pl.pallas_call(
        body, out_shape=jax.ShapeDtypeStruct((rows, width), f32), in_specs=[VM], out_specs=VM,
        scratch_shapes=[
            pltpu.VMEM((n, rows, width), bf16), pltpu.VMEM((dp_n, z_n, rows, width), bf16),
            pltpu.VMEM((dp_n - 1, z_n, rows, width), bf16), pltpu.VMEM((z_n, rows, width), bf16),
            pltpu.VMEM((z_n - 1, rows, width), bf16),
            D((n,)), D((n,)), D((n - z_n,)), D((n - z_n,)), D((z_n - 1,)), D((z_n - 1,)),
        ],
        compiler_params=pltpu.CompilerParams(collective_id=cid, has_side_effects=True, vmem_limit_bytes=60 << 20),
        name="scatter%d" % cid,
    )(g)
class PlaneGather:
    def __init__(self, fs_n, src, dst, local_sem, zs, zr, ds, dr, cs, cr):
        me_d, me_f = lax.axis_index("dp"), lax.axis_index("fsdp")
        z_n = fs_n // 2
        me_z, me_c = me_f // 2, mod(me_f, 2)
        self.z_n = z_n
        partner = (me_d, me_z * 2 + 1 - me_c)
        ds_ = [me_d, me_d // 2 * 2 + 1 - mod(me_d, 2), mod(me_d + 2, 4), 3 - me_d]
        zs_ = [mod(me_z - k + z_n, z_n) for k in range(z_n)]
        self.own = pltpu.make_async_copy(src, dst.at[me_d, me_z, me_c], local_sem)
        self.z, self.n, self.fwd, self.c = {}, {}, {}, {}
        for k in range(z_n):
            at = lambda j: dst.at[ds_[j], zs_[k], me_c]
            mine = src if k == 0 else at(0)
            if k:
                to = mod(me_z + k, z_n) * 2 + me_c
                self.z[k] = rcopy(src, dst.at[me_d, me_z, me_c], zs.at[k - 1], zr.at[k - 1], (me_d, to))
            for j in (1, 2):
                self.n[k, j] = rcopy(mine, at(0), ds.at[3 * k + j - 1], dr.at[3 * k + j - 1], (ds_[j], me_f))
            first = 1 + k % 2
            self.fwd[k] = rcopy(at(first), at(first), ds.at[3 * k + 2], dr.at[3 * k + 2], (ds_[3 - first], me_f))
            for j in range(4):
                self.c[k, j] = rcopy(mine if j == 0 else at(j), at(j), cs.at[4 * k + j], cr.at[4 * k + j], partner)

    def start(self):
        for c in self.z.values():
            c.start()
        self.own.start()
        self.spread(0)

    def spread(self, k):
        if k:
            self.z[k].wait_recv()
        self.n[k, 1].start()
        self.n[k, 2].start()
        self.c[k, 0].start()

    def hand_on(self, k):
        first = 1 + k % 2
        for j in (first, 3 - first):
            self.n[k, j].wait_recv()
            if j == first:
                self.fwd[k].start()
            self.c[k, j].start()

    def corner(self, k):
        self.fwd[k].wait_recv()
        self.c[k, 3].start()

    def wait(self):
        self.own.wait()
        for c in list(self.z.values()) + list(self.n.values()) + list(self.fwd.values()):
            c.wait_send()
        for c in self.c.values():
            c.wait()


def plane_gather_sems(fs_n):
    z, D = fs_n // 2, pltpu.SemaphoreType.DMA
    return [D, D((z - 1,)), D((z - 1,)), D((3 * z,)), D((3 * z,)), D((4 * z,)), D((4 * z,))]


class PlaneReduce:
    def __init__(self, fs_n, g, bufs, sems):
        me_d, me_f = lax.axis_index("dp"), lax.axis_index("fsdp")
        z_n = fs_n // 2
        me_z, me_c = me_f // 2, mod(me_f, 2)
        self.z_n, self.rows = z_n, g.shape[3]
        self.mine, self.from_c, self.from_n, self.from_z = bufs
        ls, cs, cr, ds, dr, zs, zr = sems
        partner = (me_d, me_z * 2 + 1 - me_c)
        ds_ = [me_d, me_d // 2 * 2 + 1 - mod(me_d, 2), mod(me_d + 2, 4), 3 - me_d]
        self.l, self.c, self.n, self.z = {}, {}, {}, {}
        for k in range(z_n):
            z = mod(me_z + k, z_n)
            for j in range(4):
                i = 4 * k + j
                self.l[k, j] = pltpu.make_async_copy(g.at[ds_[j], z, me_c], self.mine.at[k, j], ls.at[i])
                self.c[k, j] = rcopy(g.at[ds_[j], z, 1 - me_c], self.from_c.at[k, j], cs.at[i], cr.at[i], partner)
            first = 1 + k % 2
            send = [(first, first), (3, first), (3 - first, 3 - first)]
            for i, (j, to) in enumerate(send):
                self.n[k, i] = rcopy(self.mine.at[k, j], self.from_n.at[k, i], ds.at[3 * k + i], dr.at[3 * k + i], (ds_[to], me_f))
            if k:
                to = mod(me_z + k, z_n) * 2 + me_c
                self.z[k] = rcopy(self.mine.at[k, 0], self.from_z.at[k - 1], zs.at[k - 1], zr.at[k - 1], (me_d, to))

    def add(self, out, parts):
        step = 16

        def one(i, _):
            at = pl.ds(pl.multiple_of(i * step, step), step)
            total = parts[0][at, :].astype(f32)
            for p in parts[1:]:
                total = total + p[at, :].astype(f32)
            out[at, :] = total.astype(out.dtype)
            return 0

        n = self.rows // step
        lax.fori_loop(0, n, one, 0, unroll=2 if n % 2 == 0 else 1)

    def order(self):
        return list(range(1, self.z_n)) + [0]

    def start(self):
        for k in self.order():
            for j in (3, 1, 2, 0):
                self.c[k, j].start()
                self.l[k, j].start()

    def first(self, k):
        first = 1 + k % 2
        for j in (first, 3, 3 - first, 0):
            self.l[k, j].wait()
            self.c[k, j].wait_recv()
            self.add(self.mine.at[k, j], [self.mine.at[k, j], self.from_c.at[k, j]])
            if j == first:
                self.n[k, 0].start()
            if j == 3:
                self.n[k, 1].start()

    def second(self, k):
        first = 1 + k % 2
        self.n[k, 1].wait_recv()
        j = 3 - first
        self.add(self.mine.at[k, j], [self.mine.at[k, j], self.from_n.at[k, 1]])
        self.n[k, 2].start()

    def third(self, k):
        self.n[k, 0].wait_recv()
        self.n[k, 2].wait_recv()
        if k:
            self.add(self.mine.at[k, 0], [self.mine.at[k, 0], self.from_n.at[k, 0], self.from_n.at[k, 2]])
            self.z[k].start()

    def finish(self, out):
        for k in range(1, self.z_n):
            self.z[k].wait_recv()
        self.add(out, [self.mine.at[0, 0], self.from_n.at[0, 0], self.from_n.at[0, 2]] + [self.from_z.at[k - 1] for k in range(1, self.z_n)])
        for c in list(self.c.values()) + list(self.n.values()) + list(self.z.values()):
            c.wait_send()


def plane_reduce_scratch(fs_n, rows, width):
    z_n = fs_n // 2
    V, D = pltpu.VMEM, pltpu.SemaphoreType.DMA
    return [V((z_n, 4, rows, width), bf16), V((z_n, 4, rows, width), bf16), V((z_n, 3, rows, width), bf16), V((z_n - 1, rows, width), bf16),
            D((4 * z_n,)), D((4 * z_n,)), D((4 * z_n,)), D((3 * z_n,)), D((3 * z_n,)), D((z_n - 1,)), D((z_n - 1,))]


HEADS = 8
EPS = 1e-05
MASKED = -1e30
NN = (((1,), (0,)), ((), ()))
NT = (((1,), (1,)), ((), ()))
TN = (((0,), (0,)), ((), ()))


def dot(a, b, dims=NN):
    return lax.dot_general(a, b, dims, preferred_element_type=f32)


def unit(x):
    c = x - jnp.mean(x, -1, keepdims=True)
    r = lax.rsqrt(jnp.mean(c * c, -1, keepdims=True) + EPS)
    return c * r, r


def unit_back(y, u, r, gain):
    yg = y * gain
    return r * (yg - jnp.mean(yg, -1, keepdims=True) - u * jnp.mean(yg * u, -1, keepdims=True))


def blocks(total, size, body):
    lax.fori_loop(0, total // size, lambda i, c: (body(pl.ds(pl.multiple_of(i * size, size), size)), c)[1], 0)


def gelu_parts(v):
    z = jnp.abs(v) * 0.7071067811865476
    t = 1.0 / (1.0 + 0.3275911 * z)
    e = jnp.exp(-0.5 * (v * v))
    tail = t * (0.127414796 + t * (-0.142248368 + t * (0.7107068705 + t * (-0.7265760135 + t * 0.5307027145)))) * e
    return jnp.where(v >= 0, 1.0 - tail, tail), v * e * 0.3989422804014327


def head_mask(rows, second, width=128):
    lane = lax.broadcasted_iota(jnp.int32, (rows, width), 1)
    return (lane >= width // 2) if second else (lane < width // 2)


def params(cid=None):
    if cid is None:
        return pltpu.CompilerParams(vmem_limit_bytes=62 << 20)
    return pltpu.CompilerParams(collective_id=cid, has_side_effects=True, vmem_limit_bytes=62 << 20)


def head_pair(p):
    return slice(p * 128, p * 128 + 128)


def middle_call(x, o1, cot, smalls, fbias, w, tasks, chunks, unit_rows):
    pairs, samples, d = x.shape
    feats = pairs // tasks
    rows = pairs * samples
    hh = d // 64
    nd = w.shape[0]
    U = unit_rows
    OUT = (5 + chunks) * U
    fl = chunks * d // nd
    x, cot = x.reshape(rows, d), cot.reshape(rows, d)
    RB = 256
    per = RB // samples

    def body(x_ref, back_ref, cot_ref, n_ref, fb_ref, w_ref,
             lo_ref, g1_ref, do1_ref, g_ref,
             x1, a, qkv, p2, o2, acc, dacc, act, gh, dqkv, do2, o1_ref, gn_ref):
        gn_ref[...] = jnp.zeros_like(gn_ref)

        def at_unit(k):
            return pl.ds(pl.multiple_of(k * U, 16), U) if not isinstance(k, int) else slice(k * U, k * U + U)

        def mat(k):
            return w_ref[:, at_unit(k), :].reshape(d, d)

        def out_mat(c):
            if nd == 1:
                return w_ref[0, pl.ds(pl.multiple_of(OUT + c * d, 16), d), :]
            m = nd // chunks
            return w_ref[pl.ds(c * m, m), OUT:OUT + fl, :].reshape(d, d)

        def put(k, at, i, value):
            if nd == 1:
                g_ref[0, pl.ds(pl.multiple_of(16 + k * U + i * 256, 16), 256), :] = value
            else:
                m = 256 // U
                g_ref[pl.ds(i * m, m), pl.ds(pl.multiple_of(16 + k * U, 16), U), :] = value.reshape(m, U, d)

        def put_out(c, i, value):
            if nd == 1:
                g_ref[0, pl.ds(pl.multiple_of(16 + OUT + c * d + i * 256, 16), 256), :] = value
            else:
                m = 256 // fl
                g_ref[pl.ds(c * (nd // chunks) + i * m, m), 16 + OUT:16 + OUT + fl, :] = value.reshape(m, fl, d)

        def tiles(body):
            for i in range(d // 256):
                body(slice(i * 256, i * 256 + 256), i)

        def norm(i):
            return n_ref[2 * i:2 * i + 1, :], n_ref[2 * i + 1:2 * i + 2, :]

        def collect(i, _):
            at = pl.ds(pl.multiple_of(i * RB, RB), RB)
            for p in range(hh // 2):
                o1_ref[at, p * 128:p * 128 + 128] = back_ref[pl.ds(i * per, per), p].reshape(RB, 128)
            return 0

        lax.fori_loop(0, rows // RB, collect, 0)

        def first(at):
            y = x_ref[at, :].astype(f32) + dot(o1_ref[at, :], mat(0))
            x1[at, :] = y
            u, _ = unit(y)
            g, b = norm(1)
            v = (u * g + b).astype(bf16)
            a[at, :] = v
            for i in range(3):
                z = dot(v, mat(1 + i)).astype(bf16)
                qkv[i, at, :] = z * 0.125 if i == 0 else z

        blocks(rows, RB, first)

        half = lax.broadcasted_iota(jnp.int32, (256, 128), 0) // 64
        ones = (lax.rem(half, 2) == lax.broadcasted_iota(jnp.int32, (256, 128), 1) // 64).astype(bf16)

        def head_sums(prods):
            both = []
            for v in prods:
                hi = v.astype(bf16)
                both.append(jnp.concatenate([hi, (v - hi.astype(f32)).astype(bf16)], 1))
            out = dot(jnp.concatenate(both, 0), ones)
            return [out[i * samples:(i + 1) * samples] for i in range(len(prods))]

        def at_slot(t, f):
            return pl.ds(pl.multiple_of((t * feats + f) * samples, samples), samples)

        def mix(t, _):
            for p in range(hh // 2):
                lanes = head_pair(p)
                ks = [qkv[1, at_slot(t, g), lanes].astype(f32) for g in range(feats)]
                vs = [qkv[2, at_slot(t, g), lanes].astype(f32) for g in range(feats)]
                for f in range(feats):
                    q = qkv[0, at_slot(t, f), lanes].astype(f32)
                    sc = head_sums([q * k for k in ks])
                    sc = [v + fb_ref[pl.ds(t * feats + g, 1), :] for g, v in enumerate(sc)]
                    top = functools.reduce(jnp.maximum, sc)
                    sc = [jnp.exp(v - top) for v in sc]
                    inv = 1.0 / sum(sc)
                    sc = [v * inv for v in sc]
                    for g in range(feats):
                        p2[t, p, f, g] = sc[g]
                    o2[at_slot(t, f), lanes] = sum(w * v for w, v in zip(sc, vs)).astype(bf16)
            return 0

        lax.fori_loop(0, tasks, mix, 0)

        def second(at):
            y = x1[at, :] + dot(o2[at, :], mat(4))
            acc[at, :] = y
            u, _ = unit(y)
            g, b = norm(2)
            do2[at, :] = (u * g + b).astype(bf16)
            dacc[at, :] = jnp.zeros((RB, d), f32)

        blocks(rows, RB, second)

        def chunk(c, _):
            def part(at):
                hid = dot(do2[at, :], mat(5 + c)) + n_ref[pl.ds(7 + c, 1), :]
                cdf, pdf = gelu_parts(hid)
                al = (hid * cdf).astype(bf16)
                act[at, :] = al
                gl = ((cdf + pdf) * dot(cot_ref[at, :], out_mat(c), NT)).astype(bf16)
                gh[at, :] = gl
                gn_ref[pl.ds(7 + c, 1), :] += jnp.sum(gl.astype(f32), 0, keepdims=True)
                acc[at, :] += dot(al, out_mat(c))
                dacc[at, :] += dot(gl, mat(5 + c), NT)

            blocks(rows, RB, part)

            def weight(at, i):
                put_out(c, i, dot(act[:, at], cot_ref[...], TN).astype(bf16))
                put(5 + c, at, i, dot(do2[:, at], gh[...], TN).astype(bf16))

            tiles(weight)
            return 0

        lax.fori_loop(0, chunks, chunk, 0)

        def third(at):
            lo_ref[at, :] = (acc[at, :] + n_ref[6:7, :]).astype(bf16)
            u, r = unit(x1[at, :] + dot(o2[at, :], mat(4)))
            y = dacc[at, :]
            gn_ref[4:5, :] += jnp.sum(y * u, 0, keepdims=True)
            gn_ref[5:6, :] += jnp.sum(y, 0, keepdims=True)
            cf = cot_ref[at, :].astype(f32)
            gn_ref[6:7, :] += jnp.sum(cf, 0, keepdims=True)
            g2 = cf + unit_back(y, u, r, norm(2)[0])
            dacc[at, :] = g2
            e2 = g2.astype(bf16)
            act[at, :] = e2
            do2[at, :] = dot(e2, mat(4), NT).astype(bf16)

        blocks(rows, RB, third)

        def weight2(at, i):
            put(4, at, i, dot(o2[:, at], act[...], TN).astype(bf16))

        tiles(weight2)

        def unmix(t, _):
            for p in range(hh // 2):
                lanes = head_pair(p)
                ks = [qkv[1, at_slot(t, g), lanes].astype(f32) for g in range(feats)]
                vs = [qkv[2, at_slot(t, g), lanes].astype(f32) for g in range(feats)]
                dk, dv = [0.0] * feats, [0.0] * feats
                for f in range(feats):
                    q = qkv[0, at_slot(t, f), lanes].astype(f32)
                    gr = do2[at_slot(t, f), lanes].astype(f32)
                    dp = head_sums([gr * v for v in vs])
                    ws = [p2[t, p, f, g] for g in range(feats)]
                    mean = sum(w * v for w, v in zip(ws, dp))
                    ds = [(w * (v - mean)).astype(bf16).astype(f32) for w, v in zip(ws, dp)]
                    dqkv[0, at_slot(t, f), lanes] = (sum(v * k for v, k in zip(ds, ks)) * 0.125).astype(bf16)
                    for g in range(feats):
                        dk[g] += ds[g] * q
                        dv[g] += ws[g] * gr
                for g in range(feats):
                    dqkv[1, at_slot(t, g), lanes] = dk[g].astype(bf16)
                    dqkv[2, at_slot(t, g), lanes] = dv[g].astype(bf16)
            return 0

        lax.fori_loop(0, tasks, unmix, 0)

        def fourth(i, _):
            at = pl.ds(pl.multiple_of(i * RB, RB), RB)
            u, r = unit(x1[at, :])
            y = dot(dqkv[0, at, :], mat(1), NT) + dot(dqkv[1, at, :], mat(2), NT) + dot(dqkv[2, at, :], mat(3), NT)
            gn_ref[2:3, :] += jnp.sum(y * u, 0, keepdims=True)
            gn_ref[3:4, :] += jnp.sum(y, 0, keepdims=True)
            g1 = dacc[at, :] + unit_back(y, u, r, norm(1)[0])
            g1_ref[at, :] = g1
            e1 = g1.astype(bf16)
            act[at, :] = e1
            do = dot(e1, mat(0), NT).astype(bf16)
            for p in range(hh // 2):
                do1_ref[pl.ds(i * per, per), p] = do[:, p * 128:p * 128 + 128].reshape(per, samples, 128)
            return 0

        lax.fori_loop(0, rows // RB, fourth, 0)

        def weight3(at, i):
            put(0, at, i, dot(o1_ref[:, at], act[...], TN).astype(bf16))
            for j in range(3):
                put(1 + j, at, i, dot(a[:, at], dqkv[j], TN).astype(bf16))

        tiles(weight3)
        g_ref[:, 0:16, :] = jnp.broadcast_to(gn_ref[...].astype(bf16), (nd, 16, d))

    V = pltpu.VMEM
    S = jax.ShapeDtypeStruct
    return pl.pallas_call(
        body,
        out_shape=[S((rows, d), bf16), S((rows, d), f32), S((pairs, hh // 2, samples, 128), bf16),
                   S((nd, 16 + OUT + fl, d), bf16)],
        in_specs=[VM] * 6, out_specs=[VM] * 4,
        scratch_shapes=[V((rows, d), f32), V((rows, d), bf16), V((3, rows, d), bf16), V((tasks, hh // 2, feats, feats, samples, 128), f32), V((rows, d), bf16),
                        V((rows, d), f32), V((rows, d), f32), V((rows, d), bf16), V((rows, d), bf16), V((3, rows, d), bf16),
                        V((rows, d), bf16), V((rows, d), bf16), V((16, d), f32)],
        compiler_params=params(), name="middle",
    )(x, o1, cot, smalls, fbias, w)
BQ = 1024


class Turns:
    def __init__(self, fs_n, parts, src, dst, local_sem, ss, rs):
        me_d, me_f = lax.axis_index("dp"), lax.axis_index("fsdp")
        self.sets = []
        for p in range(parts):
            own = pltpu.make_async_copy(src(p, me_f), dst(p, me_f), local_sem.at[p])
            far = []
            for k in range(1, fs_n):
                to = mod(me_f + k, fs_n)
                i = p * (fs_n - 1) + k - 1
                far.append(rcopy(src(p, to), dst(p, me_f), ss.at[i], rs.at[i], (me_d, to)))
            self.sets.append((own, far))

    def start(self, p):
        own, far = self.sets[p]
        for c in far:
            c.start()
        own.start()

    def wait_recv(self, p):
        own, far = self.sets[p]
        own.wait()
        for c in far:
            c.wait_recv()

    def wait_send(self):
        for _, far in self.sets:
            for c in far:
                c.wait_send()


def turn_sems(fs_n, parts):
    D = pltpu.SemaphoreType.DMA
    return [D((parts,)), D((parts * (fs_n - 1),)), D((parts * (fs_n - 1),))]


def units(ref, start, size):
    v = ref[..., start:start + size, :]
    return v.reshape(-1, v.shape[-1])


def forward_kernel(x, packs, plain, keybias, dp_n, fs_n, rl, dh):
    slots, samples, d = x.shape
    rows = slots * samples
    heads = dh // 64
    hp = heads // 2
    np_ = len(packs)

    def body(*refs):
        it = iter(refs)
        x_ref, kb_ref = next(it), next(it)
        pack_refs = [next(it) for _ in range(np_)]
        w_ref, sm_ref = (None, None) if np_ else (next(it), next(it))
        back_ref, xg_ref, o_ref, qkv_ref, l_ref = (next(it) for _ in range(5))
        g_refs = [next(it) for _ in range(np_)]
        if np_:
            sm_ref = next(it)
        acted, vt, ot = next(it), next(it), next(it)
        swap_s = [next(it) for _ in range(3)]
        turn_s = [next(it) for _ in range(3)]
        gat_s = [[next(it) for _ in range(7)] for _ in range(np_)]

        greet(dp_n, fs_n, np_ > 0)
        gathers = [PlaneGather(fs_n, pack_refs[i], g_refs[i], *gat_s[i]) for i in range(np_)]
        swap = Swap(fs_n, x_ref, xg_ref, *swap_s)
        z_n = fs_n // 2
        if np_:
            gathers[0].start()
        swap.start()
        if np_:
            gathers[1].start()
            for k in range(1, z_n):
                gathers[0].spread(k)
            for k in range(z_n):
                gathers[0].hand_on(k)
            for k in range(1, z_n):
                gathers[1].spread(k)
            for k in range(z_n):
                gathers[0].corner(k)
        swap.wait()
        if np_:
            gathers[0].wait()
            sm_ref[...] = jnp.sum(units3(g_refs[0], 0, 16).astype(f32), 0)
        gain, bias = sm_ref[0:1, :], sm_ref[1:2, :]
        per = 256 // samples if samples < 256 else 1
        for s in range(slots // per):
            at = slice(s * per * samples, (s + 1) * per * samples)
            u, _ = unit(xg_ref[s * per:(s + 1) * per].reshape(per * samples, d).astype(f32))
            acted[at, :] = (u * gain + bias).astype(bf16)
        for i in range(3):
            w = units(g_refs[0], 16 + i * rl, rl) if np_ else w_ref[i]

            def project(at):
                y = dot(acted[at, :], w).astype(bf16)
                qkv_ref[i, at, :] = y * 0.125 if i == 0 else y

            blocks(rows, 256, project)

        turns = Turns(fs_n, hp, lambda p, j: o_ref.at[p, pl.ds(pl.multiple_of(j * samples, samples), samples)],
                      lambda p, j: back_ref.at[j, p], *turn_s)
        for p in range(hp):
            at = head_pair(p)
            vt[...] = qkv_ref[2, :, at].astype(f32).T.astype(bf16)
            for h in range(2):
                def part(i, _):
                    qa = pl.ds(pl.multiple_of(i * BQ, BQ), BQ)
                    q = qkv_ref[0, qa, at]
                    q = jnp.where(head_mask(BQ, h), q, jnp.zeros_like(q))
                    s = dot(qkv_ref[1, :, at], q, NT) + kb_ref[:, 0:1]
                    m = jnp.max(s, 0, keepdims=True)
                    e = jnp.exp(s - m)
                    tot = jnp.sum(e, 0, keepdims=True)
                    o = dot(vt[h * 64:h * 64 + 64, :], e.astype(bf16))
                    ot[h * 64:h * 64 + 64, qa] = o * (1.0 / tot)
                    l_ref[p * 2 + h:p * 2 + h + 1, qa] = m + jnp.log(tot)
                    return 0
                lax.fori_loop(0, rows // BQ, part, 0)
            o_ref[p, :, :] = ot[...].T.astype(bf16)
            turns.start(p)
            if np_ and p == 0:
                gathers[1].hand_on(0)
            if np_ and p == 2:
                gathers[1].hand_on(1)
        if np_:
            for k in range(2, z_n):
                gathers[1].hand_on(k)
            for k in range(z_n):
                gathers[1].corner(k)
        for p in range(hp):
            turns.wait_recv(p)
        turns.wait_send()
        if np_:
            gathers[1].wait()

    def units3(ref, start, size):
        v = ref[..., start:start + size, :]
        return v.reshape(-1, size, v.shape[-1])

    S, V = jax.ShapeDtypeStruct, pltpu.VMEM
    outs = [S((slots, hp, samples, 128), bf16), S((slots, samples, d), bf16), S((hp, rows, 128), bf16), S((3, rows, dh), bf16),
            S((heads, rows), f32)]
    outs += [S((dp_n, fs_n // 2, 2) + p.shape, bf16) for p in packs]
    args = [x, keybias] + list(packs)
    if np_:
        outs.append(S((16, d), f32))
    else:
        args += list(plain)
    return pl.pallas_call(
        body, out_shape=outs, in_specs=[VM] * len(args), out_specs=[ANY if np_ and i == 6 else VM for i in range(len(outs))],
        scratch_shapes=[V((rows, d), bf16), V((128, rows), bf16), V((128, rows), f32)] + swap_sems(fs_n) + turn_sems(fs_n, hp)
        + plane_gather_sems(fs_n) * np_,
        compiler_params=params(1), name="forward",
    )(*args)


def backward_kernel(do1, xg, qkv, o, lse, w, smalls, keybias, g1, gm, dp_n, fs_n, rl, dh, tasks, packed):
    slots, samples, d = xg.shape
    rows = slots * samples
    heads = dh // 64
    hp = heads // 2

    def body(*refs):
        it = iter(refs)
        do_in, xg_ref, qkv_ref, o_ref, l_ref, w_ref, n_ref, kb_ref = (next(it) for _ in range(8))
        g1_ref, gm_ref = (next(it), next(it)) if packed else (None, None)
        if packed:
            tg_ref, sm_ref, ss_ref = (next(it) for _ in range(3))
        else:
            dr_ref, gw_ref, gn_ref = (next(it) for _ in range(3))
        do, delta, kt, dqt, dk, dv, dqkv, acted, gn, dx = (next(it) for _ in range(10))
        turn_s = [next(it) for _ in range(3)]
        back_s = [next(it) for _ in range(3)]
        if packed:
            gs, dr_ref = next(it), next(it)
            rm = [next(it) for _ in range(11)]
            rs = [next(it) for _ in range(11)]

        greet(dp_n, fs_n, packed)
        turns = Turns(fs_n, hp, lambda p, j: do_in.at[j, p], lambda p, j: do.at[j, p], *turn_s)
        for p in range(hp):
            turns.start(p)
        if packed:
            red = PlaneReduce(fs_n, gm_ref, rm[:4], rm[4:])
            red_s = PlaneReduce(fs_n, gs, rs[:4], rs[4:])
            red.start()
            for k in red.order():
                red.first(k)
        gain, bias = n_ref[0:1, :], n_ref[1:2, :]
        lane = lax.broadcasted_iota(jnp.int32, (8, 128), 1) // 64
        pick = (lane == lax.broadcasted_iota(jnp.int32, (8, 128), 0)).astype(f32)
        per = BQ // samples if samples < BQ else 1

        def grad_rows(i, p):
            return do[pl.ds(i * per, per), p].reshape(per * samples, 128)

        n = per * samples
        for p in range(hp):
            at = head_pair(p)
            kt[...] = qkv_ref[1, :, at].astype(f32).T.astype(bf16)
            dk[...] = jnp.zeros_like(dk)
            dv[...] = jnp.zeros_like(dv)
            turns.wait_recv(p)

            def deltas(i, _):
                qa = pl.ds(pl.multiple_of(i * n, n), n)
                prod = grad_rows(i, p).astype(f32) * o_ref[p, qa, :].astype(f32)
                delta[:, qa] = lax.dot_general(pick, prod, NT, precision=lax.Precision.HIGHEST, preferred_element_type=f32)
                return 0

            lax.fori_loop(0, rows // n, deltas, 0)
            for h in range(2):
                def part(i, _):
                    qa = pl.ds(pl.multiple_of(i * n, n), n)
                    mask = head_mask(n, h)
                    q = qkv_ref[0, qa, at]
                    q = jnp.where(mask, q, jnp.zeros_like(q))
                    g = grad_rows(i, p)
                    g = jnp.where(mask, g, jnp.zeros_like(g))
                    s = dot(qkv_ref[1, :, at], q, NT) + kb_ref[:, 0:1]
                    e = jnp.exp(s - l_ref[p * 2 + h:p * 2 + h + 1, qa])
                    ds = (e * (dot(qkv_ref[2, :, at], g, NT) - delta[h:h + 1, qa])).astype(bf16)
                    dv[...] += dot(e.astype(bf16), g)
                    dk[...] += dot(ds, q)
                    dqt[h * 64:h * 64 + 64, qa] = dot(kt[h * 64:h * 64 + 64, :], ds) * 0.125
                    return 0
                lax.fori_loop(0, rows // n, part, 0)
            dqkv[0, :, at] = dqt[...].T.astype(bf16)
            dqkv[1, :, at] = dk[...].astype(bf16)
            dqkv[2, :, at] = dv[...].astype(bf16)
            if packed:
                if p == hp - 2:
                    for k in red.order():
                        red.second(k)
                if p == hp - 1:
                    for k in red.order():
                        red.third(k)

        def mats(i):
            return units(w_ref, 16 + i * rl, rl) if packed else w_ref[i]

        per2 = 256 // samples if samples < 256 else 1
        n2 = per2 * samples
        gn[...] = jnp.zeros_like(gn)

        def act_rows(i):
            at = pl.ds(pl.multiple_of(i * n2, n2), n2)
            u, r = unit(xg_ref[pl.ds(i * per2, per2)].reshape(n2, d).astype(f32))
            return at, u, r

        def first(i, _):
            at, u, r = act_rows(i)
            acted[at, :] = (u * gain + bias).astype(bf16)
            return 0

        lax.fori_loop(0, rows // n2, first, 0)
        for i in range(3):
            if packed:
                y = dot(acted[...], dqkv[i], TN).astype(bf16)
                gs[:, :, :, 16 + i * rl:16 + (i + 1) * rl, :] = y.reshape(gs.shape[:3] + (rl, d))
            else:
                gw_ref[i] = dot(acted[...], dqkv[i], TN).astype(bf16)

        back = Turns(fs_n, 1, lambda p, j: dx.at[j], lambda p, j: dr_ref.at[j], *back_s)

        def sums(i, _):
            at, u, r = act_rows(i)
            y = dot(dqkv[0, at, :], mats(0), NT) + dot(dqkv[1, at, :], mats(1), NT) + dot(dqkv[2, at, :], mats(2), NT)
            gn[0:1, :] += jnp.sum(y * u, 0, keepdims=True)
            gn[1:2, :] += jnp.sum(y, 0, keepdims=True)
            dx[pl.ds(i * per2, per2)] = unit_back(y, u, r, gain).astype(bf16).reshape(per2, samples, d)
            return 0

        lax.fori_loop(0, rows // n2, sums, 0)
        back.start(0)
        if packed:
            small = jnp.concatenate([gn[...].astype(bf16), jnp.zeros_like(gn).astype(bf16)], 0)
            gs[:, :, :, 0:16, :] = jnp.broadcast_to(small, gs.shape[:3] + (16, d))
            red_s.start()
            for k in red_s.order():
                red_s.first(k)
            red.finish(sm_ref)
            for k in red_s.order():
                red_s.second(k)
            for k in red_s.order():
                red_s.third(k)
            back.wait_recv(0)
            feats = slots // tasks
            for s in range(slots):
                t, f = s // feats, s % feats
                for i in range(d // 128):
                    at = pl.ds(((t * samples * (d // 128)) + i) * feats + f, samples, stride=feats * (d // 128))
                    tg_ref[at, :] = g1_ref[s * samples:(s + 1) * samples, head_pair(i)] + dr_ref[s, :, head_pair(i)].astype(f32)
            red_s.finish(ss_ref)
        else:
            gn_ref[...] = gn[...]
            back.wait_recv(0)
        back.wait_send()
        turns.wait_send()

    S, V = jax.ShapeDtypeStruct, pltpu.VMEM
    args = [do1, xg, qkv, o, lse, w, smalls, keybias]
    scratch = [V((slots, hp, samples, 128), bf16), V((8, rows), f32), V((128, rows), bf16), V((128, rows), f32), V((rows, 128), f32),
               V((rows, 128), f32), V((3, rows, dh), bf16), V((rows, d), bf16), V((8, d), f32), V((slots, samples, d), bf16)]
    scratch += turn_sems(fs_n, hp) + turn_sems(fs_n, 1)
    if packed:
        args += [g1, gm]
        mrows, srows = gm.shape[3], 16 + 3 * rl
        outs = [S((rows * d // 128, 128), f32), S((mrows, d), f32), S((srows, d), f32)]
        scratch += [V((dp_n, fs_n // 2, 2, srows, d), bf16), V((slots, samples, d), bf16)]
        scratch += plane_reduce_scratch(fs_n, mrows, d) + plane_reduce_scratch(fs_n, srows, d)
    else:
        outs = [S((slots, samples, d), bf16), S((3, d, dh), bf16), S((8, d), f32)]
    return pl.pallas_call(
        body, out_shape=outs, in_specs=[ANY if packed and i == 9 else VM for i in range(len(args))], out_specs=[VM] * len(outs), scratch_shapes=scratch,
        compiler_params=params(2), name="backward",
    )(*args)
def up16(a):
    rows = a.shape[-2]
    extra = (-rows) % 16
    return a if extra == 0 else jnp.pad(a, [(0, 0)] * (a.ndim - 2) + [(0, extra), (0, 0)])


def local(tokens, sample_counts, feature_counts, norms, sample_qkv, sample_out, feature_qkv, feature_out, mlp_in, mlp_in_bias,
          mlp_out, mlp_out_bias, cotangent):
    dp_n, fs_n = lax.axis_size("dp"), lax.axis_size("fsdp")
    nd = dp_n * fs_n
    me_d, me_f = lax.axis_index("dp"), lax.axis_index("fsdp")
    me = me_d * fs_n + me_f
    tasks, samples, feats, d = tokens.shape
    pairs = tasks * feats
    rep = fs_n // pairs
    dh = d // rep
    hp = dh // 128
    rl = sample_out.shape[0]
    chunks = mlp_in.shape[1] // d
    fl = mlp_out.shape[0]
    total = samples * fs_n
    packed = rep == 1 and dp_n == 4 and rl % 16 == 0 and 256 % fl == 0

    small = jnp.zeros((16, d), bf16)
    small = lax.dynamic_update_slice(small, norms, (0, me * rl))
    small = lax.dynamic_update_slice(small, mlp_out_bias[None, :], (6, me * rl))
    small = lax.dynamic_update_slice(small, mlp_in_bias[None, :], (7 + (me * fl) // d, lax.rem(me * fl, d)))
    split_in = mlp_in.reshape(rl, chunks, d).transpose(1, 0, 2).reshape(chunks * rl, d)
    pack_a = up16(jnp.concatenate([small, sample_qkv.reshape(3 * rl, d)], 0))
    pack_b = up16(jnp.concatenate([sample_out, feature_qkv.reshape(3 * rl, d), feature_out, split_in, mlp_out], 0))

    xp = tokens.transpose(0, 2, 1, 3).reshape(pairs, samples, d)
    cp = cotangent.transpose(0, 2, 1, 3).reshape(pairs, samples, d)
    my_task = me_f // rep // feats
    count = lax.dynamic_index_in_dim(sample_counts, my_task, keepdims=False)
    keybias = jnp.broadcast_to(jnp.where(jnp.arange(total) < count, 0.0, MASKED).astype(f32)[:, None], (total, 128))
    shown = jnp.arange(feats)[None, :] < feature_counts[:, None]
    fbias = jnp.broadcast_to(jnp.where(shown, 0.0, MASKED).astype(f32).reshape(pairs, 1), (pairs, 128))

    if packed:
        back, xg, o, qkv, lse, ga, gb, smalls = forward_kernel(xp, [pack_a, pack_b], None, keybias, dp_n, fs_n, rl, dh)
        w_mine, w_mid, size = ga, gb.reshape(nd, gb.shape[3], d), rl
    else:
        ga, gb = gather_call([pack_a, pack_b], dp_n, fs_n, 3)
        ga, gb = ga.reshape((nd,) + ga.shape[3:]), gb.reshape((nd,) + gb.shape[3:])

        def take(g, start, rows):
            return g[:, start:start + rows].reshape(nd * rows, d)

        smalls = jnp.sum(ga[:, :16].astype(f32), 0)
        w_s = jnp.stack([take(ga, 16 + i * rl, rl) for i in range(3)])
        first = lax.rem(me_f, rep) * dh
        w_mine = lax.dynamic_slice_in_dim(w_s, first, dh, 2)
        w_mid = jnp.concatenate([take(gb, i * rl, rl) for i in range(5 + chunks)] + [take(gb, (5 + chunks) * rl, fl)])[None]
        size = d
        back, xg, o, qkv, lse = forward_kernel(jnp.repeat(xp, rep, 0), [], [w_mine, smalls], keybias, dp_n, fs_n, rl, dh)

    lo, g1, do1, gm = middle_call(xp, back.reshape(pairs, rep * hp, samples, 128), cp, smalls, fbias, w_mid, tasks, chunks, size)
    do1 = do1.reshape(fs_n, hp, samples, 128)
    if packed:
        gm = gm.reshape((dp_n, fs_n // 2, 2) + gm.shape[1:])
        tokens_grad, sm, ss = backward_kernel(do1, xg, qkv, o, lse, w_mine, smalls, keybias, g1, gm, dp_n, fs_n, rl, dh, tasks, True)
        tokens_grad = tokens_grad.reshape(tasks, samples, d // 128, feats, 128).transpose(0, 1, 3, 2, 4).reshape(tokens.shape)
        gn, outs, s = ss[0:2], [ss[16:]], sm
    else:
        dxr, gs, gn_s = backward_kernel(do1, xg, qkv, o, lse, w_mine, smalls, keybias, None, None, dp_n, fs_n, rl, dh, tasks, False)
        dxr = jnp.sum(dxr.reshape(pairs, rep, samples, d).astype(f32), 1)
        tokens_grad = (g1.reshape(pairs, samples, d) + dxr).reshape(tasks, feats, samples, d).transpose(0, 2, 1, 3)
        gs = lax.dynamic_update_slice_in_dim(jnp.zeros((3, d, d), bf16), gs, first, 2)

        def give(g, parts):
            return g.reshape(parts, nd, -1, d).transpose(1, 0, 2, 3).reshape(nd, -1, d)

        gm = gm[0]
        mix = jnp.concatenate([gn_s[0:2].astype(bf16), gm[2:16]], 0)
        grads = up16(jnp.concatenate([jnp.broadcast_to(mix[None], (nd, 16, d)), give(gm[16:16 + (5 + chunks) * d], 5 + chunks),
                                      give(gm[16 + (5 + chunks) * d:], 1), give(gs, 3)], 1))
        s = scatter_call(grads.reshape((dp_n, fs_n // 2, 2) + grads.shape[1:]), dp_n, fs_n, 6)
        outs = [s[16 + (5 + chunks) * rl + fl:][:3 * rl]]
        gn = s[0:2]
    gn = jnp.concatenate([gn, s[2:16]], 0)
    layer_output = lo.reshape(tasks, feats, samples, d).transpose(0, 2, 1, 3)

    def piece(start, rows):
        return s[16 + start * rl:16 + start * rl + rows]

    return (
        layer_output,
        tokens_grad,
        lax.dynamic_slice(gn, (0, me * rl), (6, rl)),
        outs[0].reshape(3, rl, d), piece(0, rl), piece(1, 3 * rl).reshape(3, rl, d), piece(4, rl),
        piece(5, chunks * rl).reshape(chunks, rl, d).transpose(1, 0, 2).reshape(rl, chunks * d),
        lax.dynamic_slice(gn[7:7 + chunks].reshape(-1), (me * fl,), (fl,)),
        piece(5 + chunks, fl),
        lax.dynamic_slice(gn[6], (me * rl,), (rl,)),
    )


def solution(mesh):
    rows, whole = ("dp", "fsdp"), P("dp", "fsdp", None, None)
    weights = (P(None, rows), P(None, rows, None), P(rows, None), P(None, rows, None), P(rows, None), P(rows, None), P(rows),
               P(rows, None), P(rows))
    return jax.shard_map(local, mesh=mesh, in_specs=(whole, P("dp"), P("dp")) + weights + (whole,),
                         out_specs=(whole, whole) + weights, check_vma=False)
```

```python
import functools
import jax
import jax.numpy as jnp
from jax import lax
from jax.experimental import pallas as pl
from jax.experimental.pallas import tpu as pltpu
from jax.sharding import PartitionSpec as P

MESH = pl.DeviceIdType.MESH
f32, bf16 = jnp.float32, jnp.bfloat16


def mod(a, n):
    return lax.rem(a, n)


def greet(dp_n, fs_n, with_dp=True):
    me_d, me_f = lax.axis_index("dp"), lax.axis_index("fsdp")
    barrier = pltpu.get_barrier_semaphore()
    n = 0
    for k in range(1, fs_n):
        pl.semaphore_signal(barrier, inc=1, device_id=(me_d, mod(me_f + k, fs_n)), device_id_type=MESH)
        n += 1
    if with_dp:
        for k in range(1, dp_n):
            pl.semaphore_signal(barrier, inc=1, device_id=(mod(me_d + k, dp_n), me_f), device_id_type=MESH)
            n += 1
    pl.semaphore_wait(barrier, n)


def rcopy(src, dst, ss, rs, dev):
    return pltpu.make_async_remote_copy(src_ref=src, dst_ref=dst, send_sem=ss, recv_sem=rs, device_id=dev, device_id_type=MESH)


class Swap:
    def __init__(self, fs_n, src, dst, local_sem, ss, rs):
        me_d, me_f = lax.axis_index("dp"), lax.axis_index("fsdp")
        self.own = pltpu.make_async_copy(src.at[me_f], dst.at[me_f], local_sem)
        self.copies = []
        for k in range(1, fs_n):
            to = mod(me_f + k, fs_n)
            self.copies.append(rcopy(src.at[to], dst.at[me_f], ss.at[k - 1], rs.at[k - 1], (me_d, to)))

    def start(self):
        for c in self.copies:
            c.start()
        self.own.start()

    def wait(self):
        self.own.wait()
        for c in self.copies:
            c.wait()


class Gather:
    def __init__(self, dp_n, fs_n, src, dst, local_sem, zs, zr, ds, dr, cs, cr):
        me_d, me_f = lax.axis_index("dp"), lax.axis_index("fsdp")
        z_n = fs_n // 2
        me_z, me_c = me_f // 2, mod(me_f, 2)
        self.z_n, self.dp_n = z_n, dp_n
        partner = (me_d, me_z * 2 + 1 - me_c)
        self.own = pltpu.make_async_copy(src, dst.at[me_d, me_z, me_c], local_sem)
        self.z = []
        for k in range(1, z_n):
            to = mod(me_z + k, z_n) * 2 + me_c
            self.z.append(rcopy(src, dst.at[me_d, me_z, me_c], zs.at[k - 1], zr.at[k - 1], (me_d, to)))
        self.d = {}
        self.c = {}
        for k in range(z_n):
            z = mod(me_z - k + z_n, z_n)
            for j in range(dp_n):
                d = mod(me_d - j + dp_n, dp_n)
                here = src if (k == 0 and j == 0) else dst.at[d, z, me_c]
                self.c[k, j] = rcopy(here, dst.at[d, z, me_c], cs.at[k * dp_n + j], cr.at[k * dp_n + j], partner)
                if j > 0:
                    here = src if k == 0 else dst.at[me_d, z, me_c]
                    i = k * (dp_n - 1) + j - 1
                    self.d[k, j] = rcopy(here, dst.at[me_d, z, me_c], ds.at[i], dr.at[i], (mod(me_d + j, dp_n), me_f))

    def start(self):
        for c in self.z:
            c.start()
        self.own.start()
        for j in range(1, self.dp_n):
            self.d[0, j].start()
        self.c[0, 0].start()

    def forward_z(self):
        for k in range(1, self.z_n):
            self.z[k - 1].wait_recv()
            for j in range(1, self.dp_n):
                self.d[k, j].start()
            self.c[k, 0].start()

    def forward_d(self):
        for k in range(self.z_n):
            for j in range(1, self.dp_n):
                self.d[k, j].wait_recv()
                self.c[k, j].start()

    def wait(self):
        self.own.wait()
        for c in self.z:
            c.wait_send()
        for c in self.d.values():
            c.wait_send()
        for c in self.c.values():
            c.wait()


def gather_sems(dp_n, fs_n):
    z = fs_n // 2
    D = pltpu.SemaphoreType.DMA
    return [D, D((z - 1,)), D((z - 1,)), D((z * (dp_n - 1),)), D((z * (dp_n - 1),)), D((z * dp_n,)), D((z * dp_n,))]


def swap_sems(fs_n):
    D = pltpu.SemaphoreType.DMA
    return [D, D((fs_n - 1,)), D((fs_n - 1,))]


ANY = pl.BlockSpec(memory_space=pl.ANY)
VM = pl.BlockSpec(memory_space=pltpu.VMEM)


def swap_call(x, dp_n, fs_n, cid, space=ANY):
    def body(x_ref, o_ref, *sems):
        greet(dp_n, fs_n, False)
        s = Swap(fs_n, x_ref, o_ref, *sems)
        s.start()
        s.wait()

    return pl.pallas_call(
        body, out_shape=jax.ShapeDtypeStruct(x.shape, x.dtype), in_specs=[space], out_specs=space,
        scratch_shapes=swap_sems(fs_n),
        compiler_params=pltpu.CompilerParams(collective_id=cid, has_side_effects=True, vmem_limit_bytes=60 << 20),
        name="swap%d" % cid,
    )(x)


def gather_call(packs, dp_n, fs_n, cid, space=ANY):
    n = len(packs)

    def body(*refs):
        ins, outs, sems = refs[:n], refs[n:2 * n], refs[2 * n:]
        greet(dp_n, fs_n)
        gs = [Gather(dp_n, fs_n, ins[i], outs[i], *sems[7 * i:7 * i + 7]) for i in range(n)]
        for g in gs:
            g.start()
        for g in gs:
            g.forward_z()
        for g in gs:
            g.forward_d()
        for g in gs:
            g.wait()

    return pl.pallas_call(
        body,
        out_shape=[jax.ShapeDtypeStruct((dp_n, fs_n // 2, 2) + p.shape, p.dtype) for p in packs],
        in_specs=[space] * n, out_specs=[space] * n,
        scratch_shapes=gather_sems(dp_n, fs_n) * n,
        compiler_params=pltpu.CompilerParams(collective_id=cid, has_side_effects=True, vmem_limit_bytes=60 << 20),
        name="gather%d" % cid,
    )(*packs)


def scatter_call(g, dp_n, fs_n, cid):
    z_n = fs_n // 2
    rows, width = g.shape[3:]
    step = 16

    def body(g_ref, o_ref, from_c, half, from_d, quarter, from_z, cs, cr, ds, dr, zs, zr):
        me_d, me_f = lax.axis_index("dp"), lax.axis_index("fsdp")
        me_z, me_c = me_f // 2, mod(me_f, 2)
        greet(dp_n, fs_n)
        partner = (me_d, me_z * 2 + 1 - me_c)

        def add(out, parts):
            def one(i, _):
                at = pl.ds(pl.multiple_of(i * step, step), step)
                total = parts[0][at, :].astype(f32)
                for p in parts[1:]:
                    total = total + p[at, :].astype(f32)
                out[at, :] = total.astype(out.dtype)
                return 0
            lax.fori_loop(0, rows // step, one, 0, unroll=True if rows // step <= 4 else 4)

        order = [(j, k) for j in list(range(1, dp_n)) + [0] for k in list(range(1, z_n)) + [0]]
        cc, dd, zz = {}, {}, {}
        for i, (j, k) in enumerate(order):
            d, z = mod(me_d + j, dp_n), mod(me_z + k, z_n)
            cc[j, k] = rcopy(g_ref.at[d, z, 1 - me_c], from_c.at[i], cs.at[i], cr.at[i], partner)
            cc[j, k].start()
        for i, (j, k) in enumerate(order):
            d, z = mod(me_d + j, dp_n), mod(me_z + k, z_n)
            cc[j, k].wait_recv()
            add(half.at[j, k], [g_ref.at[d, z, me_c], from_c.at[i]])
            if j:
                n = (j - 1) * z_n + k
                dd[j, k] = rcopy(half.at[j, k], from_d.at[j - 1, k], ds.at[n], dr.at[n], (d, me_f))
                dd[j, k].start()
        for k in list(range(1, z_n)) + [0]:
            for j in range(1, dp_n):
                dd[j, k].wait_recv()
            if k:
                add(quarter.at[k], [half.at[0, k]] + [from_d.at[j - 1, k] for j in range(1, dp_n)])
                to = mod(me_z + k, z_n) * 2 + me_c
                zz[k] = rcopy(quarter.at[k], from_z.at[k - 1], zs.at[k - 1], zr.at[k - 1], (me_d, to))
                zz[k].start()
        for k in range(1, z_n):
            zz[k].wait_recv()
        add(o_ref, [half.at[0, 0]] + [from_d.at[j - 1, 0] for j in range(1, dp_n)] + [from_z.at[k - 1] for k in range(1, z_n)])
        for c in list(cc.values()) + list(dd.values()) + list(zz.values()):
            c.wait_send()

    D = pltpu.SemaphoreType.DMA
    n = dp_n * z_n
    return pl.pallas_call(
        body, out_shape=jax.ShapeDtypeStruct((rows, width), f32), in_specs=[VM], out_specs=VM,
        scratch_shapes=[
            pltpu.VMEM((n, rows, width), bf16), pltpu.VMEM((dp_n, z_n, rows, width), bf16),
            pltpu.VMEM((dp_n - 1, z_n, rows, width), bf16), pltpu.VMEM((z_n, rows, width), bf16),
            pltpu.VMEM((z_n - 1, rows, width), bf16),
            D((n,)), D((n,)), D((n - z_n,)), D((n - z_n,)), D((z_n - 1,)), D((z_n - 1,)),
        ],
        compiler_params=pltpu.CompilerParams(collective_id=cid, has_side_effects=True, vmem_limit_bytes=60 << 20),
        name="scatter%d" % cid,
    )(g)
class PlaneGather:
    def __init__(self, fs_n, src, dst, local_sem, zs, zr, ds, dr, cs, cr):
        me_d, me_f = lax.axis_index("dp"), lax.axis_index("fsdp")
        z_n = fs_n // 2
        me_z, me_c = me_f // 2, mod(me_f, 2)
        self.z_n = z_n
        partner = (me_d, me_z * 2 + 1 - me_c)
        ds_ = [me_d, me_d // 2 * 2 + 1 - mod(me_d, 2), mod(me_d + 2, 4), 3 - me_d]
        zs_ = [mod(me_z - k + z_n, z_n) for k in range(z_n)]
        self.own = pltpu.make_async_copy(src, dst.at[me_d, me_z, me_c], local_sem)
        self.z, self.n, self.fwd, self.c = {}, {}, {}, {}
        for k in range(z_n):
            at = lambda j: dst.at[ds_[j], zs_[k], me_c]
            mine = src if k == 0 else at(0)
            if k:
                to = mod(me_z + k, z_n) * 2 + me_c
                self.z[k] = rcopy(src, dst.at[me_d, me_z, me_c], zs.at[k - 1], zr.at[k - 1], (me_d, to))
            for j in (1, 2):
                self.n[k, j] = rcopy(mine, at(0), ds.at[3 * k + j - 1], dr.at[3 * k + j - 1], (ds_[j], me_f))
            first = 1 + k % 2
            self.fwd[k] = rcopy(at(first), at(first), ds.at[3 * k + 2], dr.at[3 * k + 2], (ds_[3 - first], me_f))
            for j in range(4):
                self.c[k, j] = rcopy(mine if j == 0 else at(j), at(j), cs.at[4 * k + j], cr.at[4 * k + j], partner)

    def start(self):
        for c in self.z.values():
            c.start()
        self.own.start()
        self.spread(0)

    def spread(self, k):
        if k:
            self.z[k].wait_recv()
        self.n[k, 1].start()
        self.n[k, 2].start()
        self.c[k, 0].start()

    def hand_on(self, k):
        first = 1 + k % 2
        for j in (first, 3 - first):
            self.n[k, j].wait_recv()
            if j == first:
                self.fwd[k].start()
            self.c[k, j].start()

    def corner(self, k):
        self.fwd[k].wait_recv()
        self.c[k, 3].start()

    def wait(self):
        self.own.wait()
        for c in list(self.z.values()) + list(self.n.values()) + list(self.fwd.values()):
            c.wait_send()
        for c in self.c.values():
            c.wait()


def plane_gather_sems(fs_n):
    z, D = fs_n // 2, pltpu.SemaphoreType.DMA
    return [D, D((z - 1,)), D((z - 1,)), D((3 * z,)), D((3 * z,)), D((4 * z,)), D((4 * z,))]


class PlaneReduce:
    def __init__(self, fs_n, g, bufs, sems):
        me_d, me_f = lax.axis_index("dp"), lax.axis_index("fsdp")
        z_n = fs_n // 2
        me_z, me_c = me_f // 2, mod(me_f, 2)
        self.z_n, self.rows = z_n, g.shape[3]
        self.from_c, self.from_n, self.from_z = bufs
        cs, cr, ds, dr, zs, zr = sems
        partner = (me_d, me_z * 2 + 1 - me_c)
        ds_ = [me_d, me_d // 2 * 2 + 1 - mod(me_d, 2), mod(me_d + 2, 4), 3 - me_d]
        self.mine, self.c, self.n, self.z = {}, {}, {}, {}
        for k in range(z_n):
            z = mod(me_z + k, z_n)
            for j in range(4):
                i = 4 * k + j
                self.mine[k, j] = g.at[ds_[j], z, me_c]
                self.c[k, j] = rcopy(g.at[ds_[j], z, 1 - me_c], self.from_c.at[k, j], cs.at[i], cr.at[i], partner)
            first = 1 + k % 2
            send = [(first, first), (3, first), (3 - first, 3 - first)]
            for i, (j, to) in enumerate(send):
                self.n[k, i] = rcopy(self.mine[k, j], self.from_n.at[k, i], ds.at[3 * k + i], dr.at[3 * k + i], (ds_[to], me_f))
            if k:
                to = mod(me_z + k, z_n) * 2 + me_c
                self.z[k] = rcopy(self.mine[k, 0], self.from_z.at[k - 1], zs.at[k - 1], zr.at[k - 1], (me_d, to))

    def add(self, out, parts):
        step = 16

        def one(i, _):
            at = pl.ds(pl.multiple_of(i * step, step), step)
            total = parts[0][at, :].astype(f32)
            for p in parts[1:]:
                total = total + p[at, :].astype(f32)
            out[at, :] = total.astype(out.dtype)
            return 0

        n = self.rows // step
        lax.fori_loop(0, n, one, 0, unroll=2 if n % 2 == 0 else 1)

    def order(self):
        return list(range(1, self.z_n)) + [0]

    def start(self):
        for k in self.order():
            for j in (1 + k % 2, 3, 2 - k % 2, 0):
                self.c[k, j].start()

    def first(self, k):
        first = 1 + k % 2
        for j in (first, 3, 3 - first, 0):
            self.c[k, j].wait_recv()
            self.add(self.mine[k, j], [self.mine[k, j], self.from_c.at[k, j]])
            if j == first:
                self.n[k, 0].start()
            if j == 3:
                self.n[k, 1].start()

    def second(self, k):
        first = 1 + k % 2
        self.n[k, 1].wait_recv()
        j = 3 - first
        self.add(self.mine[k, j], [self.mine[k, j], self.from_n.at[k, 1]])
        self.n[k, 2].start()

    def third(self, k):
        self.n[k, 0].wait_recv()
        self.n[k, 2].wait_recv()
        if k:
            self.add(self.mine[k, 0], [self.mine[k, 0], self.from_n.at[k, 0], self.from_n.at[k, 2]])
            self.z[k].start()

    def every(self, step):
        for k in self.order():
            step(k)

    def finish(self, out):
        for k in range(1, self.z_n):
            self.z[k].wait_recv()
        self.add(out, [self.mine[0, 0], self.from_n.at[0, 0], self.from_n.at[0, 2]] + [self.from_z.at[k - 1] for k in range(1, self.z_n)])
        for c in list(self.c.values()) + list(self.n.values()) + list(self.z.values()):
            c.wait_send()


def plane_reduce_scratch(fs_n, rows, width):
    z_n, V = fs_n // 2, pltpu.VMEM
    return [V((z_n, 4, rows, width), bf16), V((z_n, 3, rows, width), bf16), V((z_n - 1, rows, width), bf16)]


def plane_reduce_sems(fs_n):
    z_n, D = fs_n // 2, pltpu.SemaphoreType.DMA
    return [D((4 * z_n,)), D((4 * z_n,)), D((3 * z_n,)), D((3 * z_n,)), D((z_n - 1,)), D((z_n - 1,))]


HEADS = 8
EPS = 1e-05
MASKED = -1e30
NN = (((1,), (0,)), ((), ()))
NT = (((1,), (1,)), ((), ()))
TN = (((0,), (0,)), ((), ()))


def dot(a, b, dims=NN):
    return lax.dot_general(a, b, dims, preferred_element_type=f32)


def unit(x):
    c = x - jnp.mean(x, -1, keepdims=True)
    r = lax.rsqrt(jnp.mean(c * c, -1, keepdims=True) + EPS)
    return c * r, r


def unit_back(y, u, r, gain):
    yg = y * gain
    return r * (yg - jnp.mean(yg, -1, keepdims=True) - u * jnp.mean(yg * u, -1, keepdims=True))


def blocks(total, size, body):
    lax.fori_loop(0, total // size, lambda i, c: (body(pl.ds(pl.multiple_of(i * size, size), size)), c)[1], 0)


def gelu_parts(v):
    z = jnp.abs(v) * 0.7071067811865476
    t = 1.0 / (1.0 + 0.3275911 * z)
    e = jnp.exp(-0.5 * (v * v))
    tail = t * (0.127414796 + t * (-0.142248368 + t * (0.7107068705 + t * (-0.7265760135 + t * 0.5307027145)))) * e
    return jnp.where(v >= 0, 1.0 - tail, tail), v * e * 0.3989422804014327


def head_mask(rows, second, width=128):
    lane = lax.broadcasted_iota(jnp.int32, (rows, width), 1)
    return (lane >= width // 2) if second else (lane < width // 2)


def params(cid=None):
    if cid is None:
        return pltpu.CompilerParams(vmem_limit_bytes=62 << 20)
    return pltpu.CompilerParams(collective_id=cid, has_side_effects=True, vmem_limit_bytes=62 << 20)


def head_pair(p):
    return slice(p * 128, p * 128 + 128)


def middle_call(x, o1, cot, smalls, fbias, w, tasks, chunks, unit_rows):
    pairs, samples, d = x.shape
    feats = pairs // tasks
    rows = pairs * samples
    hh = d // 64
    nd = w.shape[0]
    U = unit_rows
    OUT = (5 + chunks) * U
    fl = chunks * d // nd
    x, cot = x.reshape(rows, d), cot.reshape(rows, d)
    RB = 256
    per = RB // samples

    def body(x_ref, back_ref, cot_ref, n_ref, fb_ref, w_ref,
             lo_ref, g1_ref, do1_ref, g_ref,
             x1, a, qkv, p2, o2, acc, dacc, act, gh, dqkv, do2, o1_ref, gn_ref):
        gn_ref[...] = jnp.zeros_like(gn_ref)

        def at_unit(k):
            return pl.ds(pl.multiple_of(k * U, 16), U) if not isinstance(k, int) else slice(k * U, k * U + U)

        def mat(k):
            return w_ref[:, at_unit(k), :].reshape(d, d)

        def out_mat(c):
            if nd == 1:
                return w_ref[0, pl.ds(pl.multiple_of(OUT + c * d, 16), d), :]
            m = nd // chunks
            return w_ref[pl.ds(c * m, m), OUT:OUT + fl, :].reshape(d, d)

        def put(k, at, i, value):
            if nd == 1:
                g_ref[0, pl.ds(pl.multiple_of(16 + k * U + i * 256, 16), 256), :] = value
            else:
                m = 256 // U
                g_ref[pl.ds(i * m, m), pl.ds(pl.multiple_of(16 + k * U, 16), U), :] = value.reshape(m, U, d)

        def put_out(c, i, value):
            if nd == 1:
                g_ref[0, pl.ds(pl.multiple_of(16 + OUT + c * d + i * 256, 16), 256), :] = value
            else:
                m = 256 // fl
                g_ref[pl.ds(c * (nd // chunks) + i * m, m), 16 + OUT:16 + OUT + fl, :] = value.reshape(m, fl, d)

        def tiles(body):
            for i in range(d // 256):
                body(slice(i * 256, i * 256 + 256), i)

        def norm(i):
            return n_ref[2 * i:2 * i + 1, :], n_ref[2 * i + 1:2 * i + 2, :]

        def collect(i, _):
            at = pl.ds(pl.multiple_of(i * RB, RB), RB)
            for p in range(hh // 2):
                o1_ref[at, p * 128:p * 128 + 128] = back_ref[pl.ds(i * per, per), p].reshape(RB, 128)
            return 0

        lax.fori_loop(0, rows // RB, collect, 0)

        def first(at):
            y = x_ref[at, :].astype(f32) + dot(o1_ref[at, :], mat(0))
            x1[at, :] = y
            u, _ = unit(y)
            g, b = norm(1)
            v = (u * g + b).astype(bf16)
            a[at, :] = v
            for i in range(3):
                z = dot(v, mat(1 + i)).astype(bf16)
                qkv[i, at, :] = z * 0.125 if i == 0 else z

        blocks(rows, RB, first)

        half = lax.broadcasted_iota(jnp.int32, (256, 128), 0) // 64
        ones = (lax.rem(half, 2) == lax.broadcasted_iota(jnp.int32, (256, 128), 1) // 64).astype(bf16)

        def head_sums(prods):
            both = []
            for v in prods:
                hi = v.astype(bf16)
                both.append(jnp.concatenate([hi, (v - hi.astype(f32)).astype(bf16)], 1))
            out = dot(jnp.concatenate(both, 0), ones)
            return [out[i * samples:(i + 1) * samples] for i in range(len(prods))]

        def at_slot(t, f):
            return pl.ds(pl.multiple_of((t * feats + f) * samples, samples), samples)

        def mix(t, _):
            for p in range(hh // 2):
                lanes = head_pair(p)
                ks = [qkv[1, at_slot(t, g), lanes].astype(f32) for g in range(feats)]
                vs = [qkv[2, at_slot(t, g), lanes].astype(f32) for g in range(feats)]
                for f in range(feats):
                    q = qkv[0, at_slot(t, f), lanes].astype(f32)
                    sc = head_sums([q * k for k in ks])
                    sc = [v + fb_ref[pl.ds(t * feats + g, 1), :] for g, v in enumerate(sc)]
                    top = functools.reduce(jnp.maximum, sc)
                    sc = [jnp.exp(v - top) for v in sc]
                    inv = 1.0 / sum(sc)
                    sc = [v * inv for v in sc]
                    for g in range(feats):
                        p2[t, p, f, g] = sc[g]
                    o2[at_slot(t, f), lanes] = sum(w * v for w, v in zip(sc, vs)).astype(bf16)
            return 0

        lax.fori_loop(0, tasks, mix, 0)

        def second(at):
            y = x1[at, :] + dot(o2[at, :], mat(4))
            acc[at, :] = y
            u, _ = unit(y)
            g, b = norm(2)
            do2[at, :] = (u * g + b).astype(bf16)
            dacc[at, :] = jnp.zeros((RB, d), f32)

        blocks(rows, RB, second)

        def chunk(c, _):
            def part(at):
                hid = dot(do2[at, :], mat(5 + c)) + n_ref[pl.ds(7 + c, 1), :]
                cdf, pdf = gelu_parts(hid)
                al = (hid * cdf).astype(bf16)
                act[at, :] = al
                gl = ((cdf + pdf) * dot(cot_ref[at, :], out_mat(c), NT)).astype(bf16)
                gh[at, :] = gl
                gn_ref[pl.ds(7 + c, 1), :] += jnp.sum(gl.astype(f32), 0, keepdims=True)
                acc[at, :] += dot(al, out_mat(c))
                dacc[at, :] += dot(gl, mat(5 + c), NT)

            blocks(rows, RB, part)

            def weight(at, i):
                put_out(c, i, dot(act[:, at], cot_ref[...], TN).astype(bf16))
                put(5 + c, at, i, dot(do2[:, at], gh[...], TN).astype(bf16))

            tiles(weight)
            return 0

        lax.fori_loop(0, chunks, chunk, 0)

        def third(at):
            lo_ref[at, :] = (acc[at, :] + n_ref[6:7, :]).astype(bf16)
            u, r = unit(x1[at, :] + dot(o2[at, :], mat(4)))
            y = dacc[at, :]
            gn_ref[4:5, :] += jnp.sum(y * u, 0, keepdims=True)
            gn_ref[5:6, :] += jnp.sum(y, 0, keepdims=True)
            cf = cot_ref[at, :].astype(f32)
            gn_ref[6:7, :] += jnp.sum(cf, 0, keepdims=True)
            g2 = cf + unit_back(y, u, r, norm(2)[0])
            dacc[at, :] = g2
            e2 = g2.astype(bf16)
            act[at, :] = e2
            do2[at, :] = dot(e2, mat(4), NT).astype(bf16)

        blocks(rows, RB, third)

        def weight2(at, i):
            put(4, at, i, dot(o2[:, at], act[...], TN).astype(bf16))

        tiles(weight2)

        def unmix(t, _):
            for p in range(hh // 2):
                lanes = head_pair(p)
                ks = [qkv[1, at_slot(t, g), lanes].astype(f32) for g in range(feats)]
                vs = [qkv[2, at_slot(t, g), lanes].astype(f32) for g in range(feats)]
                dk, dv = [0.0] * feats, [0.0] * feats
                for f in range(feats):
                    q = qkv[0, at_slot(t, f), lanes].astype(f32)
                    gr = do2[at_slot(t, f), lanes].astype(f32)
                    dp = head_sums([gr * v for v in vs])
                    ws = [p2[t, p, f, g] for g in range(feats)]
                    mean = sum(w * v for w, v in zip(ws, dp))
                    ds = [(w * (v - mean)).astype(bf16).astype(f32) for w, v in zip(ws, dp)]
                    dqkv[0, at_slot(t, f), lanes] = (sum(v * k for v, k in zip(ds, ks)) * 0.125).astype(bf16)
                    for g in range(feats):
                        dk[g] += ds[g] * q
                        dv[g] += ws[g] * gr
                for g in range(feats):
                    dqkv[1, at_slot(t, g), lanes] = dk[g].astype(bf16)
                    dqkv[2, at_slot(t, g), lanes] = dv[g].astype(bf16)
            return 0

        lax.fori_loop(0, tasks, unmix, 0)

        def fourth(i, _):
            at = pl.ds(pl.multiple_of(i * RB, RB), RB)
            u, r = unit(x1[at, :])
            y = dot(dqkv[0, at, :], mat(1), NT) + dot(dqkv[1, at, :], mat(2), NT) + dot(dqkv[2, at, :], mat(3), NT)
            gn_ref[2:3, :] += jnp.sum(y * u, 0, keepdims=True)
            gn_ref[3:4, :] += jnp.sum(y, 0, keepdims=True)
            g1 = dacc[at, :] + unit_back(y, u, r, norm(1)[0])
            g1_ref[at, :] = g1
            e1 = g1.astype(bf16)
            act[at, :] = e1
            do = dot(e1, mat(0), NT).astype(bf16)
            for p in range(hh // 2):
                do1_ref[pl.ds(i * per, per), p] = do[:, p * 128:p * 128 + 128].reshape(per, samples, 128)
            return 0

        lax.fori_loop(0, rows // RB, fourth, 0)

        def weight3(at, i):
            put(0, at, i, dot(o1_ref[:, at], act[...], TN).astype(bf16))
            for j in range(3):
                put(1 + j, at, i, dot(a[:, at], dqkv[j], TN).astype(bf16))

        tiles(weight3)
        g_ref[:, 0:16, :] = jnp.broadcast_to(gn_ref[...].astype(bf16), (nd, 16, d))

    V = pltpu.VMEM
    S = jax.ShapeDtypeStruct
    return pl.pallas_call(
        body,
        out_shape=[S((rows, d), bf16), S((rows, d), f32), S((pairs, hh // 2, samples, 128), bf16),
                   S((nd, 16 + OUT + fl, d), bf16)],
        in_specs=[VM] * 6, out_specs=[VM] * 4,
        scratch_shapes=[V((rows, d), f32), V((rows, d), bf16), V((3, rows, d), bf16), V((tasks, hh // 2, feats, feats, samples, 128), f32), V((rows, d), bf16),
                        V((rows, d), f32), V((rows, d), f32), V((rows, d), bf16), V((rows, d), bf16), V((3, rows, d), bf16),
                        V((rows, d), bf16), V((rows, d), bf16), V((16, d), f32)],
        compiler_params=params(), name="middle",
    )(x, o1, cot, smalls, fbias, w)
BQ = 1024


class Turns:
    def __init__(self, fs_n, parts, src, dst, local_sem, ss, rs):
        me_d, me_f = lax.axis_index("dp"), lax.axis_index("fsdp")
        self.sets = []
        for p in range(parts):
            own = pltpu.make_async_copy(src(p, me_f), dst(p, me_f), local_sem.at[p])
            far = []
            for k in range(1, fs_n):
                to = mod(me_f + k, fs_n)
                i = p * (fs_n - 1) + k - 1
                far.append(rcopy(src(p, to), dst(p, me_f), ss.at[i], rs.at[i], (me_d, to)))
            self.sets.append((own, far))

    def start(self, p):
        own, far = self.sets[p]
        for c in far:
            c.start()
        own.start()

    def wait_recv(self, p):
        own, far = self.sets[p]
        own.wait()
        for c in far:
            c.wait_recv()

    def wait_send(self):
        for _, far in self.sets:
            for c in far:
                c.wait_send()


def turn_sems(fs_n, parts):
    D = pltpu.SemaphoreType.DMA
    return [D((parts,)), D((parts * (fs_n - 1),)), D((parts * (fs_n - 1),))]


def units(ref, start, size):
    v = ref[..., start:start + size, :]
    return v.reshape(-1, v.shape[-1])


def forward_kernel(x, packs, plain, keybias, dp_n, fs_n, rl, dh):
    slots, samples, d = x.shape
    rows = slots * samples
    heads = dh // 64
    hp = heads // 2
    np_ = len(packs)

    def body(*refs):
        it = iter(refs)
        x_ref, kb_ref = next(it), next(it)
        pack_refs = [next(it) for _ in range(np_)]
        w_ref, sm_ref = (None, None) if np_ else (next(it), next(it))
        back_ref, xg_ref, o_ref, qkv_ref, l_ref = (next(it) for _ in range(5))
        g_refs = [next(it) for _ in range(np_)]
        if np_:
            sm_ref = next(it)
        acted, vt, ot = next(it), next(it), next(it)
        swap_s = [next(it) for _ in range(3)]
        turn_s = [next(it) for _ in range(3)]
        gat_s = [[next(it) for _ in range(7)] for _ in range(np_)]

        greet(dp_n, fs_n, np_ > 0)
        gathers = [PlaneGather(fs_n, pack_refs[i], g_refs[i], *gat_s[i]) for i in range(np_)]
        swap = Swap(fs_n, x_ref, xg_ref, *swap_s)
        z_n = fs_n // 2
        if np_:
            gathers[0].start()
        swap.start()
        if np_:
            gathers[1].start()
            for k in range(1, z_n):
                gathers[0].spread(k)
            for k in range(z_n):
                gathers[0].hand_on(k)
            for k in range(1, z_n):
                gathers[1].spread(k)
            for k in range(z_n):
                gathers[0].corner(k)
        swap.wait()
        if np_:
            gathers[0].wait()
            sm_ref[...] = jnp.sum(units3(g_refs[0], 0, 16).astype(f32), 0)
        gain, bias = sm_ref[0:1, :], sm_ref[1:2, :]
        per = 256 // samples if samples < 256 else 1
        for s in range(slots // per):
            at = slice(s * per * samples, (s + 1) * per * samples)
            u, _ = unit(xg_ref[s * per:(s + 1) * per].reshape(per * samples, d).astype(f32))
            acted[at, :] = (u * gain + bias).astype(bf16)
        for i in range(3):
            w = units(g_refs[0], 16 + i * rl, rl) if np_ else w_ref[i]

            def project(at):
                y = dot(acted[at, :], w).astype(bf16)
                qkv_ref[i, at, :] = y * 0.125 if i == 0 else y

            blocks(rows, 256, project)

        turns = Turns(fs_n, hp, lambda p, j: o_ref.at[p, pl.ds(pl.multiple_of(j * samples, samples), samples)],
                      lambda p, j: back_ref.at[j, p], *turn_s)
        for p in range(hp):
            at = head_pair(p)
            vt[...] = qkv_ref[2, :, at].astype(f32).T.astype(bf16)
            for h in range(2):
                def part(i, _):
                    qa = pl.ds(pl.multiple_of(i * BQ, BQ), BQ)
                    q = qkv_ref[0, qa, at]
                    q = jnp.where(head_mask(BQ, h), q, jnp.zeros_like(q))
                    s = dot(qkv_ref[1, :, at], q, NT) + kb_ref[:, 0:1]
                    m = jnp.max(s, 0, keepdims=True)
                    e = jnp.exp(s - m)
                    tot = jnp.sum(e, 0, keepdims=True)
                    o = dot(vt[h * 64:h * 64 + 64, :], e.astype(bf16))
                    ot[h * 64:h * 64 + 64, qa] = o * (1.0 / tot)
                    l_ref[p * 2 + h:p * 2 + h + 1, qa] = m + jnp.log(tot)
                    return 0
                lax.fori_loop(0, rows // BQ, part, 0)
            o_ref[p, :, :] = ot[...].T.astype(bf16)
            turns.start(p)
            if np_ and p == 0:
                gathers[1].hand_on(0)
            if np_ and p == 2:
                gathers[1].hand_on(1)
        if np_:
            for k in range(2, z_n):
                gathers[1].hand_on(k)
            for k in range(z_n):
                gathers[1].corner(k)
        for p in range(hp):
            turns.wait_recv(p)
        turns.wait_send()
        if np_:
            gathers[1].wait()

    def units3(ref, start, size):
        v = ref[..., start:start + size, :]
        return v.reshape(-1, size, v.shape[-1])

    S, V = jax.ShapeDtypeStruct, pltpu.VMEM
    outs = [S((slots, hp, samples, 128), bf16), S((slots, samples, d), bf16), S((hp, rows, 128), bf16), S((3, rows, dh), bf16),
            S((heads, rows), f32)]
    outs += [S((dp_n, fs_n // 2, 2) + p.shape, bf16) for p in packs]
    args = [x, keybias] + list(packs)
    if np_:
        outs.append(S((16, d), f32))
    else:
        args += list(plain)
    return pl.pallas_call(
        body, out_shape=outs, in_specs=[VM] * len(args), out_specs=[ANY if np_ and i == 6 else VM for i in range(len(outs))],
        scratch_shapes=[V((rows, d), bf16), V((128, rows), bf16), V((128, rows), f32)] + swap_sems(fs_n) + turn_sems(fs_n, hp)
        + plane_gather_sems(fs_n) * np_,
        compiler_params=params(1), name="forward",
    )(*args)


def backward_kernel(do1, xg, qkv, o, lse, w, smalls, keybias, g1, gm, dp_n, fs_n, rl, dh, tasks, packed):
    slots, samples, d = xg.shape
    rows = slots * samples
    heads = dh // 64
    hp = heads // 2

    def body(*refs):
        it = iter(refs)
        do_in, xg_ref, qkv_ref, o_ref, l_ref, w_ref, n_ref, kb_ref = (next(it) for _ in range(8))
        g1_ref, gm_ref = (next(it), next(it)) if packed else (None, None)
        if packed:
            tg_ref, sm_ref, ss_ref = (next(it) for _ in range(3))
        else:
            dr_ref, gw_ref, gn_ref = (next(it) for _ in range(3))
        do, delta, kt, dqt, dk, dv, dqkv, acted, gn, dx = (next(it) for _ in range(10))
        turn_s = [next(it) for _ in range(3)]
        back_s = [next(it) for _ in range(3)]
        if packed:
            gs, dr_ref = next(it), next(it)
            rm = [next(it) for _ in range(11)]
            rs = [next(it) for _ in range(11)]

        greet(dp_n, fs_n, packed)
        turns = Turns(fs_n, hp, lambda p, j: do_in.at[j, p], lambda p, j: do.at[j, p], *turn_s)
        for p in range(hp):
            turns.start(p)
        if packed:
            red = PlaneReduce(fs_n, gm_ref, rm[:4], rm[4:])
            red_s = PlaneReduce(fs_n, gs, rs[:4], rs[4:])
            red.start()
            for k in red.order():
                red.first(k)
        gain, bias = n_ref[0:1, :], n_ref[1:2, :]
        lane = lax.broadcasted_iota(jnp.int32, (8, 128), 1) // 64
        pick = (lane == lax.broadcasted_iota(jnp.int32, (8, 128), 0)).astype(f32)
        per = BQ // samples if samples < BQ else 1

        def grad_rows(i, p):
            return do[pl.ds(i * per, per), p].reshape(per * samples, 128)

        n = per * samples
        for p in range(hp):
            at = head_pair(p)
            kt[...] = qkv_ref[1, :, at].astype(f32).T.astype(bf16)
            dk[...] = jnp.zeros_like(dk)
            dv[...] = jnp.zeros_like(dv)
            turns.wait_recv(p)

            def deltas(i, _):
                qa = pl.ds(pl.multiple_of(i * n, n), n)
                prod = grad_rows(i, p).astype(f32) * o_ref[p, qa, :].astype(f32)
                delta[:, qa] = lax.dot_general(pick, prod, NT, precision=lax.Precision.HIGHEST, preferred_element_type=f32)
                return 0

            lax.fori_loop(0, rows // n, deltas, 0)
            for h in range(2):
                def part(i, _):
                    qa = pl.ds(pl.multiple_of(i * n, n), n)
                    mask = head_mask(n, h)
                    q = qkv_ref[0, qa, at]
                    q = jnp.where(mask, q, jnp.zeros_like(q))
                    g = grad_rows(i, p)
                    g = jnp.where(mask, g, jnp.zeros_like(g))
                    s = dot(qkv_ref[1, :, at], q, NT) + kb_ref[:, 0:1]
                    e = jnp.exp(s - l_ref[p * 2 + h:p * 2 + h + 1, qa])
                    ds = (e * (dot(qkv_ref[2, :, at], g, NT) - delta[h:h + 1, qa])).astype(bf16)
                    dv[...] += dot(e.astype(bf16), g)
                    dk[...] += dot(ds, q)
                    dqt[h * 64:h * 64 + 64, qa] = dot(kt[h * 64:h * 64 + 64, :], ds) * 0.125
                    return 0
                lax.fori_loop(0, rows // n, part, 0)
            dqkv[0, :, at] = dqt[...].T.astype(bf16)
            dqkv[1, :, at] = dk[...].astype(bf16)
            dqkv[2, :, at] = dv[...].astype(bf16)
            if packed:
                if p == hp - 2:
                    for k in red.order():
                        red.second(k)
                if p == hp - 1:
                    for k in red.order():
                        red.third(k)

        def mats(i):
            return units(w_ref, 16 + i * rl, rl) if packed else w_ref[i]

        per2 = 256 // samples if samples < 256 else 1
        n2 = per2 * samples
        gn[...] = jnp.zeros_like(gn)

        def act_rows(i):
            at = pl.ds(pl.multiple_of(i * n2, n2), n2)
            u, r = unit(xg_ref[pl.ds(i * per2, per2)].reshape(n2, d).astype(f32))
            return at, u, r

        def first(i, _):
            at, u, r = act_rows(i)
            acted[at, :] = (u * gain + bias).astype(bf16)
            return 0

        lax.fori_loop(0, rows // n2, first, 0)
        for i in range(3):
            if packed:
                y = dot(acted[...], dqkv[i], TN).astype(bf16)
                gs[:, :, :, 16 + i * rl:16 + (i + 1) * rl, :] = y.reshape(gs.shape[:3] + (rl, d))
            else:
                gw_ref[i] = dot(acted[...], dqkv[i], TN).astype(bf16)

        back = Turns(fs_n, 1, lambda p, j: dx.at[j], lambda p, j: dr_ref.at[j], *back_s)

        def sums(i, _):
            at, u, r = act_rows(i)
            y = dot(dqkv[0, at, :], mats(0), NT) + dot(dqkv[1, at, :], mats(1), NT) + dot(dqkv[2, at, :], mats(2), NT)
            gn[0:1, :] += jnp.sum(y * u, 0, keepdims=True)
            gn[1:2, :] += jnp.sum(y, 0, keepdims=True)
            dx[pl.ds(i * per2, per2)] = unit_back(y, u, r, gain).astype(bf16).reshape(per2, samples, d)
            return 0

        lax.fori_loop(0, rows // n2, sums, 0)
        back.start(0)
        if packed:
            small = jnp.concatenate([gn[...].astype(bf16), jnp.zeros_like(gn).astype(bf16)], 0)
            gs[:, :, :, 0:16, :] = jnp.broadcast_to(small, gs.shape[:3] + (16, d))
            red_s.start()
            for k in red_s.order():
                red_s.first(k)
            red.finish(sm_ref)
            for k in red_s.order():
                red_s.second(k)
            for k in red_s.order():
                red_s.third(k)
            back.wait_recv(0)
            feats = slots // tasks
            for s in range(slots):
                t, f = s // feats, s % feats
                for i in range(d // 128):
                    at = pl.ds(((t * samples * (d // 128)) + i) * feats + f, samples, stride=feats * (d // 128))
                    tg_ref[at, :] = g1_ref[s * samples:(s + 1) * samples, head_pair(i)] + dr_ref[s, :, head_pair(i)].astype(f32)
            red_s.finish(ss_ref)
        else:
            gn_ref[...] = gn[...]
            back.wait_recv(0)
        back.wait_send()
        turns.wait_send()

    S, V = jax.ShapeDtypeStruct, pltpu.VMEM
    args = [do1, xg, qkv, o, lse, w, smalls, keybias]
    scratch = [V((slots, hp, samples, 128), bf16), V((8, rows), f32), V((128, rows), bf16), V((128, rows), f32), V((rows, 128), f32),
               V((rows, 128), f32), V((3, rows, dh), bf16), V((rows, d), bf16), V((8, d), f32), V((slots, samples, d), bf16)]
    scratch += turn_sems(fs_n, hp) + turn_sems(fs_n, 1)
    if packed:
        args += [g1, gm]
        mrows, srows = gm.shape[3], 16 + 3 * rl
        outs = [S((rows * d // 128, 128), f32), S((mrows, d), f32), S((srows, d), f32)]
        scratch += [V((dp_n, fs_n // 2, 2, srows, d), bf16), V((slots, samples, d), bf16)]
        scratch += plane_reduce_scratch(fs_n, mrows, d) + plane_reduce_scratch(fs_n, srows, d)
    else:
        outs = [S((slots, samples, d), bf16), S((3, d, dh), bf16), S((8, d), f32)]
    return pl.pallas_call(
        body, out_shape=outs, in_specs=[ANY if packed and i == 9 else VM for i in range(len(args))], out_specs=[VM] * len(outs), scratch_shapes=scratch,
        compiler_params=params(2), name="backward",
    )(*args)
def ones_pairs():
    half = lax.broadcasted_iota(jnp.int32, (256, 128), 0) // 64
    return (lax.rem(half, 2) == lax.broadcasted_iota(jnp.int32, (256, 128), 1) // 64).astype(bf16)


def head_sums(prods, ones):
    both = []
    for v in prods:
        hi = v.astype(bf16)
        both.append(jnp.concatenate([hi, (v - hi.astype(f32)).astype(bf16)], 1))
    out = dot(jnp.concatenate(both, 0), ones)
    n = prods[0].shape[0]
    return [out[i * n:(i + 1) * n] for i in range(len(prods))]


def key_bias(ref, counts, feats):
    count = counts[lax.axis_index("fsdp") // feats]
    rows = lax.broadcasted_iota(jnp.int32, ref.shape, 0)
    ref[...] = jnp.where(rows < count, 0.0, MASKED)


def rows_at(i, n):
    return pl.ds(pl.multiple_of(i * n, n), n)


def first_kernel(x, scounts, fcounts, small_parts, s_qkv, s_out, f_qkv, f_out, m_in, m_out, tasks, fs_n):
    dp_n = 4
    slots, samples, d = x.shape
    feats = slots // tasks
    rows = slots * samples
    hp = d // 128
    rl = s_out.shape[0]
    fl = m_out.shape[0]
    chunks = m_in.shape[1] // d
    z_n = fs_n // 2
    ra, r1, r2 = 16 + 3 * rl, 5 * rl, chunks * rl + fl
    per = 256 // samples

    def body(x_ref, sc_ref, fc_ref, norms, ob, ib, sq, so, fq, fo, mi, mo,
             xg, qkv, o_ref, l_ref, ga, w1, w2, sm, x1, o2, a3, qkv2, p2, back_ref,
             pa, pb1, pb2, kb, acted, vt, ot, small, *sems):
        swap_s, turn_s = sems[:3], sems[3:6]
        gat_s = [sems[6 + 7 * i:13 + 7 * i] for i in range(3)]
        me = lax.axis_index("dp") * fs_n + lax.axis_index("fsdp")
        def placed(ref, first):
            n = ref.shape[1]
            hot = lax.broadcasted_iota(jnp.int32, (n, d), 1) == lax.broadcasted_iota(jnp.int32, (n, d), 0) + first
            return dot(ref[...], hot.astype(bf16))

        inner = lax.rem(me * fl, d)
        row = lax.broadcasted_iota(jnp.int32, (16, d), 0)
        small[...] = jnp.where(row == 7 + me * fl // d, placed(ib, inner), 0.0)
        small[0:6, :] = placed(norms, me * rl)
        small[6:7, :] = placed(ob, me * rl)
        pa[0:16, :] = small[...].astype(bf16)
        for i in range(3):
            pa[16 + i * rl:16 + (i + 1) * rl, :] = sq[i]
            pb1[(1 + i) * rl:(2 + i) * rl, :] = fq[i]
        pb1[0:rl, :] = so[...]
        pb1[4 * rl:5 * rl, :] = fo[...]
        for c in range(chunks):
            pb2[c * rl:(c + 1) * rl, :] = mi[:, c * d:(c + 1) * d]
        pb2[chunks * rl:, :] = mo[...]

        greet(dp_n, fs_n)
        A = PlaneGather(fs_n, pa, ga, *gat_s[0])
        B = PlaneGather(fs_n, pb1, w1, *gat_s[1])
        C = PlaneGather(fs_n, pb2, w2, *gat_s[2])
        swap = Swap(fs_n, x_ref, xg, *swap_s)
        turns = Turns(fs_n, hp, lambda p, j: o_ref.at[p, rows_at(j, samples)], lambda p, j: back_ref.at[j, p], *turn_s)
        later = list(range(1, z_n))
        A.start()
        swap.start()
        B.start()
        C.start()
        key_bias(kb, sc_ref, feats)
        for k in later:
            A.spread(k)
        for k in range(z_n):
            A.hand_on(k)
        for k in later:
            B.spread(k)
        for k in range(z_n):
            A.corner(k)
        for k in later:
            C.spread(k)
        swap.wait()
        A.wait()
        total = ga[:, :, :, 0:16, :].astype(f32)
        sm[...] = jnp.sum(total.reshape(-1, 16, d), 0)

        def act(i, _):
            u, _r = unit(xg[pl.ds(i * per, per)].reshape(256, d).astype(f32))
            acted[rows_at(i, 256), :] = (u * sm[0:1, :] + sm[1:2, :]).astype(bf16)
            return 0

        lax.fori_loop(0, rows // 256, act, 0)
        for i in range(3):
            w = units(ga, 16 + i * rl, rl)

            def project(at):
                y = dot(acted[at, :], w).astype(bf16)
                qkv[i, at, :] = y * 0.125 if i == 0 else y

            blocks(rows, 256, project)

        for p in range(hp):
            at = head_pair(p)
            vt[...] = qkv[2, :, at].astype(f32).T.astype(bf16)
            for h in range(2):
                def part(i, _):
                    qa = rows_at(i, BQ)
                    q = qkv[0, qa, at]
                    q = jnp.where(head_mask(BQ, h), q, jnp.zeros_like(q))
                    s = dot(qkv[1, :, at], q, NT) + kb[:, 0:1]
                    m = jnp.max(s, 0, keepdims=True)
                    e = jnp.exp(s - m)
                    tot = jnp.sum(e, 0, keepdims=True)
                    o = dot(vt[h * 64:h * 64 + 64, :], e.astype(bf16))
                    ot[h * 64:h * 64 + 64, qa] = o * (1.0 / tot)
                    l_ref[p * 2 + h:p * 2 + h + 1, qa] = m + jnp.log(tot)
                    return 0
                lax.fori_loop(0, rows // BQ, part, 0)
            o_ref[p, :, :] = ot[...].T.astype(bf16)
            turns.start(p)
            if p == 0:
                for k in range(z_n):
                    B.hand_on(k)
            if p == 1:
                for k in range(z_n):
                    B.corner(k)
            if p == 2:
                C.hand_on(0)
        B.wait()
        C.hand_on(1)
        for p in range(hp):
            turns.wait_recv(p)
        for k in range(2, z_n):
            C.hand_on(k)

        def first(i, _):
            at = rows_at(i, 256)
            o1 = jnp.concatenate([back_ref[pl.ds(i * per, per), p].reshape(256, 128) for p in range(hp)], 1)
            y = x_ref[pl.ds(i * per, per)].reshape(256, d).astype(f32) + dot(o1, units(w1, 0, rl))
            x1[at, :] = y
            u, _r = unit(y)
            v = (u * sm[2:3, :] + sm[3:4, :]).astype(bf16)
            for j in range(3):
                z = dot(v, units(w1, (1 + j) * rl, rl)).astype(bf16)
                qkv2[j, at, :] = z * 0.125 if j == 0 else z
            return 0

        lax.fori_loop(0, rows // 256, first, 0)
        ones = ones_pairs()

        def mix(t, _):
            slot = lambda f: rows_at(t * feats + f, samples)
            for p in range(hp):
                lanes = head_pair(p)
                ks = [qkv2[1, slot(g), lanes].astype(f32) for g in range(feats)]
                vs = [qkv2[2, slot(g), lanes].astype(f32) for g in range(feats)]
                for f in range(feats):
                    q = qkv2[0, slot(f), lanes].astype(f32)
                    sc = head_sums([q * k for k in ks], ones)
                    sc = [v + jnp.where(g < fc_ref[t], 0.0, MASKED) for g, v in enumerate(sc)]
                    top = functools.reduce(jnp.maximum, sc)
                    sc = [jnp.exp(v - top) for v in sc]
                    inv = 1.0 / sum(sc)
                    sc = [v * inv for v in sc]
                    for g in range(feats):
                        p2[t, p, f, g] = sc[g].astype(bf16)
                    o2[slot(f), lanes] = sum(w * v for w, v in zip(sc, vs)).astype(bf16)
            return 0

        lax.fori_loop(0, tasks, mix, 0)
        for k in range(z_n):
            C.corner(k)

        def second(at):
            u, _r = unit(x1[at, :] + dot(o2[at, :], units(w1, 4 * rl, rl)))
            a3[at, :] = (u * sm[4:5, :] + sm[5:6, :]).astype(bf16)

        blocks(rows, 256, second)
        turns.wait_send()
        C.wait()

    S, V = jax.ShapeDtypeStruct, pltpu.VMEM
    SM = pl.BlockSpec(memory_space=pltpu.SMEM)
    g = (dp_n, z_n, 2)
    outs = [S((slots, samples, d), bf16), S((3, rows, d), bf16), S((hp, rows, 128), bf16), S((2 * hp, rows), f32),
            S(g + (ra, d), bf16), S(g + (r1, d), bf16), S(g + (r2, d), bf16), S((16, d), f32), S((rows, d), f32), S((rows, d), bf16),
            S((rows, d), bf16), S((3, rows, d), bf16), S((tasks, hp, feats, feats, samples, 128), bf16), S((slots, hp, samples, 128), bf16)]
    return pl.pallas_call(
        body, out_shape=outs, in_specs=[VM, SM, SM] + [VM] * 9, out_specs=[ANY if i == 6 else VM for i in range(len(outs))],
        scratch_shapes=[V((ra, d), bf16), V((r1, d), bf16), V((r2, d), bf16), V((rows, 128), f32), V((rows, d), bf16), V((128, rows), bf16),
                        V((128, rows), f32), V((16, d), f32)] + swap_sems(fs_n) + turn_sems(fs_n, hp) + plane_gather_sems(fs_n) * 3,
        compiler_params=params(1), name="first",
    )(x, scounts, fcounts, *small_parts, s_qkv, s_out, f_qkv, f_out, m_in, m_out)


def second_kernel(cot, scounts, saved, tasks, rl, fl, fs_n):
    xg, qkv, o, lse, ga, w1, w2, sm, x1, o2, a3, qkv2, p2, back = saved
    slots, samples, d = xg.shape
    feats = slots // tasks
    rows = slots * samples
    hp = d // 128
    z_n = fs_n // 2
    chunks = (w2.shape[3] - fl) // rl
    r1, r2, rs = 16 + 5 * rl, chunks * rl + fl, 16 + 3 * rl
    RB = 256
    per = RB // samples
    bq = 512
    pq = bq // samples

    def body(cot_ref, sc_ref, l_ref, w2_ref, sm_ref, x1_ref, o2_ref, a3_ref,
             xg_h, qkv_h, o_h, ga_h, w1_h, qkv2_h, p2_h, back_h,
             g1, lo, dr, out2, out1, outs_,
             xg_, o_, w1_, q_, p2_, bk, acc, act, gh, do2, dqkv, G2, G1, do, do1, delta, kt, dqt, dk, dv, kb, gn,
             c2, n2, z2, c1, n1, z1, c0, n0, z0, load_sem, *sems):
        turn_s, back_s = sems[:3], sems[3:6]
        red_s = [sems[6 + 6 * i:12 + 6 * i] for i in range(3)]
        me_f = lax.axis_index("fsdp")
        me_z, me_c = me_f // 2, mod(me_f, 2)
        load = lambda i, src, dst: pltpu.make_async_copy(src, dst, load_sem.at[i])
        get_w1 = load(0, w1_h, w1_)
        get_q2 = load(1, qkv2_h, q_)
        get_p2 = load(2, p2_h, p2_)
        get_bk = load(3, back_h, bk)
        get_xg = load(4, xg_h, xg_)
        get_o = load(5, o_h, o_)
        get_q1 = load(6, qkv_h, q_)
        ga_ = w1_.at[:, :, :, 0:rs, :]
        get_ga = load(7, ga_h, ga_)
        early = [get_w1, get_q2, get_p2, get_bk, get_xg, get_o]
        for c in early:
            c.start()
        key_bias(kb, sc_ref, feats)
        gn[...] = jnp.zeros_like(gn)
        for i in range(rows // RB):
            acc[i * RB:(i + 1) * RB, :] = jnp.zeros((RB, d), f32)
            g1[i * RB:(i + 1) * RB, :] = jnp.zeros((RB, d), f32)
        greet(4, fs_n)

        def mat(k):
            return units(w1_, k * rl, rl)

        def in_mat(c):
            return w2_ref[:, :, :, pl.ds(pl.multiple_of(c * rl, rl), rl), :].reshape(d, d)

        def out_mat(c):
            return w2_ref[pl.ds(c, 1), :, :, chunks * rl:, :].reshape(d, d)

        def put(g, start, i, value):
            g[2 * i:2 * i + 2, :, :, pl.ds(start, rl), :] = value.reshape(2, z_n, 2, rl, d)

        halves = [(slice(i * 256, i * 256 + 256), i) for i in range(d // 256)]

        def chunk(c, _):
            def part(at):
                hid = dot(a3_ref[at, :], in_mat(c)) + sm_ref[pl.ds(7 + c, 1), :]
                cdf, pdf = gelu_parts(hid)
                al = (hid * cdf).astype(bf16)
                act[at, :] = al
                gl = ((cdf + pdf) * dot(cot_ref[at, :], out_mat(c), NT)).astype(bf16)
                gh[at, :] = gl
                gn[pl.ds(7 + c, 1), :] += jnp.sum(gl.astype(f32), 0, keepdims=True)
                acc[at, :] += dot(al, out_mat(c))
                g1[at, :] += dot(gl, in_mat(c), NT)

            blocks(rows, RB, part)
            for at, i in halves:
                value = dot(act[:, at], cot_ref[...], TN).astype(bf16)
                G2[pl.ds(c, 1), 2 * i:2 * i + 2, :, chunks * rl:, :] = value.reshape(1, 2, 2, fl, d)
                put(G2, pl.multiple_of(c * rl, rl), i, dot(a3_ref[:, at], gh[...], TN).astype(bf16))
            return 0

        lax.fori_loop(0, chunks, chunk, 0)
        red2 = PlaneReduce(fs_n, G2, (c2, n2, z2), red_s[0])
        red2.start()
        get_w1.wait()

        def third(at):
            x2 = x1_ref[at, :] + dot(o2_ref[at, :], mat(4))
            lo[at, :] = (x2 + acc[at, :] + sm_ref[6:7, :]).astype(bf16)
            u, r = unit(x2)
            y = g1[at, :]
            gn[4:5, :] += jnp.sum(y * u, 0, keepdims=True)
            gn[5:6, :] += jnp.sum(y, 0, keepdims=True)
            cf = cot_ref[at, :].astype(f32)
            gn[6:7, :] += jnp.sum(cf, 0, keepdims=True)
            g2 = cf + unit_back(y, u, r, sm_ref[4:5, :])
            g1[at, :] = g2
            e2 = g2.astype(bf16)
            act[at, :] = e2
            do2[at, :] = dot(e2, mat(4), NT).astype(bf16)

        blocks(rows, RB, third)
        for at, i in halves:
            put(G1, 16 + 4 * rl, i, dot(o2_ref[:, at], act[...], TN).astype(bf16))
        red2.every(red2.first)
        get_q2.wait()
        get_p2.wait()
        ones = ones_pairs()

        def unmix(t, _):
            slot = lambda f: rows_at(t * feats + f, samples)
            for p in range(hp):
                lanes = head_pair(p)
                ks = [q_[1, slot(g), lanes].astype(f32) for g in range(feats)]
                vs = [q_[2, slot(g), lanes].astype(f32) for g in range(feats)]
                dks, dvs = [0.0] * feats, [0.0] * feats
                for f in range(feats):
                    q = q_[0, slot(f), lanes].astype(f32)
                    gr = do2[slot(f), lanes].astype(f32)
                    dp = head_sums([gr * v for v in vs], ones)
                    ws = [p2_[t, p, f, g].astype(f32) for g in range(feats)]
                    mean = sum(w * v for w, v in zip(ws, dp))
                    ds = [(w * (v - mean)).astype(bf16).astype(f32) for w, v in zip(ws, dp)]
                    dqkv[0, slot(f), lanes] = (sum(v * k for v, k in zip(ds, ks)) * 0.125).astype(bf16)
                    for g in range(feats):
                        dks[g] += ds[g] * q
                        dvs[g] += ws[g] * gr
                for g in range(feats):
                    dqkv[1, slot(g), lanes] = dks[g].astype(bf16)
                    dqkv[2, slot(g), lanes] = dvs[g].astype(bf16)
            return 0

        lax.fori_loop(0, tasks, unmix, 0)
        get_q1.start()

        def far(i, r):
            return mod(me_z + i, z_n) * 2 + mod(me_c + r, 2)

        me_d = lax.axis_index("dp")
        sends = {}
        for i in range(z_n):
            for r in range(2):
                for p in range(hp):
                    n = (p * z_n + i) * 2 + r
                    to = far(i, r)
                    if i == 0 and r == 0:
                        sends[p, i, r] = pltpu.make_async_copy(do1.at[to, p], do.at[to, p], turn_s[0].at[p])
                    else:
                        sends[p, i, r] = rcopy(do1.at[to, p], do.at[me_f, p], turn_s[1].at[n], turn_s[2].at[n], (me_d, to))
        chips = list(range(1, z_n)) + [0]

        def fourth(i):
            chip = mod(me_z + i, z_n)
            at = rows_at(chip, RB)
            u, r = unit(x1_ref[at, :])
            gain = sm_ref[2:3, :]
            gh[at, :] = (u * gain + sm_ref[3:4, :]).astype(bf16)
            y = dot(dqkv[0, at, :], mat(1), NT) + dot(dqkv[1, at, :], mat(2), NT) + dot(dqkv[2, at, :], mat(3), NT)
            gn[2:3, :] += jnp.sum(y * u, 0, keepdims=True)
            gn[3:4, :] += jnp.sum(y, 0, keepdims=True)
            v = g1[at, :] + unit_back(y, u, r, gain)
            g1[at, :] = v
            e1 = v.astype(bf16)
            act[at, :] = e1
            g = dot(e1, mat(0), NT).astype(bf16)
            for p in range(hp):
                do1[pl.ds(chip * per, per), p] = g[:, head_pair(p)].reshape(per, samples, 128)
            for p in range(hp):
                for r in range(2):
                    sends[p, i, r].start()

        for i in chips:
            fourth(i)
        get_ga.start()
        red2.every(red2.second)
        get_bk.wait()
        for at, i in halves:
            o1 = jnp.concatenate([bk[:, 2 * i].reshape(rows, 128), bk[:, 2 * i + 1].reshape(rows, 128)], 1)
            put(G1, 16, i, dot(o1, act[...], TN).astype(bf16))
            for j in range(3):
                put(G1, 16 + (1 + j) * rl, i, dot(gh[:, at], dqkv[j], TN).astype(bf16))
        G1[:, :, :, 0:16, :] = jnp.broadcast_to(gn[...].astype(bf16), (4, z_n, 2, 16, d))
        red1 = PlaneReduce(fs_n, G1, (c1, n1, z1), red_s[1])
        red1.start()

        lane = lax.broadcasted_iota(jnp.int32, (8, 128), 1) // 64
        pick = (lane == lax.broadcasted_iota(jnp.int32, (8, 128), 0)).astype(f32)
        get_q1.wait()
        get_o.wait()

        def grad_rows(i, p):
            return do[pl.ds(i * pq, pq), p].reshape(bq, 128)

        for p in range(hp):
            at = head_pair(p)
            kt[...] = q_[1, :, at].astype(f32).T.astype(bf16)
            dk[...] = jnp.zeros_like(dk)
            dv[...] = jnp.zeros_like(dv)
            for i in range(z_n):
                for r in range(2):
                    if i == 0 and r == 0:
                        sends[p, i, r].wait()
                    else:
                        sends[p, i, r].wait_recv()

            def deltas(i, _):
                qa = rows_at(i, bq)
                prod = grad_rows(i, p).astype(f32) * o_[p, qa, :].astype(f32)
                delta[:, qa] = lax.dot_general(pick, prod, NT, precision=lax.Precision.HIGHEST, preferred_element_type=f32)
                return 0

            lax.fori_loop(0, rows // bq, deltas, 0)
            for h in range(2):
                def part(i, _):
                    qa = rows_at(i, bq)
                    mask = head_mask(bq, h)
                    q = q_[0, qa, at]
                    q = jnp.where(mask, q, jnp.zeros_like(q))
                    g = grad_rows(i, p)
                    g = jnp.where(mask, g, jnp.zeros_like(g))
                    s = dot(q_[1, :, at], q, NT) + kb[:, 0:1]
                    e = jnp.exp(s - l_ref[p * 2 + h:p * 2 + h + 1, qa])
                    ds = (e * (dot(q_[2, :, at], g, NT) - delta[h:h + 1, qa])).astype(bf16)
                    dv[...] += dot(e.astype(bf16), g)
                    dk[...] += dot(ds, q)
                    dqt[h * 64:h * 64 + 64, qa] = dot(kt[h * 64:h * 64 + 64, :], ds) * 0.125
                    return 0
                lax.fori_loop(0, rows // bq, part, 0)
            dqkv[0, :, at] = dqt[...].T.astype(bf16)
            dqkv[1, :, at] = dk[...].astype(bf16)
            dqkv[2, :, at] = dv[...].astype(bf16)
            if p == 0:
                red1.every(red1.first)
            if p == 1:
                red2.every(red2.third)
            if p == 2:
                red1.every(red1.second)
        red1.every(red1.third)
        red2.finish(out2)

        get_ga.wait()
        get_xg.wait()
        gn[...] = jnp.zeros_like(gn)
        gain, bias = sm_ref[0:1, :], sm_ref[1:2, :]

        def again(i, _):
            u, _r = unit(xg_[pl.ds(i * per, per)].reshape(RB, d).astype(f32))
            act[rows_at(i, RB), :] = (u * gain + bias).astype(bf16)
            return 0

        lax.fori_loop(0, rows // RB, again, 0)
        GS = G2.at[:, :, :, 0:rs, :]
        for j in range(3):
            for at, i in halves:
                put(G2, 16 + j * rl, i, dot(act[:, at], dqkv[j], TN).astype(bf16))
        backs = {}
        for i in range(z_n):
            for r in range(2):
                to = far(i, r)
                if i == 0 and r == 0:
                    backs[i, r] = pltpu.make_async_copy(xg_.at[to], dr.at[to], back_s[0].at[0])
                else:
                    n = 2 * i + r
                    backs[i, r] = rcopy(xg_.at[to], dr.at[me_f], back_s[1].at[n], back_s[2].at[n], (me_d, to))
        for i in chips:
            chip = mod(me_z + i, z_n)
            at = rows_at(chip, RB)
            u, r = unit(xg_[pl.ds(chip * per, per)].reshape(RB, d).astype(f32))
            y = (dot(dqkv[0, at, :], units(ga_, 16, rl), NT) + dot(dqkv[1, at, :], units(ga_, 16 + rl, rl), NT)
                 + dot(dqkv[2, at, :], units(ga_, 16 + 2 * rl, rl), NT))
            gn[0:1, :] += jnp.sum(y * u, 0, keepdims=True)
            gn[1:2, :] += jnp.sum(y, 0, keepdims=True)
            xg_[pl.ds(chip * per, per)] = unit_back(y, u, r, gain).astype(bf16).reshape(per, samples, d)
            for r in range(2):
                backs[i, r].start()
        G2[:, :, :, 0:16, :] = jnp.broadcast_to(gn[...].astype(bf16), (4, z_n, 2, 16, d))
        reds = PlaneReduce(fs_n, GS, (c0, n0, z0), red_s[2])
        reds.start()
        reds.every(reds.first)
        red1.finish(out1)
        reds.every(reds.second)
        reds.every(reds.third)
        reds.finish(outs_)
        for i in range(z_n):
            for r in range(2):
                backs[i, r].wait()
        for key, c in sends.items():
            if key[1:] != (0, 0):
                c.wait_send()

    S, V, D = jax.ShapeDtypeStruct, pltpu.VMEM, pltpu.SemaphoreType.DMA
    SM = pl.BlockSpec(memory_space=pltpu.SMEM)
    g = (4, z_n, 2)
    scratch = [V(xg.shape, bf16), V(o.shape, bf16), V(w1.shape, bf16), V(qkv.shape, bf16), V(p2.shape, bf16), V(back.shape, bf16),
               V((rows, d), f32), V((rows, d), bf16), V((rows, d), bf16), V((rows, d), bf16), V((3, rows, d), bf16),
               V(g + (r2, d), bf16), V(g + (r1, d), bf16), V(back.shape, bf16), V(back.shape, bf16), V((8, rows), f32),
               V((128, rows), bf16), V((128, rows), f32), V((rows, 128), f32), V((rows, 128), f32), V((rows, 128), f32), V((16, d), f32)]
    scratch += plane_reduce_scratch(fs_n, r2, d) + plane_reduce_scratch(fs_n, r1, d) + plane_reduce_scratch(fs_n, rs, d)
    n = hp * fs_n
    scratch += [D((8,)), D((hp,)), D((n,)), D((n,)), D((1,)), D((fs_n,)), D((fs_n,))] + plane_reduce_sems(fs_n) * 3
    return pl.pallas_call(
        body,
        out_shape=[S((rows, d), f32), S((rows, d), bf16), S((slots, samples, d), bf16), S((r2, d), f32), S((r1, d), f32), S((rs, d), f32)],
        in_specs=[VM, SM] + [VM] * 6 + [ANY] * 8, out_specs=[VM, VM, ANY, VM, VM, VM], scratch_shapes=scratch,
        compiler_params=params(2), name="second",
    )(cot, scounts, lse, w2, sm, x1, o2, a3, xg, qkv, o, ga, w1, qkv2, p2, back)


def last_kernel(g1, dr, lo, out2, out1, outs, tasks, rl, fl, fs_n):
    slots, samples, d = dr.shape
    feats = slots // tasks
    rows = slots * samples
    wide = d // 128
    chunks = (out2.shape[0] - fl) // rl

    def body(g1_ref, dr_ref, lo_ref, r2, r1, rs, tg, lo_out, gn, gs, gso, gf, gfo, gmi, gib, gmo, gob, low):
        me = lax.axis_index("dp") * fs_n + lax.axis_index("fsdp")
        for s in range(slots):
            t, f = s // feats, s % feats
            for i in range(wide):
                at = pl.ds((t * samples * wide + i) * feats + f, samples, stride=feats * wide)
                here = (slice(s * samples, (s + 1) * samples), head_pair(i))
                tg[at, :] = g1_ref[here] + dr_ref[s, :, head_pair(i)].astype(f32)
                low[at, :] = lo_ref[here].astype(f32)
        blocks(rows * wide, 512, lambda at: lo_out.__setitem__((at, slice(None)), low[at, :].astype(bf16)))
        for i in range(3):
            gs[i] = rs[16 + i * rl:16 + (i + 1) * rl, :]
            gf[i] = r1[16 + (1 + i) * rl:16 + (2 + i) * rl, :]
        gso[...] = r1[16:16 + rl, :]
        gfo[...] = r1[16 + 4 * rl:16 + 5 * rl, :]
        for c in range(chunks):
            gmi[:, c * d:(c + 1) * d] = r2[c * rl:(c + 1) * rl, :]
        gmo[...] = r2[chunks * rl:, :]
        row = lax.broadcasted_iota(jnp.int32, (16, d), 0)
        both = jnp.where(row < 2, rs[0:16, :], r1[0:16, :])

        def mine(v, n, first):
            hot = lax.broadcasted_iota(jnp.int32, (d, n), 0) == lax.broadcasted_iota(jnp.int32, (d, n), 1) + first
            return lax.dot_general(v, hot.astype(f32), NN, precision=lax.Precision.HIGHEST, preferred_element_type=f32)

        own = mine(both, rl, me * rl)
        gn[...] = own[0:6]
        gob[...] = own[6:7]
        line = jnp.sum(jnp.where(row == 7 + me * fl // d, both, 0.0), 0, keepdims=True)
        gib[...] = mine(jnp.broadcast_to(line, (8, d)), fl, lax.rem(me * fl, d))[0:1]

    S = jax.ShapeDtypeStruct
    shapes = [S((rows * wide, 128), f32), S((rows * wide, 128), bf16), S((6, rl), f32), S((3, rl, d), f32), S((rl, d), f32), S((3, rl, d), f32),
              S((rl, d), f32), S((rl, chunks * d), f32), S((1, fl), f32), S((fl, d), f32), S((1, rl), f32)]
    return pl.pallas_call(
        body, out_shape=shapes, in_specs=[VM] * 6, out_specs=[VM] * len(shapes), scratch_shapes=[pltpu.VMEM((rows * wide, 128), f32)],
        compiler_params=params(), name="last",
    )(g1, dr, lo, out2, out1, outs)
def up16(a):
    rows = a.shape[-2]
    extra = (-rows) % 16
    return a if extra == 0 else jnp.pad(a, [(0, 0)] * (a.ndim - 2) + [(0, extra), (0, 0)])


def local(tokens, sample_counts, feature_counts, norms, sample_qkv, sample_out, feature_qkv, feature_out, mlp_in, mlp_in_bias,
          mlp_out, mlp_out_bias, cotangent):
    dp_n, fs_n = lax.axis_size("dp"), lax.axis_size("fsdp")
    nd = dp_n * fs_n
    me_d, me_f = lax.axis_index("dp"), lax.axis_index("fsdp")
    me = me_d * fs_n + me_f
    tasks, samples, feats, d = tokens.shape
    pairs = tasks * feats
    rep = fs_n // pairs
    dh = d // rep
    hp = dh // 128
    rl = sample_out.shape[0]
    chunks = mlp_in.shape[1] // d
    fl = mlp_out.shape[0]
    total = samples * fs_n
    if rep == 1 and dp_n == 4 and rl % 16 == 0 and fs_n * fl == d:
        def turned(v):
            return v.transpose(0, 2, 1, 3).reshape(pairs, samples, d)

        saved = first_kernel(turned(tokens), sample_counts, feature_counts, (norms, mlp_out_bias[None], mlp_in_bias[None]), sample_qkv, sample_out,
                             feature_qkv, feature_out, mlp_in, mlp_out, tasks, fs_n)
        g1, lo, dr, out2, out1, outs = second_kernel(turned(cotangent).reshape(total, d), sample_counts, saved, tasks, rl, fl, fs_n)
        tg, low, gn, gs, gso, gf, gfo, gmi, gib, gmo, gob = last_kernel(g1, dr, lo, out2, out1, outs, tasks, rl, fl, fs_n)

        def rows_back(v):
            return v.reshape(tasks, samples, d // 128, feats, 128).transpose(0, 1, 3, 2, 4).reshape(tokens.shape)

        return rows_back(low), rows_back(tg), gn, gs, gso, gf, gfo, gmi, gib[0], gmo, gob[0]


    small = jnp.zeros((16, d), bf16)
    small = lax.dynamic_update_slice(small, norms, (0, me * rl))
    small = lax.dynamic_update_slice(small, mlp_out_bias[None, :], (6, me * rl))
    small = lax.dynamic_update_slice(small, mlp_in_bias[None, :], (7 + (me * fl) // d, lax.rem(me * fl, d)))
    split_in = mlp_in.reshape(rl, chunks, d).transpose(1, 0, 2).reshape(chunks * rl, d)
    pack_a = up16(jnp.concatenate([small, sample_qkv.reshape(3 * rl, d)], 0))
    pack_b = up16(jnp.concatenate([sample_out, feature_qkv.reshape(3 * rl, d), feature_out, split_in, mlp_out], 0))

    xp = tokens.transpose(0, 2, 1, 3).reshape(pairs, samples, d)
    cp = cotangent.transpose(0, 2, 1, 3).reshape(pairs, samples, d)
    my_task = me_f // rep // feats
    count = lax.dynamic_index_in_dim(sample_counts, my_task, keepdims=False)
    keybias = jnp.broadcast_to(jnp.where(jnp.arange(total) < count, 0.0, MASKED).astype(f32)[:, None], (total, 128))
    shown = jnp.arange(feats)[None, :] < feature_counts[:, None]
    fbias = jnp.broadcast_to(jnp.where(shown, 0.0, MASKED).astype(f32).reshape(pairs, 1), (pairs, 128))

    ga, gb = gather_call([pack_a, pack_b], dp_n, fs_n, 3)
    ga, gb = ga.reshape((nd,) + ga.shape[3:]), gb.reshape((nd,) + gb.shape[3:])

    def take(g, start, rows):
        return g[:, start:start + rows].reshape(nd * rows, d)

    smalls = jnp.sum(ga[:, :16].astype(f32), 0)
    w_s = jnp.stack([take(ga, 16 + i * rl, rl) for i in range(3)])
    first = lax.rem(me_f, rep) * dh
    w_mine = lax.dynamic_slice_in_dim(w_s, first, dh, 2)
    w_mid = jnp.concatenate([take(gb, i * rl, rl) for i in range(5 + chunks)] + [take(gb, (5 + chunks) * rl, fl)])[None]
    size = d
    back, xg, o, qkv, lse = forward_kernel(jnp.repeat(xp, rep, 0), [], [w_mine, smalls], keybias, dp_n, fs_n, rl, dh)

    lo, g1, do1, gm = middle_call(xp, back.reshape(pairs, rep * hp, samples, 128), cp, smalls, fbias, w_mid, tasks, chunks, size)
    do1 = do1.reshape(fs_n, hp, samples, 128)
    dxr, gs, gn_s = backward_kernel(do1, xg, qkv, o, lse, w_mine, smalls, keybias, None, None, dp_n, fs_n, rl, dh, tasks, False)
    dxr = jnp.sum(dxr.reshape(pairs, rep, samples, d).astype(f32), 1)
    tokens_grad = (g1.reshape(pairs, samples, d) + dxr).reshape(tasks, feats, samples, d).transpose(0, 2, 1, 3)
    gs = lax.dynamic_update_slice_in_dim(jnp.zeros((3, d, d), bf16), gs, first, 2)

    def give(g, parts):
        return g.reshape(parts, nd, -1, d).transpose(1, 0, 2, 3).reshape(nd, -1, d)

    gm = gm[0]
    mix = jnp.concatenate([gn_s[0:2].astype(bf16), gm[2:16]], 0)
    grads = up16(jnp.concatenate([jnp.broadcast_to(mix[None], (nd, 16, d)), give(gm[16:16 + (5 + chunks) * d], 5 + chunks),
                                  give(gm[16 + (5 + chunks) * d:], 1), give(gs, 3)], 1))
    s = scatter_call(grads.reshape((dp_n, fs_n // 2, 2) + grads.shape[1:]), dp_n, fs_n, 6)
    outs = [s[16 + (5 + chunks) * rl + fl:][:3 * rl]]
    gn = s[0:2]
    gn = jnp.concatenate([gn, s[2:16]], 0)
    layer_output = lo.reshape(tasks, feats, samples, d).transpose(0, 2, 1, 3)

    def piece(start, rows):
        return s[16 + start * rl:16 + start * rl + rows]

    return (
        layer_output,
        tokens_grad,
        lax.dynamic_slice(gn, (0, me * rl), (6, rl)),
        outs[0].reshape(3, rl, d), piece(0, rl), piece(1, 3 * rl).reshape(3, rl, d), piece(4, rl),
        piece(5, chunks * rl).reshape(chunks, rl, d).transpose(1, 0, 2).reshape(rl, chunks * d),
        lax.dynamic_slice(gn[7:7 + chunks].reshape(-1), (me * fl,), (fl,)),
        piece(5 + chunks, fl),
        lax.dynamic_slice(gn[6], (me * rl,), (rl,)),
    )


def solution(mesh):
    rows, whole = ("dp", "fsdp"), P("dp", "fsdp", None, None)
    weights = (P(None, rows), P(None, rows, None), P(rows, None), P(None, rows, None), P(rows, None), P(rows, None), P(rows),
               P(rows, None), P(rows))
    return jax.shard_map(local, mesh=mesh, in_specs=(whole, P("dp"), P("dp")) + weights + (whole,),
                         out_specs=(whole, whole) + weights, check_vma=False)
```

```python
import functools
import jax
import jax.numpy as jnp
from jax import lax
from jax.experimental import pallas as pl
from jax.experimental.pallas import tpu as pltpu
from jax.sharding import PartitionSpec as P

MESH = pl.DeviceIdType.MESH
f32, bf16 = jnp.float32, jnp.bfloat16


def mod(a, n):
    return lax.rem(a, n)


def greet(dp_n, fs_n, with_dp=True):
    me_d, me_f = lax.axis_index("dp"), lax.axis_index("fsdp")
    barrier = pltpu.get_barrier_semaphore()
    n = 0
    for k in range(1, fs_n):
        pl.semaphore_signal(barrier, inc=1, device_id=(me_d, mod(me_f + k, fs_n)), device_id_type=MESH)
        n += 1
    if with_dp:
        for k in range(1, dp_n):
            pl.semaphore_signal(barrier, inc=1, device_id=(mod(me_d + k, dp_n), me_f), device_id_type=MESH)
            n += 1
    pl.semaphore_wait(barrier, n)


def rcopy(src, dst, ss, rs, dev):
    return pltpu.make_async_remote_copy(src_ref=src, dst_ref=dst, send_sem=ss, recv_sem=rs, device_id=dev, device_id_type=MESH)


class Swap:
    def __init__(self, fs_n, src, dst, local_sem, ss, rs):
        me_d, me_f = lax.axis_index("dp"), lax.axis_index("fsdp")
        self.own = pltpu.make_async_copy(src.at[me_f], dst.at[me_f], local_sem)
        self.copies = []
        for k in range(1, fs_n):
            to = mod(me_f + k, fs_n)
            self.copies.append(rcopy(src.at[to], dst.at[me_f], ss.at[k - 1], rs.at[k - 1], (me_d, to)))

    def start(self):
        for c in self.copies:
            c.start()
        self.own.start()

    def wait(self):
        self.own.wait()
        for c in self.copies:
            c.wait()


class Gather:
    def __init__(self, dp_n, fs_n, src, dst, local_sem, zs, zr, ds, dr, cs, cr):
        me_d, me_f = lax.axis_index("dp"), lax.axis_index("fsdp")
        z_n = fs_n // 2
        me_z, me_c = me_f // 2, mod(me_f, 2)
        self.z_n, self.dp_n = z_n, dp_n
        partner = (me_d, me_z * 2 + 1 - me_c)
        self.own = pltpu.make_async_copy(src, dst.at[me_d, me_z, me_c], local_sem)
        self.z = []
        for k in range(1, z_n):
            to = mod(me_z + k, z_n) * 2 + me_c
            self.z.append(rcopy(src, dst.at[me_d, me_z, me_c], zs.at[k - 1], zr.at[k - 1], (me_d, to)))
        self.d = {}
        self.c = {}
        for k in range(z_n):
            z = mod(me_z - k + z_n, z_n)
            for j in range(dp_n):
                d = mod(me_d - j + dp_n, dp_n)
                here = src if (k == 0 and j == 0) else dst.at[d, z, me_c]
                self.c[k, j] = rcopy(here, dst.at[d, z, me_c], cs.at[k * dp_n + j], cr.at[k * dp_n + j], partner)
                if j > 0:
                    here = src if k == 0 else dst.at[me_d, z, me_c]
                    i = k * (dp_n - 1) + j - 1
                    self.d[k, j] = rcopy(here, dst.at[me_d, z, me_c], ds.at[i], dr.at[i], (mod(me_d + j, dp_n), me_f))

    def start(self):
        for c in self.z:
            c.start()
        self.own.start()
        for j in range(1, self.dp_n):
            self.d[0, j].start()
        self.c[0, 0].start()

    def forward_z(self):
        for k in range(1, self.z_n):
            self.z[k - 1].wait_recv()
            for j in range(1, self.dp_n):
                self.d[k, j].start()
            self.c[k, 0].start()

    def forward_d(self):
        for k in range(self.z_n):
            for j in range(1, self.dp_n):
                self.d[k, j].wait_recv()
                self.c[k, j].start()

    def wait(self):
        self.own.wait()
        for c in self.z:
            c.wait_send()
        for c in self.d.values():
            c.wait_send()
        for c in self.c.values():
            c.wait()


def gather_sems(dp_n, fs_n):
    z = fs_n // 2
    D = pltpu.SemaphoreType.DMA
    return [D, D((z - 1,)), D((z - 1,)), D((z * (dp_n - 1),)), D((z * (dp_n - 1),)), D((z * dp_n,)), D((z * dp_n,))]


def swap_sems(fs_n):
    D = pltpu.SemaphoreType.DMA
    return [D, D((fs_n - 1,)), D((fs_n - 1,))]


ANY = pl.BlockSpec(memory_space=pl.ANY)
VM = pl.BlockSpec(memory_space=pltpu.VMEM)


def swap_call(x, dp_n, fs_n, cid, space=ANY):
    def body(x_ref, o_ref, *sems):
        greet(dp_n, fs_n, False)
        s = Swap(fs_n, x_ref, o_ref, *sems)
        s.start()
        s.wait()

    return pl.pallas_call(
        body, out_shape=jax.ShapeDtypeStruct(x.shape, x.dtype), in_specs=[space], out_specs=space,
        scratch_shapes=swap_sems(fs_n),
        compiler_params=pltpu.CompilerParams(collective_id=cid, has_side_effects=True, vmem_limit_bytes=60 << 20),
        name="swap%d" % cid,
    )(x)


def gather_call(packs, dp_n, fs_n, cid, space=ANY):
    n = len(packs)

    def body(*refs):
        ins, outs, sems = refs[:n], refs[n:2 * n], refs[2 * n:]
        greet(dp_n, fs_n)
        gs = [Gather(dp_n, fs_n, ins[i], outs[i], *sems[7 * i:7 * i + 7]) for i in range(n)]
        for g in gs:
            g.start()
        for g in gs:
            g.forward_z()
        for g in gs:
            g.forward_d()
        for g in gs:
            g.wait()

    return pl.pallas_call(
        body,
        out_shape=[jax.ShapeDtypeStruct((dp_n, fs_n // 2, 2) + p.shape, p.dtype) for p in packs],
        in_specs=[space] * n, out_specs=[space] * n,
        scratch_shapes=gather_sems(dp_n, fs_n) * n,
        compiler_params=pltpu.CompilerParams(collective_id=cid, has_side_effects=True, vmem_limit_bytes=60 << 20),
        name="gather%d" % cid,
    )(*packs)


def scatter_call(g, dp_n, fs_n, cid):
    z_n = fs_n // 2
    rows, width = g.shape[3:]
    step = 16

    def body(g_ref, o_ref, from_c, half, from_d, quarter, from_z, cs, cr, ds, dr, zs, zr):
        me_d, me_f = lax.axis_index("dp"), lax.axis_index("fsdp")
        me_z, me_c = me_f // 2, mod(me_f, 2)
        greet(dp_n, fs_n)
        partner = (me_d, me_z * 2 + 1 - me_c)

        def add(out, parts):
            def one(i, _):
                at = pl.ds(pl.multiple_of(i * step, step), step)
                total = parts[0][at, :].astype(f32)
                for p in parts[1:]:
                    total = total + p[at, :].astype(f32)
                out[at, :] = total.astype(out.dtype)
                return 0
            lax.fori_loop(0, rows // step, one, 0, unroll=True if rows // step <= 4 else 4)

        order = [(j, k) for j in list(range(1, dp_n)) + [0] for k in list(range(1, z_n)) + [0]]
        cc, dd, zz = {}, {}, {}
        for i, (j, k) in enumerate(order):
            d, z = mod(me_d + j, dp_n), mod(me_z + k, z_n)
            cc[j, k] = rcopy(g_ref.at[d, z, 1 - me_c], from_c.at[i], cs.at[i], cr.at[i], partner)
            cc[j, k].start()
        for i, (j, k) in enumerate(order):
            d, z = mod(me_d + j, dp_n), mod(me_z + k, z_n)
            cc[j, k].wait_recv()
            add(half.at[j, k], [g_ref.at[d, z, me_c], from_c.at[i]])
            if j:
                n = (j - 1) * z_n + k
                dd[j, k] = rcopy(half.at[j, k], from_d.at[j - 1, k], ds.at[n], dr.at[n], (d, me_f))
                dd[j, k].start()
        for k in list(range(1, z_n)) + [0]:
            for j in range(1, dp_n):
                dd[j, k].wait_recv()
            if k:
                add(quarter.at[k], [half.at[0, k]] + [from_d.at[j - 1, k] for j in range(1, dp_n)])
                to = mod(me_z + k, z_n) * 2 + me_c
                zz[k] = rcopy(quarter.at[k], from_z.at[k - 1], zs.at[k - 1], zr.at[k - 1], (me_d, to))
                zz[k].start()
        for k in range(1, z_n):
            zz[k].wait_recv()
        add(o_ref, [half.at[0, 0]] + [from_d.at[j - 1, 0] for j in range(1, dp_n)] + [from_z.at[k - 1] for k in range(1, z_n)])
        for c in list(cc.values()) + list(dd.values()) + list(zz.values()):
            c.wait_send()

    D = pltpu.SemaphoreType.DMA
    n = dp_n * z_n
    return pl.pallas_call(
        body, out_shape=jax.ShapeDtypeStruct((rows, width), f32), in_specs=[VM], out_specs=VM,
        scratch_shapes=[
            pltpu.VMEM((n, rows, width), bf16), pltpu.VMEM((dp_n, z_n, rows, width), bf16),
            pltpu.VMEM((dp_n - 1, z_n, rows, width), bf16), pltpu.VMEM((z_n, rows, width), bf16),
            pltpu.VMEM((z_n - 1, rows, width), bf16),
            D((n,)), D((n,)), D((n - z_n,)), D((n - z_n,)), D((z_n - 1,)), D((z_n - 1,)),
        ],
        compiler_params=pltpu.CompilerParams(collective_id=cid, has_side_effects=True, vmem_limit_bytes=60 << 20),
        name="scatter%d" % cid,
    )(g)
class PlaneGather:
    def __init__(self, fs_n, src, dst, local_sem, zs, zr, ds, dr, cs, cr):
        me_d, me_f = lax.axis_index("dp"), lax.axis_index("fsdp")
        z_n = fs_n // 2
        me_z, me_c = me_f // 2, mod(me_f, 2)
        self.z_n = z_n
        partner = (me_d, me_z * 2 + 1 - me_c)
        ds_ = [me_d, me_d // 2 * 2 + 1 - mod(me_d, 2), mod(me_d + 2, 4), 3 - me_d]
        zs_ = [mod(me_z - k + z_n, z_n) for k in range(z_n)]
        self.own = pltpu.make_async_copy(src, dst.at[me_d, me_z, me_c], local_sem)
        self.z, self.n, self.fwd, self.c = {}, {}, {}, {}
        for k in range(z_n):
            at = lambda j: dst.at[ds_[j], zs_[k], me_c]
            mine = src if k == 0 else at(0)
            if k:
                to = mod(me_z + k, z_n) * 2 + me_c
                self.z[k] = rcopy(src, dst.at[me_d, me_z, me_c], zs.at[k - 1], zr.at[k - 1], (me_d, to))
            for j in (1, 2):
                self.n[k, j] = rcopy(mine, at(0), ds.at[3 * k + j - 1], dr.at[3 * k + j - 1], (ds_[j], me_f))
            first = 1 + k % 2
            self.fwd[k] = rcopy(at(first), at(first), ds.at[3 * k + 2], dr.at[3 * k + 2], (ds_[3 - first], me_f))
            for j in range(4):
                self.c[k, j] = rcopy(mine if j == 0 else at(j), at(j), cs.at[4 * k + j], cr.at[4 * k + j], partner)

    def start(self):
        for c in self.z.values():
            c.start()

    def begin(self):
        self.own.start()
        self.spread(0)

    def spread(self, k):
        if k:
            self.z[k].wait_recv()
        self.n[k, 1].start()
        self.n[k, 2].start()
        self.c[k, 0].start()

    def hand_on(self, k):
        first = 1 + k % 2
        for j in (first, 3 - first):
            self.n[k, j].wait_recv()
            if j == first:
                self.fwd[k].start()
            self.c[k, j].start()

    def corner(self, k):
        self.fwd[k].wait_recv()
        self.c[k, 3].start()

    def wait(self):
        self.own.wait()
        for c in list(self.z.values()) + list(self.n.values()) + list(self.fwd.values()):
            c.wait_send()
        for c in self.c.values():
            c.wait()


def plane_gather_sems(fs_n):
    z, D = fs_n // 2, pltpu.SemaphoreType.DMA
    return [D, D((z - 1,)), D((z - 1,)), D((3 * z,)), D((3 * z,)), D((4 * z,)), D((4 * z,))]


class PlaneReduce:
    def __init__(self, fs_n, g, bufs, sems):
        me_d, me_f = lax.axis_index("dp"), lax.axis_index("fsdp")
        z_n = fs_n // 2
        me_z, me_c = me_f // 2, mod(me_f, 2)
        self.z_n, self.rows = z_n, g.shape[3]
        self.from_c, self.from_n, self.from_z = bufs
        cs, cr, ds, dr, zs, zr = sems
        partner = (me_d, me_z * 2 + 1 - me_c)
        ds_ = [me_d, me_d // 2 * 2 + 1 - mod(me_d, 2), mod(me_d + 2, 4), 3 - me_d]
        self.mine, self.c, self.n, self.z = {}, {}, {}, {}
        for k in range(z_n):
            z = mod(me_z + k, z_n)
            for j in range(4):
                i = 4 * k + j
                self.mine[k, j] = g.at[ds_[j], z, me_c]
                self.c[k, j] = rcopy(g.at[ds_[j], z, 1 - me_c], self.from_c.at[k, j], cs.at[i], cr.at[i], partner)
            first = 1 + k % 2
            send = [(first, first), (3, first), (3 - first, 3 - first)]
            for i, (j, to) in enumerate(send):
                self.n[k, i] = rcopy(self.mine[k, j], self.from_n.at[k, i], ds.at[3 * k + i], dr.at[3 * k + i], (ds_[to], me_f))
            if k:
                to = mod(me_z + k, z_n) * 2 + me_c
                self.z[k] = rcopy(self.mine[k, 0], self.from_z.at[k - 1], zs.at[k - 1], zr.at[k - 1], (me_d, to))

    def add(self, out, parts):
        step = 16

        def one(i, _):
            at = pl.ds(pl.multiple_of(i * step, step), step)
            if len(parts) == 2 and out.dtype == bf16:
                out[at, :] = parts[0][at, :] + parts[1][at, :]
                return 0
            total = parts[0][at, :].astype(f32)
            for p in parts[1:]:
                total = total + p[at, :].astype(f32)
            out[at, :] = total.astype(out.dtype)
            return 0

        n = self.rows // step
        lax.fori_loop(0, n, one, 0, unroll=2 if n % 2 == 0 else 1)

    def order(self):
        return list(range(1, self.z_n)) + [0]

    def start(self):
        for k in self.order():
            for j in (1 + k % 2, 3, 2 - k % 2, 0):
                self.c[k, j].start()

    def first(self, k):
        first = 1 + k % 2
        for j in (first, 3, 3 - first, 0):
            self.c[k, j].wait_recv()
            self.add(self.mine[k, j], [self.mine[k, j], self.from_c.at[k, j]])
            if j == first:
                self.n[k, 0].start()
            if j == 3:
                self.n[k, 1].start()

    def second(self, k):
        first = 1 + k % 2
        self.n[k, 1].wait_recv()
        j = 3 - first
        self.add(self.mine[k, j], [self.mine[k, j], self.from_n.at[k, 1]])
        self.n[k, 2].start()

    def third(self, k):
        self.n[k, 0].wait_recv()
        self.n[k, 2].wait_recv()
        if k:
            self.add(self.mine[k, 0], [self.mine[k, 0], self.from_n.at[k, 0], self.from_n.at[k, 2]])
            self.z[k].start()

    def every(self, step):
        for k in self.order():
            step(k)

    def finish(self, out):
        for k in range(1, self.z_n):
            self.z[k].wait_recv()
        self.add(out, [self.mine[0, 0], self.from_n.at[0, 0], self.from_n.at[0, 2]] + [self.from_z.at[k - 1] for k in range(1, self.z_n)])
        for c in list(self.c.values()) + list(self.n.values()) + list(self.z.values()):
            c.wait_send()


def plane_reduce_scratch(fs_n, rows, width):
    z_n, V = fs_n // 2, pltpu.VMEM
    return [V((z_n, 4, rows, width), bf16), V((z_n, 3, rows, width), bf16), V((z_n - 1, rows, width), bf16)]


def plane_reduce_sems(fs_n):
    z_n, D = fs_n // 2, pltpu.SemaphoreType.DMA
    return [D((4 * z_n,)), D((4 * z_n,)), D((3 * z_n,)), D((3 * z_n,)), D((z_n - 1,)), D((z_n - 1,))]


HEADS = 8
EPS = 1e-05
MASKED = -1e30
NN = (((1,), (0,)), ((), ()))
NT = (((1,), (1,)), ((), ()))
TN = (((0,), (0,)), ((), ()))


def dot(a, b, dims=NN):
    return lax.dot_general(a, b, dims, preferred_element_type=f32)


def unit(x):
    c = x - jnp.mean(x, -1, keepdims=True)
    r = lax.rsqrt(jnp.mean(c * c, -1, keepdims=True) + EPS)
    return c * r, r


def unit_back(y, u, r, gain):
    yg = y * gain
    return r * (yg - jnp.mean(yg, -1, keepdims=True) - u * jnp.mean(yg * u, -1, keepdims=True))


def blocks(total, size, body):
    lax.fori_loop(0, total // size, lambda i, c: (body(pl.ds(pl.multiple_of(i * size, size), size)), c)[1], 0)


def gelu_parts(v):
    z = jnp.abs(v) * 0.7071067811865476
    t = 1.0 / (1.0 + 0.3275911 * z)
    e = jnp.exp(-0.5 * (v * v))
    tail = t * (0.127414796 + t * (-0.142248368 + t * (0.7107068705 + t * (-0.7265760135 + t * 0.5307027145)))) * e
    return jnp.where(v >= 0, 1.0 - tail, tail), v * e * 0.3989422804014327


def head_mask(rows, second, width=128):
    lane = lax.broadcasted_iota(jnp.int32, (rows, width), 1)
    return (lane >= width // 2) if second else (lane < width // 2)


def params(cid=None):
    if cid is None:
        return pltpu.CompilerParams(vmem_limit_bytes=62 << 20)
    return pltpu.CompilerParams(collective_id=cid, has_side_effects=True, vmem_limit_bytes=62 << 20)


def head_pair(p):
    return slice(p * 128, p * 128 + 128)


def middle_call(x, o1, cot, smalls, fbias, w, tasks, chunks, unit_rows):
    pairs, samples, d = x.shape
    feats = pairs // tasks
    rows = pairs * samples
    hh = d // 64
    nd = w.shape[0]
    U = unit_rows
    OUT = (5 + chunks) * U
    fl = chunks * d // nd
    x, cot = x.reshape(rows, d), cot.reshape(rows, d)
    RB = 256
    per = RB // samples

    def body(x_ref, back_ref, cot_ref, n_ref, fb_ref, w_ref,
             lo_ref, g1_ref, do1_ref, g_ref,
             x1, a, qkv, p2, o2, acc, dacc, act, gh, dqkv, do2, o1_ref, gn_ref):
        gn_ref[...] = jnp.zeros_like(gn_ref)

        def at_unit(k):
            return pl.ds(pl.multiple_of(k * U, 16), U) if not isinstance(k, int) else slice(k * U, k * U + U)

        def mat(k):
            return w_ref[:, at_unit(k), :].reshape(d, d)

        def out_mat(c):
            if nd == 1:
                return w_ref[0, pl.ds(pl.multiple_of(OUT + c * d, 16), d), :]
            m = nd // chunks
            return w_ref[pl.ds(c * m, m), OUT:OUT + fl, :].reshape(d, d)

        def put(k, at, i, value):
            if nd == 1:
                g_ref[0, pl.ds(pl.multiple_of(16 + k * U + i * 256, 16), 256), :] = value
            else:
                m = 256 // U
                g_ref[pl.ds(i * m, m), pl.ds(pl.multiple_of(16 + k * U, 16), U), :] = value.reshape(m, U, d)

        def put_out(c, i, value):
            if nd == 1:
                g_ref[0, pl.ds(pl.multiple_of(16 + OUT + c * d + i * 256, 16), 256), :] = value
            else:
                m = 256 // fl
                g_ref[pl.ds(c * (nd // chunks) + i * m, m), 16 + OUT:16 + OUT + fl, :] = value.reshape(m, fl, d)

        def tiles(body):
            for i in range(d // 256):
                body(slice(i * 256, i * 256 + 256), i)

        def norm(i):
            return n_ref[2 * i:2 * i + 1, :], n_ref[2 * i + 1:2 * i + 2, :]

        def collect(i, _):
            at = pl.ds(pl.multiple_of(i * RB, RB), RB)
            for p in range(hh // 2):
                o1_ref[at, p * 128:p * 128 + 128] = back_ref[pl.ds(i * per, per), p].reshape(RB, 128)
            return 0

        lax.fori_loop(0, rows // RB, collect, 0)

        def first(at):
            y = x_ref[at, :].astype(f32) + dot(o1_ref[at, :], mat(0))
            x1[at, :] = y
            u, _ = unit(y)
            g, b = norm(1)
            v = (u * g + b).astype(bf16)
            a[at, :] = v
            for i in range(3):
                z = dot(v, mat(1 + i)).astype(bf16)
                qkv[i, at, :] = z * 0.125 if i == 0 else z

        blocks(rows, RB, first)

        half = lax.broadcasted_iota(jnp.int32, (256, 128), 0) // 64
        ones = (lax.rem(half, 2) == lax.broadcasted_iota(jnp.int32, (256, 128), 1) // 64).astype(bf16)

        def head_sums(prods):
            both = []
            for v in prods:
                hi = v.astype(bf16)
                both.append(jnp.concatenate([hi, (v - hi.astype(f32)).astype(bf16)], 1))
            out = dot(jnp.concatenate(both, 0), ones)
            return [out[i * samples:(i + 1) * samples] for i in range(len(prods))]

        def at_slot(t, f):
            return pl.ds(pl.multiple_of((t * feats + f) * samples, samples), samples)

        def mix(t, _):
            for p in range(hh // 2):
                lanes = head_pair(p)
                ks = [qkv[1, at_slot(t, g), lanes].astype(f32) for g in range(feats)]
                vs = [qkv[2, at_slot(t, g), lanes].astype(f32) for g in range(feats)]
                for f in range(feats):
                    q = qkv[0, at_slot(t, f), lanes].astype(f32)
                    sc = head_sums([q * k for k in ks])
                    sc = [v + fb_ref[pl.ds(t * feats + g, 1), :] for g, v in enumerate(sc)]
                    top = functools.reduce(jnp.maximum, sc)
                    sc = [jnp.exp(v - top) for v in sc]
                    inv = 1.0 / sum(sc)
                    sc = [v * inv for v in sc]
                    for g in range(feats):
                        p2[t, p, f, g] = sc[g]
                    o2[at_slot(t, f), lanes] = sum(w * v for w, v in zip(sc, vs)).astype(bf16)
            return 0

        lax.fori_loop(0, tasks, mix, 0)

        def second(at):
            y = x1[at, :] + dot(o2[at, :], mat(4))
            acc[at, :] = y
            u, _ = unit(y)
            g, b = norm(2)
            do2[at, :] = (u * g + b).astype(bf16)
            dacc[at, :] = jnp.zeros((RB, d), f32)

        blocks(rows, RB, second)

        def chunk(c, _):
            def part(at):
                hid = dot(do2[at, :], mat(5 + c)) + n_ref[pl.ds(7 + c, 1), :]
                cdf, pdf = gelu_parts(hid)
                al = (hid * cdf).astype(bf16)
                act[at, :] = al
                gl = ((cdf + pdf) * dot(cot_ref[at, :], out_mat(c), NT)).astype(bf16)
                gh[at, :] = gl
                gn_ref[pl.ds(7 + c, 1), :] += jnp.sum(gl.astype(f32), 0, keepdims=True)
                acc[at, :] += dot(al, out_mat(c))
                dacc[at, :] += dot(gl, mat(5 + c), NT)

            blocks(rows, RB, part)

            def weight(at, i):
                put_out(c, i, dot(act[:, at], cot_ref[...], TN).astype(bf16))
                put(5 + c, at, i, dot(do2[:, at], gh[...], TN).astype(bf16))

            tiles(weight)
            return 0

        lax.fori_loop(0, chunks, chunk, 0)

        def third(at):
            lo_ref[at, :] = (acc[at, :] + n_ref[6:7, :]).astype(bf16)
            u, r = unit(x1[at, :] + dot(o2[at, :], mat(4)))
            y = dacc[at, :]
            gn_ref[4:5, :] += jnp.sum(y * u, 0, keepdims=True)
            gn_ref[5:6, :] += jnp.sum(y, 0, keepdims=True)
            cf = cot_ref[at, :].astype(f32)
            gn_ref[6:7, :] += jnp.sum(cf, 0, keepdims=True)
            g2 = cf + unit_back(y, u, r, norm(2)[0])
            dacc[at, :] = g2
            e2 = g2.astype(bf16)
            act[at, :] = e2
            do2[at, :] = dot(e2, mat(4), NT).astype(bf16)

        blocks(rows, RB, third)

        def weight2(at, i):
            put(4, at, i, dot(o2[:, at], act[...], TN).astype(bf16))

        tiles(weight2)

        def unmix(t, _):
            for p in range(hh // 2):
                lanes = head_pair(p)
                ks = [qkv[1, at_slot(t, g), lanes].astype(f32) for g in range(feats)]
                vs = [qkv[2, at_slot(t, g), lanes].astype(f32) for g in range(feats)]
                dk, dv = [0.0] * feats, [0.0] * feats
                for f in range(feats):
                    q = qkv[0, at_slot(t, f), lanes].astype(f32)
                    gr = do2[at_slot(t, f), lanes].astype(f32)
                    dp = head_sums([gr * v for v in vs])
                    ws = [p2[t, p, f, g] for g in range(feats)]
                    mean = sum(w * v for w, v in zip(ws, dp))
                    ds = [(w * (v - mean)).astype(bf16).astype(f32) for w, v in zip(ws, dp)]
                    dqkv[0, at_slot(t, f), lanes] = (sum(v * k for v, k in zip(ds, ks)) * 0.125).astype(bf16)
                    for g in range(feats):
                        dk[g] += ds[g] * q
                        dv[g] += ws[g] * gr
                for g in range(feats):
                    dqkv[1, at_slot(t, g), lanes] = dk[g].astype(bf16)
                    dqkv[2, at_slot(t, g), lanes] = dv[g].astype(bf16)
            return 0

        lax.fori_loop(0, tasks, unmix, 0)

        def fourth(i, _):
            at = pl.ds(pl.multiple_of(i * RB, RB), RB)
            u, r = unit(x1[at, :])
            y = dot(dqkv[0, at, :], mat(1), NT) + dot(dqkv[1, at, :], mat(2), NT) + dot(dqkv[2, at, :], mat(3), NT)
            gn_ref[2:3, :] += jnp.sum(y * u, 0, keepdims=True)
            gn_ref[3:4, :] += jnp.sum(y, 0, keepdims=True)
            g1 = dacc[at, :] + unit_back(y, u, r, norm(1)[0])
            g1_ref[at, :] = g1
            e1 = g1.astype(bf16)
            act[at, :] = e1
            do = dot(e1, mat(0), NT).astype(bf16)
            for p in range(hh // 2):
                do1_ref[pl.ds(i * per, per), p] = do[:, p * 128:p * 128 + 128].reshape(per, samples, 128)
            return 0

        lax.fori_loop(0, rows // RB, fourth, 0)

        def weight3(at, i):
            put(0, at, i, dot(o1_ref[:, at], act[...], TN).astype(bf16))
            for j in range(3):
                put(1 + j, at, i, dot(a[:, at], dqkv[j], TN).astype(bf16))

        tiles(weight3)
        g_ref[:, 0:16, :] = jnp.broadcast_to(gn_ref[...].astype(bf16), (nd, 16, d))

    V = pltpu.VMEM
    S = jax.ShapeDtypeStruct
    return pl.pallas_call(
        body,
        out_shape=[S((rows, d), bf16), S((rows, d), f32), S((pairs, hh // 2, samples, 128), bf16),
                   S((nd, 16 + OUT + fl, d), bf16)],
        in_specs=[VM] * 6, out_specs=[VM] * 4,
        scratch_shapes=[V((rows, d), f32), V((rows, d), bf16), V((3, rows, d), bf16), V((tasks, hh // 2, feats, feats, samples, 128), f32), V((rows, d), bf16),
                        V((rows, d), f32), V((rows, d), f32), V((rows, d), bf16), V((rows, d), bf16), V((3, rows, d), bf16),
                        V((rows, d), bf16), V((rows, d), bf16), V((16, d), f32)],
        compiler_params=params(), name="middle",
    )(x, o1, cot, smalls, fbias, w)
BQ = 1024


class Turns:
    def __init__(self, fs_n, parts, src, dst, local_sem, ss, rs):
        me_d, me_f = lax.axis_index("dp"), lax.axis_index("fsdp")
        self.sets = []
        for p in range(parts):
            own = pltpu.make_async_copy(src(p, me_f), dst(p, me_f), local_sem.at[p])
            far = []
            for k in range(1, fs_n):
                to = mod(me_f + k, fs_n)
                i = p * (fs_n - 1) + k - 1
                far.append(rcopy(src(p, to), dst(p, me_f), ss.at[i], rs.at[i], (me_d, to)))
            self.sets.append((own, far))

    def start(self, p):
        own, far = self.sets[p]
        for c in far:
            c.start()
        own.start()

    def wait_recv(self, p):
        own, far = self.sets[p]
        own.wait()
        for c in far:
            c.wait_recv()

    def wait_send(self):
        for _, far in self.sets:
            for c in far:
                c.wait_send()


def turn_sems(fs_n, parts):
    D = pltpu.SemaphoreType.DMA
    return [D((parts,)), D((parts * (fs_n - 1),)), D((parts * (fs_n - 1),))]


def units(ref, start, size):
    v = ref[..., start:start + size, :]
    return v.reshape(-1, v.shape[-1])


def forward_kernel(x, packs, plain, keybias, dp_n, fs_n, rl, dh):
    slots, samples, d = x.shape
    rows = slots * samples
    heads = dh // 64
    hp = heads // 2
    np_ = len(packs)

    def body(*refs):
        it = iter(refs)
        x_ref, kb_ref = next(it), next(it)
        pack_refs = [next(it) for _ in range(np_)]
        w_ref, sm_ref = (None, None) if np_ else (next(it), next(it))
        back_ref, xg_ref, o_ref, qkv_ref, l_ref = (next(it) for _ in range(5))
        g_refs = [next(it) for _ in range(np_)]
        if np_:
            sm_ref = next(it)
        acted, vt, ot = next(it), next(it), next(it)
        swap_s = [next(it) for _ in range(3)]
        turn_s = [next(it) for _ in range(3)]
        gat_s = [[next(it) for _ in range(7)] for _ in range(np_)]

        greet(dp_n, fs_n, np_ > 0)
        gathers = [PlaneGather(fs_n, pack_refs[i], g_refs[i], *gat_s[i]) for i in range(np_)]
        swap = Swap(fs_n, x_ref, xg_ref, *swap_s)
        z_n = fs_n // 2
        if np_:
            gathers[0].start()
        swap.start()
        if np_:
            gathers[1].start()
            for k in range(1, z_n):
                gathers[0].spread(k)
            for k in range(z_n):
                gathers[0].hand_on(k)
            for k in range(1, z_n):
                gathers[1].spread(k)
            for k in range(z_n):
                gathers[0].corner(k)
        swap.wait()
        if np_:
            gathers[0].wait()
            sm_ref[...] = jnp.sum(units3(g_refs[0], 0, 16).astype(f32), 0)
        gain, bias = sm_ref[0:1, :], sm_ref[1:2, :]
        per = 256 // samples if samples < 256 else 1
        for s in range(slots // per):
            at = slice(s * per * samples, (s + 1) * per * samples)
            u, _ = unit(xg_ref[s * per:(s + 1) * per].reshape(per * samples, d).astype(f32))
            acted[at, :] = (u * gain + bias).astype(bf16)
        for i in range(3):
            w = units(g_refs[0], 16 + i * rl, rl) if np_ else w_ref[i]

            def project(at):
                y = dot(acted[at, :], w).astype(bf16)
                qkv_ref[i, at, :] = y * 0.125 if i == 0 else y

            blocks(rows, 256, project)

        turns = Turns(fs_n, hp, lambda p, j: o_ref.at[p, pl.ds(pl.multiple_of(j * samples, samples), samples)],
                      lambda p, j: back_ref.at[j, p], *turn_s)
        for p in range(hp):
            at = head_pair(p)
            vt[...] = qkv_ref[2, :, at].astype(f32).T.astype(bf16)
            for h in range(2):
                def part(i, _):
                    qa = pl.ds(pl.multiple_of(i * BQ, BQ), BQ)
                    q = qkv_ref[0, qa, at]
                    q = jnp.where(head_mask(BQ, h), q, jnp.zeros_like(q))
                    s = dot(qkv_ref[1, :, at], q, NT) + kb_ref[:, 0:1]
                    m = jnp.max(s, 0, keepdims=True)
                    e = jnp.exp(s - m)
                    tot = jnp.sum(e, 0, keepdims=True)
                    o = dot(vt[h * 64:h * 64 + 64, :], e.astype(bf16))
                    ot[h * 64:h * 64 + 64, qa] = o * (1.0 / tot)
                    l_ref[p * 2 + h:p * 2 + h + 1, qa] = m + jnp.log(tot)
                    return 0
                lax.fori_loop(0, rows // BQ, part, 0)
            o_ref[p, :, :] = ot[...].T.astype(bf16)
            turns.start(p)
            if np_ and p == 0:
                gathers[1].hand_on(0)
            if np_ and p == 2:
                gathers[1].hand_on(1)
        if np_:
            for k in range(2, z_n):
                gathers[1].hand_on(k)
            for k in range(z_n):
                gathers[1].corner(k)
        for p in range(hp):
            turns.wait_recv(p)
        turns.wait_send()
        if np_:
            gathers[1].wait()

    def units3(ref, start, size):
        v = ref[..., start:start + size, :]
        return v.reshape(-1, size, v.shape[-1])

    S, V = jax.ShapeDtypeStruct, pltpu.VMEM
    outs = [S((slots, hp, samples, 128), bf16), S((slots, samples, d), bf16), S((hp, rows, 128), bf16), S((3, rows, dh), bf16),
            S((heads, rows), f32)]
    outs += [S((dp_n, fs_n // 2, 2) + p.shape, bf16) for p in packs]
    args = [x, keybias] + list(packs)
    if np_:
        outs.append(S((16, d), f32))
    else:
        args += list(plain)
    return pl.pallas_call(
        body, out_shape=outs, in_specs=[VM] * len(args), out_specs=[ANY if np_ and i == 6 else VM for i in range(len(outs))],
        scratch_shapes=[V((rows, d), bf16), V((128, rows), bf16), V((128, rows), f32)] + swap_sems(fs_n) + turn_sems(fs_n, hp)
        + plane_gather_sems(fs_n) * np_,
        compiler_params=params(1), name="forward",
    )(*args)


def backward_kernel(do1, xg, qkv, o, lse, w, smalls, keybias, g1, gm, dp_n, fs_n, rl, dh, tasks, packed):
    slots, samples, d = xg.shape
    rows = slots * samples
    heads = dh // 64
    hp = heads // 2

    def body(*refs):
        it = iter(refs)
        do_in, xg_ref, qkv_ref, o_ref, l_ref, w_ref, n_ref, kb_ref = (next(it) for _ in range(8))
        g1_ref, gm_ref = (next(it), next(it)) if packed else (None, None)
        if packed:
            tg_ref, sm_ref, ss_ref = (next(it) for _ in range(3))
        else:
            dr_ref, gw_ref, gn_ref = (next(it) for _ in range(3))
        do, delta, kt, dqt, dk, dv, dqkv, acted, gn, dx = (next(it) for _ in range(10))
        turn_s = [next(it) for _ in range(3)]
        back_s = [next(it) for _ in range(3)]
        if packed:
            gs, dr_ref = next(it), next(it)
            rm = [next(it) for _ in range(11)]
            rs = [next(it) for _ in range(11)]

        greet(dp_n, fs_n, packed)
        turns = Turns(fs_n, hp, lambda p, j: do_in.at[j, p], lambda p, j: do.at[j, p], *turn_s)
        for p in range(hp):
            turns.start(p)
        if packed:
            red = PlaneReduce(fs_n, gm_ref, rm[:4], rm[4:])
            red_s = PlaneReduce(fs_n, gs, rs[:4], rs[4:])
            red.start()
            for k in red.order():
                red.first(k)
        gain, bias = n_ref[0:1, :], n_ref[1:2, :]
        lane = lax.broadcasted_iota(jnp.int32, (8, 128), 1) // 64
        pick = (lane == lax.broadcasted_iota(jnp.int32, (8, 128), 0)).astype(f32)
        per = BQ // samples if samples < BQ else 1

        def grad_rows(i, p):
            return do[pl.ds(i * per, per), p].reshape(per * samples, 128)

        n = per * samples
        for p in range(hp):
            at = head_pair(p)
            kt[...] = qkv_ref[1, :, at].astype(f32).T.astype(bf16)
            dk[...] = jnp.zeros_like(dk)
            dv[...] = jnp.zeros_like(dv)
            turns.wait_recv(p)

            def deltas(i, _):
                qa = pl.ds(pl.multiple_of(i * n, n), n)
                prod = grad_rows(i, p).astype(f32) * o_ref[p, qa, :].astype(f32)
                delta[:, qa] = lax.dot_general(pick, prod, NT, precision=lax.Precision.HIGHEST, preferred_element_type=f32)
                return 0

            lax.fori_loop(0, rows // n, deltas, 0)
            for h in range(2):
                def part(i, _):
                    qa = pl.ds(pl.multiple_of(i * n, n), n)
                    mask = head_mask(n, h)
                    q = qkv_ref[0, qa, at]
                    q = jnp.where(mask, q, jnp.zeros_like(q))
                    g = grad_rows(i, p)
                    g = jnp.where(mask, g, jnp.zeros_like(g))
                    s = dot(qkv_ref[1, :, at], q, NT) + kb_ref[:, 0:1]
                    e = jnp.exp(s - l_ref[p * 2 + h:p * 2 + h + 1, qa])
                    ds = (e * (dot(qkv_ref[2, :, at], g, NT) - delta[h:h + 1, qa])).astype(bf16)
                    dv[...] += dot(e.astype(bf16), g)
                    dk[...] += dot(ds, q)
                    dqt[h * 64:h * 64 + 64, qa] = dot(kt[h * 64:h * 64 + 64, :], ds) * 0.125
                    return 0
                lax.fori_loop(0, rows // n, part, 0)
            dqkv[0, :, at] = dqt[...].T.astype(bf16)
            dqkv[1, :, at] = dk[...].astype(bf16)
            dqkv[2, :, at] = dv[...].astype(bf16)
            if packed:
                if p == hp - 2:
                    for k in red.order():
                        red.second(k)
                if p == hp - 1:
                    for k in red.order():
                        red.third(k)

        def mats(i):
            return units(w_ref, 16 + i * rl, rl) if packed else w_ref[i]

        per2 = 256 // samples if samples < 256 else 1
        n2 = per2 * samples
        gn[...] = jnp.zeros_like(gn)

        def act_rows(i):
            at = pl.ds(pl.multiple_of(i * n2, n2), n2)
            u, r = unit(xg_ref[pl.ds(i * per2, per2)].reshape(n2, d).astype(f32))
            return at, u, r

        def first(i, _):
            at, u, r = act_rows(i)
            acted[at, :] = (u * gain + bias).astype(bf16)
            return 0

        lax.fori_loop(0, rows // n2, first, 0)
        for i in range(3):
            if packed:
                y = dot(acted[...], dqkv[i], TN).astype(bf16)
                gs[:, :, :, 16 + i * rl:16 + (i + 1) * rl, :] = y.reshape(gs.shape[:3] + (rl, d))
            else:
                gw_ref[i] = dot(acted[...], dqkv[i], TN).astype(bf16)

        back = Turns(fs_n, 1, lambda p, j: dx.at[j], lambda p, j: dr_ref.at[j], *back_s)

        def sums(i, _):
            at, u, r = act_rows(i)
            y = dot(dqkv[0, at, :], mats(0), NT) + dot(dqkv[1, at, :], mats(1), NT) + dot(dqkv[2, at, :], mats(2), NT)
            gn[0:1, :] += jnp.sum(y * u, 0, keepdims=True)
            gn[1:2, :] += jnp.sum(y, 0, keepdims=True)
            dx[pl.ds(i * per2, per2)] = unit_back(y, u, r, gain).astype(bf16).reshape(per2, samples, d)
            return 0

        lax.fori_loop(0, rows // n2, sums, 0)
        back.start(0)
        if packed:
            small = jnp.concatenate([gn[...].astype(bf16), jnp.zeros_like(gn).astype(bf16)], 0)
            gs[:, :, :, 0:16, :] = jnp.broadcast_to(small, gs.shape[:3] + (16, d))
            red_s.start()
            for k in red_s.order():
                red_s.first(k)
            red.finish(sm_ref)
            for k in red_s.order():
                red_s.second(k)
            for k in red_s.order():
                red_s.third(k)
            back.wait_recv(0)
            feats = slots // tasks
            for s in range(slots):
                t, f = s // feats, s % feats
                for i in range(d // 128):
                    at = pl.ds(((t * samples * (d // 128)) + i) * feats + f, samples, stride=feats * (d // 128))
                    tg_ref[at, :] = g1_ref[s * samples:(s + 1) * samples, head_pair(i)] + dr_ref[s, :, head_pair(i)].astype(f32)
            red_s.finish(ss_ref)
        else:
            gn_ref[...] = gn[...]
            back.wait_recv(0)
        back.wait_send()
        turns.wait_send()

    S, V = jax.ShapeDtypeStruct, pltpu.VMEM
    args = [do1, xg, qkv, o, lse, w, smalls, keybias]
    scratch = [V((slots, hp, samples, 128), bf16), V((8, rows), f32), V((128, rows), bf16), V((128, rows), f32), V((rows, 128), f32),
               V((rows, 128), f32), V((3, rows, dh), bf16), V((rows, d), bf16), V((8, d), f32), V((slots, samples, d), bf16)]
    scratch += turn_sems(fs_n, hp) + turn_sems(fs_n, 1)
    if packed:
        args += [g1, gm]
        mrows, srows = gm.shape[3], 16 + 3 * rl
        outs = [S((rows * d // 128, 128), f32), S((mrows, d), f32), S((srows, d), f32)]
        scratch += [V((dp_n, fs_n // 2, 2, srows, d), bf16), V((slots, samples, d), bf16)]
        scratch += plane_reduce_scratch(fs_n, mrows, d) + plane_reduce_scratch(fs_n, srows, d)
    else:
        outs = [S((slots, samples, d), bf16), S((3, d, dh), bf16), S((8, d), f32)]
    return pl.pallas_call(
        body, out_shape=outs, in_specs=[ANY if packed and i == 9 else VM for i in range(len(args))], out_specs=[VM] * len(outs), scratch_shapes=scratch,
        compiler_params=params(2), name="backward",
    )(*args)
def ones_pairs():
    half = lax.broadcasted_iota(jnp.int32, (256, 128), 0) // 64
    return (lax.rem(half, 2) == lax.broadcasted_iota(jnp.int32, (256, 128), 1) // 64).astype(bf16)


def head_sums(prods, ones):
    both = []
    for v in prods:
        hi = v.astype(bf16)
        both.append(jnp.concatenate([hi, (v - hi.astype(f32)).astype(bf16)], 1))
    out = dot(jnp.concatenate(both, 0), ones)
    n = prods[0].shape[0]
    return [out[i * n:(i + 1) * n] for i in range(len(prods))]


def key_bias(ref, counts, feats):
    count = counts[lax.axis_index("fsdp") // feats]
    rows = lax.broadcasted_iota(jnp.int32, ref.shape, 0)
    ref[...] = jnp.where(rows < count, 0.0, MASKED)


def rows_at(i, n):
    return pl.ds(pl.multiple_of(i * n, n), n)


def first_kernel(x, scounts, fcounts, small_parts, s_qkv, s_out, f_qkv, f_out, m_in, m_out, tasks, fs_n):
    dp_n = 4
    slots, samples, d = x.shape
    feats = slots // tasks
    rows = slots * samples
    hp = d // 128
    rl = s_out.shape[0]
    fl = m_out.shape[0]
    chunks = m_in.shape[1] // d
    z_n = fs_n // 2
    ra, r1, r2 = 16 + 3 * rl, 5 * rl, chunks * rl + fl
    per = 256 // samples

    def body(x_ref, sc_ref, fc_ref, norms, ob, ib, sq, so, fq, fo, mi, mo,
             xg_h, qkv_h, o_h, l_ref, ga_h, w1_h, w2, sm, x1_h, o2_h, a3_h, qkv2_h, p2_h, back_h,
             xg, qkv, o_ref, ga, w1, x1, o2, a3, qkv2, p2, back_ref,
             pa, pb1, pb2, kb, acted, vt, ot, small, out_sem, p2_sem, a3_sem, *sems):
        swap_s, turn_s = sems[:3], sems[3:6]
        gat_s = [sems[6 + 7 * i:13 + 7 * i] for i in range(3)]
        me = lax.axis_index("dp") * fs_n + lax.axis_index("fsdp")
        def placed(ref, first):
            n = ref.shape[1]
            hot = lax.broadcasted_iota(jnp.int32, (n, d), 1) == lax.broadcasted_iota(jnp.int32, (n, d), 0) + first
            return dot(ref[...], hot.astype(bf16))

        inner = lax.rem(me * fl, d)
        row = lax.broadcasted_iota(jnp.int32, (16, d), 0)
        small[...] = jnp.where(row == 7 + me * fl // d, placed(ib, inner), 0.0)
        small[0:6, :] = placed(norms, me * rl)
        small[6:7, :] = placed(ob, me * rl)
        pa[0:16, :] = small[...].astype(bf16)
        for i in range(3):
            pa[16 + i * rl:16 + (i + 1) * rl, :] = sq[i]
            pb1[(1 + i) * rl:(2 + i) * rl, :] = fq[i]
        pb1[0:rl, :] = so[...]
        pb1[4 * rl:5 * rl, :] = fo[...]
        for c in range(chunks):
            pb2[c * rl:(c + 1) * rl, :] = mi[:, c * d:(c + 1) * d]
        pb2[chunks * rl:, :] = mo[...]

        pairs_out = [(xg, xg_h), (qkv, qkv_h), (o_ref, o_h), (ga, ga_h), (w1, w1_h), (x1, x1_h), (o2, o2_h), (qkv2, qkv2_h), (back_ref, back_h)]
        outs_c = [pltpu.make_async_copy(v, h, out_sem.at[i]) for i, (v, h) in enumerate(pairs_out)]
        out_xg, out_qkv, out_o, out_ga, out_w1, out_x1, out_o2, out_qkv2, out_back = outs_c

        def out_p2(t):
            return pltpu.make_async_copy(p2.at[t], p2_h.at[t], p2_sem.at[t])

        def out_a3(i):
            return pltpu.make_async_copy(a3.at[rows_at(i, 256)], a3_h.at[rows_at(i, 256)], a3_sem.at[i])

        greet(dp_n, fs_n)
        A = PlaneGather(fs_n, pa, ga, *gat_s[0])
        B = PlaneGather(fs_n, pb1, w1, *gat_s[1])
        C = PlaneGather(fs_n, pb2, w2, *gat_s[2])
        swap = Swap(fs_n, x_ref, xg, *swap_s)
        turns = Turns(fs_n, hp, lambda p, j: o_ref.at[p, rows_at(j, samples)], lambda p, j: back_ref.at[j, p], *turn_s)
        later = list(range(1, z_n))
        A.start()
        swap.start()
        for G in (A, B, C):
            G.begin()
        key_bias(kb, sc_ref, feats)
        for k in later:
            A.spread(k)
        for k in range(z_n):
            A.hand_on(k)
        for k in range(z_n):
            A.corner(k)
        swap.wait()
        B.start()
        C.start()
        out_xg.start()
        A.wait()
        out_ga.start()
        total = ga[:, :, :, 0:16, :].astype(f32)
        sm[...] = jnp.sum(total.reshape(-1, 16, d), 0)

        def act(i, _):
            u, _r = unit(xg[pl.ds(i * per, per)].reshape(256, d).astype(f32))
            acted[rows_at(i, 256), :] = (u * sm[0:1, :] + sm[1:2, :]).astype(bf16)
            return 0

        lax.fori_loop(0, rows // 256, act, 0)
        for i in range(3):
            w = units(ga, 16 + i * rl, rl)

            def project(at):
                y = dot(acted[at, :], w).astype(bf16)
                qkv[i, at, :] = y * 0.125 if i == 0 else y

            blocks(rows, 256, project)
        out_qkv.start()
        for k in later:
            B.spread(k)

        for p in range(hp):
            at = head_pair(p)
            vt[...] = qkv[2, :, at].astype(f32).T.astype(bf16)
            for h in range(2):
                def part(i, _):
                    qa = rows_at(i, BQ)
                    q = qkv[0, qa, at]
                    q = jnp.where(head_mask(BQ, h), q, jnp.zeros_like(q))
                    s = dot(qkv[1, :, at], q, NT) + kb[:, 0:1]
                    m = jnp.max(s, 0, keepdims=True)
                    e = jnp.exp(s - m)
                    tot = jnp.sum(e, 0, keepdims=True)
                    o = dot(vt[h * 64:h * 64 + 64, :], e.astype(bf16))
                    ot[h * 64:h * 64 + 64, qa] = o * (1.0 / tot)
                    l_ref[p * 2 + h:p * 2 + h + 1, qa] = m + jnp.log(tot)
                    return 0
                lax.fori_loop(0, rows // BQ, part, 0)
            o_ref[p, :, :] = ot[...].T.astype(bf16)
            turns.start(p)
            if p == 0:
                for k in range(z_n):
                    B.hand_on(k)
                for k in later:
                    C.spread(k)
            if p == 1:
                for k in range(z_n):
                    B.corner(k)
            if p == 2:
                C.hand_on(0)
        out_o.start()
        B.wait()
        out_w1.start()
        C.hand_on(1)
        for p in range(hp):
            turns.wait_recv(p)
        out_back.start()
        for k in range(2, z_n):
            C.hand_on(k)

        def first(i, _):
            at = rows_at(i, 256)
            o1 = jnp.concatenate([back_ref[pl.ds(i * per, per), p].reshape(256, 128) for p in range(hp)], 1)
            y = x_ref[pl.ds(i * per, per)].reshape(256, d).astype(f32) + dot(o1, units(w1, 0, rl))
            x1[at, :] = y
            u, _r = unit(y)
            v = (u * sm[2:3, :] + sm[3:4, :]).astype(bf16)
            for j in range(3):
                z = dot(v, units(w1, (1 + j) * rl, rl)).astype(bf16)
                qkv2[j, at, :] = z * 0.125 if j == 0 else z
            return 0

        lax.fori_loop(0, rows // 256, first, 0)
        out_x1.start()
        out_qkv2.start()
        ones = ones_pairs()

        def mix(t, _):
            slot = lambda f: rows_at(t * feats + f, samples)
            for p in range(hp):
                lanes = head_pair(p)
                ks = [qkv2[1, slot(g), lanes].astype(f32) for g in range(feats)]
                vs = [qkv2[2, slot(g), lanes].astype(f32) for g in range(feats)]
                for f in range(feats):
                    q = qkv2[0, slot(f), lanes].astype(f32)
                    sc = head_sums([q * k for k in ks], ones)
                    sc = [v + jnp.where(g < fc_ref[t], 0.0, MASKED) for g, v in enumerate(sc)]
                    top = functools.reduce(jnp.maximum, sc)
                    sc = [jnp.exp(v - top) for v in sc]
                    inv = 1.0 / sum(sc)
                    sc = [v * inv for v in sc]
                    for g in range(feats):
                        p2[t, p, f, g] = sc[g].astype(bf16)
                    o2[slot(f), lanes] = sum(w * v for w, v in zip(sc, vs)).astype(bf16)
            out_p2(t).start()
            return 0

        lax.fori_loop(0, tasks, mix, 0)
        out_o2.start()
        for k in range(z_n):
            C.corner(k)

        def second(i, _):
            at = rows_at(i, 256)
            u, _r = unit(x1[at, :] + dot(o2[at, :], units(w1, 4 * rl, rl)))
            a3[at, :] = (u * sm[4:5, :] + sm[5:6, :]).astype(bf16)
            out_a3(i).start()
            return 0

        lax.fori_loop(0, rows // 256, second, 0)
        turns.wait_send()
        C.wait()
        for c in outs_c:
            c.wait()
        for t in range(tasks):
            out_p2(t).wait()
        for i in range(rows // 256):
            out_a3(i).wait()

    S, V, D = jax.ShapeDtypeStruct, pltpu.VMEM, pltpu.SemaphoreType.DMA
    SM = pl.BlockSpec(memory_space=pltpu.SMEM)
    g = (dp_n, z_n, 2)
    outs = [S((slots, samples, d), bf16), S((3, rows, d), bf16), S((hp, rows, 128), bf16), S((2 * hp, rows), f32),
            S(g + (ra, d), bf16), S(g + (r1, d), bf16), S(g + (r2, d), bf16), S((16, d), f32), S((rows, d), f32), S((rows, d), bf16),
            S((rows, d), bf16), S((3, rows, d), bf16), S((tasks, hp, feats, feats, samples, 128), bf16), S((slots, hp, samples, 128), bf16)]
    return pl.pallas_call(
        body, out_shape=outs, in_specs=[VM, SM, SM] + [VM] * 9, out_specs=[VM if i in (3, 7) else ANY for i in range(len(outs))],
        scratch_shapes=[V(outs[i].shape, outs[i].dtype) for i in (0, 1, 2, 4, 5, 8, 9, 10, 11, 12, 13)] + [V((ra, d), bf16), V((r1, d), bf16), V((r2, d), bf16), V((rows, 128), f32), V((rows, d), bf16), V((128, rows), bf16),
                        V((128, rows), f32), V((16, d), f32), D((9,)), D((tasks,)), D((rows // 256,))] + swap_sems(fs_n) + turn_sems(fs_n, hp) + plane_gather_sems(fs_n) * 3,
        compiler_params=params(1), name="first",
    )(x, scounts, fcounts, *small_parts, s_qkv, s_out, f_qkv, f_out, m_in, m_out)


def second_kernel(cot, scounts, saved, tasks, rl, fl, fs_n):
    xg, qkv, o, lse, ga, w1, w2, sm, x1, o2, a3, qkv2, p2, back = saved
    slots, samples, d = xg.shape
    feats = slots // tasks
    rows = slots * samples
    hp = d // 128
    z_n = fs_n // 2
    chunks = (w2.shape[3] - fl) // rl
    r1, r2, rs = 16 + 5 * rl, chunks * rl + fl, 3 * rl
    RB = 256
    per = RB // samples
    bq = 512
    pq = bq // samples

    def body(sc_ref, l_ref, sm_ref, cot_h, w2_h, x1_h, o2_h, a3_h,
             xg_h, qkv_h, o_h, ga_h, w1_h, qkv2_h, p2_h, back_h,
             g1_h, lo_h, dr, out2, out1, outs_, outn,
             g1, lo, cot_ref, w2_ref, x1_ref, o2_ref, a3_ref, o_, w1_, q_, p2_, bk, acc, act, gh, ev, a2, do2, dqkv, G2, G1, GS, GN, do, do1, delta, kt, dqt, kb, gn,
             c2, n2, z2, c1, n1, z1, c0, n0, z0, c3, n3, z3, load_sem, *sems):
        turn_s, back_s = sems[:3], sems[3:6]
        red_s = [sems[6 + 6 * i:12 + 6 * i] for i in range(4)]
        me_f = lax.axis_index("fsdp")
        me_z, me_c = me_f // 2, mod(me_f, 2)
        load = lambda i, src, dst: pltpu.make_async_copy(src, dst, load_sem.at[i])
        get_w1 = load(0, w1_h, w1_)
        get_q2 = load(1, qkv2_h, q_)
        get_p2 = load(2, p2_h, p2_)
        get_bk = load(3, back_h, bk)
        xg_ = a3_ref
        dk, dv = acc.at[:, 0:128], acc.at[:, 128:256]
        get_xg = load(4, xg_h, xg_)
        get_o = load(5, o_h, o_)
        get_q1 = load(6, qkv_h, q_)
        ga_ = w1_.at[:, :, :, 0:16 + rs, :]
        get_ga = load(7, ga_h, ga_)
        heads_in = [load(8 + i, a, b) for i, (a, b) in enumerate([(a3_h, a3_ref), (w2_h, w2_ref), (cot_h, cot_ref), (x1_h, x1_ref), (o2_h, o2_ref)])]
        put_g1 = load(13, g1, g1_h)
        put_lo = load(14, lo, lo_h)
        for c in heads_in + [get_w1, get_q2, get_p2, get_bk, get_o]:
            c.start()
        key_bias(kb, sc_ref, feats)
        gn[...] = jnp.zeros_like(gn)
        for i in range(rows // RB):
            acc[i * RB:(i + 1) * RB, :] = jnp.zeros((RB, d), f32)
            g1[i * RB:(i + 1) * RB, :] = jnp.zeros((RB, d), f32)
        greet(4, fs_n)
        for c in heads_in[:3]:
            c.wait()

        def mat(k):
            return units(w1_, k * rl, rl)

        def in_mat(c):
            return w2_ref[:, :, :, pl.ds(pl.multiple_of(c * rl, rl), rl), :].reshape(d, d)

        def out_mat(c):
            return w2_ref[pl.ds(c, 1), :, :, chunks * rl:, :].reshape(d, d)

        def put(g, start, i, value):
            g[2 * i:2 * i + 2, :, :, pl.ds(start, rl), :] = value.reshape(2, z_n, 2, rl, d)

        halves = [(slice(i * 256, i * 256 + 256), i) for i in range(d // 256)]

        def chunk(c, _):
            def part(at):
                hid = dot(a3_ref[at, :], in_mat(c)) + sm_ref[pl.ds(7 + c, 1), :]
                cdf, pdf = gelu_parts(hid)
                al = (hid * cdf).astype(bf16)
                act[at, :] = al
                gl = ((cdf + pdf) * dot(cot_ref[at, :], out_mat(c), NT)).astype(bf16)
                gh[at, :] = gl
                gn[pl.ds(7 + c, 1), :] += jnp.sum(gl.astype(f32), 0, keepdims=True)
                acc[at, :] += dot(al, out_mat(c))
                g1[at, :] += dot(gl, in_mat(c), NT)

            blocks(rows, RB, part)
            for at, i in halves:
                value = dot(act[:, at], cot_ref[...], TN).astype(bf16)
                G2[pl.ds(c, 1), 2 * i:2 * i + 2, :, chunks * rl:, :] = value.reshape(1, 2, 2, fl, d)
                put(G2, pl.multiple_of(c * rl, rl), i, dot(a3_ref[:, at], gh[...], TN).astype(bf16))
            return 0

        lax.fori_loop(0, chunks, chunk, 0)
        red2 = PlaneReduce(fs_n, G2, (c2, n2, z2), red_s[0])
        red2.start()
        for c in heads_in[3:]:
            c.wait()
        get_w1.wait()

        def third(at):
            x2 = x1_ref[at, :] + dot(o2_ref[at, :], mat(4))
            lo[at, :] = (x2 + acc[at, :] + sm_ref[6:7, :]).astype(bf16)
            u, r = unit(x2)
            y = g1[at, :]
            gn[4:5, :] += jnp.sum(y * u, 0, keepdims=True)
            gn[5:6, :] += jnp.sum(y, 0, keepdims=True)
            cf = cot_ref[at, :].astype(f32)
            gn[6:7, :] += jnp.sum(cf, 0, keepdims=True)
            g2 = cf + unit_back(y, u, r, sm_ref[4:5, :])
            g1[at, :] = g2
            e2 = g2.astype(bf16)
            ev[at, :] = e2
            do2[at, :] = dot(e2, mat(4), NT).astype(bf16)

        blocks(rows, RB, third)
        put_lo.start()
        for at, i in halves:
            put(G1, 16 + 4 * rl, i, dot(o2_ref[:, at], ev[...], TN).astype(bf16))
        red2.every(red2.first)
        get_q2.wait()
        get_p2.wait()
        ones = ones_pairs()

        def unmix(t, _):
            slot = lambda f: rows_at(t * feats + f, samples)
            for p in range(hp):
                lanes = head_pair(p)
                ks = [q_[1, slot(g), lanes].astype(f32) for g in range(feats)]
                vs = [q_[2, slot(g), lanes].astype(f32) for g in range(feats)]
                dks, dvs = [0.0] * feats, [0.0] * feats
                for f in range(feats):
                    q = q_[0, slot(f), lanes].astype(f32)
                    gr = do2[slot(f), lanes].astype(f32)
                    dp = head_sums([gr * v for v in vs], ones)
                    ws = [p2_[t, p, f, g].astype(f32) for g in range(feats)]
                    mean = sum(w * v for w, v in zip(ws, dp))
                    ds = [(w * (v - mean)).astype(bf16).astype(f32) for w, v in zip(ws, dp)]
                    dqkv[0, slot(f), lanes] = (sum(v * k for v, k in zip(ds, ks)) * 0.125).astype(bf16)
                    for g in range(feats):
                        dks[g] += ds[g] * q
                        dvs[g] += ws[g] * gr
                for g in range(feats):
                    dqkv[1, slot(g), lanes] = dks[g].astype(bf16)
                    dqkv[2, slot(g), lanes] = dvs[g].astype(bf16)
            return 0

        lax.fori_loop(0, tasks, unmix, 0)
        get_q1.start()

        def far(i, r):
            return mod(me_z + i, z_n) * 2 + mod(me_c + r, 2)

        me_d = lax.axis_index("dp")
        sends = {}
        for i in range(z_n):
            for r in range(2):
                for p in range(hp):
                    n = (p * z_n + i) * 2 + r
                    to = far(i, r)
                    if i == 0 and r == 0:
                        sends[p, i, r] = pltpu.make_async_copy(do1.at[to, p], do.at[to, p], turn_s[0].at[p])
                    else:
                        sends[p, i, r] = rcopy(do1.at[to, p], do.at[me_f, p], turn_s[1].at[n], turn_s[2].at[n], (me_d, to))
        chips = list(range(1, z_n)) + [0]

        def fourth(i):
            chip = mod(me_z + i, z_n)
            at = rows_at(chip, RB)
            u, r = unit(x1_ref[at, :])
            gain = sm_ref[2:3, :]
            a2[at, :] = (u * gain + sm_ref[3:4, :]).astype(bf16)
            y = dot(dqkv[0, at, :], mat(1), NT) + dot(dqkv[1, at, :], mat(2), NT) + dot(dqkv[2, at, :], mat(3), NT)
            gn[2:3, :] += jnp.sum(y * u, 0, keepdims=True)
            gn[3:4, :] += jnp.sum(y, 0, keepdims=True)
            v = g1[at, :] + unit_back(y, u, r, gain)
            g1[at, :] = v
            e1 = v.astype(bf16)
            ev[at, :] = e1
            g = dot(e1, mat(0), NT).astype(bf16)
            for p in range(hp):
                do1[pl.ds(chip * per, per), p] = g[:, head_pair(p)].reshape(per, samples, 128)
            for r in range(2):
                sends[0, i, r].start()

        for i in chips:
            fourth(i)
        for p in range(1, hp):
            for i in chips:
                for r in range(2):
                    sends[p, i, r].start()
        put_g1.start()
        get_ga.start()

        get_xg.start()
        red2.every(red2.second)
        get_bk.wait()
        for at, i in halves:
            o1 = jnp.concatenate([bk[:, 2 * i].reshape(rows, 128), bk[:, 2 * i + 1].reshape(rows, 128)], 1)
            put(G1, 16, i, dot(o1, ev[...], TN).astype(bf16))
            for j in range(3):
                put(G1, 16 + (1 + j) * rl, i, dot(a2[:, at], dqkv[j], TN).astype(bf16))
        G1[:, :, :, 0:16, :] = jnp.broadcast_to(gn[...].astype(bf16), (4, z_n, 2, 16, d))
        red1 = PlaneReduce(fs_n, G1, (c1, n1, z1), red_s[1])
        red1.start()
        red2.every(red2.third)

        lane = lax.broadcasted_iota(jnp.int32, (8, 128), 1) // 64
        pick = (lane == lax.broadcasted_iota(jnp.int32, (8, 128), 0)).astype(f32)
        get_q1.wait()
        get_o.wait()

        def grad_rows(i, p):
            return do[pl.ds(i * pq, pq), p].reshape(bq, 128)

        for p in range(hp):
            at = head_pair(p)
            kt[...] = q_[1, :, at].astype(f32).T.astype(bf16)
            dk[...] = jnp.zeros((rows, 128), f32)
            dv[...] = jnp.zeros((rows, 128), f32)
            for i in range(z_n):
                for r in range(2):
                    if i == 0 and r == 0:
                        sends[p, i, r].wait()
                    else:
                        sends[p, i, r].wait_recv()

            def deltas(i, _):
                qa = rows_at(i, bq)
                prod = grad_rows(i, p).astype(f32) * o_[p, qa, :].astype(f32)
                delta[:, qa] = lax.dot_general(pick, prod, NT, precision=lax.Precision.HIGHEST, preferred_element_type=f32)
                return 0

            lax.fori_loop(0, rows // bq, deltas, 0)
            for h in range(2):
                def part(i, _):
                    qa = rows_at(i, bq)
                    mask = head_mask(bq, h)
                    q = q_[0, qa, at]
                    q = jnp.where(mask, q, jnp.zeros_like(q))
                    g = grad_rows(i, p)
                    g = jnp.where(mask, g, jnp.zeros_like(g))
                    s = dot(q_[1, :, at], q, NT) + kb[:, 0:1]
                    e = jnp.exp(s - l_ref[p * 2 + h:p * 2 + h + 1, qa])
                    ds = (e * (dot(q_[2, :, at], g, NT) - delta[h:h + 1, qa])).astype(bf16)
                    dv[...] += dot(e.astype(bf16), g)
                    dk[...] += dot(ds, q)
                    dqt[h * 64:h * 64 + 64, qa] = dot(kt[h * 64:h * 64 + 64, :], ds) * 0.125
                    return 0
                lax.fori_loop(0, rows // bq, part, 0)
            dqkv[0, :, at] = dqt[...].T.astype(bf16)
            dqkv[1, :, at] = dk[...].astype(bf16)
            dqkv[2, :, at] = dv[...].astype(bf16)
            if p == 0:
                red1.every(red1.first)
            if p == 2:
                red1.every(red1.second)
        red1.every(red1.third)

        get_ga.wait()
        get_xg.wait()
        gn[...] = jnp.zeros_like(gn)
        gain, bias = sm_ref[0:1, :], sm_ref[1:2, :]

        def again(i, _):
            u, _r = unit(xg_[rows_at(i, RB), :].astype(f32))
            ev[rows_at(i, RB), :] = (u * gain + bias).astype(bf16)
            return 0

        lax.fori_loop(0, rows // RB, again, 0)
        for j in range(3):
            for at, i in halves:
                put(GS, j * rl, i, dot(ev[:, at], dqkv[j], TN).astype(bf16))
        reds = PlaneReduce(fs_n, GS, (c0, n0, z0), red_s[2])
        reds.start()
        backs = {}
        for i in range(z_n):
            for r in range(2):
                to = far(i, r)
                if i == 0 and r == 0:
                    backs[i, r] = pltpu.make_async_copy(xg_.at[rows_at(to, samples)], dr.at[to], back_s[0].at[0])
                else:
                    n = 2 * i + r
                    backs[i, r] = rcopy(xg_.at[rows_at(to, samples)], dr.at[me_f], back_s[1].at[n], back_s[2].at[n], (me_d, to))
        for i in chips:
            chip = mod(me_z + i, z_n)
            at = rows_at(chip, RB)
            u, r = unit(xg_[at, :].astype(f32))
            y = (dot(dqkv[0, at, :], units(ga_, 16, rl), NT) + dot(dqkv[1, at, :], units(ga_, 16 + rl, rl), NT)
                 + dot(dqkv[2, at, :], units(ga_, 16 + 2 * rl, rl), NT))
            gn[0:1, :] += jnp.sum(y * u, 0, keepdims=True)
            gn[1:2, :] += jnp.sum(y, 0, keepdims=True)
            xg_[at, :] = unit_back(y, u, r, gain).astype(bf16)
            for r in range(2):
                backs[i, r].start()
            if i == 1:
                reds.every(reds.first)
        GN[...] = jnp.broadcast_to(gn[...].astype(bf16), (4, z_n, 2, 16, d))
        redn = PlaneReduce(fs_n, GN, (c3, n3, z3), red_s[3])
        redn.start()
        redn.every(redn.first)
        reds.every(reds.second)
        redn.every(redn.second)
        reds.every(reds.third)
        redn.every(redn.third)
        red2.finish(out2)
        red1.finish(out1)
        reds.finish(outs_)
        redn.finish(outn)
        put_g1.wait()
        put_lo.wait()
        for i in range(z_n):
            for r in range(2):
                backs[i, r].wait()
        for key, c in sends.items():
            if key[1:] != (0, 0):
                c.wait_send()

    S, V, D = jax.ShapeDtypeStruct, pltpu.VMEM, pltpu.SemaphoreType.DMA
    SM = pl.BlockSpec(memory_space=pltpu.SMEM)
    g = (4, z_n, 2)
    scratch = [V((rows, d), f32), V((rows, d), bf16), V((rows, d), bf16), V(w2.shape, bf16), V((rows, d), f32), V((rows, d), bf16),
               V((rows, d), bf16)]
    scratch += [V(o.shape, bf16), V(w1.shape, bf16), V(qkv.shape, bf16), V(p2.shape, bf16), V(back.shape, bf16),
               V((rows, d), f32), V((rows, d), bf16), V((rows, d), bf16), V((rows, d), bf16), V((rows, d), bf16), V((rows, d), bf16),
               V((3, rows, d), bf16), V(g + (r2, d), bf16), V(g + (r1, d), bf16), V(g + (rs, d), bf16), V(g + (16, d), bf16), V(back.shape, bf16), V(back.shape, bf16), V((8, rows), f32),
               V((128, rows), bf16), V((128, rows), f32), V((rows, 128), f32), V((16, d), f32)]
    scratch += plane_reduce_scratch(fs_n, r2, d) + plane_reduce_scratch(fs_n, r1, d) + plane_reduce_scratch(fs_n, rs, d)
    scratch += plane_reduce_scratch(fs_n, 16, d)
    n = hp * fs_n
    scratch += [D((15,)), D((hp,)), D((n,)), D((n,)), D((1,)), D((fs_n,)), D((fs_n,))] + plane_reduce_sems(fs_n) * 4
    return pl.pallas_call(
        body,
        out_shape=[S((rows, d), f32), S((rows, d), bf16), S((slots, samples, d), bf16), S((r2, d), f32), S((r1, d), f32), S((rs, d), f32),
                   S((16, d), f32)],
        in_specs=[SM, VM, VM] + [ANY] * 13, out_specs=[ANY, ANY, ANY, VM, VM, VM, VM], scratch_shapes=scratch,
        compiler_params=params(2), name="second",
    )(scounts, lse, sm, cot, w2, x1, o2, a3, xg.reshape(rows, d), qkv, o, ga, w1, qkv2, p2, back)


def last_kernel(g1, dr, lo, out2, out1, outs, outn, tasks, rl, fl, fs_n):
    slots, samples, d = dr.shape
    feats = slots // tasks
    rows = slots * samples
    wide = d // 128
    chunks = (out2.shape[0] - fl) // rl

    def body(g1_ref, dr_ref, lo_ref, r2, r1, rs, rn, tg, lo_out, gn, gs, gso, gf, gfo, gmi, gib, gmo, gob, low):
        me = lax.axis_index("dp") * fs_n + lax.axis_index("fsdp")
        for s in range(slots):
            t, f = s // feats, s % feats
            for i in range(wide):
                at = pl.ds((t * samples * wide + i) * feats + f, samples, stride=feats * wide)
                here = (slice(s * samples, (s + 1) * samples), head_pair(i))
                tg[at, :] = g1_ref[here] + dr_ref[s, :, head_pair(i)].astype(f32)
                low[at, :] = lo_ref[here].astype(f32)
        blocks(rows * wide, 512, lambda at: lo_out.__setitem__((at, slice(None)), low[at, :].astype(bf16)))
        for i in range(3):
            gs[i] = rs[i * rl:(i + 1) * rl, :]
            gf[i] = r1[16 + (1 + i) * rl:16 + (2 + i) * rl, :]
        gso[...] = r1[16:16 + rl, :]
        gfo[...] = r1[16 + 4 * rl:16 + 5 * rl, :]
        for c in range(chunks):
            gmi[:, c * d:(c + 1) * d] = r2[c * rl:(c + 1) * rl, :]
        gmo[...] = r2[chunks * rl:, :]
        row = lax.broadcasted_iota(jnp.int32, (16, d), 0)
        both = jnp.where(row < 2, rn[...], r1[0:16, :])

        def mine(v, n, first):
            hot = lax.broadcasted_iota(jnp.int32, (d, n), 0) == lax.broadcasted_iota(jnp.int32, (d, n), 1) + first
            return lax.dot_general(v, hot.astype(f32), NN, precision=lax.Precision.HIGHEST, preferred_element_type=f32)

        own = mine(both, rl, me * rl)
        gn[...] = own[0:6]
        gob[...] = own[6:7]
        line = jnp.sum(jnp.where(row == 7 + me * fl // d, both, 0.0), 0, keepdims=True)
        gib[...] = mine(jnp.broadcast_to(line, (8, d)), fl, lax.rem(me * fl, d))[0:1]

    S = jax.ShapeDtypeStruct
    shapes = [S((rows * wide, 128), f32), S((rows * wide, 128), bf16), S((6, rl), f32), S((3, rl, d), f32), S((rl, d), f32), S((3, rl, d), f32),
              S((rl, d), f32), S((rl, chunks * d), f32), S((1, fl), f32), S((fl, d), f32), S((1, rl), f32)]
    return pl.pallas_call(
        body, out_shape=shapes, in_specs=[VM] * 7, out_specs=[VM] * len(shapes), scratch_shapes=[pltpu.VMEM((rows * wide, 128), f32)],
        compiler_params=params(), name="last",
    )(g1, dr, lo, out2, out1, outs, outn)
def up16(a):
    rows = a.shape[-2]
    extra = (-rows) % 16
    return a if extra == 0 else jnp.pad(a, [(0, 0)] * (a.ndim - 2) + [(0, extra), (0, 0)])


def local(tokens, sample_counts, feature_counts, norms, sample_qkv, sample_out, feature_qkv, feature_out, mlp_in, mlp_in_bias,
          mlp_out, mlp_out_bias, cotangent):
    dp_n, fs_n = lax.axis_size("dp"), lax.axis_size("fsdp")
    nd = dp_n * fs_n
    me_d, me_f = lax.axis_index("dp"), lax.axis_index("fsdp")
    me = me_d * fs_n + me_f
    tasks, samples, feats, d = tokens.shape
    pairs = tasks * feats
    rep = fs_n // pairs
    dh = d // rep
    hp = dh // 128
    rl = sample_out.shape[0]
    chunks = mlp_in.shape[1] // d
    fl = mlp_out.shape[0]
    total = samples * fs_n
    if rep == 1 and dp_n == 4 and rl % 16 == 0 and fs_n * fl == d:
        def turned(v):
            return v.transpose(0, 2, 1, 3).reshape(pairs, samples, d)

        saved = first_kernel(turned(tokens), sample_counts, feature_counts, (norms, mlp_out_bias[None], mlp_in_bias[None]), sample_qkv, sample_out,
                             feature_qkv, feature_out, mlp_in, mlp_out, tasks, fs_n)
        g1, lo, dr, out2, out1, outs, outn = second_kernel(turned(cotangent).reshape(total, d), sample_counts, saved, tasks, rl, fl, fs_n)
        tg, low, gn, gs, gso, gf, gfo, gmi, gib, gmo, gob = last_kernel(g1, dr, lo, out2, out1, outs, outn, tasks, rl, fl, fs_n)

        def rows_back(v):
            return v.reshape(tasks, samples, d // 128, feats, 128).transpose(0, 1, 3, 2, 4).reshape(tokens.shape)

        return rows_back(low), rows_back(tg), gn, gs, gso, gf, gfo, gmi, gib[0], gmo, gob[0]


    small = jnp.zeros((16, d), bf16)
    small = lax.dynamic_update_slice(small, norms, (0, me * rl))
    small = lax.dynamic_update_slice(small, mlp_out_bias[None, :], (6, me * rl))
    small = lax.dynamic_update_slice(small, mlp_in_bias[None, :], (7 + (me * fl) // d, lax.rem(me * fl, d)))
    split_in = mlp_in.reshape(rl, chunks, d).transpose(1, 0, 2).reshape(chunks * rl, d)
    pack_a = up16(jnp.concatenate([small, sample_qkv.reshape(3 * rl, d)], 0))
    pack_b = up16(jnp.concatenate([sample_out, feature_qkv.reshape(3 * rl, d), feature_out, split_in, mlp_out], 0))

    xp = tokens.transpose(0, 2, 1, 3).reshape(pairs, samples, d)
    cp = cotangent.transpose(0, 2, 1, 3).reshape(pairs, samples, d)
    my_task = me_f // rep // feats
    count = lax.dynamic_index_in_dim(sample_counts, my_task, keepdims=False)
    keybias = jnp.broadcast_to(jnp.where(jnp.arange(total) < count, 0.0, MASKED).astype(f32)[:, None], (total, 128))
    shown = jnp.arange(feats)[None, :] < feature_counts[:, None]
    fbias = jnp.broadcast_to(jnp.where(shown, 0.0, MASKED).astype(f32).reshape(pairs, 1), (pairs, 128))

    ga, gb = gather_call([pack_a, pack_b], dp_n, fs_n, 3)
    ga, gb = ga.reshape((nd,) + ga.shape[3:]), gb.reshape((nd,) + gb.shape[3:])

    def take(g, start, rows):
        return g[:, start:start + rows].reshape(nd * rows, d)

    smalls = jnp.sum(ga[:, :16].astype(f32), 0)
    w_s = jnp.stack([take(ga, 16 + i * rl, rl) for i in range(3)])
    first = lax.rem(me_f, rep) * dh
    w_mine = lax.dynamic_slice_in_dim(w_s, first, dh, 2)
    w_mid = jnp.concatenate([take(gb, i * rl, rl) for i in range(5 + chunks)] + [take(gb, (5 + chunks) * rl, fl)])[None]
    size = d
    back, xg, o, qkv, lse = forward_kernel(jnp.repeat(xp, rep, 0), [], [w_mine, smalls], keybias, dp_n, fs_n, rl, dh)

    lo, g1, do1, gm = middle_call(xp, back.reshape(pairs, rep * hp, samples, 128), cp, smalls, fbias, w_mid, tasks, chunks, size)
    do1 = do1.reshape(fs_n, hp, samples, 128)
    dxr, gs, gn_s = backward_kernel(do1, xg, qkv, o, lse, w_mine, smalls, keybias, None, None, dp_n, fs_n, rl, dh, tasks, False)
    dxr = jnp.sum(dxr.reshape(pairs, rep, samples, d).astype(f32), 1)
    tokens_grad = (g1.reshape(pairs, samples, d) + dxr).reshape(tasks, feats, samples, d).transpose(0, 2, 1, 3)
    gs = lax.dynamic_update_slice_in_dim(jnp.zeros((3, d, d), bf16), gs, first, 2)

    def give(g, parts):
        return g.reshape(parts, nd, -1, d).transpose(1, 0, 2, 3).reshape(nd, -1, d)

    gm = gm[0]
    mix = jnp.concatenate([gn_s[0:2].astype(bf16), gm[2:16]], 0)
    grads = up16(jnp.concatenate([jnp.broadcast_to(mix[None], (nd, 16, d)), give(gm[16:16 + (5 + chunks) * d], 5 + chunks),
                                  give(gm[16 + (5 + chunks) * d:], 1), give(gs, 3)], 1))
    s = scatter_call(grads.reshape((dp_n, fs_n // 2, 2) + grads.shape[1:]), dp_n, fs_n, 6)
    outs = [s[16 + (5 + chunks) * rl + fl:][:3 * rl]]
    gn = s[0:2]
    gn = jnp.concatenate([gn, s[2:16]], 0)
    layer_output = lo.reshape(tasks, feats, samples, d).transpose(0, 2, 1, 3)

    def piece(start, rows):
        return s[16 + start * rl:16 + start * rl + rows]

    return (
        layer_output,
        tokens_grad,
        lax.dynamic_slice(gn, (0, me * rl), (6, rl)),
        outs[0].reshape(3, rl, d), piece(0, rl), piece(1, 3 * rl).reshape(3, rl, d), piece(4, rl),
        piece(5, chunks * rl).reshape(chunks, rl, d).transpose(1, 0, 2).reshape(rl, chunks * d),
        lax.dynamic_slice(gn[7:7 + chunks].reshape(-1), (me * fl,), (fl,)),
        piece(5 + chunks, fl),
        lax.dynamic_slice(gn[6], (me * rl,), (rl,)),
    )


def solution(mesh):
    rows, whole = ("dp", "fsdp"), P("dp", "fsdp", None, None)
    weights = (P(None, rows), P(None, rows, None), P(rows, None), P(None, rows, None), P(rows, None), P(rows, None), P(rows),
               P(rows, None), P(rows))
    return jax.shard_map(local, mesh=mesh, in_specs=(whole, P("dp"), P("dp")) + weights + (whole,),
                         out_specs=(whole, whole) + weights, check_vma=False)
```

```python
import functools
import jax
import jax.numpy as jnp
from jax import lax
from jax.experimental import pallas as pl
from jax.experimental.pallas import tpu as pltpu
from jax.sharding import PartitionSpec as P

MESH = pl.DeviceIdType.MESH
f32, bf16 = jnp.float32, jnp.bfloat16


def mod(a, n):
    return lax.rem(a, n)


def greet(dp_n, fs_n, with_dp=True):
    me_d, me_f = lax.axis_index("dp"), lax.axis_index("fsdp")
    barrier = pltpu.get_barrier_semaphore()
    n = 0
    for k in range(1, fs_n):
        pl.semaphore_signal(barrier, inc=1, device_id=(me_d, mod(me_f + k, fs_n)), device_id_type=MESH)
        n += 1
    if with_dp:
        for k in range(1, dp_n):
            pl.semaphore_signal(barrier, inc=1, device_id=(mod(me_d + k, dp_n), me_f), device_id_type=MESH)
            n += 1
    pl.semaphore_wait(barrier, n)


def rcopy(src, dst, ss, rs, dev):
    return pltpu.make_async_remote_copy(src_ref=src, dst_ref=dst, send_sem=ss, recv_sem=rs, device_id=dev, device_id_type=MESH)


class Swap:
    def __init__(self, fs_n, src, dst, local_sem, ss, rs):
        me_d, me_f = lax.axis_index("dp"), lax.axis_index("fsdp")
        self.own = pltpu.make_async_copy(src.at[me_f], dst.at[me_f], local_sem)
        self.copies = []
        for k in range(1, fs_n):
            to = mod(me_f + k, fs_n)
            self.copies.append(rcopy(src.at[to], dst.at[me_f], ss.at[k - 1], rs.at[k - 1], (me_d, to)))

    def start(self):
        for c in self.copies:
            c.start()
        self.own.start()

    def wait(self):
        self.own.wait()
        for c in self.copies:
            c.wait()


class Gather:
    def __init__(self, dp_n, fs_n, src, dst, local_sem, zs, zr, ds, dr, cs, cr):
        me_d, me_f = lax.axis_index("dp"), lax.axis_index("fsdp")
        z_n = fs_n // 2
        me_z, me_c = me_f // 2, mod(me_f, 2)
        self.z_n, self.dp_n = z_n, dp_n
        partner = (me_d, me_z * 2 + 1 - me_c)
        self.own = pltpu.make_async_copy(src, dst.at[me_d, me_z, me_c], local_sem)
        self.z = []
        for k in range(1, z_n):
            to = mod(me_z + k, z_n) * 2 + me_c
            self.z.append(rcopy(src, dst.at[me_d, me_z, me_c], zs.at[k - 1], zr.at[k - 1], (me_d, to)))
        self.d = {}
        self.c = {}
        for k in range(z_n):
            z = mod(me_z - k + z_n, z_n)
            for j in range(dp_n):
                d = mod(me_d - j + dp_n, dp_n)
                here = src if (k == 0 and j == 0) else dst.at[d, z, me_c]
                self.c[k, j] = rcopy(here, dst.at[d, z, me_c], cs.at[k * dp_n + j], cr.at[k * dp_n + j], partner)
                if j > 0:
                    here = src if k == 0 else dst.at[me_d, z, me_c]
                    i = k * (dp_n - 1) + j - 1
                    self.d[k, j] = rcopy(here, dst.at[me_d, z, me_c], ds.at[i], dr.at[i], (mod(me_d + j, dp_n), me_f))

    def start(self):
        for c in self.z:
            c.start()
        self.own.start()
        for j in range(1, self.dp_n):
            self.d[0, j].start()
        self.c[0, 0].start()

    def forward_z(self):
        for k in range(1, self.z_n):
            self.z[k - 1].wait_recv()
            for j in range(1, self.dp_n):
                self.d[k, j].start()
            self.c[k, 0].start()

    def forward_d(self):
        for k in range(self.z_n):
            for j in range(1, self.dp_n):
                self.d[k, j].wait_recv()
                self.c[k, j].start()

    def wait(self):
        self.own.wait()
        for c in self.z:
            c.wait_send()
        for c in self.d.values():
            c.wait_send()
        for c in self.c.values():
            c.wait()


def gather_sems(dp_n, fs_n):
    z = fs_n // 2
    D = pltpu.SemaphoreType.DMA
    return [D, D((z - 1,)), D((z - 1,)), D((z * (dp_n - 1),)), D((z * (dp_n - 1),)), D((z * dp_n,)), D((z * dp_n,))]


def swap_sems(fs_n):
    D = pltpu.SemaphoreType.DMA
    return [D, D((fs_n - 1,)), D((fs_n - 1,))]


ANY = pl.BlockSpec(memory_space=pl.ANY)
VM = pl.BlockSpec(memory_space=pltpu.VMEM)


def swap_call(x, dp_n, fs_n, cid, space=ANY):
    def body(x_ref, o_ref, *sems):
        greet(dp_n, fs_n, False)
        s = Swap(fs_n, x_ref, o_ref, *sems)
        s.start()
        s.wait()

    return pl.pallas_call(
        body, out_shape=jax.ShapeDtypeStruct(x.shape, x.dtype), in_specs=[space], out_specs=space,
        scratch_shapes=swap_sems(fs_n),
        compiler_params=pltpu.CompilerParams(collective_id=cid, has_side_effects=True, vmem_limit_bytes=60 << 20),
        name="swap%d" % cid,
    )(x)


def gather_call(packs, dp_n, fs_n, cid, space=ANY):
    n = len(packs)

    def body(*refs):
        ins, outs, sems = refs[:n], refs[n:2 * n], refs[2 * n:]
        greet(dp_n, fs_n)
        gs = [Gather(dp_n, fs_n, ins[i], outs[i], *sems[7 * i:7 * i + 7]) for i in range(n)]
        for g in gs:
            g.start()
        for g in gs:
            g.forward_z()
        for g in gs:
            g.forward_d()
        for g in gs:
            g.wait()

    return pl.pallas_call(
        body,
        out_shape=[jax.ShapeDtypeStruct((dp_n, fs_n // 2, 2) + p.shape, p.dtype) for p in packs],
        in_specs=[space] * n, out_specs=[space] * n,
        scratch_shapes=gather_sems(dp_n, fs_n) * n,
        compiler_params=pltpu.CompilerParams(collective_id=cid, has_side_effects=True, vmem_limit_bytes=60 << 20),
        name="gather%d" % cid,
    )(*packs)


def scatter_call(g, dp_n, fs_n, cid):
    z_n = fs_n // 2
    rows, width = g.shape[3:]
    step = 16

    def body(g_ref, o_ref, from_c, half, from_d, quarter, from_z, cs, cr, ds, dr, zs, zr):
        me_d, me_f = lax.axis_index("dp"), lax.axis_index("fsdp")
        me_z, me_c = me_f // 2, mod(me_f, 2)
        greet(dp_n, fs_n)
        partner = (me_d, me_z * 2 + 1 - me_c)

        def add(out, parts):
            def one(i, _):
                at = pl.ds(pl.multiple_of(i * step, step), step)
                total = parts[0][at, :].astype(f32)
                for p in parts[1:]:
                    total = total + p[at, :].astype(f32)
                out[at, :] = total.astype(out.dtype)
                return 0
            lax.fori_loop(0, rows // step, one, 0, unroll=True if rows // step <= 4 else 4)

        order = [(j, k) for j in list(range(1, dp_n)) + [0] for k in list(range(1, z_n)) + [0]]
        cc, dd, zz = {}, {}, {}
        for i, (j, k) in enumerate(order):
            d, z = mod(me_d + j, dp_n), mod(me_z + k, z_n)
            cc[j, k] = rcopy(g_ref.at[d, z, 1 - me_c], from_c.at[i], cs.at[i], cr.at[i], partner)
            cc[j, k].start()
        for i, (j, k) in enumerate(order):
            d, z = mod(me_d + j, dp_n), mod(me_z + k, z_n)
            cc[j, k].wait_recv()
            add(half.at[j, k], [g_ref.at[d, z, me_c], from_c.at[i]])
            if j:
                n = (j - 1) * z_n + k
                dd[j, k] = rcopy(half.at[j, k], from_d.at[j - 1, k], ds.at[n], dr.at[n], (d, me_f))
                dd[j, k].start()
        for k in list(range(1, z_n)) + [0]:
            for j in range(1, dp_n):
                dd[j, k].wait_recv()
            if k:
                add(quarter.at[k], [half.at[0, k]] + [from_d.at[j - 1, k] for j in range(1, dp_n)])
                to = mod(me_z + k, z_n) * 2 + me_c
                zz[k] = rcopy(quarter.at[k], from_z.at[k - 1], zs.at[k - 1], zr.at[k - 1], (me_d, to))
                zz[k].start()
        for k in range(1, z_n):
            zz[k].wait_recv()
        add(o_ref, [half.at[0, 0]] + [from_d.at[j - 1, 0] for j in range(1, dp_n)] + [from_z.at[k - 1] for k in range(1, z_n)])
        for c in list(cc.values()) + list(dd.values()) + list(zz.values()):
            c.wait_send()

    D = pltpu.SemaphoreType.DMA
    n = dp_n * z_n
    return pl.pallas_call(
        body, out_shape=jax.ShapeDtypeStruct((rows, width), f32), in_specs=[VM], out_specs=VM,
        scratch_shapes=[
            pltpu.VMEM((n, rows, width), bf16), pltpu.VMEM((dp_n, z_n, rows, width), bf16),
            pltpu.VMEM((dp_n - 1, z_n, rows, width), bf16), pltpu.VMEM((z_n, rows, width), bf16),
            pltpu.VMEM((z_n - 1, rows, width), bf16),
            D((n,)), D((n,)), D((n - z_n,)), D((n - z_n,)), D((z_n - 1,)), D((z_n - 1,)),
        ],
        compiler_params=pltpu.CompilerParams(collective_id=cid, has_side_effects=True, vmem_limit_bytes=60 << 20),
        name="scatter%d" % cid,
    )(g)
class PlaneGather:
    def __init__(self, fs_n, src, dst, local_sem, zs, zr, ds, dr, cs, cr):
        me_d, me_f = lax.axis_index("dp"), lax.axis_index("fsdp")
        z_n = fs_n // 2
        me_z, me_c = me_f // 2, mod(me_f, 2)
        self.z_n = z_n
        partner = (me_d, me_z * 2 + 1 - me_c)
        ds_ = [me_d, me_d // 2 * 2 + 1 - mod(me_d, 2), mod(me_d + 2, 4), 3 - me_d]
        zs_ = [mod(me_z - k + z_n, z_n) for k in range(z_n)]
        self.own = pltpu.make_async_copy(src, dst.at[me_d, me_z, me_c], local_sem)
        self.z, self.n, self.fwd, self.c = {}, {}, {}, {}
        for k in range(z_n):
            at = lambda j: dst.at[ds_[j], zs_[k], me_c]
            mine = src if k == 0 else at(0)
            if k:
                to = mod(me_z + k, z_n) * 2 + me_c
                self.z[k] = rcopy(src, dst.at[me_d, me_z, me_c], zs.at[k - 1], zr.at[k - 1], (me_d, to))
            for j in (1, 2):
                self.n[k, j] = rcopy(mine, at(0), ds.at[3 * k + j - 1], dr.at[3 * k + j - 1], (ds_[j], me_f))
            first = 1 + k % 2
            self.fwd[k] = rcopy(at(first), at(first), ds.at[3 * k + 2], dr.at[3 * k + 2], (ds_[3 - first], me_f))
            for j in range(4):
                self.c[k, j] = rcopy(mine if j == 0 else at(j), at(j), cs.at[4 * k + j], cr.at[4 * k + j], partner)

    def start(self):
        for c in self.z.values():
            c.start()

    def begin(self):
        self.own.start()
        self.spread(0)

    def spread(self, k):
        if k:
            self.z[k].wait_recv()
        self.n[k, 1].start()
        self.n[k, 2].start()
        self.c[k, 0].start()

    def hand_on(self, k):
        first = 1 + k % 2
        for j in (first, 3 - first):
            self.n[k, j].wait_recv()
            if j == first:
                self.fwd[k].start()
            self.c[k, j].start()

    def corner(self, k):
        self.fwd[k].wait_recv()
        self.c[k, 3].start()

    def wait(self):
        self.own.wait()
        for c in list(self.z.values()) + list(self.n.values()) + list(self.fwd.values()):
            c.wait_send()
        for c in self.c.values():
            c.wait()


def plane_gather_sems(fs_n):
    z, D = fs_n // 2, pltpu.SemaphoreType.DMA
    return [D, D((z - 1,)), D((z - 1,)), D((3 * z,)), D((3 * z,)), D((4 * z,)), D((4 * z,))]


class PlaneReduce:
    def __init__(self, fs_n, g, bufs, sems):
        me_d, me_f = lax.axis_index("dp"), lax.axis_index("fsdp")
        z_n = fs_n // 2
        me_z, me_c = me_f // 2, mod(me_f, 2)
        self.z_n, self.rows = z_n, g.shape[3]
        self.from_c, self.from_n, self.from_z = bufs
        cs, cr, ds, dr, zs, zr = sems
        partner = (me_d, me_z * 2 + 1 - me_c)
        ds_ = [me_d, me_d // 2 * 2 + 1 - mod(me_d, 2), mod(me_d + 2, 4), 3 - me_d]
        self.mine, self.c, self.n, self.z = {}, {}, {}, {}
        for k in range(z_n):
            z = mod(me_z + k, z_n)
            for j in range(4):
                i = 4 * k + j
                self.mine[k, j] = g.at[ds_[j], z, me_c]
                self.c[k, j] = rcopy(g.at[ds_[j], z, 1 - me_c], self.from_c.at[k, j], cs.at[i], cr.at[i], partner)
            first = 1 + k % 2
            send = [(first, first), (3, first), (3 - first, 3 - first)]
            for i, (j, to) in enumerate(send):
                self.n[k, i] = rcopy(self.mine[k, j], self.from_n.at[k, i], ds.at[3 * k + i], dr.at[3 * k + i], (ds_[to], me_f))
            if k:
                to = mod(me_z + k, z_n) * 2 + me_c
                self.z[k] = rcopy(self.mine[k, 0], self.from_z.at[k - 1], zs.at[k - 1], zr.at[k - 1], (me_d, to))

    def add(self, out, parts):
        step = 16

        def one(i, _):
            at = pl.ds(pl.multiple_of(i * step, step), step)
            if len(parts) == 2 and out.dtype == bf16:
                out[at, :] = parts[0][at, :] + parts[1][at, :]
                return 0
            total = parts[0][at, :].astype(f32)
            for p in parts[1:]:
                total = total + p[at, :].astype(f32)
            out[at, :] = total.astype(out.dtype)
            return 0

        n = self.rows // step
        lax.fori_loop(0, n, one, 0, unroll=2 if n % 2 == 0 else 1)

    def order(self):
        return list(range(1, self.z_n)) + [0]

    def start(self):
        for k in self.order():
            for j in (1 + k % 2, 3, 2 - k % 2, 0):
                self.c[k, j].start()

    def first(self, k):
        first = 1 + k % 2
        for j in (first, 3, 3 - first, 0):
            self.c[k, j].wait_recv()
            self.add(self.mine[k, j], [self.mine[k, j], self.from_c.at[k, j]])
            if j == first:
                self.n[k, 0].start()
            if j == 3:
                self.n[k, 1].start()

    def second(self, k):
        first = 1 + k % 2
        self.n[k, 1].wait_recv()
        j = 3 - first
        self.add(self.mine[k, j], [self.mine[k, j], self.from_n.at[k, 1]])
        self.n[k, 2].start()

    def third(self, k):
        self.n[k, 0].wait_recv()
        self.n[k, 2].wait_recv()
        if k:
            self.add(self.mine[k, 0], [self.mine[k, 0], self.from_n.at[k, 0], self.from_n.at[k, 2]])
            self.z[k].start()

    def every(self, step):
        for k in self.order():
            step(k)

    def finish(self, out):
        for k in range(1, self.z_n):
            self.z[k].wait_recv()
        self.add(out, [self.mine[0, 0], self.from_n.at[0, 0], self.from_n.at[0, 2]] + [self.from_z.at[k - 1] for k in range(1, self.z_n)])
        for c in list(self.c.values()) + list(self.n.values()) + list(self.z.values()):
            c.wait_send()


def plane_reduce_scratch(fs_n, rows, width):
    z_n, V = fs_n // 2, pltpu.VMEM
    return [V((z_n, 4, rows, width), bf16), V((z_n, 3, rows, width), bf16), V((z_n - 1, rows, width), bf16)]


def plane_reduce_sems(fs_n):
    z_n, D = fs_n // 2, pltpu.SemaphoreType.DMA
    return [D((4 * z_n,)), D((4 * z_n,)), D((3 * z_n,)), D((3 * z_n,)), D((z_n - 1,)), D((z_n - 1,))]


HEADS = 8
EPS = 1e-05
MASKED = -1e30
NN = (((1,), (0,)), ((), ()))
NT = (((1,), (1,)), ((), ()))
TN = (((0,), (0,)), ((), ()))


def dot(a, b, dims=NN):
    return lax.dot_general(a, b, dims, preferred_element_type=f32)


def unit(x):
    c = x - jnp.mean(x, -1, keepdims=True)
    r = lax.rsqrt(jnp.mean(c * c, -1, keepdims=True) + EPS)
    return c * r, r


def unit_back(y, u, r, gain):
    yg = y * gain
    return r * (yg - jnp.mean(yg, -1, keepdims=True) - u * jnp.mean(yg * u, -1, keepdims=True))


def blocks(total, size, body):
    lax.fori_loop(0, total // size, lambda i, c: (body(pl.ds(pl.multiple_of(i * size, size), size)), c)[1], 0)


def gelu_parts(v):
    z = jnp.abs(v) * 0.7071067811865476
    t = 1.0 / (1.0 + 0.3275911 * z)
    e = jnp.exp(-0.5 * (v * v))
    tail = t * (0.127414796 + t * (-0.142248368 + t * (0.7107068705 + t * (-0.7265760135 + t * 0.5307027145)))) * e
    return jnp.where(v >= 0, 1.0 - tail, tail), v * e * 0.3989422804014327


def head_mask(rows, second, width=128):
    lane = lax.broadcasted_iota(jnp.int32, (rows, width), 1)
    return (lane >= width // 2) if second else (lane < width // 2)


def params(cid=None):
    if cid is None:
        return pltpu.CompilerParams(vmem_limit_bytes=62 << 20)
    return pltpu.CompilerParams(collective_id=cid, has_side_effects=True, vmem_limit_bytes=62 << 20)


def head_pair(p):
    return slice(p * 128, p * 128 + 128)


def middle_call(x, o1, cot, smalls, fbias, w, tasks, chunks, unit_rows):
    pairs, samples, d = x.shape
    feats = pairs // tasks
    rows = pairs * samples
    hh = d // 64
    nd = w.shape[0]
    U = unit_rows
    OUT = (5 + chunks) * U
    fl = chunks * d // nd
    x, cot = x.reshape(rows, d), cot.reshape(rows, d)
    RB = 256
    per = RB // samples

    def body(x_ref, back_ref, cot_ref, n_ref, fb_ref, w_ref,
             lo_ref, g1_ref, do1_ref, g_ref,
             x1, a, qkv, p2, o2, acc, dacc, act, gh, dqkv, do2, o1_ref, gn_ref):
        gn_ref[...] = jnp.zeros_like(gn_ref)

        def at_unit(k):
            return pl.ds(pl.multiple_of(k * U, 16), U) if not isinstance(k, int) else slice(k * U, k * U + U)

        def mat(k):
            return w_ref[:, at_unit(k), :].reshape(d, d)

        def out_mat(c):
            if nd == 1:
                return w_ref[0, pl.ds(pl.multiple_of(OUT + c * d, 16), d), :]
            m = nd // chunks
            return w_ref[pl.ds(c * m, m), OUT:OUT + fl, :].reshape(d, d)

        def put(k, at, i, value):
            if nd == 1:
                g_ref[0, pl.ds(pl.multiple_of(16 + k * U + i * 256, 16), 256), :] = value
            else:
                m = 256 // U
                g_ref[pl.ds(i * m, m), pl.ds(pl.multiple_of(16 + k * U, 16), U), :] = value.reshape(m, U, d)

        def put_out(c, i, value):
            if nd == 1:
                g_ref[0, pl.ds(pl.multiple_of(16 + OUT + c * d + i * 256, 16), 256), :] = value
            else:
                m = 256 // fl
                g_ref[pl.ds(c * (nd // chunks) + i * m, m), 16 + OUT:16 + OUT + fl, :] = value.reshape(m, fl, d)

        def tiles(body):
            for i in range(d // 256):
                body(slice(i * 256, i * 256 + 256), i)

        def norm(i):
            return n_ref[2 * i:2 * i + 1, :], n_ref[2 * i + 1:2 * i + 2, :]

        def collect(i, _):
            at = pl.ds(pl.multiple_of(i * RB, RB), RB)
            for p in range(hh // 2):
                o1_ref[at, p * 128:p * 128 + 128] = back_ref[pl.ds(i * per, per), p].reshape(RB, 128)
            return 0

        lax.fori_loop(0, rows // RB, collect, 0)

        def first(at):
            y = x_ref[at, :].astype(f32) + dot(o1_ref[at, :], mat(0))
            x1[at, :] = y
            u, _ = unit(y)
            g, b = norm(1)
            v = (u * g + b).astype(bf16)
            a[at, :] = v
            for i in range(3):
                z = dot(v, mat(1 + i)).astype(bf16)
                qkv[i, at, :] = z * 0.125 if i == 0 else z

        blocks(rows, RB, first)

        half = lax.broadcasted_iota(jnp.int32, (256, 128), 0) // 64
        ones = (lax.rem(half, 2) == lax.broadcasted_iota(jnp.int32, (256, 128), 1) // 64).astype(bf16)

        def head_sums(prods):
            both = []
            for v in prods:
                hi = v.astype(bf16)
                both.append(jnp.concatenate([hi, (v - hi.astype(f32)).astype(bf16)], 1))
            out = dot(jnp.concatenate(both, 0), ones)
            return [out[i * samples:(i + 1) * samples] for i in range(len(prods))]

        def at_slot(t, f):
            return pl.ds(pl.multiple_of((t * feats + f) * samples, samples), samples)

        def mix(t, _):
            for p in range(hh // 2):
                lanes = head_pair(p)
                ks = [qkv[1, at_slot(t, g), lanes].astype(f32) for g in range(feats)]
                vs = [qkv[2, at_slot(t, g), lanes].astype(f32) for g in range(feats)]
                for f in range(feats):
                    q = qkv[0, at_slot(t, f), lanes].astype(f32)
                    sc = head_sums([q * k for k in ks])
                    sc = [v + fb_ref[pl.ds(t * feats + g, 1), :] for g, v in enumerate(sc)]
                    top = functools.reduce(jnp.maximum, sc)
                    sc = [jnp.exp(v - top) for v in sc]
                    inv = 1.0 / sum(sc)
                    sc = [v * inv for v in sc]
                    for g in range(feats):
                        p2[t, p, f, g] = sc[g]
                    o2[at_slot(t, f), lanes] = sum(w * v for w, v in zip(sc, vs)).astype(bf16)
            return 0

        lax.fori_loop(0, tasks, mix, 0)

        def second(at):
            y = x1[at, :] + dot(o2[at, :], mat(4))
            acc[at, :] = y
            u, _ = unit(y)
            g, b = norm(2)
            do2[at, :] = (u * g + b).astype(bf16)
            dacc[at, :] = jnp.zeros((RB, d), f32)

        blocks(rows, RB, second)

        def chunk(c, _):
            def part(at):
                hid = dot(do2[at, :], mat(5 + c)) + n_ref[pl.ds(7 + c, 1), :]
                cdf, pdf = gelu_parts(hid)
                al = (hid * cdf).astype(bf16)
                act[at, :] = al
                gl = ((cdf + pdf) * dot(cot_ref[at, :], out_mat(c), NT)).astype(bf16)
                gh[at, :] = gl
                gn_ref[pl.ds(7 + c, 1), :] += jnp.sum(gl.astype(f32), 0, keepdims=True)
                acc[at, :] += dot(al, out_mat(c))
                dacc[at, :] += dot(gl, mat(5 + c), NT)

            blocks(rows, RB, part)

            def weight(at, i):
                put_out(c, i, dot(act[:, at], cot_ref[...], TN).astype(bf16))
                put(5 + c, at, i, dot(do2[:, at], gh[...], TN).astype(bf16))

            tiles(weight)
            return 0

        lax.fori_loop(0, chunks, chunk, 0)

        def third(at):
            lo_ref[at, :] = (acc[at, :] + n_ref[6:7, :]).astype(bf16)
            u, r = unit(x1[at, :] + dot(o2[at, :], mat(4)))
            y = dacc[at, :]
            gn_ref[4:5, :] += jnp.sum(y * u, 0, keepdims=True)
            gn_ref[5:6, :] += jnp.sum(y, 0, keepdims=True)
            cf = cot_ref[at, :].astype(f32)
            gn_ref[6:7, :] += jnp.sum(cf, 0, keepdims=True)
            g2 = cf + unit_back(y, u, r, norm(2)[0])
            dacc[at, :] = g2
            e2 = g2.astype(bf16)
            act[at, :] = e2
            do2[at, :] = dot(e2, mat(4), NT).astype(bf16)

        blocks(rows, RB, third)

        def weight2(at, i):
            put(4, at, i, dot(o2[:, at], act[...], TN).astype(bf16))

        tiles(weight2)

        def unmix(t, _):
            for p in range(hh // 2):
                lanes = head_pair(p)
                ks = [qkv[1, at_slot(t, g), lanes].astype(f32) for g in range(feats)]
                vs = [qkv[2, at_slot(t, g), lanes].astype(f32) for g in range(feats)]
                dk, dv = [0.0] * feats, [0.0] * feats
                for f in range(feats):
                    q = qkv[0, at_slot(t, f), lanes].astype(f32)
                    gr = do2[at_slot(t, f), lanes].astype(f32)
                    dp = head_sums([gr * v for v in vs])
                    ws = [p2[t, p, f, g] for g in range(feats)]
                    mean = sum(w * v for w, v in zip(ws, dp))
                    ds = [(w * (v - mean)).astype(bf16).astype(f32) for w, v in zip(ws, dp)]
                    dqkv[0, at_slot(t, f), lanes] = (sum(v * k for v, k in zip(ds, ks)) * 0.125).astype(bf16)
                    for g in range(feats):
                        dk[g] += ds[g] * q
                        dv[g] += ws[g] * gr
                for g in range(feats):
                    dqkv[1, at_slot(t, g), lanes] = dk[g].astype(bf16)
                    dqkv[2, at_slot(t, g), lanes] = dv[g].astype(bf16)
            return 0

        lax.fori_loop(0, tasks, unmix, 0)

        def fourth(i, _):
            at = pl.ds(pl.multiple_of(i * RB, RB), RB)
            u, r = unit(x1[at, :])
            y = dot(dqkv[0, at, :], mat(1), NT) + dot(dqkv[1, at, :], mat(2), NT) + dot(dqkv[2, at, :], mat(3), NT)
            gn_ref[2:3, :] += jnp.sum(y * u, 0, keepdims=True)
            gn_ref[3:4, :] += jnp.sum(y, 0, keepdims=True)
            g1 = dacc[at, :] + unit_back(y, u, r, norm(1)[0])
            g1_ref[at, :] = g1
            e1 = g1.astype(bf16)
            act[at, :] = e1
            do = dot(e1, mat(0), NT).astype(bf16)
            for p in range(hh // 2):
                do1_ref[pl.ds(i * per, per), p] = do[:, p * 128:p * 128 + 128].reshape(per, samples, 128)
            return 0

        lax.fori_loop(0, rows // RB, fourth, 0)

        def weight3(at, i):
            put(0, at, i, dot(o1_ref[:, at], act[...], TN).astype(bf16))
            for j in range(3):
                put(1 + j, at, i, dot(a[:, at], dqkv[j], TN).astype(bf16))

        tiles(weight3)
        g_ref[:, 0:16, :] = jnp.broadcast_to(gn_ref[...].astype(bf16), (nd, 16, d))

    V = pltpu.VMEM
    S = jax.ShapeDtypeStruct
    return pl.pallas_call(
        body,
        out_shape=[S((rows, d), bf16), S((rows, d), f32), S((pairs, hh // 2, samples, 128), bf16),
                   S((nd, 16 + OUT + fl, d), bf16)],
        in_specs=[VM] * 6, out_specs=[VM] * 4,
        scratch_shapes=[V((rows, d), f32), V((rows, d), bf16), V((3, rows, d), bf16), V((tasks, hh // 2, feats, feats, samples, 128), f32), V((rows, d), bf16),
                        V((rows, d), f32), V((rows, d), f32), V((rows, d), bf16), V((rows, d), bf16), V((3, rows, d), bf16),
                        V((rows, d), bf16), V((rows, d), bf16), V((16, d), f32)],
        compiler_params=params(), name="middle",
    )(x, o1, cot, smalls, fbias, w)
BQ = 1024


class Turns:
    def __init__(self, fs_n, parts, src, dst, local_sem, ss, rs):
        me_d, me_f = lax.axis_index("dp"), lax.axis_index("fsdp")
        self.sets = []
        for p in range(parts):
            own = pltpu.make_async_copy(src(p, me_f), dst(p, me_f), local_sem.at[p])
            far = []
            for k in range(1, fs_n):
                to = mod(me_f + k, fs_n)
                i = p * (fs_n - 1) + k - 1
                far.append(rcopy(src(p, to), dst(p, me_f), ss.at[i], rs.at[i], (me_d, to)))
            self.sets.append((own, far))

    def start(self, p):
        own, far = self.sets[p]
        for c in far:
            c.start()
        own.start()

    def wait_recv(self, p):
        own, far = self.sets[p]
        own.wait()
        for c in far:
            c.wait_recv()

    def wait_send(self):
        for _, far in self.sets:
            for c in far:
                c.wait_send()


def turn_sems(fs_n, parts):
    D = pltpu.SemaphoreType.DMA
    return [D((parts,)), D((parts * (fs_n - 1),)), D((parts * (fs_n - 1),))]


def units(ref, start, size):
    v = ref[..., start:start + size, :]
    return v.reshape(-1, v.shape[-1])


def forward_kernel(x, packs, plain, keybias, dp_n, fs_n, rl, dh):
    slots, samples, d = x.shape
    rows = slots * samples
    heads = dh // 64
    hp = heads // 2
    np_ = len(packs)

    def body(*refs):
        it = iter(refs)
        x_ref, kb_ref = next(it), next(it)
        pack_refs = [next(it) for _ in range(np_)]
        w_ref, sm_ref = (None, None) if np_ else (next(it), next(it))
        back_ref, xg_ref, o_ref, qkv_ref, l_ref = (next(it) for _ in range(5))
        g_refs = [next(it) for _ in range(np_)]
        if np_:
            sm_ref = next(it)
        acted, vt, ot = next(it), next(it), next(it)
        swap_s = [next(it) for _ in range(3)]
        turn_s = [next(it) for _ in range(3)]
        gat_s = [[next(it) for _ in range(7)] for _ in range(np_)]

        greet(dp_n, fs_n, np_ > 0)
        gathers = [PlaneGather(fs_n, pack_refs[i], g_refs[i], *gat_s[i]) for i in range(np_)]
        swap = Swap(fs_n, x_ref, xg_ref, *swap_s)
        z_n = fs_n // 2
        if np_:
            gathers[0].start()
        swap.start()
        if np_:
            gathers[1].start()
            for k in range(1, z_n):
                gathers[0].spread(k)
            for k in range(z_n):
                gathers[0].hand_on(k)
            for k in range(1, z_n):
                gathers[1].spread(k)
            for k in range(z_n):
                gathers[0].corner(k)
        swap.wait()
        if np_:
            gathers[0].wait()
            sm_ref[...] = jnp.sum(units3(g_refs[0], 0, 16).astype(f32), 0)
        gain, bias = sm_ref[0:1, :], sm_ref[1:2, :]
        per = 256 // samples if samples < 256 else 1
        for s in range(slots // per):
            at = slice(s * per * samples, (s + 1) * per * samples)
            u, _ = unit(xg_ref[s * per:(s + 1) * per].reshape(per * samples, d).astype(f32))
            acted[at, :] = (u * gain + bias).astype(bf16)
        for i in range(3):
            w = units(g_refs[0], 16 + i * rl, rl) if np_ else w_ref[i]

            def project(at):
                y = dot(acted[at, :], w).astype(bf16)
                qkv_ref[i, at, :] = y * 0.125 if i == 0 else y

            blocks(rows, 256, project)

        turns = Turns(fs_n, hp, lambda p, j: o_ref.at[p, pl.ds(pl.multiple_of(j * samples, samples), samples)],
                      lambda p, j: back_ref.at[j, p], *turn_s)
        for p in range(hp):
            at = head_pair(p)
            vt[...] = qkv_ref[2, :, at].astype(f32).T.astype(bf16)
            for h in range(2):
                def part(i, _):
                    qa = pl.ds(pl.multiple_of(i * BQ, BQ), BQ)
                    q = qkv_ref[0, qa, at]
                    q = jnp.where(head_mask(BQ, h), q, jnp.zeros_like(q))
                    s = dot(qkv_ref[1, :, at], q, NT) + kb_ref[:, 0:1]
                    m = jnp.max(s, 0, keepdims=True)
                    e = jnp.exp(s - m)
                    tot = jnp.sum(e, 0, keepdims=True)
                    o = dot(vt[h * 64:h * 64 + 64, :], e.astype(bf16))
                    ot[h * 64:h * 64 + 64, qa] = o * (1.0 / tot)
                    l_ref[p * 2 + h:p * 2 + h + 1, qa] = m + jnp.log(tot)
                    return 0
                lax.fori_loop(0, rows // BQ, part, 0)
            o_ref[p, :, :] = ot[...].T.astype(bf16)
            turns.start(p)
            if np_ and p == 0:
                gathers[1].hand_on(0)
            if np_ and p == 2:
                gathers[1].hand_on(1)
        if np_:
            for k in range(2, z_n):
                gathers[1].hand_on(k)
            for k in range(z_n):
                gathers[1].corner(k)
        for p in range(hp):
            turns.wait_recv(p)
        turns.wait_send()
        if np_:
            gathers[1].wait()

    def units3(ref, start, size):
        v = ref[..., start:start + size, :]
        return v.reshape(-1, size, v.shape[-1])

    S, V = jax.ShapeDtypeStruct, pltpu.VMEM
    outs = [S((slots, hp, samples, 128), bf16), S((slots, samples, d), bf16), S((hp, rows, 128), bf16), S((3, rows, dh), bf16),
            S((heads, rows), f32)]
    outs += [S((dp_n, fs_n // 2, 2) + p.shape, bf16) for p in packs]
    args = [x, keybias] + list(packs)
    if np_:
        outs.append(S((16, d), f32))
    else:
        args += list(plain)
    return pl.pallas_call(
        body, out_shape=outs, in_specs=[VM] * len(args), out_specs=[ANY if np_ and i == 6 else VM for i in range(len(outs))],
        scratch_shapes=[V((rows, d), bf16), V((128, rows), bf16), V((128, rows), f32)] + swap_sems(fs_n) + turn_sems(fs_n, hp)
        + plane_gather_sems(fs_n) * np_,
        compiler_params=params(1), name="forward",
    )(*args)


def backward_kernel(do1, xg, qkv, o, lse, w, smalls, keybias, g1, gm, dp_n, fs_n, rl, dh, tasks, packed):
    slots, samples, d = xg.shape
    rows = slots * samples
    heads = dh // 64
    hp = heads // 2

    def body(*refs):
        it = iter(refs)
        do_in, xg_ref, qkv_ref, o_ref, l_ref, w_ref, n_ref, kb_ref = (next(it) for _ in range(8))
        g1_ref, gm_ref = (next(it), next(it)) if packed else (None, None)
        if packed:
            tg_ref, sm_ref, ss_ref = (next(it) for _ in range(3))
        else:
            dr_ref, gw_ref, gn_ref = (next(it) for _ in range(3))
        do, delta, kt, dqt, dk, dv, dqkv, acted, gn, dx = (next(it) for _ in range(10))
        turn_s = [next(it) for _ in range(3)]
        back_s = [next(it) for _ in range(3)]
        if packed:
            gs, dr_ref = next(it), next(it)
            rm = [next(it) for _ in range(11)]
            rs = [next(it) for _ in range(11)]

        greet(dp_n, fs_n, packed)
        turns = Turns(fs_n, hp, lambda p, j: do_in.at[j, p], lambda p, j: do.at[j, p], *turn_s)
        for p in range(hp):
            turns.start(p)
        if packed:
            red = PlaneReduce(fs_n, gm_ref, rm[:4], rm[4:])
            red_s = PlaneReduce(fs_n, gs, rs[:4], rs[4:])
            red.start()
            for k in red.order():
                red.first(k)
        gain, bias = n_ref[0:1, :], n_ref[1:2, :]
        lane = lax.broadcasted_iota(jnp.int32, (8, 128), 1) // 64
        pick = (lane == lax.broadcasted_iota(jnp.int32, (8, 128), 0)).astype(f32)
        per = BQ // samples if samples < BQ else 1

        def grad_rows(i, p):
            return do[pl.ds(i * per, per), p].reshape(per * samples, 128)

        n = per * samples
        for p in range(hp):
            at = head_pair(p)
            kt[...] = qkv_ref[1, :, at].astype(f32).T.astype(bf16)
            dk[...] = jnp.zeros_like(dk)
            dv[...] = jnp.zeros_like(dv)
            turns.wait_recv(p)

            def deltas(i, _):
                qa = pl.ds(pl.multiple_of(i * n, n), n)
                prod = grad_rows(i, p).astype(f32) * o_ref[p, qa, :].astype(f32)
                delta[:, qa] = lax.dot_general(pick, prod, NT, precision=lax.Precision.HIGHEST, preferred_element_type=f32)
                return 0

            lax.fori_loop(0, rows // n, deltas, 0)
            for h in range(2):
                def part(i, _):
                    qa = pl.ds(pl.multiple_of(i * n, n), n)
                    mask = head_mask(n, h)
                    q = qkv_ref[0, qa, at]
                    q = jnp.where(mask, q, jnp.zeros_like(q))
                    g = grad_rows(i, p)
                    g = jnp.where(mask, g, jnp.zeros_like(g))
                    s = dot(qkv_ref[1, :, at], q, NT) + kb_ref[:, 0:1]
                    e = jnp.exp(s - l_ref[p * 2 + h:p * 2 + h + 1, qa])
                    ds = (e * (dot(qkv_ref[2, :, at], g, NT) - delta[h:h + 1, qa])).astype(bf16)
                    dv[...] += dot(e.astype(bf16), g)
                    dk[...] += dot(ds, q)
                    dqt[h * 64:h * 64 + 64, qa] = dot(kt[h * 64:h * 64 + 64, :], ds) * 0.125
                    return 0
                lax.fori_loop(0, rows // n, part, 0)
            dqkv[0, :, at] = dqt[...].T.astype(bf16)
            dqkv[1, :, at] = dk[...].astype(bf16)
            dqkv[2, :, at] = dv[...].astype(bf16)
            if packed:
                if p == hp - 2:
                    for k in red.order():
                        red.second(k)
                if p == hp - 1:
                    for k in red.order():
                        red.third(k)

        def mats(i):
            return units(w_ref, 16 + i * rl, rl) if packed else w_ref[i]

        per2 = 256 // samples if samples < 256 else 1
        n2 = per2 * samples
        gn[...] = jnp.zeros_like(gn)

        def act_rows(i):
            at = pl.ds(pl.multiple_of(i * n2, n2), n2)
            u, r = unit(xg_ref[pl.ds(i * per2, per2)].reshape(n2, d).astype(f32))
            return at, u, r

        def first(i, _):
            at, u, r = act_rows(i)
            acted[at, :] = (u * gain + bias).astype(bf16)
            return 0

        lax.fori_loop(0, rows // n2, first, 0)
        for i in range(3):
            if packed:
                y = dot(acted[...], dqkv[i], TN).astype(bf16)
                gs[:, :, :, 16 + i * rl:16 + (i + 1) * rl, :] = y.reshape(gs.shape[:3] + (rl, d))
            else:
                gw_ref[i] = dot(acted[...], dqkv[i], TN).astype(bf16)

        back = Turns(fs_n, 1, lambda p, j: dx.at[j], lambda p, j: dr_ref.at[j], *back_s)

        def sums(i, _):
            at, u, r = act_rows(i)
            y = dot(dqkv[0, at, :], mats(0), NT) + dot(dqkv[1, at, :], mats(1), NT) + dot(dqkv[2, at, :], mats(2), NT)
            gn[0:1, :] += jnp.sum(y * u, 0, keepdims=True)
            gn[1:2, :] += jnp.sum(y, 0, keepdims=True)
            dx[pl.ds(i * per2, per2)] = unit_back(y, u, r, gain).astype(bf16).reshape(per2, samples, d)
            return 0

        lax.fori_loop(0, rows // n2, sums, 0)
        back.start(0)
        if packed:
            small = jnp.concatenate([gn[...].astype(bf16), jnp.zeros_like(gn).astype(bf16)], 0)
            gs[:, :, :, 0:16, :] = jnp.broadcast_to(small, gs.shape[:3] + (16, d))
            red_s.start()
            for k in red_s.order():
                red_s.first(k)
            red.finish(sm_ref)
            for k in red_s.order():
                red_s.second(k)
            for k in red_s.order():
                red_s.third(k)
            back.wait_recv(0)
            feats = slots // tasks
            for s in range(slots):
                t, f = s // feats, s % feats
                for i in range(d // 128):
                    at = pl.ds(((t * samples * (d // 128)) + i) * feats + f, samples, stride=feats * (d // 128))
                    tg_ref[at, :] = g1_ref[s * samples:(s + 1) * samples, head_pair(i)] + dr_ref[s, :, head_pair(i)].astype(f32)
            red_s.finish(ss_ref)
        else:
            gn_ref[...] = gn[...]
            back.wait_recv(0)
        back.wait_send()
        turns.wait_send()

    S, V = jax.ShapeDtypeStruct, pltpu.VMEM
    args = [do1, xg, qkv, o, lse, w, smalls, keybias]
    scratch = [V((slots, hp, samples, 128), bf16), V((8, rows), f32), V((128, rows), bf16), V((128, rows), f32), V((rows, 128), f32),
               V((rows, 128), f32), V((3, rows, dh), bf16), V((rows, d), bf16), V((8, d), f32), V((slots, samples, d), bf16)]
    scratch += turn_sems(fs_n, hp) + turn_sems(fs_n, 1)
    if packed:
        args += [g1, gm]
        mrows, srows = gm.shape[3], 16 + 3 * rl
        outs = [S((rows * d // 128, 128), f32), S((mrows, d), f32), S((srows, d), f32)]
        scratch += [V((dp_n, fs_n // 2, 2, srows, d), bf16), V((slots, samples, d), bf16)]
        scratch += plane_reduce_scratch(fs_n, mrows, d) + plane_reduce_scratch(fs_n, srows, d)
    else:
        outs = [S((slots, samples, d), bf16), S((3, d, dh), bf16), S((8, d), f32)]
    return pl.pallas_call(
        body, out_shape=outs, in_specs=[ANY if packed and i == 9 else VM for i in range(len(args))], out_specs=[VM] * len(outs), scratch_shapes=scratch,
        compiler_params=params(2), name="backward",
    )(*args)
def ones_pairs():
    half = lax.broadcasted_iota(jnp.int32, (256, 128), 0) // 64
    return (lax.rem(half, 2) == lax.broadcasted_iota(jnp.int32, (256, 128), 1) // 64).astype(bf16)


def head_sums(prods, ones):
    both = []
    for v in prods:
        hi = v.astype(bf16)
        both.append(jnp.concatenate([hi, (v - hi.astype(f32)).astype(bf16)], 1))
    out = dot(jnp.concatenate(both, 0), ones)
    n = prods[0].shape[0]
    return [out[i * n:(i + 1) * n] for i in range(len(prods))]


def key_bias(ref, counts, feats):
    count = counts[lax.axis_index("fsdp") // feats]
    rows = lax.broadcasted_iota(jnp.int32, ref.shape, 0)
    ref[...] = jnp.where(rows < count, 0.0, MASKED)


def rows_at(i, n):
    return pl.ds(pl.multiple_of(i * n, n), n)


def turn_rows(pieces, wide, out, tasks, feats, samples):
    blocks(wide.shape[0], 512, lambda at: wide.__setitem__((at, slice(None)), pieces[at, :].astype(f32)))
    parts = wide.shape[0] // (tasks * samples * feats)
    for s in range(tasks * feats):
        for i in range(parts):
            start = (s // feats * samples * parts + i) * feats + s % feats
            out(s, head_pair(i), wide[pl.ds(start, samples, stride=feats * parts), :].astype(bf16))


def first_kernel(tok, cot, scounts, fcounts, small_parts, s_qkv, s_out, f_qkv, f_out, m_in, m_out, tasks, samples, fs_n):
    dp_n = 4
    d = s_out.shape[1]
    slots = tok.shape[0] // (samples * d // 128)
    feats = slots // tasks
    rows = slots * samples
    hp = d // 128
    rl = s_out.shape[0]
    fl = m_out.shape[0]
    chunks = m_in.shape[1] // d
    z_n = fs_n // 2
    ra, r1, r2 = 16 + 3 * rl, 5 * rl, chunks * rl + fl
    per = 256 // samples

    def body(tok_ref, cot_ref, sc_ref, fc_ref, norms, ob, ib, sq, so, fq, fo, mi, mo,
             xg_h, qkv_h, o_h, l_ref, ga_h, w1_h, w2, sm, x1_h, o2_h, a3_h, qkv2_h, p2_h, back_h, cot_h,
             wide, x_ref, turned, xg, qkv, o_ref, ga, w1, x1, o2, a3, qkv2, p2, back_ref,
             pa, pb1, pb2, kb, acted, vt, ot, small, out_sem, p2_sem, a3_sem, *sems):
        swap_s, turn_s = sems[:3], sems[3:6]
        gat_s = [sems[6 + 7 * i:13 + 7 * i] for i in range(3)]
        me = lax.axis_index("dp") * fs_n + lax.axis_index("fsdp")
        def placed(ref, first):
            n = ref.shape[1]
            hot = lax.broadcasted_iota(jnp.int32, (n, d), 1) == lax.broadcasted_iota(jnp.int32, (n, d), 0) + first
            return dot(ref[...], hot.astype(bf16))

        inner = lax.rem(me * fl, d)
        row = lax.broadcasted_iota(jnp.int32, (16, d), 0)
        small[...] = jnp.where(row == 7 + me * fl // d, placed(ib, inner), 0.0)
        small[0:6, :] = placed(norms, me * rl)
        small[6:7, :] = placed(ob, me * rl)
        pa[0:16, :] = small[...].astype(bf16)
        for i in range(3):
            pa[16 + i * rl:16 + (i + 1) * rl, :] = sq[i]
            pb1[(1 + i) * rl:(2 + i) * rl, :] = fq[i]
        pb1[0:rl, :] = so[...]
        pb1[4 * rl:5 * rl, :] = fo[...]
        for c in range(chunks):
            pb2[c * rl:(c + 1) * rl, :] = mi[:, c * d:(c + 1) * d]
        pb2[chunks * rl:, :] = mo[...]

        pairs_out = [(xg, xg_h), (qkv, qkv_h), (o_ref, o_h), (ga, ga_h), (w1, w1_h), (x1, x1_h), (o2, o2_h), (qkv2, qkv2_h), (back_ref, back_h), (turned, cot_h)]
        outs_c = [pltpu.make_async_copy(v, h, out_sem.at[i]) for i, (v, h) in enumerate(pairs_out)]
        out_xg, out_qkv, out_o, out_ga, out_w1, out_x1, out_o2, out_qkv2, out_back, out_cot = outs_c

        def out_p2(t):
            return pltpu.make_async_copy(p2.at[t], p2_h.at[t], p2_sem.at[t])

        def out_a3(i):
            return pltpu.make_async_copy(a3.at[rows_at(i, 256)], a3_h.at[rows_at(i, 256)], a3_sem.at[i])

        greet(dp_n, fs_n)
        A = PlaneGather(fs_n, pa, ga, *gat_s[0])
        B = PlaneGather(fs_n, pb1, w1, *gat_s[1])
        C = PlaneGather(fs_n, pb2, w2, *gat_s[2])
        swap = Swap(fs_n, x_ref, xg, *swap_s)
        turns = Turns(fs_n, hp, lambda p, j: o_ref.at[p, rows_at(j, samples)], lambda p, j: back_ref.at[j, p], *turn_s)
        later = list(range(1, z_n))
        A.start()
        turn_rows(tok_ref, wide, lambda s, lanes, v: x_ref.__setitem__((s, slice(None), lanes), v), tasks, feats, samples)
        swap.start()
        for G in (A, B, C):
            G.begin()
        key_bias(kb, sc_ref, feats)
        for k in later:
            A.spread(k)
        for k in range(z_n):
            A.hand_on(k)
        for k in range(z_n):
            A.corner(k)
        turn_rows(cot_ref, wide, lambda s, lanes, v: turned.__setitem__((slice(s * samples, (s + 1) * samples), lanes), v), tasks, feats, samples)
        out_cot.start()
        A.wait()
        out_ga.start()
        total = ga[:, :, :, 0:16, :].astype(f32)
        sm[...] = jnp.sum(total.reshape(-1, 16, d), 0)
        swap.wait()
        B.start()
        C.start()
        out_xg.start()

        def act(i, _):
            u, _r = unit(xg[pl.ds(i * per, per)].reshape(256, d).astype(f32))
            acted[rows_at(i, 256), :] = (u * sm[0:1, :] + sm[1:2, :]).astype(bf16)
            return 0

        lax.fori_loop(0, rows // 256, act, 0)
        for i in range(3):
            w = units(ga, 16 + i * rl, rl)

            def project(at):
                y = dot(acted[at, :], w).astype(bf16)
                qkv[i, at, :] = y * 0.125 if i == 0 else y

            blocks(rows, 256, project)
        out_qkv.start()
        for k in later:
            B.spread(k)

        for p in range(hp):
            at = head_pair(p)
            vt[...] = qkv[2, :, at].astype(f32).T.astype(bf16)
            for h in range(2):
                def part(i, _):
                    qa = rows_at(i, BQ)
                    q = qkv[0, qa, at]
                    q = jnp.where(head_mask(BQ, h), q, jnp.zeros_like(q))
                    s = dot(qkv[1, :, at], q, NT) + kb[:, 0:1]
                    m = jnp.max(s, 0, keepdims=True)
                    e = jnp.exp(s - m)
                    tot = jnp.sum(e, 0, keepdims=True)
                    o = dot(vt[h * 64:h * 64 + 64, :], e.astype(bf16))
                    ot[h * 64:h * 64 + 64, qa] = o * (1.0 / tot)
                    l_ref[p * 2 + h:p * 2 + h + 1, qa] = m + jnp.log(tot)
                    return 0
                lax.fori_loop(0, rows // BQ, part, 0)
            o_ref[p, :, :] = ot[...].T.astype(bf16)
            turns.start(p)
            if p == 0:
                for k in range(z_n):
                    B.hand_on(k)
                for k in later:
                    C.spread(k)
            if p == 1:
                for k in range(z_n):
                    B.corner(k)
            if p == 2:
                C.hand_on(0)
        out_o.start()
        B.wait()
        out_w1.start()
        for k in range(1, z_n):
            C.hand_on(k)
        for p in range(hp):
            turns.wait_recv(p)
        out_back.start()

        def first(i, _):
            at = rows_at(i, 256)
            o1 = jnp.concatenate([back_ref[pl.ds(i * per, per), p].reshape(256, 128) for p in range(hp)], 1)
            y = x_ref[pl.ds(i * per, per)].reshape(256, d).astype(f32) + dot(o1, units(w1, 0, rl))
            x1[at, :] = y
            u, _r = unit(y)
            v = (u * sm[2:3, :] + sm[3:4, :]).astype(bf16)
            for j in range(3):
                z = dot(v, units(w1, (1 + j) * rl, rl)).astype(bf16)
                qkv2[j, at, :] = z * 0.125 if j == 0 else z
            return 0

        lax.fori_loop(0, rows // 256, first, 0)
        for k in range(z_n):
            C.corner(k)
        out_x1.start()
        out_qkv2.start()
        ones = ones_pairs()

        def mix(t, _):
            slot = lambda f: rows_at(t * feats + f, samples)
            for p in range(hp):
                lanes = head_pair(p)
                ks = [qkv2[1, slot(g), lanes].astype(f32) for g in range(feats)]
                vs = [qkv2[2, slot(g), lanes].astype(f32) for g in range(feats)]
                for f in range(feats):
                    q = qkv2[0, slot(f), lanes].astype(f32)
                    sc = head_sums([q * k for k in ks], ones)
                    sc = [v + jnp.where(g < fc_ref[t], 0.0, MASKED) for g, v in enumerate(sc)]
                    top = functools.reduce(jnp.maximum, sc)
                    sc = [jnp.exp(v - top) for v in sc]
                    inv = 1.0 / sum(sc)
                    sc = [v * inv for v in sc]
                    for g in range(feats):
                        p2[t, p, f, g] = sc[g].astype(bf16)
                    o2[slot(f), lanes] = sum(w * v for w, v in zip(sc, vs)).astype(bf16)
            out_p2(t).start()
            return 0

        lax.fori_loop(0, tasks, mix, 0)
        out_o2.start()

        def second(i, _):
            at = rows_at(i, 256)
            u, _r = unit(x1[at, :] + dot(o2[at, :], units(w1, 4 * rl, rl)))
            a3[at, :] = (u * sm[4:5, :] + sm[5:6, :]).astype(bf16)
            out_a3(i).start()
            return 0

        lax.fori_loop(0, rows // 256, second, 0)
        turns.wait_send()
        C.wait()
        for c in outs_c:
            c.wait()
        for t in range(tasks):
            out_p2(t).wait()
        for i in range(rows // 256):
            out_a3(i).wait()

    S, V, D = jax.ShapeDtypeStruct, pltpu.VMEM, pltpu.SemaphoreType.DMA
    SM = pl.BlockSpec(memory_space=pltpu.SMEM)
    g = (dp_n, z_n, 2)
    outs = [S((slots, samples, d), bf16), S((3, rows, d), bf16), S((hp, rows, 128), bf16), S((2 * hp, rows), f32),
            S(g + (ra, d), bf16), S(g + (r1, d), bf16), S(g + (r2, d), bf16), S((16, d), f32), S((rows, d), f32), S((rows, d), bf16),
            S((rows, d), bf16), S((3, rows, d), bf16), S((tasks, hp, feats, feats, samples, 128), bf16), S((slots, hp, samples, 128), bf16),
            S((rows, d), bf16)]
    return pl.pallas_call(
        body, out_shape=outs, in_specs=[VM, VM, SM, SM] + [VM] * 9, out_specs=[VM if i in (3, 7) else ANY for i in range(len(outs))],
        scratch_shapes=[V(tok.shape, f32), V((slots, samples, d), bf16), V((rows, d), bf16)] + [V(outs[i].shape, outs[i].dtype) for i in (0, 1, 2, 4, 5, 8, 9, 10, 11, 12, 13)] + [V((ra, d), bf16), V((r1, d), bf16), V((r2, d), bf16), V((rows, 128), f32), V((rows, d), bf16), V((128, rows), bf16),
                        V((128, rows), f32), V((16, d), f32), D((10,)), D((tasks,)), D((rows // 256,))] + swap_sems(fs_n) + turn_sems(fs_n, hp) + plane_gather_sems(fs_n) * 3,
        compiler_params=params(1), name="first",
    )(tok, cot, scounts, fcounts, *small_parts, s_qkv, s_out, f_qkv, f_out, m_in, m_out)


def second_kernel(scounts, saved, tasks, rl, fl, fs_n):
    xg, qkv, o, lse, ga, w1, w2, sm, x1, o2, a3, qkv2, p2, back, cot = saved
    slots, samples, d = xg.shape
    feats = slots // tasks
    rows = slots * samples
    hp = d // 128
    z_n = fs_n // 2
    chunks = (w2.shape[3] - fl) // rl
    r1, r2, rs = 16 + 5 * rl, chunks * rl + fl, 16 + 3 * rl
    RB = 256
    per = RB // samples
    bq = 512
    pq = bq // samples

    def body(sc_ref, l_ref, sm_ref, cot_h, w2_h, x1_h, o2_h, a3_h,
             xg_h, qkv_h, o_h, ga_h, w1_h, qkv2_h, p2_h, back_h,
             g1_h, lo_h, dr, out2, out1, outs_,
             g1, lo, cot_ref, w2_ref, x1_ref, o2_ref, a3_ref, o_, w1_, q_, p2_, bk, acc, act, gh, ev, a2, do2, dqkv, G2, G1, GS, do, do1, delta, kt, dqt, kb, gn,
             c2, n2, z2, c1, n1, z1, c0, n0, z0, load_sem, *sems):
        turn_s, back_s = sems[:3], sems[3:6]
        red_s = [sems[6 + 6 * i:12 + 6 * i] for i in range(3)]
        me_f = lax.axis_index("fsdp")
        me_z, me_c = me_f // 2, mod(me_f, 2)
        load = lambda i, src, dst: pltpu.make_async_copy(src, dst, load_sem.at[i])
        get_w1 = load(0, w1_h, w1_)
        get_q2 = load(1, qkv2_h, q_)
        get_p2 = load(2, p2_h, p2_)
        get_bk = load(3, back_h, bk)
        xg_ = a3_ref
        dk, dv = acc.at[:, 0:128], acc.at[:, 128:256]
        get_xg = load(4, xg_h, xg_)
        get_o = load(5, o_h, o_)
        get_q1 = load(6, qkv_h, q_)
        ga_ = w1_.at[:, :, :, 0:rs, :]
        get_ga = load(7, ga_h, ga_)
        heads_in = [load(8 + i, a, b) for i, (a, b) in enumerate([(a3_h, a3_ref), (w2_h, w2_ref), (cot_h, cot_ref), (x1_h, x1_ref), (o2_h, o2_ref)])]
        put_g1 = load(13, g1, g1_h)
        put_lo = load(14, lo, lo_h)
        for c in heads_in + [get_w1, get_q2, get_p2, get_bk, get_o]:
            c.start()
        key_bias(kb, sc_ref, feats)
        gn[...] = jnp.zeros_like(gn)
        for i in range(rows // RB):
            acc[i * RB:(i + 1) * RB, :] = jnp.zeros((RB, d), f32)
            g1[i * RB:(i + 1) * RB, :] = jnp.zeros((RB, d), f32)
        greet(4, fs_n)
        for c in heads_in[:3]:
            c.wait()

        def mat(k):
            return units(w1_, k * rl, rl)

        def in_mat(c):
            return w2_ref[:, :, :, pl.ds(pl.multiple_of(c * rl, rl), rl), :].reshape(d, d)

        def out_mat(c):
            return w2_ref[pl.ds(c, 1), :, :, chunks * rl:, :].reshape(d, d)

        def put(g, start, i, value):
            g[2 * i:2 * i + 2, :, :, pl.ds(start, rl), :] = value.reshape(2, z_n, 2, rl, d)

        halves = [(slice(i * 256, i * 256 + 256), i) for i in range(d // 256)]

        def chunk(c, _):
            def part(at):
                hid = dot(a3_ref[at, :], in_mat(c)) + sm_ref[pl.ds(7 + c, 1), :]
                cdf, pdf = gelu_parts(hid)
                al = (hid * cdf).astype(bf16)
                act[at, :] = al
                gl = ((cdf + pdf) * dot(cot_ref[at, :], out_mat(c), NT)).astype(bf16)
                gh[at, :] = gl
                gn[pl.ds(7 + c, 1), :] += jnp.sum(gl.astype(f32), 0, keepdims=True)
                acc[at, :] += dot(al, out_mat(c))
                g1[at, :] += dot(gl, in_mat(c), NT)

            blocks(rows, RB, part)
            for at, i in halves:
                value = dot(act[:, at], cot_ref[...], TN).astype(bf16)
                G2[pl.ds(c, 1), 2 * i:2 * i + 2, :, chunks * rl:, :] = value.reshape(1, 2, 2, fl, d)
                put(G2, pl.multiple_of(c * rl, rl), i, dot(a3_ref[:, at], gh[...], TN).astype(bf16))
            return 0

        lax.fori_loop(0, chunks, chunk, 0)
        red2 = PlaneReduce(fs_n, G2, (c2, n2, z2), red_s[0])
        red2.start()
        for c in heads_in[3:]:
            c.wait()
        get_w1.wait()

        def third(at):
            x2 = x1_ref[at, :] + dot(o2_ref[at, :], mat(4))
            lo[at, :] = (x2 + acc[at, :] + sm_ref[6:7, :]).astype(bf16)
            u, r = unit(x2)
            y = g1[at, :]
            gn[4:5, :] += jnp.sum(y * u, 0, keepdims=True)
            gn[5:6, :] += jnp.sum(y, 0, keepdims=True)
            cf = cot_ref[at, :].astype(f32)
            gn[6:7, :] += jnp.sum(cf, 0, keepdims=True)
            g2 = cf + unit_back(y, u, r, sm_ref[4:5, :])
            g1[at, :] = g2
            e2 = g2.astype(bf16)
            ev[at, :] = e2
            do2[at, :] = dot(e2, mat(4), NT).astype(bf16)

        blocks(rows, RB, third)
        put_lo.start()
        for at, i in halves:
            put(G1, 16 + 4 * rl, i, dot(o2_ref[:, at], ev[...], TN).astype(bf16))
        red2.every(red2.first)
        get_q2.wait()
        get_p2.wait()
        ones = ones_pairs()

        def unmix(t, _):
            slot = lambda f: rows_at(t * feats + f, samples)
            for p in range(hp):
                lanes = head_pair(p)
                ks = [q_[1, slot(g), lanes].astype(f32) for g in range(feats)]
                vs = [q_[2, slot(g), lanes].astype(f32) for g in range(feats)]
                dks, dvs = [0.0] * feats, [0.0] * feats
                for f in range(feats):
                    q = q_[0, slot(f), lanes].astype(f32)
                    gr = do2[slot(f), lanes].astype(f32)
                    dp = head_sums([gr * v for v in vs], ones)
                    ws = [p2_[t, p, f, g].astype(f32) for g in range(feats)]
                    mean = sum(w * v for w, v in zip(ws, dp))
                    ds = [(w * (v - mean)).astype(bf16).astype(f32) for w, v in zip(ws, dp)]
                    dqkv[0, slot(f), lanes] = (sum(v * k for v, k in zip(ds, ks)) * 0.125).astype(bf16)
                    for g in range(feats):
                        dks[g] += ds[g] * q
                        dvs[g] += ws[g] * gr
                for g in range(feats):
                    dqkv[1, slot(g), lanes] = dks[g].astype(bf16)
                    dqkv[2, slot(g), lanes] = dvs[g].astype(bf16)
            return 0

        lax.fori_loop(0, tasks, unmix, 0)
        get_q1.start()

        def far(i, r):
            return mod(me_z + i, z_n) * 2 + mod(me_c + r, 2)

        me_d = lax.axis_index("dp")
        sends = {}
        for i in range(z_n):
            for r in range(2):
                for p in range(hp):
                    n = (p * z_n + i) * 2 + r
                    to = far(i, r)
                    if i == 0 and r == 0:
                        sends[p, i, r] = pltpu.make_async_copy(do1.at[to, p], do.at[to, p], turn_s[0].at[p])
                    else:
                        sends[p, i, r] = rcopy(do1.at[to, p], do.at[me_f, p], turn_s[1].at[n], turn_s[2].at[n], (me_d, to))
        chips = list(range(1, z_n)) + [0]

        def fourth(i):
            chip = mod(me_z + i, z_n)
            at = rows_at(chip, RB)
            u, r = unit(x1_ref[at, :])
            gain = sm_ref[2:3, :]
            a2[at, :] = (u * gain + sm_ref[3:4, :]).astype(bf16)
            y = dot(dqkv[0, at, :], mat(1), NT) + dot(dqkv[1, at, :], mat(2), NT) + dot(dqkv[2, at, :], mat(3), NT)
            gn[2:3, :] += jnp.sum(y * u, 0, keepdims=True)
            gn[3:4, :] += jnp.sum(y, 0, keepdims=True)
            v = g1[at, :] + unit_back(y, u, r, gain)
            g1[at, :] = v
            e1 = v.astype(bf16)
            ev[at, :] = e1
            g = dot(e1, mat(0), NT).astype(bf16)
            for p in range(hp):
                do1[pl.ds(chip * per, per), p] = g[:, head_pair(p)].reshape(per, samples, 128)
            for r in range(2):
                sends[0, i, r].start()

        for i in chips:
            fourth(i)
        for p in range(1, hp):
            for i in chips:
                for r in range(2):
                    sends[p, i, r].start()
        put_g1.start()
        get_ga.start()

        get_xg.start()
        red2.every(red2.second)
        get_bk.wait()
        for at, i in halves:
            o1 = jnp.concatenate([bk[:, 2 * i].reshape(rows, 128), bk[:, 2 * i + 1].reshape(rows, 128)], 1)
            put(G1, 16, i, dot(o1, ev[...], TN).astype(bf16))
            for j in range(3):
                put(G1, 16 + (1 + j) * rl, i, dot(a2[:, at], dqkv[j], TN).astype(bf16))
        G1[:, :, :, 0:16, :] = jnp.broadcast_to(gn[...].astype(bf16), (4, z_n, 2, 16, d))
        red1 = PlaneReduce(fs_n, G1, (c1, n1, z1), red_s[1])
        red1.start()
        red2.every(red2.third)

        lane = lax.broadcasted_iota(jnp.int32, (8, 128), 1) // 64
        pick = (lane == lax.broadcasted_iota(jnp.int32, (8, 128), 0)).astype(f32)
        get_q1.wait()
        get_o.wait()

        def grad_rows(i, p):
            return do[pl.ds(i * pq, pq), p].reshape(bq, 128)

        for p in range(hp):
            at = head_pair(p)
            kt[...] = q_[1, :, at].astype(f32).T.astype(bf16)
            dk[...] = jnp.zeros((rows, 128), f32)
            dv[...] = jnp.zeros((rows, 128), f32)
            for i in range(z_n):
                for r in range(2):
                    if i == 0 and r == 0:
                        sends[p, i, r].wait()
                    else:
                        sends[p, i, r].wait_recv()

            def deltas(i, _):
                qa = rows_at(i, bq)
                prod = grad_rows(i, p).astype(f32) * o_[p, qa, :].astype(f32)
                delta[:, qa] = lax.dot_general(pick, prod, NT, precision=lax.Precision.HIGHEST, preferred_element_type=f32)
                return 0

            lax.fori_loop(0, rows // bq, deltas, 0)
            if p == 0:
                red1.every(red1.first)
            for h in range(2):
                def part(i, _):
                    qa = rows_at(i, bq)
                    mask = head_mask(bq, h)
                    q = q_[0, qa, at]
                    q = jnp.where(mask, q, jnp.zeros_like(q))
                    g = grad_rows(i, p)
                    g = jnp.where(mask, g, jnp.zeros_like(g))
                    s = dot(q_[1, :, at], q, NT) + kb[:, 0:1]
                    e = jnp.exp(s - l_ref[p * 2 + h:p * 2 + h + 1, qa])
                    ds = (e * (dot(q_[2, :, at], g, NT) - delta[h:h + 1, qa])).astype(bf16)
                    dv[...] += dot(e.astype(bf16), g)
                    dk[...] += dot(ds, q)
                    dqt[h * 64:h * 64 + 64, qa] = dot(kt[h * 64:h * 64 + 64, :], ds) * 0.125
                    return 0
                lax.fori_loop(0, rows // bq, part, 0)
            dqkv[0, :, at] = dqt[...].T.astype(bf16)
            dqkv[1, :, at] = dk[...].astype(bf16)
            dqkv[2, :, at] = dv[...].astype(bf16)
            if p == 1:
                red1.every(red1.second)
            if p == 2:
                red1.every(red1.third)

        get_ga.wait()
        get_xg.wait()
        gn[...] = jnp.zeros_like(gn)
        gain, bias = sm_ref[0:1, :], sm_ref[1:2, :]

        backs = {}
        for i in range(z_n):
            for r in range(2):
                to = far(i, r)
                if i == 0 and r == 0:
                    backs[i, r] = pltpu.make_async_copy(xg_.at[rows_at(to, samples)], dr.at[to], back_s[0].at[0])
                else:
                    n = 2 * i + r
                    backs[i, r] = rcopy(xg_.at[rows_at(to, samples)], dr.at[me_f], back_s[1].at[n], back_s[2].at[n], (me_d, to))
        for i in chips:
            chip = mod(me_z + i, z_n)
            at = rows_at(chip, RB)
            u, r = unit(xg_[at, :].astype(f32))
            y = (dot(dqkv[0, at, :], units(ga_, 16, rl), NT) + dot(dqkv[1, at, :], units(ga_, 16 + rl, rl), NT)
                 + dot(dqkv[2, at, :], units(ga_, 16 + 2 * rl, rl), NT))
            gn[0:1, :] += jnp.sum(y * u, 0, keepdims=True)
            gn[1:2, :] += jnp.sum(y, 0, keepdims=True)
            xg_[at, :] = unit_back(y, u, r, gain).astype(bf16)
            ev[at, :] = (u * gain + bias).astype(bf16)
            for r in range(2):
                backs[i, r].start()
        for j in range(3):
            for at, i in halves:
                put(GS, 16 + j * rl, i, dot(ev[:, at], dqkv[j], TN).astype(bf16))
        GS[:, :, :, 0:16, :] = jnp.broadcast_to(gn[...].astype(bf16), (4, z_n, 2, 16, d))
        reds = PlaneReduce(fs_n, GS, (c0, n0, z0), red_s[2])
        reds.start()
        red2.finish(out2)
        reds.every(reds.first)
        red1.finish(out1)
        reds.every(reds.second)
        reds.every(reds.third)
        reds.finish(outs_)
        put_g1.wait()
        put_lo.wait()
        for i in range(z_n):
            for r in range(2):
                backs[i, r].wait()
        for key, c in sends.items():
            if key[1:] != (0, 0):
                c.wait_send()

    S, V, D = jax.ShapeDtypeStruct, pltpu.VMEM, pltpu.SemaphoreType.DMA
    SM = pl.BlockSpec(memory_space=pltpu.SMEM)
    g = (4, z_n, 2)
    scratch = [V((rows, d), f32), V((rows, d), bf16), V((rows, d), bf16), V(w2.shape, bf16), V((rows, d), f32), V((rows, d), bf16),
               V((rows, d), bf16)]
    scratch += [V(o.shape, bf16), V(w1.shape, bf16), V(qkv.shape, bf16), V(p2.shape, bf16), V(back.shape, bf16),
               V((rows, d), f32), V((rows, d), bf16), V((rows, d), bf16), V((rows, d), bf16), V((rows, d), bf16), V((rows, d), bf16),
               V((3, rows, d), bf16), V(g + (r2, d), bf16), V(g + (r1, d), bf16), V(g + (rs, d), bf16), V(back.shape, bf16), V(back.shape, bf16), V((8, rows), f32),
               V((128, rows), bf16), V((128, rows), f32), V((rows, 128), f32), V((16, d), f32)]
    scratch += plane_reduce_scratch(fs_n, r2, d) + plane_reduce_scratch(fs_n, r1, d) + plane_reduce_scratch(fs_n, rs, d)
    n = hp * fs_n
    scratch += [D((15,)), D((hp,)), D((n,)), D((n,)), D((1,)), D((fs_n,)), D((fs_n,))] + plane_reduce_sems(fs_n) * 3
    return pl.pallas_call(
        body,
        out_shape=[S((rows, d), f32), S((rows, d), bf16), S((slots, samples, d), bf16), S((r2, d), f32), S((r1, d), f32), S((rs, d), f32)],
        in_specs=[SM, VM, VM] + [ANY] * 13, out_specs=[ANY, ANY, ANY, VM, VM, VM], scratch_shapes=scratch,
        compiler_params=params(2), name="second",
    )(scounts, lse, sm, cot, w2, x1, o2, a3, xg.reshape(rows, d), qkv, o, ga, w1, qkv2, p2, back)


def last_kernel(g1, dr, lo, out2, out1, outs, tasks, rl, fl, fs_n):
    slots, samples, d = dr.shape
    feats = slots // tasks
    part = feats * samples
    wide = d // 128
    chunks = (out2.shape[0] - fl) // rl

    def body(g1_ref, dr_ref, lo_ref, r2, r1, rs, tg, lo_out, gn, gs, gso, gf, gfo, gmi, gib, gmo, gob, low):
        for f in range(feats):
            for i in range(wide):
                at = pl.ds(i * feats + f, samples, stride=feats * wide)
                here = (slice(f * samples, (f + 1) * samples), head_pair(i))
                tg[at, :] = g1_ref[here] + dr_ref[f, :, head_pair(i)].astype(f32)
                low[at, :] = lo_ref[here].astype(f32)
        blocks(part * wide, 512, lambda at: lo_out.__setitem__((at, slice(None)), low[at, :].astype(bf16)))

        @pl.when(pl.program_id(0) == 0)
        def _():
            me = lax.axis_index("dp") * fs_n + lax.axis_index("fsdp")
            for i in range(3):
                gs[i] = rs[16 + i * rl:16 + (i + 1) * rl, :]
                gf[i] = r1[16 + (1 + i) * rl:16 + (2 + i) * rl, :]
            gso[...] = r1[16:16 + rl, :]
            gfo[...] = r1[16 + 4 * rl:16 + 5 * rl, :]
            for c in range(chunks):
                gmi[:, c * d:(c + 1) * d] = r2[c * rl:(c + 1) * rl, :]
            gmo[...] = r2[chunks * rl:, :]
            row = lax.broadcasted_iota(jnp.int32, (16, d), 0)
            both = jnp.where(row < 2, rs[0:16, :], r1[0:16, :])

            def mine(v, n, first):
                hot = lax.broadcasted_iota(jnp.int32, (d, n), 0) == lax.broadcasted_iota(jnp.int32, (d, n), 1) + first
                return lax.dot_general(v, hot.astype(f32), NN, precision=lax.Precision.HIGHEST, preferred_element_type=f32)

            own = mine(both, rl, me * rl)
            gn[...] = own[0:6]
            gob[...] = own[6:7]
            line = jnp.sum(jnp.where(row == 7 + me * fl // d, both, 0.0), 0, keepdims=True)
            gib[...] = mine(jnp.broadcast_to(line, (8, d)), fl, lax.rem(me * fl, d))[0:1]

    S = jax.ShapeDtypeStruct
    shapes = [S((tasks * part * wide, 128), f32), S((tasks * part * wide, 128), bf16), S((6, rl), f32), S((3, rl, d), f32), S((rl, d), f32),
              S((3, rl, d), f32), S((rl, d), f32), S((rl, chunks * d), f32), S((1, fl), f32), S((fl, d), f32), S((1, rl), f32)]
    by_task = lambda *shape: pl.BlockSpec(shape, lambda t: (t,) + (0,) * (len(shape) - 1))
    whole = lambda shape: pl.BlockSpec(shape, lambda t: (0,) * len(shape))
    return pl.pallas_call(
        body, out_shape=shapes, grid=(tasks,),
        in_specs=[by_task(part, d), by_task(feats, samples, d), by_task(part, d)] + [whole(v.shape) for v in (out2, out1, outs)],
        out_specs=[by_task(part * wide, 128), by_task(part * wide, 128)] + [whole(v.shape) for v in shapes[2:]],
        scratch_shapes=[pltpu.VMEM((part * wide, 128), f32)],
        compiler_params=params(), name="last",
    )(g1, dr, lo, out2, out1, outs)


def up16(a):
    rows = a.shape[-2]
    extra = (-rows) % 16
    return a if extra == 0 else jnp.pad(a, [(0, 0)] * (a.ndim - 2) + [(0, extra), (0, 0)])


def local(tokens, sample_counts, feature_counts, norms, sample_qkv, sample_out, feature_qkv, feature_out, mlp_in, mlp_in_bias,
          mlp_out, mlp_out_bias, cotangent):
    dp_n, fs_n = lax.axis_size("dp"), lax.axis_size("fsdp")
    nd = dp_n * fs_n
    me_d, me_f = lax.axis_index("dp"), lax.axis_index("fsdp")
    me = me_d * fs_n + me_f
    tasks, samples, feats, d = tokens.shape
    pairs = tasks * feats
    rep = fs_n // pairs
    dh = d // rep
    hp = dh // 128
    rl = sample_out.shape[0]
    chunks = mlp_in.shape[1] // d
    fl = mlp_out.shape[0]
    total = samples * fs_n
    if rep == 1 and dp_n == 4 and rl % 16 == 0 and fs_n * fl == d:
        def pieces(v):
            return v.reshape(tasks, samples, feats, d // 128, 128).transpose(0, 1, 3, 2, 4).reshape(-1, 128)

        saved = first_kernel(pieces(tokens), pieces(cotangent), sample_counts, feature_counts, (norms, mlp_out_bias[None], mlp_in_bias[None]),
                             sample_qkv, sample_out, feature_qkv, feature_out, mlp_in, mlp_out, tasks, samples, fs_n)
        g1, lo, dr, out2, out1, outs = second_kernel(sample_counts, saved, tasks, rl, fl, fs_n)
        tg, low, gn, gs, gso, gf, gfo, gmi, gib, gmo, gob = last_kernel(g1, dr, lo, out2, out1, outs, tasks, rl, fl, fs_n)

        def rows_back(v):
            return v.reshape(tasks, samples, d // 128, feats, 128).transpose(0, 1, 3, 2, 4).reshape(tokens.shape)

        return rows_back(low), rows_back(tg), gn, gs, gso, gf, gfo, gmi, gib[0], gmo, gob[0]


    small = jnp.zeros((16, d), bf16)
    small = lax.dynamic_update_slice(small, norms, (0, me * rl))
    small = lax.dynamic_update_slice(small, mlp_out_bias[None, :], (6, me * rl))
    small = lax.dynamic_update_slice(small, mlp_in_bias[None, :], (7 + (me * fl) // d, lax.rem(me * fl, d)))
    split_in = mlp_in.reshape(rl, chunks, d).transpose(1, 0, 2).reshape(chunks * rl, d)
    pack_a = up16(jnp.concatenate([small, sample_qkv.reshape(3 * rl, d)], 0))
    pack_b = up16(jnp.concatenate([sample_out, feature_qkv.reshape(3 * rl, d), feature_out, split_in, mlp_out], 0))

    xp = tokens.transpose(0, 2, 1, 3).reshape(pairs, samples, d)
    cp = cotangent.transpose(0, 2, 1, 3).reshape(pairs, samples, d)
    my_task = me_f // rep // feats
    count = lax.dynamic_index_in_dim(sample_counts, my_task, keepdims=False)
    keybias = jnp.broadcast_to(jnp.where(jnp.arange(total) < count, 0.0, MASKED).astype(f32)[:, None], (total, 128))
    shown = jnp.arange(feats)[None, :] < feature_counts[:, None]
    fbias = jnp.broadcast_to(jnp.where(shown, 0.0, MASKED).astype(f32).reshape(pairs, 1), (pairs, 128))

    ga, gb = gather_call([pack_a, pack_b], dp_n, fs_n, 3)
    ga, gb = ga.reshape((nd,) + ga.shape[3:]), gb.reshape((nd,) + gb.shape[3:])

    def take(g, start, rows):
        return g[:, start:start + rows].reshape(nd * rows, d)

    smalls = jnp.sum(ga[:, :16].astype(f32), 0)
    w_s = jnp.stack([take(ga, 16 + i * rl, rl) for i in range(3)])
    first = lax.rem(me_f, rep) * dh
    w_mine = lax.dynamic_slice_in_dim(w_s, first, dh, 2)
    w_mid = jnp.concatenate([take(gb, i * rl, rl) for i in range(5 + chunks)] + [take(gb, (5 + chunks) * rl, fl)])[None]
    size = d
    back, xg, o, qkv, lse = forward_kernel(jnp.repeat(xp, rep, 0), [], [w_mine, smalls], keybias, dp_n, fs_n, rl, dh)

    lo, g1, do1, gm = middle_call(xp, back.reshape(pairs, rep * hp, samples, 128), cp, smalls, fbias, w_mid, tasks, chunks, size)
    do1 = do1.reshape(fs_n, hp, samples, 128)
    dxr, gs, gn_s = backward_kernel(do1, xg, qkv, o, lse, w_mine, smalls, keybias, None, None, dp_n, fs_n, rl, dh, tasks, False)
    dxr = jnp.sum(dxr.reshape(pairs, rep, samples, d).astype(f32), 1)
    tokens_grad = (g1.reshape(pairs, samples, d) + dxr).reshape(tasks, feats, samples, d).transpose(0, 2, 1, 3)
    gs = lax.dynamic_update_slice_in_dim(jnp.zeros((3, d, d), bf16), gs, first, 2)

    def give(g, parts):
        return g.reshape(parts, nd, -1, d).transpose(1, 0, 2, 3).reshape(nd, -1, d)

    gm = gm[0]
    mix = jnp.concatenate([gn_s[0:2].astype(bf16), gm[2:16]], 0)
    grads = up16(jnp.concatenate([jnp.broadcast_to(mix[None], (nd, 16, d)), give(gm[16:16 + (5 + chunks) * d], 5 + chunks),
                                  give(gm[16 + (5 + chunks) * d:], 1), give(gs, 3)], 1))
    s = scatter_call(grads.reshape((dp_n, fs_n // 2, 2) + grads.shape[1:]), dp_n, fs_n, 6)
    outs = [s[16 + (5 + chunks) * rl + fl:][:3 * rl]]
    gn = s[0:2]
    gn = jnp.concatenate([gn, s[2:16]], 0)
    layer_output = lo.reshape(tasks, feats, samples, d).transpose(0, 2, 1, 3)

    def piece(start, rows):
        return s[16 + start * rl:16 + start * rl + rows]

    return (
        layer_output,
        tokens_grad,
        lax.dynamic_slice(gn, (0, me * rl), (6, rl)),
        outs[0].reshape(3, rl, d), piece(0, rl), piece(1, 3 * rl).reshape(3, rl, d), piece(4, rl),
        piece(5, chunks * rl).reshape(chunks, rl, d).transpose(1, 0, 2).reshape(rl, chunks * d),
        lax.dynamic_slice(gn[7:7 + chunks].reshape(-1), (me * fl,), (fl,)),
        piece(5 + chunks, fl),
        lax.dynamic_slice(gn[6], (me * rl,), (rl,)),
    )


def solution(mesh):
    rows, whole = ("dp", "fsdp"), P("dp", "fsdp", None, None)
    weights = (P(None, rows), P(None, rows, None), P(rows, None), P(None, rows, None), P(rows, None), P(rows, None), P(rows),
               P(rows, None), P(rows))
    return jax.shard_map(local, mesh=mesh, in_specs=(whole, P("dp"), P("dp")) + weights + (whole,),
                         out_specs=(whole, whole) + weights, check_vma=False)
```

```python
import functools
import jax
import jax.numpy as jnp
from jax import lax
from jax.experimental import pallas as pl
from jax.experimental.pallas import tpu as pltpu
from jax.sharding import PartitionSpec as P

MESH = pl.DeviceIdType.MESH
f32, bf16 = jnp.float32, jnp.bfloat16


def mod(a, n):
    return lax.rem(a, n)


def greet(dp_n, fs_n, with_dp=True):
    me_d, me_f = lax.axis_index("dp"), lax.axis_index("fsdp")
    barrier = pltpu.get_barrier_semaphore()
    n = 0
    for k in range(1, fs_n):
        pl.semaphore_signal(barrier, inc=1, device_id=(me_d, mod(me_f + k, fs_n)), device_id_type=MESH)
        n += 1
    if with_dp:
        for k in range(1, dp_n):
            pl.semaphore_signal(barrier, inc=1, device_id=(mod(me_d + k, dp_n), me_f), device_id_type=MESH)
            n += 1
    pl.semaphore_wait(barrier, n)


def rcopy(src, dst, ss, rs, dev):
    return pltpu.make_async_remote_copy(src_ref=src, dst_ref=dst, send_sem=ss, recv_sem=rs, device_id=dev, device_id_type=MESH)


class Swap:
    def __init__(self, fs_n, src, dst, local_sem, ss, rs):
        me_d, me_f = lax.axis_index("dp"), lax.axis_index("fsdp")
        self.own = pltpu.make_async_copy(src.at[me_f], dst.at[me_f], local_sem)
        self.copies = []
        for k in range(1, fs_n):
            to = mod(me_f + k, fs_n)
            self.copies.append(rcopy(src.at[to], dst.at[me_f], ss.at[k - 1], rs.at[k - 1], (me_d, to)))

    def start(self):
        for c in self.copies:
            c.start()
        self.own.start()

    def wait(self):
        self.own.wait()
        for c in self.copies:
            c.wait()


class Gather:
    def __init__(self, dp_n, fs_n, src, dst, local_sem, zs, zr, ds, dr, cs, cr):
        me_d, me_f = lax.axis_index("dp"), lax.axis_index("fsdp")
        z_n = fs_n // 2
        me_z, me_c = me_f // 2, mod(me_f, 2)
        self.z_n, self.dp_n = z_n, dp_n
        partner = (me_d, me_z * 2 + 1 - me_c)
        self.own = pltpu.make_async_copy(src, dst.at[me_d, me_z, me_c], local_sem)
        self.z = []
        for k in range(1, z_n):
            to = mod(me_z + k, z_n) * 2 + me_c
            self.z.append(rcopy(src, dst.at[me_d, me_z, me_c], zs.at[k - 1], zr.at[k - 1], (me_d, to)))
        self.d = {}
        self.c = {}
        for k in range(z_n):
            z = mod(me_z - k + z_n, z_n)
            for j in range(dp_n):
                d = mod(me_d - j + dp_n, dp_n)
                here = src if (k == 0 and j == 0) else dst.at[d, z, me_c]
                self.c[k, j] = rcopy(here, dst.at[d, z, me_c], cs.at[k * dp_n + j], cr.at[k * dp_n + j], partner)
                if j > 0:
                    here = src if k == 0 else dst.at[me_d, z, me_c]
                    i = k * (dp_n - 1) + j - 1
                    self.d[k, j] = rcopy(here, dst.at[me_d, z, me_c], ds.at[i], dr.at[i], (mod(me_d + j, dp_n), me_f))

    def start(self):
        for c in self.z:
            c.start()
        self.own.start()
        for j in range(1, self.dp_n):
            self.d[0, j].start()
        self.c[0, 0].start()

    def forward_z(self):
        for k in range(1, self.z_n):
            self.z[k - 1].wait_recv()
            for j in range(1, self.dp_n):
                self.d[k, j].start()
            self.c[k, 0].start()

    def forward_d(self):
        for k in range(self.z_n):
            for j in range(1, self.dp_n):
                self.d[k, j].wait_recv()
                self.c[k, j].start()

    def wait(self):
        self.own.wait()
        for c in self.z:
            c.wait_send()
        for c in self.d.values():
            c.wait_send()
        for c in self.c.values():
            c.wait()


def gather_sems(dp_n, fs_n):
    z = fs_n // 2
    D = pltpu.SemaphoreType.DMA
    return [D, D((z - 1,)), D((z - 1,)), D((z * (dp_n - 1),)), D((z * (dp_n - 1),)), D((z * dp_n,)), D((z * dp_n,))]


def swap_sems(fs_n):
    D = pltpu.SemaphoreType.DMA
    return [D, D((fs_n - 1,)), D((fs_n - 1,))]


ANY = pl.BlockSpec(memory_space=pl.ANY)
VM = pl.BlockSpec(memory_space=pltpu.VMEM)


def swap_call(x, dp_n, fs_n, cid, space=ANY):
    def body(x_ref, o_ref, *sems):
        greet(dp_n, fs_n, False)
        s = Swap(fs_n, x_ref, o_ref, *sems)
        s.start()
        s.wait()

    return pl.pallas_call(
        body, out_shape=jax.ShapeDtypeStruct(x.shape, x.dtype), in_specs=[space], out_specs=space,
        scratch_shapes=swap_sems(fs_n),
        compiler_params=pltpu.CompilerParams(collective_id=cid, has_side_effects=True, vmem_limit_bytes=60 << 20),
        name="swap%d" % cid,
    )(x)


def gather_call(packs, dp_n, fs_n, cid, space=ANY):
    n = len(packs)

    def body(*refs):
        ins, outs, sems = refs[:n], refs[n:2 * n], refs[2 * n:]
        greet(dp_n, fs_n)
        gs = [Gather(dp_n, fs_n, ins[i], outs[i], *sems[7 * i:7 * i + 7]) for i in range(n)]
        for g in gs:
            g.start()
        for g in gs:
            g.forward_z()
        for g in gs:
            g.forward_d()
        for g in gs:
            g.wait()

    return pl.pallas_call(
        body,
        out_shape=[jax.ShapeDtypeStruct((dp_n, fs_n // 2, 2) + p.shape, p.dtype) for p in packs],
        in_specs=[space] * n, out_specs=[space] * n,
        scratch_shapes=gather_sems(dp_n, fs_n) * n,
        compiler_params=pltpu.CompilerParams(collective_id=cid, has_side_effects=True, vmem_limit_bytes=60 << 20),
        name="gather%d" % cid,
    )(*packs)


def scatter_call(g, dp_n, fs_n, cid):
    z_n = fs_n // 2
    rows, width = g.shape[3:]
    step = 16

    def body(g_ref, o_ref, from_c, half, from_d, quarter, from_z, cs, cr, ds, dr, zs, zr):
        me_d, me_f = lax.axis_index("dp"), lax.axis_index("fsdp")
        me_z, me_c = me_f // 2, mod(me_f, 2)
        greet(dp_n, fs_n)
        partner = (me_d, me_z * 2 + 1 - me_c)

        def add(out, parts):
            def one(i, _):
                at = pl.ds(pl.multiple_of(i * step, step), step)
                total = parts[0][at, :].astype(f32)
                for p in parts[1:]:
                    total = total + p[at, :].astype(f32)
                out[at, :] = total.astype(out.dtype)
                return 0
            lax.fori_loop(0, rows // step, one, 0, unroll=True if rows // step <= 4 else 4)

        order = [(j, k) for j in list(range(1, dp_n)) + [0] for k in list(range(1, z_n)) + [0]]
        cc, dd, zz = {}, {}, {}
        for i, (j, k) in enumerate(order):
            d, z = mod(me_d + j, dp_n), mod(me_z + k, z_n)
            cc[j, k] = rcopy(g_ref.at[d, z, 1 - me_c], from_c.at[i], cs.at[i], cr.at[i], partner)
            cc[j, k].start()
        for i, (j, k) in enumerate(order):
            d, z = mod(me_d + j, dp_n), mod(me_z + k, z_n)
            cc[j, k].wait_recv()
            add(half.at[j, k], [g_ref.at[d, z, me_c], from_c.at[i]])
            if j:
                n = (j - 1) * z_n + k
                dd[j, k] = rcopy(half.at[j, k], from_d.at[j - 1, k], ds.at[n], dr.at[n], (d, me_f))
                dd[j, k].start()
        for k in list(range(1, z_n)) + [0]:
            for j in range(1, dp_n):
                dd[j, k].wait_recv()
            if k:
                add(quarter.at[k], [half.at[0, k]] + [from_d.at[j - 1, k] for j in range(1, dp_n)])
                to = mod(me_z + k, z_n) * 2 + me_c
                zz[k] = rcopy(quarter.at[k], from_z.at[k - 1], zs.at[k - 1], zr.at[k - 1], (me_d, to))
                zz[k].start()
        for k in range(1, z_n):
            zz[k].wait_recv()
        add(o_ref, [half.at[0, 0]] + [from_d.at[j - 1, 0] for j in range(1, dp_n)] + [from_z.at[k - 1] for k in range(1, z_n)])
        for c in list(cc.values()) + list(dd.values()) + list(zz.values()):
            c.wait_send()

    D = pltpu.SemaphoreType.DMA
    n = dp_n * z_n
    return pl.pallas_call(
        body, out_shape=jax.ShapeDtypeStruct((rows, width), f32), in_specs=[VM], out_specs=VM,
        scratch_shapes=[
            pltpu.VMEM((n, rows, width), bf16), pltpu.VMEM((dp_n, z_n, rows, width), bf16),
            pltpu.VMEM((dp_n - 1, z_n, rows, width), bf16), pltpu.VMEM((z_n, rows, width), bf16),
            pltpu.VMEM((z_n - 1, rows, width), bf16),
            D((n,)), D((n,)), D((n - z_n,)), D((n - z_n,)), D((z_n - 1,)), D((z_n - 1,)),
        ],
        compiler_params=pltpu.CompilerParams(collective_id=cid, has_side_effects=True, vmem_limit_bytes=60 << 20),
        name="scatter%d" % cid,
    )(g)
class PlaneGather:
    def __init__(self, fs_n, src, dst, local_sem, zs, zr, ds, dr, cs, cr):
        me_d, me_f = lax.axis_index("dp"), lax.axis_index("fsdp")
        z_n = fs_n // 2
        me_z, me_c = me_f // 2, mod(me_f, 2)
        self.z_n = z_n
        partner = (me_d, me_z * 2 + 1 - me_c)
        ds_ = [me_d, me_d // 2 * 2 + 1 - mod(me_d, 2), mod(me_d + 2, 4), 3 - me_d]
        zs_ = [mod(me_z - k + z_n, z_n) for k in range(z_n)]
        self.own = pltpu.make_async_copy(src, dst.at[me_d, me_z, me_c], local_sem)
        self.z, self.n, self.fwd, self.c = {}, {}, {}, {}
        for k in range(z_n):
            at = lambda j: dst.at[ds_[j], zs_[k], me_c]
            mine = src if k == 0 else at(0)
            if k:
                to = mod(me_z + k, z_n) * 2 + me_c
                self.z[k] = rcopy(src, dst.at[me_d, me_z, me_c], zs.at[k - 1], zr.at[k - 1], (me_d, to))
            for j in (1, 2):
                self.n[k, j] = rcopy(mine, at(0), ds.at[3 * k + j - 1], dr.at[3 * k + j - 1], (ds_[j], me_f))
            first = 1 + k % 2
            self.fwd[k] = rcopy(at(first), at(first), ds.at[3 * k + 2], dr.at[3 * k + 2], (ds_[3 - first], me_f))

        for j in range(4):
            all_z = dst.at[ds_[j], :, me_c]
            self.c[j] = rcopy(all_z, all_z, cs.at[j], cr.at[j], partner)

    def start(self):
        for c in self.z.values():
            c.start()

    def begin(self):
        self.own.start()
        self.spread(0)

    def spread(self, k):
        if k:
            self.z[k].wait_recv()
        self.n[k, 1].start()
        self.n[k, 2].start()
        if k == self.z_n - 1:
            self.own.wait()
            self.c[0].start()

    def hand_on(self, k):
        first = 1 + k % 2
        for j in (first, 3 - first):
            self.n[k, j].wait_recv()
            if j == first:
                self.fwd[k].start()
        if k == self.z_n - 1:
            self.c[1].start()
            self.c[2].start()

    def corner(self, k):
        self.fwd[k].wait_recv()
        if k == self.z_n - 1:
            self.c[3].start()

    def wait(self):
        for c in list(self.z.values()) + list(self.n.values()) + list(self.fwd.values()):
            c.wait_send()
        for c in self.c.values():
            c.wait()


def plane_gather_sems(fs_n):
    z, D = fs_n // 2, pltpu.SemaphoreType.DMA
    return [D, D((z - 1,)), D((z - 1,)), D((3 * z,)), D((3 * z,)), D((4,)), D((4,))]


class PlaneReduce:
    def __init__(self, fs_n, g, bufs, sems):
        me_d, me_f = lax.axis_index("dp"), lax.axis_index("fsdp")
        z_n = fs_n // 2
        me_z, me_c = me_f // 2, mod(me_f, 2)
        self.halves, self.z_n, self.rows = z_n // 2, z_n, g.shape[4]
        self.from_c, self.from_n, self.from_z = bufs
        cs, cr, ds, dr, zs, zr = sems
        partner = (me_d, me_z * 2 + 1 - me_c)
        ds_ = [me_d, me_d // 2 * 2 + 1 - mod(me_d, 2), mod(me_d + 2, 4), 3 - me_d]
        self.mine = lambda j, h, a: g.at[ds_[j], h, a, me_c]
        self.c = [rcopy(g.at[ds_[j], :, :, 1 - me_c], self.from_c.at[j], cs.at[j], cr.at[j], partner) for j in range(4)]
        self.n, self.z, self.line = {}, {}, {}
        for a in range(2):
            first = 1 + a
            for i, (j, to) in enumerate([(first, first), (3, first), (3 - first, 3 - first)]):
                self.n[a, i] = rcopy(g.at[ds_[j], :, a, me_c], self.from_n.at[a, i], ds.at[3 * a + i], dr.at[3 * a + i], (ds_[to], me_f))
        for k in range(z_n):
            z = mod(me_z + k, z_n)
            h, a = z // 2, mod(z, 2)
            own = g.at[me_d, h, a, me_c]
            self.line[k] = [own, self.from_n.at[a, 0, h], self.from_n.at[a, 2, h]]
            if k:
                self.z[k] = rcopy(own, self.from_z.at[k - 1], zs.at[k - 1], zr.at[k - 1], (me_d, z * 2 + me_c))

    def add(self, *sums):
        step = 16

        def one(i, _):
            at = pl.ds(pl.multiple_of(i * step, step), step)
            for out, parts in sums:
                if len(parts) == 2:
                    out[at, :] = parts[0][at, :] + parts[1][at, :]
                else:
                    total = parts[0][at, :].astype(f32)
                    for p in parts[1:]:
                        total = total + p[at, :].astype(f32)
                    out[at, :] = total.astype(out.dtype)
            return 0

        lax.fori_loop(0, self.rows // step, one, 0)

    def start(self):
        for j in (1, 2, 3, 0):
            self.c[j].start()

    def first(self):
        for j in (1, 2, 3, 0):
            self.c[j].wait_recv()
            self.add(*[(self.mine(j, h, a), [self.mine(j, h, a), self.from_c.at[j, h, a]]) for h in range(self.halves) for a in range(2)])
            if j in (1, 2):
                self.n[j - 1, 0].start()
            if j == 3:
                self.n[0, 1].start()
                self.n[1, 1].start()

    def second(self):
        for a in range(2):
            j = 2 - a
            self.n[a, 1].wait_recv()
            self.add(*[(self.mine(j, h, a), [self.mine(j, h, a), self.from_n.at[a, 1, h]]) for h in range(self.halves)])
            self.n[a, 2].start()

    def third(self):
        for a in range(2):
            self.n[a, 0].wait_recv()
            self.n[a, 2].wait_recv()
        for k in range(1, self.z_n):
            self.add((self.line[k][0], self.line[k]))
            self.z[k].start()

    def every(self, step):
        step()

    def finish(self, out):
        for k in range(1, self.z_n):
            self.z[k].wait_recv()
        self.add((out, self.line[0] + [self.from_z.at[k - 1] for k in range(1, self.z_n)]))
        for c in self.c + list(self.n.values()) + list(self.z.values()):
            c.wait_send()


def plane_reduce_scratch(fs_n, rows, width):
    z_n, V = fs_n // 2, pltpu.VMEM
    return [V((4, z_n // 2, 2, rows, width), bf16), V((2, 3, z_n // 2, rows, width), bf16), V((z_n - 1, rows, width), bf16)]


def plane_reduce_sems(fs_n):
    z_n, D = fs_n // 2, pltpu.SemaphoreType.DMA
    return [D((4,)), D((4,)), D((6,)), D((6,)), D((z_n - 1,)), D((z_n - 1,))]


HEADS = 8
EPS = 1e-05
MASKED = -1e30
NN = (((1,), (0,)), ((), ()))
NT = (((1,), (1,)), ((), ()))
TN = (((0,), (0,)), ((), ()))


def dot(a, b, dims=NN):
    return lax.dot_general(a, b, dims, preferred_element_type=f32)


def unit(x):
    c = x - jnp.mean(x, -1, keepdims=True)
    r = lax.rsqrt(jnp.mean(c * c, -1, keepdims=True) + EPS)
    return c * r, r


def unit_back(y, u, r, gain):
    yg = y * gain
    return r * (yg - jnp.mean(yg, -1, keepdims=True) - u * jnp.mean(yg * u, -1, keepdims=True))


def blocks(total, size, body):
    lax.fori_loop(0, total // size, lambda i, c: (body(pl.ds(pl.multiple_of(i * size, size), size)), c)[1], 0)


def gelu_parts(v):
    z = jnp.abs(v) * 0.7071067811865476
    t = pl.reciprocal(1.0 + 0.3275911 * z, approx=False)
    e = jnp.exp(-0.5 * (v * v))
    tail = t * (0.127414796 + t * (-0.142248368 + t * (0.7107068705 + t * (-0.7265760135 + t * 0.5307027145)))) * e
    return jnp.where(v >= 0, 1.0 - tail, tail), v * e * 0.3989422804014327


def head_mask(rows, second, width=128):
    lane = lax.broadcasted_iota(jnp.int32, (rows, width), 1)
    return (lane >= width // 2) if second else (lane < width // 2)


def params(cid=None):
    if cid is None:
        return pltpu.CompilerParams(vmem_limit_bytes=62 << 20)
    return pltpu.CompilerParams(collective_id=cid, has_side_effects=True, vmem_limit_bytes=62 << 20)


def head_pair(p):
    return slice(p * 128, p * 128 + 128)


def middle_call(x, o1, cot, smalls, fbias, w, tasks, chunks, unit_rows):
    pairs, samples, d = x.shape
    feats = pairs // tasks
    rows = pairs * samples
    hh = d // 64
    nd = w.shape[0]
    U = unit_rows
    OUT = (5 + chunks) * U
    fl = chunks * d // nd
    x, cot = x.reshape(rows, d), cot.reshape(rows, d)
    RB = 256
    per = RB // samples

    def body(x_ref, back_ref, cot_ref, n_ref, fb_ref, w_ref,
             lo_ref, g1_ref, do1_ref, g_ref,
             x1, a, qkv, p2, o2, acc, dacc, act, gh, dqkv, do2, o1_ref, gn_ref):
        gn_ref[...] = jnp.zeros_like(gn_ref)

        def at_unit(k):
            return pl.ds(pl.multiple_of(k * U, 16), U) if not isinstance(k, int) else slice(k * U, k * U + U)

        def mat(k):
            return w_ref[:, at_unit(k), :].reshape(d, d)

        def out_mat(c):
            if nd == 1:
                return w_ref[0, pl.ds(pl.multiple_of(OUT + c * d, 16), d), :]
            m = nd // chunks
            return w_ref[pl.ds(c * m, m), OUT:OUT + fl, :].reshape(d, d)

        def put(k, at, i, value):
            if nd == 1:
                g_ref[0, pl.ds(pl.multiple_of(16 + k * U + i * 256, 16), 256), :] = value
            else:
                m = 256 // U
                g_ref[pl.ds(i * m, m), pl.ds(pl.multiple_of(16 + k * U, 16), U), :] = value.reshape(m, U, d)

        def put_out(c, i, value):
            if nd == 1:
                g_ref[0, pl.ds(pl.multiple_of(16 + OUT + c * d + i * 256, 16), 256), :] = value
            else:
                m = 256 // fl
                g_ref[pl.ds(c * (nd // chunks) + i * m, m), 16 + OUT:16 + OUT + fl, :] = value.reshape(m, fl, d)

        def tiles(body):
            for i in range(d // 256):
                body(slice(i * 256, i * 256 + 256), i)

        def norm(i):
            return n_ref[2 * i:2 * i + 1, :], n_ref[2 * i + 1:2 * i + 2, :]

        def collect(i, _):
            at = pl.ds(pl.multiple_of(i * RB, RB), RB)
            for p in range(hh // 2):
                o1_ref[at, p * 128:p * 128 + 128] = back_ref[pl.ds(i * per, per), p].reshape(RB, 128)
            return 0

        lax.fori_loop(0, rows // RB, collect, 0)

        def first(at):
            y = x_ref[at, :].astype(f32) + dot(o1_ref[at, :], mat(0))
            x1[at, :] = y
            u, _ = unit(y)
            g, b = norm(1)
            v = (u * g + b).astype(bf16)
            a[at, :] = v
            for i in range(3):
                z = dot(v, mat(1 + i)).astype(bf16)
                qkv[i, at, :] = z * 0.125 if i == 0 else z

        blocks(rows, RB, first)

        half = lax.broadcasted_iota(jnp.int32, (256, 128), 0) // 64
        ones = (lax.rem(half, 2) == lax.broadcasted_iota(jnp.int32, (256, 128), 1) // 64).astype(bf16)

        def head_sums(prods):
            both = []
            for v in prods:
                hi = v.astype(bf16)
                both.append(jnp.concatenate([hi, (v - hi.astype(f32)).astype(bf16)], 1))
            out = dot(jnp.concatenate(both, 0), ones)
            return [out[i * samples:(i + 1) * samples] for i in range(len(prods))]

        def at_slot(t, f):
            return pl.ds(pl.multiple_of((t * feats + f) * samples, samples), samples)

        def mix(t, _):
            for p in range(hh // 2):
                lanes = head_pair(p)
                ks = [qkv[1, at_slot(t, g), lanes].astype(f32) for g in range(feats)]
                vs = [qkv[2, at_slot(t, g), lanes].astype(f32) for g in range(feats)]
                for f in range(feats):
                    q = qkv[0, at_slot(t, f), lanes].astype(f32)
                    sc = head_sums([q * k for k in ks])
                    sc = [v + fb_ref[pl.ds(t * feats + g, 1), :] for g, v in enumerate(sc)]
                    top = functools.reduce(jnp.maximum, sc)
                    sc = [jnp.exp(v - top) for v in sc]
                    inv = 1.0 / sum(sc)
                    sc = [v * inv for v in sc]
                    for g in range(feats):
                        p2[t, p, f, g] = sc[g]
                    o2[at_slot(t, f), lanes] = sum(w * v for w, v in zip(sc, vs)).astype(bf16)
            return 0

        lax.fori_loop(0, tasks, mix, 0)

        def second(at):
            y = x1[at, :] + dot(o2[at, :], mat(4))
            acc[at, :] = y
            u, _ = unit(y)
            g, b = norm(2)
            do2[at, :] = (u * g + b).astype(bf16)
            dacc[at, :] = jnp.zeros((RB, d), f32)

        blocks(rows, RB, second)

        def chunk(c, _):
            def part(at):
                hid = dot(do2[at, :], mat(5 + c)) + n_ref[pl.ds(7 + c, 1), :]
                cdf, pdf = gelu_parts(hid)
                al = (hid * cdf).astype(bf16)
                act[at, :] = al
                gl = ((cdf + pdf) * dot(cot_ref[at, :], out_mat(c), NT)).astype(bf16)
                gh[at, :] = gl
                gn_ref[pl.ds(7 + c, 1), :] += jnp.sum(gl.astype(f32), 0, keepdims=True)
                acc[at, :] += dot(al, out_mat(c))
                dacc[at, :] += dot(gl, mat(5 + c), NT)

            blocks(rows, RB, part)

            def weight(at, i):
                put_out(c, i, dot(act[:, at], cot_ref[...], TN).astype(bf16))
                put(5 + c, at, i, dot(do2[:, at], gh[...], TN).astype(bf16))

            tiles(weight)
            return 0

        lax.fori_loop(0, chunks, chunk, 0)

        def third(at):
            lo_ref[at, :] = (acc[at, :] + n_ref[6:7, :]).astype(bf16)
            u, r = unit(x1[at, :] + dot(o2[at, :], mat(4)))
            y = dacc[at, :]
            gn_ref[4:5, :] += jnp.sum(y * u, 0, keepdims=True)
            gn_ref[5:6, :] += jnp.sum(y, 0, keepdims=True)
            cf = cot_ref[at, :].astype(f32)
            gn_ref[6:7, :] += jnp.sum(cf, 0, keepdims=True)
            g2 = cf + unit_back(y, u, r, norm(2)[0])
            dacc[at, :] = g2
            e2 = g2.astype(bf16)
            act[at, :] = e2
            do2[at, :] = dot(e2, mat(4), NT).astype(bf16)

        blocks(rows, RB, third)

        def weight2(at, i):
            put(4, at, i, dot(o2[:, at], act[...], TN).astype(bf16))

        tiles(weight2)

        def unmix(t, _):
            for p in range(hh // 2):
                lanes = head_pair(p)
                ks = [qkv[1, at_slot(t, g), lanes].astype(f32) for g in range(feats)]
                vs = [qkv[2, at_slot(t, g), lanes].astype(f32) for g in range(feats)]
                dk, dv = [0.0] * feats, [0.0] * feats
                for f in range(feats):
                    q = qkv[0, at_slot(t, f), lanes].astype(f32)
                    gr = do2[at_slot(t, f), lanes].astype(f32)
                    dp = head_sums([gr * v for v in vs])
                    ws = [p2[t, p, f, g] for g in range(feats)]
                    mean = sum(w * v for w, v in zip(ws, dp))
                    ds = [(w * (v - mean)).astype(bf16).astype(f32) for w, v in zip(ws, dp)]
                    dqkv[0, at_slot(t, f), lanes] = (sum(v * k for v, k in zip(ds, ks)) * 0.125).astype(bf16)
                    for g in range(feats):
                        dk[g] += ds[g] * q
                        dv[g] += ws[g] * gr
                for g in range(feats):
                    dqkv[1, at_slot(t, g), lanes] = dk[g].astype(bf16)
                    dqkv[2, at_slot(t, g), lanes] = dv[g].astype(bf16)
            return 0

        lax.fori_loop(0, tasks, unmix, 0)

        def fourth(i, _):
            at = pl.ds(pl.multiple_of(i * RB, RB), RB)
            u, r = unit(x1[at, :])
            y = dot(dqkv[0, at, :], mat(1), NT) + dot(dqkv[1, at, :], mat(2), NT) + dot(dqkv[2, at, :], mat(3), NT)
            gn_ref[2:3, :] += jnp.sum(y * u, 0, keepdims=True)
            gn_ref[3:4, :] += jnp.sum(y, 0, keepdims=True)
            g1 = dacc[at, :] + unit_back(y, u, r, norm(1)[0])
            g1_ref[at, :] = g1
            e1 = g1.astype(bf16)
            act[at, :] = e1
            do = dot(e1, mat(0), NT).astype(bf16)
            for p in range(hh // 2):
                do1_ref[pl.ds(i * per, per), p] = do[:, p * 128:p * 128 + 128].reshape(per, samples, 128)
            return 0

        lax.fori_loop(0, rows // RB, fourth, 0)

        def weight3(at, i):
            put(0, at, i, dot(o1_ref[:, at], act[...], TN).astype(bf16))
            for j in range(3):
                put(1 + j, at, i, dot(a[:, at], dqkv[j], TN).astype(bf16))

        tiles(weight3)
        g_ref[:, 0:16, :] = jnp.broadcast_to(gn_ref[...].astype(bf16), (nd, 16, d))

    V = pltpu.VMEM
    S = jax.ShapeDtypeStruct
    return pl.pallas_call(
        body,
        out_shape=[S((rows, d), bf16), S((rows, d), f32), S((pairs, hh // 2, samples, 128), bf16),
                   S((nd, 16 + OUT + fl, d), bf16)],
        in_specs=[VM] * 6, out_specs=[VM] * 4,
        scratch_shapes=[V((rows, d), f32), V((rows, d), bf16), V((3, rows, d), bf16), V((tasks, hh // 2, feats, feats, samples, 128), f32), V((rows, d), bf16),
                        V((rows, d), f32), V((rows, d), f32), V((rows, d), bf16), V((rows, d), bf16), V((3, rows, d), bf16),
                        V((rows, d), bf16), V((rows, d), bf16), V((16, d), f32)],
        compiler_params=params(), name="middle",
    )(x, o1, cot, smalls, fbias, w)
BQ = 1024


class Turns:
    def __init__(self, fs_n, parts, src, dst, local_sem, ss, rs):
        me_d, me_f = lax.axis_index("dp"), lax.axis_index("fsdp")
        self.sets = []
        for p in range(parts):
            own = pltpu.make_async_copy(src(p, me_f), dst(p, me_f), local_sem.at[p])
            far = []
            for k in range(1, fs_n):
                to = mod(me_f + k, fs_n)
                i = p * (fs_n - 1) + k - 1
                far.append(rcopy(src(p, to), dst(p, me_f), ss.at[i], rs.at[i], (me_d, to)))
            self.sets.append((own, far))

    def start(self, p):
        own, far = self.sets[p]
        for c in far:
            c.start()
        own.start()

    def wait_recv(self, p):
        own, far = self.sets[p]
        own.wait()
        for c in far:
            c.wait_recv()

    def wait_send(self):
        for _, far in self.sets:
            for c in far:
                c.wait_send()


def turn_sems(fs_n, parts):
    D = pltpu.SemaphoreType.DMA
    return [D((parts,)), D((parts * (fs_n - 1),)), D((parts * (fs_n - 1),))]


def units(ref, start, size):
    v = ref[..., start:start + size, :]
    return v.reshape(-1, v.shape[-1])


def forward_kernel(x, packs, plain, keybias, dp_n, fs_n, rl, dh):
    slots, samples, d = x.shape
    rows = slots * samples
    heads = dh // 64
    hp = heads // 2
    np_ = len(packs)

    def body(*refs):
        it = iter(refs)
        x_ref, kb_ref = next(it), next(it)
        pack_refs = [next(it) for _ in range(np_)]
        w_ref, sm_ref = (None, None) if np_ else (next(it), next(it))
        back_ref, xg_ref, o_ref, qkv_ref, l_ref = (next(it) for _ in range(5))
        g_refs = [next(it) for _ in range(np_)]
        if np_:
            sm_ref = next(it)
        acted, vt, ot = next(it), next(it), next(it)
        swap_s = [next(it) for _ in range(3)]
        turn_s = [next(it) for _ in range(3)]
        gat_s = [[next(it) for _ in range(7)] for _ in range(np_)]

        greet(dp_n, fs_n, np_ > 0)
        gathers = [PlaneGather(fs_n, pack_refs[i], g_refs[i], *gat_s[i]) for i in range(np_)]
        swap = Swap(fs_n, x_ref, xg_ref, *swap_s)
        z_n = fs_n // 2
        if np_:
            gathers[0].start()
        swap.start()
        if np_:
            gathers[1].start()
            for k in range(1, z_n):
                gathers[0].spread(k)
            for k in range(z_n):
                gathers[0].hand_on(k)
            for k in range(1, z_n):
                gathers[1].spread(k)
            for k in range(z_n):
                gathers[0].corner(k)
        swap.wait()
        if np_:
            gathers[0].wait()
            sm_ref[...] = jnp.sum(units3(g_refs[0], 0, 16).astype(f32), 0)
        gain, bias = sm_ref[0:1, :], sm_ref[1:2, :]
        per = 256 // samples if samples < 256 else 1
        for s in range(slots // per):
            at = slice(s * per * samples, (s + 1) * per * samples)
            u, _ = unit(xg_ref[s * per:(s + 1) * per].reshape(per * samples, d).astype(f32))
            acted[at, :] = (u * gain + bias).astype(bf16)
        for i in range(3):
            w = units(g_refs[0], 16 + i * rl, rl) if np_ else w_ref[i]

            def project(at):
                y = dot(acted[at, :], w).astype(bf16)
                qkv_ref[i, at, :] = y * 0.125 if i == 0 else y

            blocks(rows, 256, project)

        turns = Turns(fs_n, hp, lambda p, j: o_ref.at[p, pl.ds(pl.multiple_of(j * samples, samples), samples)],
                      lambda p, j: back_ref.at[j, p], *turn_s)
        for p in range(hp):
            at = head_pair(p)
            vt[...] = qkv_ref[2, :, at].astype(f32).T.astype(bf16)
            for h in range(2):
                def part(i, _):
                    qa = pl.ds(pl.multiple_of(i * BQ, BQ), BQ)
                    q = qkv_ref[0, qa, at]
                    q = jnp.where(head_mask(BQ, h), q, jnp.zeros_like(q))
                    s = dot(qkv_ref[1, :, at], q, NT) + kb_ref[:, 0:1]
                    m = jnp.max(s, 0, keepdims=True)
                    e = jnp.exp(s - m)
                    tot = jnp.sum(e, 0, keepdims=True)
                    o = dot(vt[h * 64:h * 64 + 64, :], e.astype(bf16))
                    ot[h * 64:h * 64 + 64, qa] = o * (1.0 / tot)
                    l_ref[p * 2 + h:p * 2 + h + 1, qa] = m + jnp.log(tot)
                    return 0
                lax.fori_loop(0, rows // BQ, part, 0)
            o_ref[p, :, :] = ot[...].T.astype(bf16)
            turns.start(p)
            if np_ and p == 0:
                gathers[1].hand_on(0)
            if np_ and p == 2:
                gathers[1].hand_on(1)
        if np_:
            for k in range(2, z_n):
                gathers[1].hand_on(k)
            for k in range(z_n):
                gathers[1].corner(k)
        for p in range(hp):
            turns.wait_recv(p)
        turns.wait_send()
        if np_:
            gathers[1].wait()

    def units3(ref, start, size):
        v = ref[..., start:start + size, :]
        return v.reshape(-1, size, v.shape[-1])

    S, V = jax.ShapeDtypeStruct, pltpu.VMEM
    outs = [S((slots, hp, samples, 128), bf16), S((slots, samples, d), bf16), S((hp, rows, 128), bf16), S((3, rows, dh), bf16),
            S((heads, rows), f32)]
    outs += [S((dp_n, fs_n // 2, 2) + p.shape, bf16) for p in packs]
    args = [x, keybias] + list(packs)
    if np_:
        outs.append(S((16, d), f32))
    else:
        args += list(plain)
    return pl.pallas_call(
        body, out_shape=outs, in_specs=[VM] * len(args), out_specs=[ANY if np_ and i == 6 else VM for i in range(len(outs))],
        scratch_shapes=[V((rows, d), bf16), V((128, rows), bf16), V((128, rows), f32)] + swap_sems(fs_n) + turn_sems(fs_n, hp)
        + plane_gather_sems(fs_n) * np_,
        compiler_params=params(1), name="forward",
    )(*args)


def backward_kernel(do1, xg, qkv, o, lse, w, smalls, keybias, g1, gm, dp_n, fs_n, rl, dh, tasks, packed):
    slots, samples, d = xg.shape
    rows = slots * samples
    heads = dh // 64
    hp = heads // 2

    def body(*refs):
        it = iter(refs)
        do_in, xg_ref, qkv_ref, o_ref, l_ref, w_ref, n_ref, kb_ref = (next(it) for _ in range(8))
        g1_ref, gm_ref = (next(it), next(it)) if packed else (None, None)
        if packed:
            tg_ref, sm_ref, ss_ref = (next(it) for _ in range(3))
        else:
            dr_ref, gw_ref, gn_ref = (next(it) for _ in range(3))
        do, delta, kt, dqt, dk, dv, dqkv, acted, gn, dx = (next(it) for _ in range(10))
        turn_s = [next(it) for _ in range(3)]
        back_s = [next(it) for _ in range(3)]
        if packed:
            gs, dr_ref = next(it), next(it)
            rm = [next(it) for _ in range(11)]
            rs = [next(it) for _ in range(11)]

        greet(dp_n, fs_n, packed)
        turns = Turns(fs_n, hp, lambda p, j: do_in.at[j, p], lambda p, j: do.at[j, p], *turn_s)
        for p in range(hp):
            turns.start(p)
        if packed:
            red = PlaneReduce(fs_n, gm_ref, rm[:4], rm[4:])
            red_s = PlaneReduce(fs_n, gs, rs[:4], rs[4:])
            red.start()
            for k in red.order():
                red.first(k)
        gain, bias = n_ref[0:1, :], n_ref[1:2, :]
        lane = lax.broadcasted_iota(jnp.int32, (8, 128), 1) // 64
        pick = (lane == lax.broadcasted_iota(jnp.int32, (8, 128), 0)).astype(f32)
        per = BQ // samples if samples < BQ else 1

        def grad_rows(i, p):
            return do[pl.ds(i * per, per), p].reshape(per * samples, 128)

        n = per * samples
        for p in range(hp):
            at = head_pair(p)
            kt[...] = qkv_ref[1, :, at].astype(f32).T.astype(bf16)
            dk[...] = jnp.zeros_like(dk)
            dv[...] = jnp.zeros_like(dv)
            turns.wait_recv(p)

            def deltas(i, _):
                qa = pl.ds(pl.multiple_of(i * n, n), n)
                prod = grad_rows(i, p).astype(f32) * o_ref[p, qa, :].astype(f32)
                delta[:, qa] = lax.dot_general(pick, prod, NT, precision=lax.Precision.HIGHEST, preferred_element_type=f32)
                return 0

            lax.fori_loop(0, rows // n, deltas, 0)
            for h in range(2):
                def part(i, _):
                    qa = pl.ds(pl.multiple_of(i * n, n), n)
                    mask = head_mask(n, h)
                    q = qkv_ref[0, qa, at]
                    q = jnp.where(mask, q, jnp.zeros_like(q))
                    g = grad_rows(i, p)
                    g = jnp.where(mask, g, jnp.zeros_like(g))
                    s = dot(qkv_ref[1, :, at], q, NT) + kb_ref[:, 0:1]
                    e = jnp.exp(s - l_ref[p * 2 + h:p * 2 + h + 1, qa])
                    ds = (e * (dot(qkv_ref[2, :, at], g, NT) - delta[h:h + 1, qa])).astype(bf16)
                    dv[...] += dot(e.astype(bf16), g)
                    dk[...] += dot(ds, q)
                    dqt[h * 64:h * 64 + 64, qa] = dot(kt[h * 64:h * 64 + 64, :], ds) * 0.125
                    return 0
                lax.fori_loop(0, rows // n, part, 0)
            dqkv[0, :, at] = dqt[...].T.astype(bf16)
            dqkv[1, :, at] = dk[...].astype(bf16)
            dqkv[2, :, at] = dv[...].astype(bf16)
            if packed:
                if p == hp - 2:
                    for k in red.order():
                        red.second(k)
                if p == hp - 1:
                    for k in red.order():
                        red.third(k)

        def mats(i):
            return units(w_ref, 16 + i * rl, rl) if packed else w_ref[i]

        per2 = 256 // samples if samples < 256 else 1
        n2 = per2 * samples
        gn[...] = jnp.zeros_like(gn)

        def act_rows(i):
            at = pl.ds(pl.multiple_of(i * n2, n2), n2)
            u, r = unit(xg_ref[pl.ds(i * per2, per2)].reshape(n2, d).astype(f32))
            return at, u, r

        def first(i, _):
            at, u, r = act_rows(i)
            acted[at, :] = (u * gain + bias).astype(bf16)
            return 0

        lax.fori_loop(0, rows // n2, first, 0)
        for i in range(3):
            if packed:
                y = dot(acted[...], dqkv[i], TN).astype(bf16)
                gs[:, :, :, 16 + i * rl:16 + (i + 1) * rl, :] = y.reshape(gs.shape[:3] + (rl, d))
            else:
                gw_ref[i] = dot(acted[...], dqkv[i], TN).astype(bf16)

        back = Turns(fs_n, 1, lambda p, j: dx.at[j], lambda p, j: dr_ref.at[j], *back_s)

        def sums(i, _):
            at, u, r = act_rows(i)
            y = dot(dqkv[0, at, :], mats(0), NT) + dot(dqkv[1, at, :], mats(1), NT) + dot(dqkv[2, at, :], mats(2), NT)
            gn[0:1, :] += jnp.sum(y * u, 0, keepdims=True)
            gn[1:2, :] += jnp.sum(y, 0, keepdims=True)
            dx[pl.ds(i * per2, per2)] = unit_back(y, u, r, gain).astype(bf16).reshape(per2, samples, d)
            return 0

        lax.fori_loop(0, rows // n2, sums, 0)
        back.start(0)
        if packed:
            small = jnp.concatenate([gn[...].astype(bf16), jnp.zeros_like(gn).astype(bf16)], 0)
            gs[:, :, :, 0:16, :] = jnp.broadcast_to(small, gs.shape[:3] + (16, d))
            red_s.start()
            for k in red_s.order():
                red_s.first(k)
            red.finish(sm_ref)
            for k in red_s.order():
                red_s.second(k)
            for k in red_s.order():
                red_s.third(k)
            back.wait_recv(0)
            feats = slots // tasks
            for s in range(slots):
                t, f = s // feats, s % feats
                for i in range(d // 128):
                    at = pl.ds(((t * samples * (d // 128)) + i) * feats + f, samples, stride=feats * (d // 128))
                    tg_ref[at, :] = g1_ref[s * samples:(s + 1) * samples, head_pair(i)] + dr_ref[s, :, head_pair(i)].astype(f32)
            red_s.finish(ss_ref)
        else:
            gn_ref[...] = gn[...]
            back.wait_recv(0)
        back.wait_send()
        turns.wait_send()

    S, V = jax.ShapeDtypeStruct, pltpu.VMEM
    args = [do1, xg, qkv, o, lse, w, smalls, keybias]
    scratch = [V((slots, hp, samples, 128), bf16), V((8, rows), f32), V((128, rows), bf16), V((128, rows), f32), V((rows, 128), f32),
               V((rows, 128), f32), V((3, rows, dh), bf16), V((rows, d), bf16), V((8, d), f32), V((slots, samples, d), bf16)]
    scratch += turn_sems(fs_n, hp) + turn_sems(fs_n, 1)
    if packed:
        args += [g1, gm]
        mrows, srows = gm.shape[3], 16 + 3 * rl
        outs = [S((rows * d // 128, 128), f32), S((mrows, d), f32), S((srows, d), f32)]
        scratch += [V((dp_n, fs_n // 2, 2, srows, d), bf16), V((slots, samples, d), bf16)]
        scratch += plane_reduce_scratch(fs_n, mrows, d) + plane_reduce_scratch(fs_n, srows, d)
    else:
        outs = [S((slots, samples, d), bf16), S((3, d, dh), bf16), S((8, d), f32)]
    return pl.pallas_call(
        body, out_shape=outs, in_specs=[ANY if packed and i == 9 else VM for i in range(len(args))], out_specs=[VM] * len(outs), scratch_shapes=scratch,
        compiler_params=params(2), name="backward",
    )(*args)
def ones_pairs():
    half = lax.broadcasted_iota(jnp.int32, (256, 128), 0) // 64
    return (lax.rem(half, 2) == lax.broadcasted_iota(jnp.int32, (256, 128), 1) // 64).astype(bf16)


def head_sums(prods, ones):
    both = []
    for v in prods:
        hi = v.astype(bf16)
        both.append(jnp.concatenate([hi, (v - hi.astype(f32)).astype(bf16)], 1))
    out = dot(jnp.concatenate(both, 0), ones)
    n = prods[0].shape[0]
    return [out[i * n:(i + 1) * n] for i in range(len(prods))]


def key_bias(ref, counts, feats):
    count = counts[lax.axis_index("fsdp") // feats]
    rows = lax.broadcasted_iota(jnp.int32, ref.shape, 0)
    ref[...] = jnp.where(rows < count, 0.0, MASKED)


def rows_at(i, n):
    return pl.ds(pl.multiple_of(i * n, n), n)


def turn_rows(pieces, wide, out, tasks, feats, samples):
    blocks(wide.shape[0], 512, lambda at: wide.__setitem__((at, slice(None)), pieces[at, :].astype(f32)))
    parts = wide.shape[0] // (tasks * samples * feats)
    for s in range(tasks * feats):
        for i in range(parts):
            start = (s // feats * samples * parts + i) * feats + s % feats
            out(s, head_pair(i), wide[pl.ds(start, samples, stride=feats * parts), :].astype(bf16))


def first_kernel(tok, cot, scounts, fcounts, small_parts, s_qkv, s_out, f_qkv, f_out, m_in, m_out, tasks, samples, fs_n):
    dp_n = 4
    d = s_out.shape[1]
    slots = tok.shape[0] // (samples * d // 128)
    feats = slots // tasks
    rows = slots * samples
    hp = d // 128
    rl = s_out.shape[0]
    fl = m_out.shape[0]
    chunks = m_in.shape[1] // d
    z_n = fs_n // 2
    ra, r1, r2 = 16 + 3 * rl, 5 * rl, chunks * rl + fl
    per = 512 // samples

    def body(tok_ref, cot_ref, sc_ref, fc_ref, norms, ob, ib, sq, so, fq, fo, mi, mo,
             xg_h, qkv_h, o_h, l_ref, ga_h, w1_h, w2, sm, x1_h, o2_h, a3_h, qkv2_h, p2_h, back_h, cot_h,
             wide, x_ref, turned, xg, qkv, o_ref, ga, w1, x1, o2, a3, qkv2, p2, back_ref,
             pa, pb1, pb2, kb, acted, vt, ot, small, out_sem, p2_sem, a3_sem, *sems):
        swap_s, turn_s = sems[:3], sems[3:6]
        gat_s = [sems[6 + 7 * i:13 + 7 * i] for i in range(3)]
        me = lax.axis_index("dp") * fs_n + lax.axis_index("fsdp")
        def placed(ref, first):
            n = ref.shape[1]
            hot = lax.broadcasted_iota(jnp.int32, (n, d), 1) == lax.broadcasted_iota(jnp.int32, (n, d), 0) + first
            return dot(ref[...], hot.astype(bf16))

        inner = lax.rem(me * fl, d)
        row = lax.broadcasted_iota(jnp.int32, (16, d), 0)
        small[...] = jnp.where(row == 7 + me * fl // d, placed(ib, inner), 0.0)
        small[0:6, :] = placed(norms, me * rl)
        small[6:7, :] = placed(ob, me * rl)
        pa[0:16, :] = small[...].astype(bf16)
        for i in range(3):
            pa[16 + i * rl:16 + (i + 1) * rl, :] = sq[i]
            pb1[(1 + i) * rl:(2 + i) * rl, :] = fq[i]
        pb1[0:rl, :] = so[...]
        pb1[4 * rl:5 * rl, :] = fo[...]
        for c in range(chunks):
            pb2[c * rl:(c + 1) * rl, :] = mi[:, c * d:(c + 1) * d]
        pb2[chunks * rl:, :] = mo[...]

        pairs_out = [(xg, xg_h), (qkv, qkv_h), (o_ref, o_h), (ga, ga_h), (w1, w1_h), (x1, x1_h), (o2, o2_h), (qkv2, qkv2_h), (back_ref, back_h), (turned, cot_h)]
        outs_c = [pltpu.make_async_copy(v, h, out_sem.at[i]) for i, (v, h) in enumerate(pairs_out)]
        out_xg, out_qkv, out_o, out_ga, out_w1, out_x1, out_o2, out_qkv2, out_back, out_cot = outs_c

        def out_p2(t):
            return pltpu.make_async_copy(p2.at[t], p2_h.at[t], p2_sem.at[t])

        def out_a3(i):
            return pltpu.make_async_copy(a3.at[rows_at(i, 512)], a3_h.at[rows_at(i, 512)], a3_sem.at[i])

        greet(dp_n, fs_n)
        A = PlaneGather(fs_n, pa, ga, *gat_s[0])
        B = PlaneGather(fs_n, pb1, w1, *gat_s[1])
        C = PlaneGather(fs_n, pb2, w2, *gat_s[2])
        swap = Swap(fs_n, x_ref, xg, *swap_s)
        turns = Turns(fs_n, hp, lambda p, j: o_ref.at[p, rows_at(j, samples)], lambda p, j: back_ref.at[j, p], *turn_s)
        later = list(range(1, z_n))
        A.start()
        turn_rows(tok_ref, wide, lambda s, lanes, v: x_ref.__setitem__((s, slice(None), lanes), v), tasks, feats, samples)
        swap.start()
        for G in (A, B, C):
            G.begin()
        key_bias(kb, sc_ref, feats)
        for k in later:
            A.spread(k)
        for k in range(z_n):
            A.hand_on(k)
        for k in range(z_n):
            A.corner(k)
        turn_rows(cot_ref, wide, lambda s, lanes, v: turned.__setitem__((slice(s * samples, (s + 1) * samples), lanes), v), tasks, feats, samples)
        out_cot.start()
        A.wait()
        out_ga.start()
        total = ga[:, :, :, 0:16, :].astype(f32)
        sm[...] = jnp.sum(total.reshape(-1, 16, d), 0)
        swap.wait()
        B.start()
        C.start()
        out_xg.start()

        def act(i, _):
            u, _r = unit(xg[pl.ds(i * per, per)].reshape(512, d).astype(f32))
            acted[rows_at(i, 512), :] = (u * sm[0:1, :] + sm[1:2, :]).astype(bf16)
            return 0

        lax.fori_loop(0, rows // 512, act, 0)
        for i in range(3):
            w = units(ga, 16 + i * rl, rl)

            def project(at):
                y = dot(acted[at, :], w).astype(bf16)
                qkv[i, at, :] = y * 0.125 if i == 0 else y

            blocks(rows, 512, project)
        out_qkv.start()
        for k in later:
            B.spread(k)

        for p in range(hp):
            at = head_pair(p)
            vt[...] = qkv[2, :, at].astype(f32).T.astype(bf16)
            for h in range(2):
                def part(i, _):
                    qa = rows_at(i, BQ)
                    q = qkv[0, qa, at]
                    q = jnp.where(head_mask(BQ, h), q, jnp.zeros_like(q))
                    s = dot(qkv[1, :, at], q, NT) + kb[:, 0:1]
                    m = jnp.max(s, 0, keepdims=True)
                    e = jnp.exp(s - m)
                    tot = jnp.sum(e, 0, keepdims=True)
                    o = dot(vt[h * 64:h * 64 + 64, :], e.astype(bf16))
                    ot[h * 64:h * 64 + 64, qa] = o * (1.0 / tot)
                    l_ref[p * 2 + h:p * 2 + h + 1, qa] = m + jnp.log(tot)
                    return 0
                lax.fori_loop(0, rows // BQ, part, 0)
            o_ref[p, :, :] = ot[...].T.astype(bf16)
            turns.start(p)
            if p == 0:
                for k in range(z_n):
                    B.hand_on(k)
                for k in later:
                    C.spread(k)
            if p == 1:
                for k in range(z_n):
                    B.corner(k)
            if p == 2:
                C.hand_on(0)
        out_o.start()
        B.wait()
        out_w1.start()
        for k in range(1, z_n):
            C.hand_on(k)
        for p in range(hp):
            turns.wait_recv(p)
        out_back.start()

        def first(i, _):
            at = rows_at(i, 512)
            o1 = jnp.concatenate([back_ref[pl.ds(i * per, per), p].reshape(512, 128) for p in range(hp)], 1)
            y = x_ref[pl.ds(i * per, per)].reshape(512, d).astype(f32) + dot(o1, units(w1, 0, rl))
            x1[at, :] = y
            u, _r = unit(y)
            v = (u * sm[2:3, :] + sm[3:4, :]).astype(bf16)
            for j in range(3):
                z = dot(v, units(w1, (1 + j) * rl, rl)).astype(bf16)
                qkv2[j, at, :] = z * 0.125 if j == 0 else z
            return 0

        lax.fori_loop(0, rows // 512, first, 0)
        for k in range(z_n):
            C.corner(k)
        out_x1.start()
        out_qkv2.start()
        ones = ones_pairs()

        def mix(t, _):
            slot = lambda f: rows_at(t * feats + f, samples)
            for p in range(hp):
                lanes = head_pair(p)
                ks = [qkv2[1, slot(g), lanes].astype(f32) for g in range(feats)]
                vs = [qkv2[2, slot(g), lanes].astype(f32) for g in range(feats)]
                for f in range(feats):
                    q = qkv2[0, slot(f), lanes].astype(f32)
                    sc = head_sums([q * k for k in ks], ones)
                    sc = [v + jnp.where(g < fc_ref[t], 0.0, MASKED) for g, v in enumerate(sc)]
                    top = functools.reduce(jnp.maximum, sc)
                    sc = [jnp.exp(v - top) for v in sc]
                    inv = 1.0 / sum(sc)
                    sc = [v * inv for v in sc]
                    for g in range(feats):
                        p2[t, p, f, g] = sc[g].astype(bf16)
                    o2[slot(f), lanes] = sum(w * v for w, v in zip(sc, vs)).astype(bf16)
            out_p2(t).start()
            return 0

        lax.fori_loop(0, tasks, mix, 0)
        out_o2.start()

        def second(i, _):
            at = rows_at(i, 512)
            u, _r = unit(x1[at, :] + dot(o2[at, :], units(w1, 4 * rl, rl)))
            a3[at, :] = (u * sm[4:5, :] + sm[5:6, :]).astype(bf16)
            out_a3(i).start()
            return 0

        lax.fori_loop(0, rows // 512, second, 0)
        turns.wait_send()
        C.wait()
        for c in outs_c:
            c.wait()
        for t in range(tasks):
            out_p2(t).wait()
        for i in range(rows // 512):
            out_a3(i).wait()

    S, V, D = jax.ShapeDtypeStruct, pltpu.VMEM, pltpu.SemaphoreType.DMA
    SM = pl.BlockSpec(memory_space=pltpu.SMEM)
    g = (dp_n, z_n, 2)
    outs = [S((slots, samples, d), bf16), S((3, rows, d), bf16), S((hp, rows, 128), bf16), S((2 * hp, rows), f32),
            S(g + (ra, d), bf16), S(g + (r1, d), bf16), S(g + (r2, d), bf16), S((16, d), f32), S((rows, d), f32), S((rows, d), bf16),
            S((rows, d), bf16), S((3, rows, d), bf16), S((tasks, hp, feats, feats, samples, 128), bf16), S((slots, hp, samples, 128), bf16),
            S((rows, d), bf16)]
    return pl.pallas_call(
        body, out_shape=outs, in_specs=[VM, VM, SM, SM] + [VM] * 9, out_specs=[VM if i in (3, 7) else ANY for i in range(len(outs))],
        scratch_shapes=[V(tok.shape, f32), V((slots, samples, d), bf16), V((rows, d), bf16)] + [V(outs[i].shape, outs[i].dtype) for i in (0, 1, 2, 4, 5, 8, 9, 10, 11, 12, 13)] + [V((ra, d), bf16), V((r1, d), bf16), V((r2, d), bf16), V((rows, 128), f32), V((rows, d), bf16), V((128, rows), bf16),
                        V((128, rows), f32), V((16, d), f32), D((10,)), D((tasks,)), D((rows // 512,))] + swap_sems(fs_n) + turn_sems(fs_n, hp) + plane_gather_sems(fs_n) * 3,
        compiler_params=params(1), name="first",
    )(tok, cot, scounts, fcounts, *small_parts, s_qkv, s_out, f_qkv, f_out, m_in, m_out)


def second_kernel(scounts, saved, tasks, rl, fl, fs_n):
    xg, qkv, o, lse, ga, w1, w2, sm, x1, o2, a3, qkv2, p2, back, cot = saved
    slots, samples, d = xg.shape
    feats = slots // tasks
    rows = slots * samples
    hp = d // 128
    z_n = fs_n // 2
    chunks = (w2.shape[3] - fl) // rl
    r1, r2, rs = 16 + 5 * rl, chunks * rl + fl, 16 + 3 * rl
    RB = 256
    per = RB // samples
    bq = 512
    pq = bq // samples

    def body(sc_ref, l_ref, sm_ref, cot_h, w2_h, x1_h, o2_h, a3_h,
             xg_h, qkv_h, o_h, ga_h, w1_h, qkv2_h, p2_h, back_h,
             g1_h, lo_h, dr, out2, out1, outs_,
             g1, lo, cot_ref, w2_ref, x1_ref, o2_ref, a3_ref, o_, w1_, q_, p2_, bk, acc, act, gh, ev, a2, do2, dqkv, G2, G1, GS, do, do1, delta, kt, dqt, kb, gn,
             c2, n2, z2, c1, n1, z1, c0, n0, z0, load_sem, *sems):
        turn_s, back_s = sems[:3], sems[3:6]
        red_s = [sems[6 + 6 * i:12 + 6 * i] for i in range(3)]
        me_f = lax.axis_index("fsdp")
        me_z, me_c = me_f // 2, mod(me_f, 2)
        load = lambda i, src, dst: pltpu.make_async_copy(src, dst, load_sem.at[i])
        get_w1 = load(0, w1_h, w1_)
        get_q2 = load(1, qkv2_h, q_)
        get_p2 = load(2, p2_h, p2_)
        get_bk = load(3, back_h, bk)
        xg_ = a3_ref
        dk, dv = acc.at[:, 0:128], acc.at[:, 128:256]
        get_xg = load(4, xg_h, xg_)
        get_o = load(5, o_h, o_)
        get_q1 = load(6, qkv_h, q_)
        ga_ = w1_.at[:, :, :, 0:rs, :]
        get_ga = load(7, ga_h, ga_)
        heads_in = [load(8 + i, a, b) for i, (a, b) in enumerate([(a3_h, a3_ref), (w2_h, w2_ref), (cot_h, cot_ref), (x1_h, x1_ref), (o2_h, o2_ref)])]
        put_g1 = load(13, g1, g1_h)
        put_lo = load(14, lo, lo_h)
        for c in heads_in + [get_w1, get_q2, get_p2, get_bk, get_o]:
            c.start()
        key_bias(kb, sc_ref, feats)
        gn[...] = jnp.zeros_like(gn)
        for i in range(rows // RB):
            acc[i * RB:(i + 1) * RB, :] = jnp.zeros((RB, d), f32)
            g1[i * RB:(i + 1) * RB, :] = jnp.zeros((RB, d), f32)
        greet(4, fs_n)
        for c in heads_in[:3]:
            c.wait()

        def mat(k):
            return units(w1_, k * rl, rl)

        def in_mat(c):
            return w2_ref[:, :, :, pl.ds(pl.multiple_of(c * rl, rl), rl), :].reshape(d, d)

        def out_mat(c):
            return w2_ref[pl.ds(c, 1), :, :, chunks * rl:, :].reshape(d, d)

        def put(g, start, i, value):
            g[2 * i:2 * i + 2, :, :, :, pl.ds(start, rl), :] = value.reshape(2, z_n // 2, 2, 2, rl, d)

        halves = [(slice(i * 256, i * 256 + 256), i) for i in range(d // 256)]

        def chunk(c, _):
            def part(at):
                hid = dot(a3_ref[at, :], in_mat(c)) + sm_ref[pl.ds(7 + c, 1), :]
                cdf, pdf = gelu_parts(hid)
                al = (hid * cdf).astype(bf16)
                act[at, :] = al
                gl = ((cdf + pdf) * dot(cot_ref[at, :], out_mat(c), NT)).astype(bf16)
                gh[at, :] = gl
                gn[pl.ds(7 + c, 1), :] += jnp.sum(gl.astype(f32), 0, keepdims=True)
                acc[at, :] += dot(al, out_mat(c))
                g1[at, :] += dot(gl, in_mat(c), NT)

            blocks(rows, 512, part)
            for at, i in halves:
                value = dot(act[:, at], cot_ref[...], TN).astype(bf16)
                G2[pl.ds(c, 1), i:i + 1, :, :, chunks * rl:, :] = value.reshape(1, 1, 2, 2, fl, d)
                put(G2, pl.multiple_of(c * rl, rl), i, dot(a3_ref[:, at], gh[...], TN).astype(bf16))
            return 0

        lax.fori_loop(0, chunks, chunk, 0)
        red2 = PlaneReduce(fs_n, G2, (c2, n2, z2), red_s[0])
        red2.start()
        for c in heads_in[3:]:
            c.wait()
        get_w1.wait()

        def third(at):
            x2 = x1_ref[at, :] + dot(o2_ref[at, :], mat(4))
            lo[at, :] = (x2 + acc[at, :] + sm_ref[6:7, :]).astype(bf16)
            u, r = unit(x2)
            y = g1[at, :]
            gn[4:5, :] += jnp.sum(y * u, 0, keepdims=True)
            gn[5:6, :] += jnp.sum(y, 0, keepdims=True)
            cf = cot_ref[at, :].astype(f32)
            gn[6:7, :] += jnp.sum(cf, 0, keepdims=True)
            g2 = cf + unit_back(y, u, r, sm_ref[4:5, :])
            g1[at, :] = g2
            e2 = g2.astype(bf16)
            ev[at, :] = e2
            do2[at, :] = dot(e2, mat(4), NT).astype(bf16)

        blocks(rows, 512, third)
        put_lo.start()
        for at, i in halves:
            put(G1, 16 + 4 * rl, i, dot(o2_ref[:, at], ev[...], TN).astype(bf16))
        red2.every(red2.first)
        get_q2.wait()
        get_p2.wait()
        ones = ones_pairs()

        def unmix(t, _):
            slot = lambda f: rows_at(t * feats + f, samples)
            for p in range(hp):
                lanes = head_pair(p)
                ks = [q_[1, slot(g), lanes].astype(f32) for g in range(feats)]
                vs = [q_[2, slot(g), lanes].astype(f32) for g in range(feats)]
                dks, dvs = [0.0] * feats, [0.0] * feats
                for f in range(feats):
                    q = q_[0, slot(f), lanes].astype(f32)
                    gr = do2[slot(f), lanes].astype(f32)
                    dp = head_sums([gr * v for v in vs], ones)
                    ws = [p2_[t, p, f, g].astype(f32) for g in range(feats)]
                    mean = sum(w * v for w, v in zip(ws, dp))
                    ds = [(w * (v - mean)).astype(bf16).astype(f32) for w, v in zip(ws, dp)]
                    dqkv[0, slot(f), lanes] = (sum(v * k for v, k in zip(ds, ks)) * 0.125).astype(bf16)
                    for g in range(feats):
                        dks[g] += ds[g] * q
                        dvs[g] += ws[g] * gr
                for g in range(feats):
                    dqkv[1, slot(g), lanes] = dks[g].astype(bf16)
                    dqkv[2, slot(g), lanes] = dvs[g].astype(bf16)
            return 0

        lax.fori_loop(0, tasks, unmix, 0)
        get_q1.start()

        def far(i, r):
            return mod(me_z + i, z_n) * 2 + mod(me_c + r, 2)

        me_d = lax.axis_index("dp")
        sends = {}
        for i in range(z_n):
            for r in range(2):
                for p in range(hp):
                    n = (p * z_n + i) * 2 + r
                    to = far(i, r)
                    if i == 0 and r == 0:
                        sends[p, i, r] = pltpu.make_async_copy(do1.at[to, p], do.at[to, p], turn_s[0].at[p])
                    else:
                        sends[p, i, r] = rcopy(do1.at[to, p], do.at[me_f, p], turn_s[1].at[n], turn_s[2].at[n], (me_d, to))
        chips = list(range(1, z_n)) + [0]

        def fourth(i):
            chip = mod(me_z + i, z_n)
            at = rows_at(chip, RB)
            u, r = unit(x1_ref[at, :])
            gain = sm_ref[2:3, :]
            a2[at, :] = (u * gain + sm_ref[3:4, :]).astype(bf16)
            y = dot(dqkv[0, at, :], mat(1), NT) + dot(dqkv[1, at, :], mat(2), NT) + dot(dqkv[2, at, :], mat(3), NT)
            gn[2:3, :] += jnp.sum(y * u, 0, keepdims=True)
            gn[3:4, :] += jnp.sum(y, 0, keepdims=True)
            v = g1[at, :] + unit_back(y, u, r, gain)
            g1[at, :] = v
            e1 = v.astype(bf16)
            ev[at, :] = e1
            g = dot(e1, mat(0), NT).astype(bf16)
            for p in range(hp):
                do1[pl.ds(chip * per, per), p] = g[:, head_pair(p)].reshape(per, samples, 128)
            for r in range(2):
                sends[0, i, r].start()

        for i in chips:
            fourth(i)
        for p in range(1, hp):
            for i in chips:
                for r in range(2):
                    sends[p, i, r].start()
        put_g1.start()
        get_ga.start()

        get_xg.start()
        red2.every(red2.second)
        get_bk.wait()
        for at, i in halves:
            o1 = jnp.concatenate([bk[:, 2 * i].reshape(rows, 128), bk[:, 2 * i + 1].reshape(rows, 128)], 1)
            put(G1, 16, i, dot(o1, ev[...], TN).astype(bf16))
            for j in range(3):
                put(G1, 16 + (1 + j) * rl, i, dot(a2[:, at], dqkv[j], TN).astype(bf16))
        G1[:, :, :, :, 0:16, :] = jnp.broadcast_to(gn[...].astype(bf16), (4, z_n // 2, 2, 2, 16, d))
        red1 = PlaneReduce(fs_n, G1, (c1, n1, z1), red_s[1])
        red1.start()
        red2.every(red2.third)

        lane = lax.broadcasted_iota(jnp.int32, (8, 128), 1) // 64
        pick = (lane == lax.broadcasted_iota(jnp.int32, (8, 128), 0)).astype(f32)
        get_q1.wait()
        get_o.wait()

        def grad_rows(i, p):
            return do[pl.ds(i * pq, pq), p].reshape(bq, 128)

        for p in range(hp):
            at = head_pair(p)
            kt[...] = q_[1, :, at].astype(f32).T.astype(bf16)
            dk[...] = jnp.zeros((rows, 128), f32)
            dv[...] = jnp.zeros((rows, 128), f32)
            for i in range(z_n):
                for r in range(2):
                    if i == 0 and r == 0:
                        sends[p, i, r].wait()
                    else:
                        sends[p, i, r].wait_recv()

            def deltas(i, _):
                qa = rows_at(i, bq)
                prod = grad_rows(i, p).astype(f32) * o_[p, qa, :].astype(f32)
                delta[:, qa] = lax.dot_general(pick, prod, NT, precision=lax.Precision.HIGHEST, preferred_element_type=f32)
                return 0

            lax.fori_loop(0, rows // bq, deltas, 0)
            if p == 0:
                red1.every(red1.first)
            for h in range(2):
                def part(i, _):
                    qa = rows_at(i, bq)
                    mask = head_mask(bq, h)
                    q = q_[0, qa, at]
                    q = jnp.where(mask, q, jnp.zeros_like(q))
                    g = grad_rows(i, p)
                    g = jnp.where(mask, g, jnp.zeros_like(g))
                    s = dot(q_[1, :, at], q, NT) + kb[:, 0:1]
                    e = jnp.exp(s - l_ref[p * 2 + h:p * 2 + h + 1, qa])
                    ds = (e * (dot(q_[2, :, at], g, NT) - delta[h:h + 1, qa])).astype(bf16)
                    dv[...] += dot(e.astype(bf16), g)
                    dk[...] += dot(ds, q)
                    dqt[h * 64:h * 64 + 64, qa] = dot(kt[h * 64:h * 64 + 64, :], ds) * 0.125
                    return 0
                lax.fori_loop(0, rows // bq, part, 0)
            dqkv[0, :, at] = dqt[...].T.astype(bf16)
            dqkv[1, :, at] = dk[...].astype(bf16)
            dqkv[2, :, at] = dv[...].astype(bf16)
            if p == 1:
                red1.every(red1.second)
            if p == 2:
                red1.every(red1.third)

        get_ga.wait()
        get_xg.wait()
        gn[...] = jnp.zeros_like(gn)
        gain, bias = sm_ref[0:1, :], sm_ref[1:2, :]

        backs = {}
        for i in range(z_n):
            for r in range(2):
                to = far(i, r)
                if i == 0 and r == 0:
                    backs[i, r] = pltpu.make_async_copy(xg_.at[rows_at(to, samples)], dr.at[to], back_s[0].at[0])
                else:
                    n = 2 * i + r
                    backs[i, r] = rcopy(xg_.at[rows_at(to, samples)], dr.at[me_f], back_s[1].at[n], back_s[2].at[n], (me_d, to))
        for i in chips:
            chip = mod(me_z + i, z_n)
            at = rows_at(chip, RB)
            u, r = unit(xg_[at, :].astype(f32))
            y = (dot(dqkv[0, at, :], units(ga_, 16, rl), NT) + dot(dqkv[1, at, :], units(ga_, 16 + rl, rl), NT)
                 + dot(dqkv[2, at, :], units(ga_, 16 + 2 * rl, rl), NT))
            gn[0:1, :] += jnp.sum(y * u, 0, keepdims=True)
            gn[1:2, :] += jnp.sum(y, 0, keepdims=True)
            xg_[at, :] = unit_back(y, u, r, gain).astype(bf16)
            ev[at, :] = (u * gain + bias).astype(bf16)
            for r in range(2):
                backs[i, r].start()
        for j in range(3):
            for at, i in halves:
                put(GS, 16 + j * rl, i, dot(ev[:, at], dqkv[j], TN).astype(bf16))
        GS[:, :, :, :, 0:16, :] = jnp.broadcast_to(gn[...].astype(bf16), (4, z_n // 2, 2, 2, 16, d))
        reds = PlaneReduce(fs_n, GS, (c0, n0, z0), red_s[2])
        reds.start()
        red2.finish(out2)
        reds.every(reds.first)
        red1.finish(out1)
        reds.every(reds.second)
        reds.every(reds.third)
        reds.finish(outs_)
        put_g1.wait()
        put_lo.wait()
        for i in range(z_n):
            for r in range(2):
                backs[i, r].wait()
        for key, c in sends.items():
            if key[1:] != (0, 0):
                c.wait_send()

    S, V, D = jax.ShapeDtypeStruct, pltpu.VMEM, pltpu.SemaphoreType.DMA
    SM = pl.BlockSpec(memory_space=pltpu.SMEM)
    g = (4, z_n // 2, 2, 2)
    scratch = [V((rows, d), f32), V((rows, d), bf16), V((rows, d), bf16), V(w2.shape, bf16), V((rows, d), f32), V((rows, d), bf16),
               V((rows, d), bf16)]
    scratch += [V(o.shape, bf16), V(w1.shape, bf16), V(qkv.shape, bf16), V(p2.shape, bf16), V(back.shape, bf16),
               V((rows, d), f32), V((rows, d), bf16), V((rows, d), bf16), V((rows, d), bf16), V((rows, d), bf16), V((rows, d), bf16),
               V((3, rows, d), bf16), V(g + (r2, d), bf16), V(g + (r1, d), bf16), V(g + (rs, d), bf16), V(back.shape, bf16), V(back.shape, bf16), V((8, rows), f32),
               V((128, rows), bf16), V((128, rows), f32), V((rows, 128), f32), V((16, d), f32)]
    scratch += plane_reduce_scratch(fs_n, r2, d) + plane_reduce_scratch(fs_n, r1, d) + plane_reduce_scratch(fs_n, rs, d)
    n = hp * fs_n
    scratch += [D((15,)), D((hp,)), D((n,)), D((n,)), D((1,)), D((fs_n,)), D((fs_n,))] + plane_reduce_sems(fs_n) * 3
    return pl.pallas_call(
        body,
        out_shape=[S((rows, d), f32), S((rows, d), bf16), S((slots, samples, d), bf16), S((r2, d), f32), S((r1, d), f32), S((rs, d), f32)],
        in_specs=[SM, VM, VM] + [ANY] * 13, out_specs=[ANY, ANY, ANY, VM, VM, VM], scratch_shapes=scratch,
        compiler_params=params(2), name="second",
    )(scounts, lse, sm, cot, w2, x1, o2, a3, xg.reshape(rows, d), qkv, o, ga, w1, qkv2, p2, back)


def last_kernel(g1, dr, lo, out2, out1, outs, tasks, rl, fl, fs_n):
    slots, samples, d = dr.shape
    feats = slots // tasks
    part = feats * samples
    wide = d // 128
    chunks = (out2.shape[0] - fl) // rl

    def body(g1_ref, dr_ref, lo_ref, r2, r1, rs, tg, lo_out, gn, gs, gso, gf, gfo, gmi, gib, gmo, gob, low):
        for f in range(feats):
            for i in range(wide):
                at = pl.ds(i * feats + f, samples, stride=feats * wide)
                here = (slice(f * samples, (f + 1) * samples), head_pair(i))
                tg[at, :] = g1_ref[here] + dr_ref[f, :, head_pair(i)].astype(f32)
                low[at, :] = lo_ref[here].astype(f32)
        blocks(part * wide, 512, lambda at: lo_out.__setitem__((at, slice(None)), low[at, :].astype(bf16)))

        @pl.when(pl.program_id(0) == 0)
        def _():
            me = lax.axis_index("dp") * fs_n + lax.axis_index("fsdp")
            for i in range(3):
                gs[i] = rs[16 + i * rl:16 + (i + 1) * rl, :]
                gf[i] = r1[16 + (1 + i) * rl:16 + (2 + i) * rl, :]
            gso[...] = r1[16:16 + rl, :]
            gfo[...] = r1[16 + 4 * rl:16 + 5 * rl, :]
            for c in range(chunks):
                gmi[:, c * d:(c + 1) * d] = r2[c * rl:(c + 1) * rl, :]
            gmo[...] = r2[chunks * rl:, :]
            row = lax.broadcasted_iota(jnp.int32, (16, d), 0)
            both = jnp.where(row < 2, rs[0:16, :], r1[0:16, :])

            def mine(v, n, first):
                hot = lax.broadcasted_iota(jnp.int32, (d, n), 0) == lax.broadcasted_iota(jnp.int32, (d, n), 1) + first
                return lax.dot_general(v, hot.astype(f32), NN, precision=lax.Precision.HIGHEST, preferred_element_type=f32)

            own = mine(both, rl, me * rl)
            gn[...] = own[0:6]
            gob[...] = own[6:7]
            line = jnp.sum(jnp.where(row == 7 + me * fl // d, both, 0.0), 0, keepdims=True)
            gib[...] = mine(jnp.broadcast_to(line, (8, d)), fl, lax.rem(me * fl, d))[0:1]

    S = jax.ShapeDtypeStruct
    shapes = [S((tasks * part * wide, 128), f32), S((tasks * part * wide, 128), bf16), S((6, rl), f32), S((3, rl, d), f32), S((rl, d), f32),
              S((3, rl, d), f32), S((rl, d), f32), S((rl, chunks * d), f32), S((1, fl), f32), S((fl, d), f32), S((1, rl), f32)]
    by_task = lambda *shape: pl.BlockSpec(shape, lambda t: (t,) + (0,) * (len(shape) - 1))
    whole = lambda shape: pl.BlockSpec(shape, lambda t: (0,) * len(shape))
    return pl.pallas_call(
        body, out_shape=shapes, grid=(tasks,),
        in_specs=[by_task(part, d), by_task(feats, samples, d), by_task(part, d)] + [whole(v.shape) for v in (out2, out1, outs)],
        out_specs=[by_task(part * wide, 128), by_task(part * wide, 128)] + [whole(v.shape) for v in shapes[2:]],
        scratch_shapes=[pltpu.VMEM((part * wide, 128), f32)],
        compiler_params=params(), name="last",
    )(g1, dr, lo, out2, out1, outs)


def up16(a):
    rows = a.shape[-2]
    extra = (-rows) % 16
    return a if extra == 0 else jnp.pad(a, [(0, 0)] * (a.ndim - 2) + [(0, extra), (0, 0)])


def local(tokens, sample_counts, feature_counts, norms, sample_qkv, sample_out, feature_qkv, feature_out, mlp_in, mlp_in_bias,
          mlp_out, mlp_out_bias, cotangent):
    dp_n, fs_n = lax.axis_size("dp"), lax.axis_size("fsdp")
    nd = dp_n * fs_n
    me_d, me_f = lax.axis_index("dp"), lax.axis_index("fsdp")
    me = me_d * fs_n + me_f
    tasks, samples, feats, d = tokens.shape
    pairs = tasks * feats
    rep = fs_n // pairs
    dh = d // rep
    hp = dh // 128
    rl = sample_out.shape[0]
    chunks = mlp_in.shape[1] // d
    fl = mlp_out.shape[0]
    total = samples * fs_n
    if rep == 1 and dp_n == 4 and rl % 16 == 0 and fs_n * fl == d and fs_n == 8:
        def pieces(v):
            return v.reshape(tasks, samples, feats, d // 128, 128).transpose(0, 1, 3, 2, 4).reshape(-1, 128)

        saved = first_kernel(pieces(tokens), pieces(cotangent), sample_counts, feature_counts, (norms, mlp_out_bias[None], mlp_in_bias[None]),
                             sample_qkv, sample_out, feature_qkv, feature_out, mlp_in, mlp_out, tasks, samples, fs_n)
        g1, lo, dr, out2, out1, outs = second_kernel(sample_counts, saved, tasks, rl, fl, fs_n)
        tg, low, gn, gs, gso, gf, gfo, gmi, gib, gmo, gob = last_kernel(g1, dr, lo, out2, out1, outs, tasks, rl, fl, fs_n)

        def rows_back(v):
            return v.reshape(tasks, samples, d // 128, feats, 128).transpose(0, 1, 3, 2, 4).reshape(tokens.shape)

        return rows_back(low), rows_back(tg), gn, gs, gso, gf, gfo, gmi, gib[0], gmo, gob[0]


    small = jnp.zeros((16, d), bf16)
    small = lax.dynamic_update_slice(small, norms, (0, me * rl))
    small = lax.dynamic_update_slice(small, mlp_out_bias[None, :], (6, me * rl))
    small = lax.dynamic_update_slice(small, mlp_in_bias[None, :], (7 + (me * fl) // d, lax.rem(me * fl, d)))
    split_in = mlp_in.reshape(rl, chunks, d).transpose(1, 0, 2).reshape(chunks * rl, d)
    pack_a = up16(jnp.concatenate([small, sample_qkv.reshape(3 * rl, d)], 0))
    pack_b = up16(jnp.concatenate([sample_out, feature_qkv.reshape(3 * rl, d), feature_out, split_in, mlp_out], 0))

    xp = tokens.transpose(0, 2, 1, 3).reshape(pairs, samples, d)
    cp = cotangent.transpose(0, 2, 1, 3).reshape(pairs, samples, d)
    my_task = me_f // rep // feats
    count = lax.dynamic_index_in_dim(sample_counts, my_task, keepdims=False)
    keybias = jnp.broadcast_to(jnp.where(jnp.arange(total) < count, 0.0, MASKED).astype(f32)[:, None], (total, 128))
    shown = jnp.arange(feats)[None, :] < feature_counts[:, None]
    fbias = jnp.broadcast_to(jnp.where(shown, 0.0, MASKED).astype(f32).reshape(pairs, 1), (pairs, 128))

    ga, gb = gather_call([pack_a, pack_b], dp_n, fs_n, 3)
    ga, gb = ga.reshape((nd,) + ga.shape[3:]), gb.reshape((nd,) + gb.shape[3:])

    def take(g, start, rows):
        return g[:, start:start + rows].reshape(nd * rows, d)

    smalls = jnp.sum(ga[:, :16].astype(f32), 0)
    w_s = jnp.stack([take(ga, 16 + i * rl, rl) for i in range(3)])
    first = lax.rem(me_f, rep) * dh
    w_mine = lax.dynamic_slice_in_dim(w_s, first, dh, 2)
    w_mid = jnp.concatenate([take(gb, i * rl, rl) for i in range(5 + chunks)] + [take(gb, (5 + chunks) * rl, fl)])[None]
    size = d
    back, xg, o, qkv, lse = forward_kernel(jnp.repeat(xp, rep, 0), [], [w_mine, smalls], keybias, dp_n, fs_n, rl, dh)

    lo, g1, do1, gm = middle_call(xp, back.reshape(pairs, rep * hp, samples, 128), cp, smalls, fbias, w_mid, tasks, chunks, size)
    do1 = do1.reshape(fs_n, hp, samples, 128)
    dxr, gs, gn_s = backward_kernel(do1, xg, qkv, o, lse, w_mine, smalls, keybias, None, None, dp_n, fs_n, rl, dh, tasks, False)
    dxr = jnp.sum(dxr.reshape(pairs, rep, samples, d).astype(f32), 1)
    tokens_grad = (g1.reshape(pairs, samples, d) + dxr).reshape(tasks, feats, samples, d).transpose(0, 2, 1, 3)
    gs = lax.dynamic_update_slice_in_dim(jnp.zeros((3, d, d), bf16), gs, first, 2)

    def give(g, parts):
        return g.reshape(parts, nd, -1, d).transpose(1, 0, 2, 3).reshape(nd, -1, d)

    gm = gm[0]
    mix = jnp.concatenate([gn_s[0:2].astype(bf16), gm[2:16]], 0)
    grads = up16(jnp.concatenate([jnp.broadcast_to(mix[None], (nd, 16, d)), give(gm[16:16 + (5 + chunks) * d], 5 + chunks),
                                  give(gm[16 + (5 + chunks) * d:], 1), give(gs, 3)], 1))
    s = scatter_call(grads.reshape((dp_n, fs_n // 2, 2) + grads.shape[1:]), dp_n, fs_n, 6)
    outs = [s[16 + (5 + chunks) * rl + fl:][:3 * rl]]
    gn = s[0:2]
    gn = jnp.concatenate([gn, s[2:16]], 0)
    layer_output = lo.reshape(tasks, feats, samples, d).transpose(0, 2, 1, 3)

    def piece(start, rows):
        return s[16 + start * rl:16 + start * rl + rows]

    return (
        layer_output,
        tokens_grad,
        lax.dynamic_slice(gn, (0, me * rl), (6, rl)),
        outs[0].reshape(3, rl, d), piece(0, rl), piece(1, 3 * rl).reshape(3, rl, d), piece(4, rl),
        piece(5, chunks * rl).reshape(chunks, rl, d).transpose(1, 0, 2).reshape(rl, chunks * d),
        lax.dynamic_slice(gn[7:7 + chunks].reshape(-1), (me * fl,), (fl,)),
        piece(5 + chunks, fl),
        lax.dynamic_slice(gn[6], (me * rl,), (rl,)),
    )


def solution(mesh):
    rows, whole = ("dp", "fsdp"), P("dp", "fsdp", None, None)
    weights = (P(None, rows), P(None, rows, None), P(rows, None), P(None, rows, None), P(rows, None), P(rows, None), P(rows),
               P(rows, None), P(rows))
    return jax.shard_map(local, mesh=mesh, in_specs=(whole, P("dp"), P("dp")) + weights + (whole,),
                         out_specs=(whole, whole) + weights, check_vma=False)
```

```python
import functools
import jax
import jax.numpy as jnp
from jax import lax
from jax.experimental import pallas as pl
from jax.experimental.pallas import tpu as pltpu
from jax.sharding import PartitionSpec as P

MESH = pl.DeviceIdType.MESH
f32, bf16 = jnp.float32, jnp.bfloat16


def mod(a, n):
    return lax.rem(a, n)


def greet(dp_n, fs_n, with_dp=True):
    me_d, me_f = lax.axis_index("dp"), lax.axis_index("fsdp")
    barrier = pltpu.get_barrier_semaphore()
    n = 0
    for k in range(1, fs_n):
        pl.semaphore_signal(barrier, inc=1, device_id=(me_d, mod(me_f + k, fs_n)), device_id_type=MESH)
        n += 1
    if with_dp:
        for k in range(1, dp_n):
            pl.semaphore_signal(barrier, inc=1, device_id=(mod(me_d + k, dp_n), me_f), device_id_type=MESH)
            n += 1
    pl.semaphore_wait(barrier, n)


def rcopy(src, dst, ss, rs, dev):
    return pltpu.make_async_remote_copy(src_ref=src, dst_ref=dst, send_sem=ss, recv_sem=rs, device_id=dev, device_id_type=MESH)


class Swap:
    def __init__(self, fs_n, src, dst, local_sem, ss, rs):
        me_d, me_f = lax.axis_index("dp"), lax.axis_index("fsdp")
        self.own = pltpu.make_async_copy(src.at[me_f], dst.at[me_f], local_sem)
        self.copies = []
        for k in range(1, fs_n):
            to = mod(me_f + k, fs_n)
            self.copies.append(rcopy(src.at[to], dst.at[me_f], ss.at[k - 1], rs.at[k - 1], (me_d, to)))

    def start(self):
        for c in self.copies:
            c.start()
        self.own.start()

    def wait(self):
        self.own.wait()
        for c in self.copies:
            c.wait()


class Gather:
    def __init__(self, dp_n, fs_n, src, dst, local_sem, zs, zr, ds, dr, cs, cr):
        me_d, me_f = lax.axis_index("dp"), lax.axis_index("fsdp")
        z_n = fs_n // 2
        me_z, me_c = me_f // 2, mod(me_f, 2)
        self.z_n, self.dp_n = z_n, dp_n
        partner = (me_d, me_z * 2 + 1 - me_c)
        self.own = pltpu.make_async_copy(src, dst.at[me_d, me_z, me_c], local_sem)
        self.z = []
        for k in range(1, z_n):
            to = mod(me_z + k, z_n) * 2 + me_c
            self.z.append(rcopy(src, dst.at[me_d, me_z, me_c], zs.at[k - 1], zr.at[k - 1], (me_d, to)))
        self.d = {}
        self.c = {}
        for k in range(z_n):
            z = mod(me_z - k + z_n, z_n)
            for j in range(dp_n):
                d = mod(me_d - j + dp_n, dp_n)
                here = src if (k == 0 and j == 0) else dst.at[d, z, me_c]
                self.c[k, j] = rcopy(here, dst.at[d, z, me_c], cs.at[k * dp_n + j], cr.at[k * dp_n + j], partner)
                if j > 0:
                    here = src if k == 0 else dst.at[me_d, z, me_c]
                    i = k * (dp_n - 1) + j - 1
                    self.d[k, j] = rcopy(here, dst.at[me_d, z, me_c], ds.at[i], dr.at[i], (mod(me_d + j, dp_n), me_f))

    def start(self):
        for c in self.z:
            c.start()
        self.own.start()
        for j in range(1, self.dp_n):
            self.d[0, j].start()
        self.c[0, 0].start()

    def forward_z(self):
        for k in range(1, self.z_n):
            self.z[k - 1].wait_recv()
            for j in range(1, self.dp_n):
                self.d[k, j].start()
            self.c[k, 0].start()

    def forward_d(self):
        for k in range(self.z_n):
            for j in range(1, self.dp_n):
                self.d[k, j].wait_recv()
                self.c[k, j].start()

    def wait(self):
        self.own.wait()
        for c in self.z:
            c.wait_send()
        for c in self.d.values():
            c.wait_send()
        for c in self.c.values():
            c.wait()


def gather_sems(dp_n, fs_n):
    z = fs_n // 2
    D = pltpu.SemaphoreType.DMA
    return [D, D((z - 1,)), D((z - 1,)), D((z * (dp_n - 1),)), D((z * (dp_n - 1),)), D((z * dp_n,)), D((z * dp_n,))]


def swap_sems(fs_n):
    D = pltpu.SemaphoreType.DMA
    return [D, D((fs_n - 1,)), D((fs_n - 1,))]


ANY = pl.BlockSpec(memory_space=pl.ANY)
VM = pl.BlockSpec(memory_space=pltpu.VMEM)


def swap_call(x, dp_n, fs_n, cid, space=ANY):
    def body(x_ref, o_ref, *sems):
        greet(dp_n, fs_n, False)
        s = Swap(fs_n, x_ref, o_ref, *sems)
        s.start()
        s.wait()

    return pl.pallas_call(
        body, out_shape=jax.ShapeDtypeStruct(x.shape, x.dtype), in_specs=[space], out_specs=space,
        scratch_shapes=swap_sems(fs_n),
        compiler_params=pltpu.CompilerParams(collective_id=cid, has_side_effects=True, vmem_limit_bytes=60 << 20),
        name="swap%d" % cid,
    )(x)


def gather_call(packs, dp_n, fs_n, cid, space=ANY):
    n = len(packs)

    def body(*refs):
        ins, outs, sems = refs[:n], refs[n:2 * n], refs[2 * n:]
        greet(dp_n, fs_n)
        gs = [Gather(dp_n, fs_n, ins[i], outs[i], *sems[7 * i:7 * i + 7]) for i in range(n)]
        for g in gs:
            g.start()
        for g in gs:
            g.forward_z()
        for g in gs:
            g.forward_d()
        for g in gs:
            g.wait()

    return pl.pallas_call(
        body,
        out_shape=[jax.ShapeDtypeStruct((dp_n, fs_n // 2, 2) + p.shape, p.dtype) for p in packs],
        in_specs=[space] * n, out_specs=[space] * n,
        scratch_shapes=gather_sems(dp_n, fs_n) * n,
        compiler_params=pltpu.CompilerParams(collective_id=cid, has_side_effects=True, vmem_limit_bytes=60 << 20),
        name="gather%d" % cid,
    )(*packs)


def scatter_call(g, dp_n, fs_n, cid):
    z_n = fs_n // 2
    rows, width = g.shape[3:]
    step = 16

    def body(g_ref, o_ref, from_c, half, from_d, quarter, from_z, cs, cr, ds, dr, zs, zr):
        me_d, me_f = lax.axis_index("dp"), lax.axis_index("fsdp")
        me_z, me_c = me_f // 2, mod(me_f, 2)
        greet(dp_n, fs_n)
        partner = (me_d, me_z * 2 + 1 - me_c)

        def add(out, parts):
            def one(i, _):
                at = pl.ds(pl.multiple_of(i * step, step), step)
                total = parts[0][at, :].astype(f32)
                for p in parts[1:]:
                    total = total + p[at, :].astype(f32)
                out[at, :] = total.astype(out.dtype)
                return 0
            lax.fori_loop(0, rows // step, one, 0, unroll=True if rows // step <= 4 else 4)

        order = [(j, k) for j in list(range(1, dp_n)) + [0] for k in list(range(1, z_n)) + [0]]
        cc, dd, zz = {}, {}, {}
        for i, (j, k) in enumerate(order):
            d, z = mod(me_d + j, dp_n), mod(me_z + k, z_n)
            cc[j, k] = rcopy(g_ref.at[d, z, 1 - me_c], from_c.at[i], cs.at[i], cr.at[i], partner)
            cc[j, k].start()
        for i, (j, k) in enumerate(order):
            d, z = mod(me_d + j, dp_n), mod(me_z + k, z_n)
            cc[j, k].wait_recv()
            add(half.at[j, k], [g_ref.at[d, z, me_c], from_c.at[i]])
            if j:
                n = (j - 1) * z_n + k
                dd[j, k] = rcopy(half.at[j, k], from_d.at[j - 1, k], ds.at[n], dr.at[n], (d, me_f))
                dd[j, k].start()
        for k in list(range(1, z_n)) + [0]:
            for j in range(1, dp_n):
                dd[j, k].wait_recv()
            if k:
                add(quarter.at[k], [half.at[0, k]] + [from_d.at[j - 1, k] for j in range(1, dp_n)])
                to = mod(me_z + k, z_n) * 2 + me_c
                zz[k] = rcopy(quarter.at[k], from_z.at[k - 1], zs.at[k - 1], zr.at[k - 1], (me_d, to))
                zz[k].start()
        for k in range(1, z_n):
            zz[k].wait_recv()
        add(o_ref, [half.at[0, 0]] + [from_d.at[j - 1, 0] for j in range(1, dp_n)] + [from_z.at[k - 1] for k in range(1, z_n)])
        for c in list(cc.values()) + list(dd.values()) + list(zz.values()):
            c.wait_send()

    D = pltpu.SemaphoreType.DMA
    n = dp_n * z_n
    return pl.pallas_call(
        body, out_shape=jax.ShapeDtypeStruct((rows, width), f32), in_specs=[VM], out_specs=VM,
        scratch_shapes=[
            pltpu.VMEM((n, rows, width), bf16), pltpu.VMEM((dp_n, z_n, rows, width), bf16),
            pltpu.VMEM((dp_n - 1, z_n, rows, width), bf16), pltpu.VMEM((z_n, rows, width), bf16),
            pltpu.VMEM((z_n - 1, rows, width), bf16),
            D((n,)), D((n,)), D((n - z_n,)), D((n - z_n,)), D((z_n - 1,)), D((z_n - 1,)),
        ],
        compiler_params=pltpu.CompilerParams(collective_id=cid, has_side_effects=True, vmem_limit_bytes=60 << 20),
        name="scatter%d" % cid,
    )(g)
class PlaneGather:
    def __init__(self, fs_n, src, dst, local_sem, zs, zr, ds, dr, cs, cr):
        me_d, me_f = lax.axis_index("dp"), lax.axis_index("fsdp")
        z_n = fs_n // 2
        me_z, me_c = me_f // 2, mod(me_f, 2)
        self.z_n = z_n
        partner = (me_d, me_z * 2 + 1 - me_c)
        ds_ = [me_d, me_d // 2 * 2 + 1 - mod(me_d, 2), mod(me_d + 2, 4), 3 - me_d]
        zs_ = [mod(me_z - k + z_n, z_n) for k in range(z_n)]
        self.own = pltpu.make_async_copy(src, dst.at[me_d, me_z, me_c], local_sem)
        self.z, self.n, self.fwd, self.c = {}, {}, {}, {}
        for k in range(z_n):
            at = lambda j: dst.at[ds_[j], zs_[k], me_c]
            mine = src if k == 0 else at(0)
            if k:
                to = mod(me_z + k, z_n) * 2 + me_c
                self.z[k] = rcopy(src, dst.at[me_d, me_z, me_c], zs.at[k - 1], zr.at[k - 1], (me_d, to))
            for j in (1, 2):
                self.n[k, j] = rcopy(mine, at(0), ds.at[3 * k + j - 1], dr.at[3 * k + j - 1], (ds_[j], me_f))
            first = 1 + k % 2
            self.fwd[k] = rcopy(at(first), at(first), ds.at[3 * k + 2], dr.at[3 * k + 2], (ds_[3 - first], me_f))

        for j in range(4):
            all_z = dst.at[ds_[j], :, me_c]
            self.c[j] = rcopy(all_z, all_z, cs.at[j], cr.at[j], partner)

    def start(self):
        for c in self.z.values():
            c.start()

    def begin(self):
        self.own.start()
        self.spread(0)

    def spread(self, k):
        if k:
            self.z[k].wait_recv()
        self.n[k, 1].start()
        self.n[k, 2].start()
        if k == self.z_n - 1:
            self.own.wait()
            self.c[0].start()

    def hand_on(self, k):
        first = 1 + k % 2
        for j in (first, 3 - first):
            self.n[k, j].wait_recv()
            if j == first:
                self.fwd[k].start()
        if k == self.z_n - 1:
            self.c[1].start()
            self.c[2].start()

    def corner(self, k):
        self.fwd[k].wait_recv()
        if k == self.z_n - 1:
            self.c[3].start()

    def wait(self):
        for c in list(self.z.values()) + list(self.n.values()) + list(self.fwd.values()):
            c.wait_send()
        for c in self.c.values():
            c.wait()


def plane_gather_sems(fs_n):
    z, D = fs_n // 2, pltpu.SemaphoreType.DMA
    return [D, D((z - 1,)), D((z - 1,)), D((3 * z,)), D((3 * z,)), D((4,)), D((4,))]


class PlaneReduce:
    def __init__(self, fs_n, g, bufs, sems):
        me_d, me_f = lax.axis_index("dp"), lax.axis_index("fsdp")
        z_n = fs_n // 2
        me_z, me_c = me_f // 2, mod(me_f, 2)
        self.halves, self.z_n, self.rows = z_n // 2, z_n, g.shape[4]
        self.from_c, self.from_n, self.from_z = bufs
        cs, cr, ds, dr, zs, zr = sems
        partner = (me_d, me_z * 2 + 1 - me_c)
        ds_ = [me_d, me_d // 2 * 2 + 1 - mod(me_d, 2), mod(me_d + 2, 4), 3 - me_d]
        self.mine = lambda j, h, a: g.at[ds_[j], h, a, me_c]
        self.c = [rcopy(g.at[ds_[j], :, :, 1 - me_c], self.from_c.at[j], cs.at[j], cr.at[j], partner) for j in range(4)]
        self.n, self.z, self.line = {}, {}, {}
        for a in range(2):
            first = 1 + a
            for i, (j, to) in enumerate([(first, first), (3, first), (3 - first, 3 - first)]):
                self.n[a, i] = rcopy(g.at[ds_[j], :, a, me_c], self.from_n.at[a, i], ds.at[3 * a + i], dr.at[3 * a + i], (ds_[to], me_f))
        for k in range(z_n):
            z = mod(me_z + k, z_n)
            h, a = z // 2, mod(z, 2)
            own = g.at[me_d, h, a, me_c]
            self.line[k] = [own, self.from_n.at[a, 0, h], self.from_n.at[a, 2, h]]
            if k:
                self.z[k] = rcopy(own, self.from_z.at[k - 1], zs.at[k - 1], zr.at[k - 1], (me_d, z * 2 + me_c))

    def add(self, *sums):
        step = 16

        def one(i, _):
            at = pl.ds(pl.multiple_of(i * step, step), step)
            for out, parts in sums:
                if len(parts) == 2:
                    out[at, :] = parts[0][at, :] + parts[1][at, :]
                else:
                    total = parts[0][at, :].astype(f32)
                    for p in parts[1:]:
                        total = total + p[at, :].astype(f32)
                    out[at, :] = total.astype(out.dtype)
            return 0

        lax.fori_loop(0, self.rows // step, one, 0)

    def start(self):
        for j in (1, 2, 3, 0):
            self.c[j].start()

    def first(self):
        for j in (1, 2, 3, 0):
            self.c[j].wait_recv()
            self.add(*[(self.mine(j, h, a), [self.mine(j, h, a), self.from_c.at[j, h, a]]) for h in range(self.halves) for a in range(2)])
            if j in (1, 2):
                self.n[j - 1, 0].start()
            if j == 3:
                self.n[0, 1].start()
                self.n[1, 1].start()

    def second(self):
        for a in range(2):
            j = 2 - a
            self.n[a, 1].wait_recv()
            self.add(*[(self.mine(j, h, a), [self.mine(j, h, a), self.from_n.at[a, 1, h]]) for h in range(self.halves)])
            self.n[a, 2].start()

    def third(self):
        for a in range(2):
            self.n[a, 0].wait_recv()
            self.n[a, 2].wait_recv()
        for k in range(1, self.z_n):
            self.add((self.line[k][0], self.line[k]))
            self.z[k].start()

    def every(self, step):
        step()

    def finish(self, out):
        for k in range(1, self.z_n):
            self.z[k].wait_recv()
        self.add((out, self.line[0] + [self.from_z.at[k - 1] for k in range(1, self.z_n)]))
        for c in self.c + list(self.n.values()) + list(self.z.values()):
            c.wait_send()


def plane_reduce_scratch(fs_n, rows, width):
    z_n, V = fs_n // 2, pltpu.VMEM
    return [V((4, z_n // 2, 2, rows, width), bf16), V((2, 3, z_n // 2, rows, width), bf16), V((z_n - 1, rows, width), bf16)]


def plane_reduce_sems(fs_n):
    z_n, D = fs_n // 2, pltpu.SemaphoreType.DMA
    return [D((4,)), D((4,)), D((6,)), D((6,)), D((z_n - 1,)), D((z_n - 1,))]


HEADS = 8
EPS = 1e-05
MASKED = -1e30
NN = (((1,), (0,)), ((), ()))
NT = (((1,), (1,)), ((), ()))
TN = (((0,), (0,)), ((), ()))


def dot(a, b, dims=NN):
    return lax.dot_general(a, b, dims, preferred_element_type=f32)


def unit(x):
    c = x - jnp.mean(x, -1, keepdims=True)
    r = lax.rsqrt(jnp.mean(c * c, -1, keepdims=True) + EPS)
    return c * r, r


def unit_back(y, u, r, gain):
    yg = y * gain
    return r * (yg - jnp.mean(yg, -1, keepdims=True) - u * jnp.mean(yg * u, -1, keepdims=True))


def blocks(total, size, body):
    lax.fori_loop(0, total // size, lambda i, c: (body(pl.ds(pl.multiple_of(i * size, size), size)), c)[1], 0)


def gelu_parts(v):
    z = jnp.abs(v) * 0.7071067811865476
    t = pl.reciprocal(1.0 + 0.3275911 * z, approx=False)
    e = jnp.exp(-0.5 * (v * v))
    tail = t * (0.127414796 + t * (-0.142248368 + t * (0.7107068705 + t * (-0.7265760135 + t * 0.5307027145)))) * e
    return jnp.where(v >= 0, 1.0 - tail, tail), v * e * 0.3989422804014327


def head_mask(rows, second, width=128):
    lane = lax.broadcasted_iota(jnp.int32, (rows, width), 1)
    return (lane >= width // 2) if second else (lane < width // 2)


def params(cid=None):
    if cid is None:
        return pltpu.CompilerParams(vmem_limit_bytes=62 << 20)
    return pltpu.CompilerParams(collective_id=cid, has_side_effects=True, vmem_limit_bytes=62 << 20)


def head_pair(p):
    return slice(p * 128, p * 128 + 128)


def middle_call(x, o1, cot, smalls, fbias, w, tasks, chunks, unit_rows):
    pairs, samples, d = x.shape
    feats = pairs // tasks
    rows = pairs * samples
    hh = d // 64
    nd = w.shape[0]
    U = unit_rows
    OUT = (5 + chunks) * U
    fl = chunks * d // nd
    x, cot = x.reshape(rows, d), cot.reshape(rows, d)
    RB = 256
    per = RB // samples

    def body(x_ref, back_ref, cot_ref, n_ref, fb_ref, w_ref,
             lo_ref, g1_ref, do1_ref, g_ref,
             x1, a, qkv, p2, o2, acc, dacc, act, gh, dqkv, do2, o1_ref, gn_ref):
        gn_ref[...] = jnp.zeros_like(gn_ref)

        def at_unit(k):
            return pl.ds(pl.multiple_of(k * U, 16), U) if not isinstance(k, int) else slice(k * U, k * U + U)

        def mat(k):
            return w_ref[:, at_unit(k), :].reshape(d, d)

        def out_mat(c):
            if nd == 1:
                return w_ref[0, pl.ds(pl.multiple_of(OUT + c * d, 16), d), :]
            m = nd // chunks
            return w_ref[pl.ds(c * m, m), OUT:OUT + fl, :].reshape(d, d)

        def put(k, at, i, value):
            if nd == 1:
                g_ref[0, pl.ds(pl.multiple_of(16 + k * U + i * 256, 16), 256), :] = value
            else:
                m = 256 // U
                g_ref[pl.ds(i * m, m), pl.ds(pl.multiple_of(16 + k * U, 16), U), :] = value.reshape(m, U, d)

        def put_out(c, i, value):
            if nd == 1:
                g_ref[0, pl.ds(pl.multiple_of(16 + OUT + c * d + i * 256, 16), 256), :] = value
            else:
                m = 256 // fl
                g_ref[pl.ds(c * (nd // chunks) + i * m, m), 16 + OUT:16 + OUT + fl, :] = value.reshape(m, fl, d)

        def tiles(body):
            for i in range(d // 256):
                body(slice(i * 256, i * 256 + 256), i)

        def norm(i):
            return n_ref[2 * i:2 * i + 1, :], n_ref[2 * i + 1:2 * i + 2, :]

        def collect(i, _):
            at = pl.ds(pl.multiple_of(i * RB, RB), RB)
            for p in range(hh // 2):
                o1_ref[at, p * 128:p * 128 + 128] = back_ref[pl.ds(i * per, per), p].reshape(RB, 128)
            return 0

        lax.fori_loop(0, rows // RB, collect, 0)

        def first(at):
            y = x_ref[at, :].astype(f32) + dot(o1_ref[at, :], mat(0))
            x1[at, :] = y
            u, _ = unit(y)
            g, b = norm(1)
            v = (u * g + b).astype(bf16)
            a[at, :] = v
            for i in range(3):
                z = dot(v, mat(1 + i)).astype(bf16)
                qkv[i, at, :] = z * 0.125 if i == 0 else z

        blocks(rows, RB, first)

        half = lax.broadcasted_iota(jnp.int32, (256, 128), 0) // 64
        ones = (lax.rem(half, 2) == lax.broadcasted_iota(jnp.int32, (256, 128), 1) // 64).astype(bf16)

        def head_sums(prods):
            both = []
            for v in prods:
                hi = v.astype(bf16)
                both.append(jnp.concatenate([hi, (v - hi.astype(f32)).astype(bf16)], 1))
            out = dot(jnp.concatenate(both, 0), ones)
            return [out[i * samples:(i + 1) * samples] for i in range(len(prods))]

        def at_slot(t, f):
            return pl.ds(pl.multiple_of((t * feats + f) * samples, samples), samples)

        def mix(t, _):
            for p in range(hh // 2):
                lanes = head_pair(p)
                ks = [qkv[1, at_slot(t, g), lanes].astype(f32) for g in range(feats)]
                vs = [qkv[2, at_slot(t, g), lanes].astype(f32) for g in range(feats)]
                for f in range(feats):
                    q = qkv[0, at_slot(t, f), lanes].astype(f32)
                    sc = head_sums([q * k for k in ks])
                    sc = [v + fb_ref[pl.ds(t * feats + g, 1), :] for g, v in enumerate(sc)]
                    top = functools.reduce(jnp.maximum, sc)
                    sc = [jnp.exp(v - top) for v in sc]
                    inv = 1.0 / sum(sc)
                    sc = [v * inv for v in sc]
                    for g in range(feats):
                        p2[t, p, f, g] = sc[g]
                    o2[at_slot(t, f), lanes] = sum(w * v for w, v in zip(sc, vs)).astype(bf16)
            return 0

        lax.fori_loop(0, tasks, mix, 0)

        def second(at):
            y = x1[at, :] + dot(o2[at, :], mat(4))
            acc[at, :] = y
            u, _ = unit(y)
            g, b = norm(2)
            do2[at, :] = (u * g + b).astype(bf16)
            dacc[at, :] = jnp.zeros((RB, d), f32)

        blocks(rows, RB, second)

        def chunk(c, _):
            def part(at):
                hid = dot(do2[at, :], mat(5 + c)) + n_ref[pl.ds(7 + c, 1), :]
                cdf, pdf = gelu_parts(hid)
                al = (hid * cdf).astype(bf16)
                act[at, :] = al
                gl = ((cdf + pdf) * dot(cot_ref[at, :], out_mat(c), NT)).astype(bf16)
                gh[at, :] = gl
                gn_ref[pl.ds(7 + c, 1), :] += jnp.sum(gl.astype(f32), 0, keepdims=True)
                acc[at, :] += dot(al, out_mat(c))
                dacc[at, :] += dot(gl, mat(5 + c), NT)

            blocks(rows, RB, part)

            def weight(at, i):
                put_out(c, i, dot(act[:, at], cot_ref[...], TN).astype(bf16))
                put(5 + c, at, i, dot(do2[:, at], gh[...], TN).astype(bf16))

            tiles(weight)
            return 0

        lax.fori_loop(0, chunks, chunk, 0)

        def third(at):
            lo_ref[at, :] = (acc[at, :] + n_ref[6:7, :]).astype(bf16)
            u, r = unit(x1[at, :] + dot(o2[at, :], mat(4)))
            y = dacc[at, :]
            gn_ref[4:5, :] += jnp.sum(y * u, 0, keepdims=True)
            gn_ref[5:6, :] += jnp.sum(y, 0, keepdims=True)
            cf = cot_ref[at, :].astype(f32)
            gn_ref[6:7, :] += jnp.sum(cf, 0, keepdims=True)
            g2 = cf + unit_back(y, u, r, norm(2)[0])
            dacc[at, :] = g2
            e2 = g2.astype(bf16)
            act[at, :] = e2
            do2[at, :] = dot(e2, mat(4), NT).astype(bf16)

        blocks(rows, RB, third)

        def weight2(at, i):
            put(4, at, i, dot(o2[:, at], act[...], TN).astype(bf16))

        tiles(weight2)

        def unmix(t, _):
            for p in range(hh // 2):
                lanes = head_pair(p)
                ks = [qkv[1, at_slot(t, g), lanes].astype(f32) for g in range(feats)]
                vs = [qkv[2, at_slot(t, g), lanes].astype(f32) for g in range(feats)]
                dk, dv = [0.0] * feats, [0.0] * feats
                for f in range(feats):
                    q = qkv[0, at_slot(t, f), lanes].astype(f32)
                    gr = do2[at_slot(t, f), lanes].astype(f32)
                    dp = head_sums([gr * v for v in vs])
                    ws = [p2[t, p, f, g] for g in range(feats)]
                    mean = sum(w * v for w, v in zip(ws, dp))
                    ds = [(w * (v - mean)).astype(bf16).astype(f32) for w, v in zip(ws, dp)]
                    dqkv[0, at_slot(t, f), lanes] = (sum(v * k for v, k in zip(ds, ks)) * 0.125).astype(bf16)
                    for g in range(feats):
                        dk[g] += ds[g] * q
                        dv[g] += ws[g] * gr
                for g in range(feats):
                    dqkv[1, at_slot(t, g), lanes] = dk[g].astype(bf16)
                    dqkv[2, at_slot(t, g), lanes] = dv[g].astype(bf16)
            return 0

        lax.fori_loop(0, tasks, unmix, 0)

        def fourth(i, _):
            at = pl.ds(pl.multiple_of(i * RB, RB), RB)
            u, r = unit(x1[at, :])
            y = dot(dqkv[0, at, :], mat(1), NT) + dot(dqkv[1, at, :], mat(2), NT) + dot(dqkv[2, at, :], mat(3), NT)
            gn_ref[2:3, :] += jnp.sum(y * u, 0, keepdims=True)
            gn_ref[3:4, :] += jnp.sum(y, 0, keepdims=True)
            g1 = dacc[at, :] + unit_back(y, u, r, norm(1)[0])
            g1_ref[at, :] = g1
            e1 = g1.astype(bf16)
            act[at, :] = e1
            do = dot(e1, mat(0), NT).astype(bf16)
            for p in range(hh // 2):
                do1_ref[pl.ds(i * per, per), p] = do[:, p * 128:p * 128 + 128].reshape(per, samples, 128)
            return 0

        lax.fori_loop(0, rows // RB, fourth, 0)

        def weight3(at, i):
            put(0, at, i, dot(o1_ref[:, at], act[...], TN).astype(bf16))
            for j in range(3):
                put(1 + j, at, i, dot(a[:, at], dqkv[j], TN).astype(bf16))

        tiles(weight3)
        g_ref[:, 0:16, :] = jnp.broadcast_to(gn_ref[...].astype(bf16), (nd, 16, d))

    V = pltpu.VMEM
    S = jax.ShapeDtypeStruct
    return pl.pallas_call(
        body,
        out_shape=[S((rows, d), bf16), S((rows, d), f32), S((pairs, hh // 2, samples, 128), bf16),
                   S((nd, 16 + OUT + fl, d), bf16)],
        in_specs=[VM] * 6, out_specs=[VM] * 4,
        scratch_shapes=[V((rows, d), f32), V((rows, d), bf16), V((3, rows, d), bf16), V((tasks, hh // 2, feats, feats, samples, 128), f32), V((rows, d), bf16),
                        V((rows, d), f32), V((rows, d), f32), V((rows, d), bf16), V((rows, d), bf16), V((3, rows, d), bf16),
                        V((rows, d), bf16), V((rows, d), bf16), V((16, d), f32)],
        compiler_params=params(), name="middle",
    )(x, o1, cot, smalls, fbias, w)
BQ = 1024


class Turns:
    def __init__(self, fs_n, parts, src, dst, local_sem, ss, rs):
        me_d, me_f = lax.axis_index("dp"), lax.axis_index("fsdp")
        self.sets = []
        for p in range(parts):
            own = pltpu.make_async_copy(src(p, me_f), dst(p, me_f), local_sem.at[p])
            far = []
            for k in range(1, fs_n):
                to = mod(me_f + k, fs_n)
                i = p * (fs_n - 1) + k - 1
                far.append(rcopy(src(p, to), dst(p, me_f), ss.at[i], rs.at[i], (me_d, to)))
            self.sets.append((own, far))

    def start(self, p):
        own, far = self.sets[p]
        for c in far:
            c.start()
        own.start()

    def wait_recv(self, p):
        own, far = self.sets[p]
        own.wait()
        for c in far:
            c.wait_recv()

    def wait_send(self):
        for _, far in self.sets:
            for c in far:
                c.wait_send()


def turn_sems(fs_n, parts):
    D = pltpu.SemaphoreType.DMA
    return [D((parts,)), D((parts * (fs_n - 1),)), D((parts * (fs_n - 1),))]


def units(ref, start, size):
    v = ref[..., start:start + size, :]
    return v.reshape(-1, v.shape[-1])


def forward_kernel(x, packs, plain, keybias, dp_n, fs_n, rl, dh):
    slots, samples, d = x.shape
    rows = slots * samples
    heads = dh // 64
    hp = heads // 2
    np_ = len(packs)

    def body(*refs):
        it = iter(refs)
        x_ref, kb_ref = next(it), next(it)
        pack_refs = [next(it) for _ in range(np_)]
        w_ref, sm_ref = (None, None) if np_ else (next(it), next(it))
        back_ref, xg_ref, o_ref, qkv_ref, l_ref = (next(it) for _ in range(5))
        g_refs = [next(it) for _ in range(np_)]
        if np_:
            sm_ref = next(it)
        acted, vt, ot = next(it), next(it), next(it)
        swap_s = [next(it) for _ in range(3)]
        turn_s = [next(it) for _ in range(3)]
        gat_s = [[next(it) for _ in range(7)] for _ in range(np_)]

        greet(dp_n, fs_n, np_ > 0)
        gathers = [PlaneGather(fs_n, pack_refs[i], g_refs[i], *gat_s[i]) for i in range(np_)]
        swap = Swap(fs_n, x_ref, xg_ref, *swap_s)
        z_n = fs_n // 2
        if np_:
            gathers[0].start()
        swap.start()
        if np_:
            gathers[1].start()
            for k in range(1, z_n):
                gathers[0].spread(k)
            for k in range(z_n):
                gathers[0].hand_on(k)
            for k in range(1, z_n):
                gathers[1].spread(k)
            for k in range(z_n):
                gathers[0].corner(k)
        swap.wait()
        if np_:
            gathers[0].wait()
            sm_ref[...] = jnp.sum(units3(g_refs[0], 0, 16).astype(f32), 0)
        gain, bias = sm_ref[0:1, :], sm_ref[1:2, :]
        per = 256 // samples if samples < 256 else 1
        for s in range(slots // per):
            at = slice(s * per * samples, (s + 1) * per * samples)
            u, _ = unit(xg_ref[s * per:(s + 1) * per].reshape(per * samples, d).astype(f32))
            acted[at, :] = (u * gain + bias).astype(bf16)
        for i in range(3):
            w = units(g_refs[0], 16 + i * rl, rl) if np_ else w_ref[i]

            def project(at):
                y = dot(acted[at, :], w).astype(bf16)
                qkv_ref[i, at, :] = y * 0.125 if i == 0 else y

            blocks(rows, 256, project)

        turns = Turns(fs_n, hp, lambda p, j: o_ref.at[p, pl.ds(pl.multiple_of(j * samples, samples), samples)],
                      lambda p, j: back_ref.at[j, p], *turn_s)
        for p in range(hp):
            at = head_pair(p)
            vt[...] = qkv_ref[2, :, at].astype(f32).T.astype(bf16)
            for h in range(2):
                def part(i, _):
                    qa = pl.ds(pl.multiple_of(i * BQ, BQ), BQ)
                    q = qkv_ref[0, qa, at]
                    q = jnp.where(head_mask(BQ, h), q, jnp.zeros_like(q))
                    s = dot(qkv_ref[1, :, at], q, NT) + kb_ref[:, 0:1]
                    m = jnp.max(s, 0, keepdims=True)
                    e = jnp.exp(s - m)
                    tot = jnp.sum(e, 0, keepdims=True)
                    o = dot(vt[h * 64:h * 64 + 64, :], e.astype(bf16))
                    ot[h * 64:h * 64 + 64, qa] = o * (1.0 / tot)
                    l_ref[p * 2 + h:p * 2 + h + 1, qa] = m + jnp.log(tot)
                    return 0
                lax.fori_loop(0, rows // BQ, part, 0)
            o_ref[p, :, :] = ot[...].T.astype(bf16)
            turns.start(p)
            if np_ and p == 0:
                gathers[1].hand_on(0)
            if np_ and p == 2:
                gathers[1].hand_on(1)
        if np_:
            for k in range(2, z_n):
                gathers[1].hand_on(k)
            for k in range(z_n):
                gathers[1].corner(k)
        for p in range(hp):
            turns.wait_recv(p)
        turns.wait_send()
        if np_:
            gathers[1].wait()

    def units3(ref, start, size):
        v = ref[..., start:start + size, :]
        return v.reshape(-1, size, v.shape[-1])

    S, V = jax.ShapeDtypeStruct, pltpu.VMEM
    outs = [S((slots, hp, samples, 128), bf16), S((slots, samples, d), bf16), S((hp, rows, 128), bf16), S((3, rows, dh), bf16),
            S((heads, rows), f32)]
    outs += [S((dp_n, fs_n // 2, 2) + p.shape, bf16) for p in packs]
    args = [x, keybias] + list(packs)
    if np_:
        outs.append(S((16, d), f32))
    else:
        args += list(plain)
    return pl.pallas_call(
        body, out_shape=outs, in_specs=[VM] * len(args), out_specs=[ANY if np_ and i == 6 else VM for i in range(len(outs))],
        scratch_shapes=[V((rows, d), bf16), V((128, rows), bf16), V((128, rows), f32)] + swap_sems(fs_n) + turn_sems(fs_n, hp)
        + plane_gather_sems(fs_n) * np_,
        compiler_params=params(1), name="forward",
    )(*args)


def backward_kernel(do1, xg, qkv, o, lse, w, smalls, keybias, g1, gm, dp_n, fs_n, rl, dh, tasks, packed):
    slots, samples, d = xg.shape
    rows = slots * samples
    heads = dh // 64
    hp = heads // 2

    def body(*refs):
        it = iter(refs)
        do_in, xg_ref, qkv_ref, o_ref, l_ref, w_ref, n_ref, kb_ref = (next(it) for _ in range(8))
        g1_ref, gm_ref = (next(it), next(it)) if packed else (None, None)
        if packed:
            tg_ref, sm_ref, ss_ref = (next(it) for _ in range(3))
        else:
            dr_ref, gw_ref, gn_ref = (next(it) for _ in range(3))
        do, delta, kt, dqt, dk, dv, dqkv, acted, gn, dx = (next(it) for _ in range(10))
        turn_s = [next(it) for _ in range(3)]
        back_s = [next(it) for _ in range(3)]
        if packed:
            gs, dr_ref = next(it), next(it)
            rm = [next(it) for _ in range(11)]
            rs = [next(it) for _ in range(11)]

        greet(dp_n, fs_n, packed)
        turns = Turns(fs_n, hp, lambda p, j: do_in.at[j, p], lambda p, j: do.at[j, p], *turn_s)
        for p in range(hp):
            turns.start(p)
        if packed:
            red = PlaneReduce(fs_n, gm_ref, rm[:4], rm[4:])
            red_s = PlaneReduce(fs_n, gs, rs[:4], rs[4:])
            red.start()
            for k in red.order():
                red.first(k)
        gain, bias = n_ref[0:1, :], n_ref[1:2, :]
        lane = lax.broadcasted_iota(jnp.int32, (8, 128), 1) // 64
        pick = (lane == lax.broadcasted_iota(jnp.int32, (8, 128), 0)).astype(f32)
        per = BQ // samples if samples < BQ else 1

        def grad_rows(i, p):
            return do[pl.ds(i * per, per), p].reshape(per * samples, 128)

        n = per * samples
        for p in range(hp):
            at = head_pair(p)
            kt[...] = qkv_ref[1, :, at].astype(f32).T.astype(bf16)
            dk[...] = jnp.zeros_like(dk)
            dv[...] = jnp.zeros_like(dv)
            turns.wait_recv(p)

            def deltas(i, _):
                qa = pl.ds(pl.multiple_of(i * n, n), n)
                prod = grad_rows(i, p).astype(f32) * o_ref[p, qa, :].astype(f32)
                delta[:, qa] = lax.dot_general(pick, prod, NT, precision=lax.Precision.HIGHEST, preferred_element_type=f32)
                return 0

            lax.fori_loop(0, rows // n, deltas, 0)
            for h in range(2):
                def part(i, _):
                    qa = pl.ds(pl.multiple_of(i * n, n), n)
                    mask = head_mask(n, h)
                    q = qkv_ref[0, qa, at]
                    q = jnp.where(mask, q, jnp.zeros_like(q))
                    g = grad_rows(i, p)
                    g = jnp.where(mask, g, jnp.zeros_like(g))
                    s = dot(qkv_ref[1, :, at], q, NT) + kb_ref[:, 0:1]
                    e = jnp.exp(s - l_ref[p * 2 + h:p * 2 + h + 1, qa])
                    ds = (e * (dot(qkv_ref[2, :, at], g, NT) - delta[h:h + 1, qa])).astype(bf16)
                    dv[...] += dot(e.astype(bf16), g)
                    dk[...] += dot(ds, q)
                    dqt[h * 64:h * 64 + 64, qa] = dot(kt[h * 64:h * 64 + 64, :], ds) * 0.125
                    return 0
                lax.fori_loop(0, rows // n, part, 0)
            dqkv[0, :, at] = dqt[...].T.astype(bf16)
            dqkv[1, :, at] = dk[...].astype(bf16)
            dqkv[2, :, at] = dv[...].astype(bf16)
            if packed:
                if p == hp - 2:
                    for k in red.order():
                        red.second(k)
                if p == hp - 1:
                    for k in red.order():
                        red.third(k)

        def mats(i):
            return units(w_ref, 16 + i * rl, rl) if packed else w_ref[i]

        per2 = 256 // samples if samples < 256 else 1
        n2 = per2 * samples
        gn[...] = jnp.zeros_like(gn)

        def act_rows(i):
            at = pl.ds(pl.multiple_of(i * n2, n2), n2)
            u, r = unit(xg_ref[pl.ds(i * per2, per2)].reshape(n2, d).astype(f32))
            return at, u, r

        def first(i, _):
            at, u, r = act_rows(i)
            acted[at, :] = (u * gain + bias).astype(bf16)
            return 0

        lax.fori_loop(0, rows // n2, first, 0)
        for i in range(3):
            if packed:
                y = dot(acted[...], dqkv[i], TN).astype(bf16)
                gs[:, :, :, 16 + i * rl:16 + (i + 1) * rl, :] = y.reshape(gs.shape[:3] + (rl, d))
            else:
                gw_ref[i] = dot(acted[...], dqkv[i], TN).astype(bf16)

        back = Turns(fs_n, 1, lambda p, j: dx.at[j], lambda p, j: dr_ref.at[j], *back_s)

        def sums(i, _):
            at, u, r = act_rows(i)
            y = dot(dqkv[0, at, :], mats(0), NT) + dot(dqkv[1, at, :], mats(1), NT) + dot(dqkv[2, at, :], mats(2), NT)
            gn[0:1, :] += jnp.sum(y * u, 0, keepdims=True)
            gn[1:2, :] += jnp.sum(y, 0, keepdims=True)
            dx[pl.ds(i * per2, per2)] = unit_back(y, u, r, gain).astype(bf16).reshape(per2, samples, d)
            return 0

        lax.fori_loop(0, rows // n2, sums, 0)
        back.start(0)
        if packed:
            small = jnp.concatenate([gn[...].astype(bf16), jnp.zeros_like(gn).astype(bf16)], 0)
            gs[:, :, :, 0:16, :] = jnp.broadcast_to(small, gs.shape[:3] + (16, d))
            red_s.start()
            for k in red_s.order():
                red_s.first(k)
            red.finish(sm_ref)
            for k in red_s.order():
                red_s.second(k)
            for k in red_s.order():
                red_s.third(k)
            back.wait_recv(0)
            feats = slots // tasks
            for s in range(slots):
                t, f = s // feats, s % feats
                for i in range(d // 128):
                    at = pl.ds(((t * samples * (d // 128)) + i) * feats + f, samples, stride=feats * (d // 128))
                    tg_ref[at, :] = g1_ref[s * samples:(s + 1) * samples, head_pair(i)] + dr_ref[s, :, head_pair(i)].astype(f32)
            red_s.finish(ss_ref)
        else:
            gn_ref[...] = gn[...]
            back.wait_recv(0)
        back.wait_send()
        turns.wait_send()

    S, V = jax.ShapeDtypeStruct, pltpu.VMEM
    args = [do1, xg, qkv, o, lse, w, smalls, keybias]
    scratch = [V((slots, hp, samples, 128), bf16), V((8, rows), f32), V((128, rows), bf16), V((128, rows), f32), V((rows, 128), f32),
               V((rows, 128), f32), V((3, rows, dh), bf16), V((rows, d), bf16), V((8, d), f32), V((slots, samples, d), bf16)]
    scratch += turn_sems(fs_n, hp) + turn_sems(fs_n, 1)
    if packed:
        args += [g1, gm]
        mrows, srows = gm.shape[3], 16 + 3 * rl
        outs = [S((rows * d // 128, 128), f32), S((mrows, d), f32), S((srows, d), f32)]
        scratch += [V((dp_n, fs_n // 2, 2, srows, d), bf16), V((slots, samples, d), bf16)]
        scratch += plane_reduce_scratch(fs_n, mrows, d) + plane_reduce_scratch(fs_n, srows, d)
    else:
        outs = [S((slots, samples, d), bf16), S((3, d, dh), bf16), S((8, d), f32)]
    return pl.pallas_call(
        body, out_shape=outs, in_specs=[ANY if packed and i == 9 else VM for i in range(len(args))], out_specs=[VM] * len(outs), scratch_shapes=scratch,
        compiler_params=params(2), name="backward",
    )(*args)
def ones_pairs():
    half = lax.broadcasted_iota(jnp.int32, (256, 128), 0) // 64
    return (lax.rem(half, 2) == lax.broadcasted_iota(jnp.int32, (256, 128), 1) // 64).astype(bf16)


def head_sums(prods, ones):
    both = []
    for v in prods:
        hi = v.astype(bf16)
        both.append(jnp.concatenate([hi, (v - hi.astype(f32)).astype(bf16)], 1))
    out = dot(jnp.concatenate(both, 0), ones)
    n = prods[0].shape[0]
    return [out[i * n:(i + 1) * n] for i in range(len(prods))]


def key_bias(ref, counts, feats):
    count = counts[lax.axis_index("fsdp") // feats]
    rows = lax.broadcasted_iota(jnp.int32, ref.shape, 0)
    ref[...] = jnp.where(rows < count, 0.0, MASKED)


def rows_at(i, n):
    return pl.ds(pl.multiple_of(i * n, n), n)


def turn_rows(pieces, wide, out, tasks, feats, samples):
    blocks(wide.shape[0], 512, lambda at: wide.__setitem__((at, slice(None)), pieces[at, :].astype(f32)))
    parts = wide.shape[0] // (tasks * samples * feats)
    for s in range(tasks * feats):
        for i in range(parts):
            start = (s // feats * samples * parts + i) * feats + s % feats
            out(s, head_pair(i), wide[pl.ds(start, samples, stride=feats * parts), :].astype(bf16))


def first_kernel(tok, cot, scounts, fcounts, small_parts, s_qkv, s_out, f_qkv, f_out, m_in, m_out, tasks, samples, fs_n):
    dp_n = 4
    d = s_out.shape[1]
    slots = tok.shape[0] // (samples * d // 128)
    feats = slots // tasks
    rows = slots * samples
    hp = d // 128
    rl = s_out.shape[0]
    fl = m_out.shape[0]
    chunks = m_in.shape[1] // d
    z_n = fs_n // 2
    ra, r1, r2 = 16 + 3 * rl, 5 * rl, chunks * rl + fl
    per = 512 // samples

    def body(tok_ref, cot_ref, sc_ref, fc_ref, norms, ob, ib, sq, so, fq, fo, mi, mo,
             xg_h, qkv_h, o_h, l_ref, ga_h, w1_h, w2, sm, x1_h, o2_h, a3_h, qkv2_h, p2_h, back_h, cot_h,
             wide, x_ref, turned, xg, qkv, o_ref, ga, w1, x1, o2, a3, qkv2, p2, back_ref,
             pa, pb1, pb2, kb, acted, vt, ot, small, out_sem, p2_sem, a3_sem, *sems):
        swap_s, turn_s = sems[:3], sems[3:6]
        gat_s = [sems[6 + 7 * i:13 + 7 * i] for i in range(3)]
        me = lax.axis_index("dp") * fs_n + lax.axis_index("fsdp")
        def placed(ref, first):
            n = ref.shape[1]
            hot = lax.broadcasted_iota(jnp.int32, (n, d), 1) == lax.broadcasted_iota(jnp.int32, (n, d), 0) + first
            return dot(ref[...], hot.astype(bf16))

        inner = lax.rem(me * fl, d)
        row = lax.broadcasted_iota(jnp.int32, (16, d), 0)
        small[...] = jnp.where(row == 7 + me * fl // d, placed(ib, inner), 0.0)
        small[0:6, :] = placed(norms, me * rl)
        small[6:7, :] = placed(ob, me * rl)
        pa[0:16, :] = small[...].astype(bf16)
        for i in range(3):
            pa[16 + i * rl:16 + (i + 1) * rl, :] = sq[i]
            pb1[(1 + i) * rl:(2 + i) * rl, :] = fq[i]
        pb1[0:rl, :] = so[...]
        pb1[4 * rl:5 * rl, :] = fo[...]
        for c in range(chunks):
            pb2[c * rl:(c + 1) * rl, :] = mi[:, c * d:(c + 1) * d]
        pb2[chunks * rl:, :] = mo[...]

        pairs_out = [(xg, xg_h), (qkv, qkv_h), (o_ref, o_h), (ga, ga_h), (w1, w1_h), (x1, x1_h), (o2, o2_h), (qkv2, qkv2_h), (back_ref, back_h), (turned, cot_h)]
        outs_c = [pltpu.make_async_copy(v, h, out_sem.at[i]) for i, (v, h) in enumerate(pairs_out)]
        out_xg, out_qkv, out_o, out_ga, out_w1, out_x1, out_o2, out_qkv2, out_back, out_cot = outs_c

        def out_p2(t):
            return pltpu.make_async_copy(p2.at[t], p2_h.at[t], p2_sem.at[t])

        def out_a3(i):
            return pltpu.make_async_copy(a3.at[rows_at(i, 512)], a3_h.at[rows_at(i, 512)], a3_sem.at[i])

        greet(dp_n, fs_n)
        A = PlaneGather(fs_n, pa, ga, *gat_s[0])
        B = PlaneGather(fs_n, pb1, w1, *gat_s[1])
        C = PlaneGather(fs_n, pb2, w2, *gat_s[2])
        swap = Swap(fs_n, x_ref, xg, *swap_s)
        turns = Turns(fs_n, hp, lambda p, j: o_ref.at[p, rows_at(j, samples)], lambda p, j: back_ref.at[j, p], *turn_s)
        later = list(range(1, z_n))
        A.start()
        turn_rows(tok_ref, wide, lambda s, lanes, v: x_ref.__setitem__((s, slice(None), lanes), v), tasks, feats, samples)
        swap.start()
        A.begin()
        key_bias(kb, sc_ref, feats)
        for k in later:
            A.spread(k)
        for k in range(z_n):
            A.hand_on(k)
        for k in range(z_n):
            A.corner(k)
        B.begin()
        C.begin()
        turn_rows(cot_ref, wide, lambda s, lanes, v: turned.__setitem__((slice(s * samples, (s + 1) * samples), lanes), v), tasks, feats, samples)
        out_cot.start()
        A.wait()
        out_ga.start()
        total = ga[:, :, :, 0:16, :].astype(f32)
        sm[...] = jnp.sum(total.reshape(-1, 16, d), 0)
        swap.wait()
        B.start()
        C.start()
        out_xg.start()

        def act(i, _):
            u, _r = unit(xg[pl.ds(i * per, per)].reshape(512, d).astype(f32))
            acted[rows_at(i, 512), :] = (u * sm[0:1, :] + sm[1:2, :]).astype(bf16)
            return 0

        lax.fori_loop(0, rows // 512, act, 0)
        for i in range(3):
            w = units(ga, 16 + i * rl, rl)

            def project(at):
                y = dot(acted[at, :], w).astype(bf16)
                qkv[i, at, :] = y * 0.125 if i == 0 else y

            blocks(rows, 512, project)
        out_qkv.start()
        for k in later:
            B.spread(k)

        for p in range(hp):
            at = head_pair(p)
            vt[...] = qkv[2, :, at].astype(f32).T.astype(bf16)
            for h in range(2):
                def part(i, _):
                    qa = rows_at(i, BQ)
                    q = qkv[0, qa, at]
                    q = jnp.where(head_mask(BQ, h), q, jnp.zeros_like(q))
                    s = dot(qkv[1, :, at], q, NT) + kb[:, 0:1]
                    m = jnp.max(s, 0, keepdims=True)
                    e = jnp.exp(s - m)
                    tot = jnp.sum(e, 0, keepdims=True)
                    o = dot(vt[h * 64:h * 64 + 64, :], e.astype(bf16))
                    ot[h * 64:h * 64 + 64, qa] = o * (1.0 / tot)
                    l_ref[p * 2 + h:p * 2 + h + 1, qa] = m + jnp.log(tot)
                    return 0
                lax.fori_loop(0, rows // BQ, part, 0)
            o_ref[p, :, :] = ot[...].T.astype(bf16)
            turns.start(p)
            if p == 0:
                for k in range(z_n):
                    B.hand_on(k)
                for k in later:
                    C.spread(k)
            if p == 1:
                for k in range(z_n):
                    B.corner(k)
            if p == 2:
                C.hand_on(0)
        out_o.start()
        B.wait()
        out_w1.start()
        for k in range(1, z_n):
            C.hand_on(k)
        for p in range(hp):
            turns.wait_recv(p)
        out_back.start()

        def first(i, _):
            at = rows_at(i, 512)
            o1 = jnp.concatenate([back_ref[pl.ds(i * per, per), p].reshape(512, 128) for p in range(hp)], 1)
            y = x_ref[pl.ds(i * per, per)].reshape(512, d).astype(f32) + dot(o1, units(w1, 0, rl))
            x1[at, :] = y
            u, _r = unit(y)
            v = (u * sm[2:3, :] + sm[3:4, :]).astype(bf16)
            for j in range(3):
                z = dot(v, units(w1, (1 + j) * rl, rl)).astype(bf16)
                qkv2[j, at, :] = z * 0.125 if j == 0 else z
            return 0

        lax.fori_loop(0, rows // 512, first, 0)
        for k in range(z_n):
            C.corner(k)
        out_x1.start()
        out_qkv2.start()
        ones = ones_pairs()

        def mix(t, _):
            slot = lambda f: rows_at(t * feats + f, samples)
            for p in range(hp):
                lanes = head_pair(p)
                ks = [qkv2[1, slot(g), lanes].astype(f32) for g in range(feats)]
                vs = [qkv2[2, slot(g), lanes].astype(f32) for g in range(feats)]
                for f in range(feats):
                    q = qkv2[0, slot(f), lanes].astype(f32)
                    sc = head_sums([q * k for k in ks], ones)
                    sc = [v + jnp.where(g < fc_ref[t], 0.0, MASKED) for g, v in enumerate(sc)]
                    top = functools.reduce(jnp.maximum, sc)
                    sc = [jnp.exp(v - top) for v in sc]
                    inv = 1.0 / sum(sc)
                    sc = [v * inv for v in sc]
                    for g in range(feats):
                        p2[t, p, f, g] = sc[g].astype(bf16)
                    o2[slot(f), lanes] = sum(w * v for w, v in zip(sc, vs)).astype(bf16)
            out_p2(t).start()
            return 0

        lax.fori_loop(0, tasks, mix, 0)
        out_o2.start()

        def second(i, _):
            at = rows_at(i, 512)
            u, _r = unit(x1[at, :] + dot(o2[at, :], units(w1, 4 * rl, rl)))
            a3[at, :] = (u * sm[4:5, :] + sm[5:6, :]).astype(bf16)
            out_a3(i).start()
            return 0

        lax.fori_loop(0, rows // 512, second, 0)
        turns.wait_send()
        C.wait()
        for c in outs_c:
            c.wait()
        for t in range(tasks):
            out_p2(t).wait()
        for i in range(rows // 512):
            out_a3(i).wait()

    S, V, D = jax.ShapeDtypeStruct, pltpu.VMEM, pltpu.SemaphoreType.DMA
    SM = pl.BlockSpec(memory_space=pltpu.SMEM)
    g = (dp_n, z_n, 2)
    outs = [S((slots, samples, d), bf16), S((3, rows, d), bf16), S((hp, rows, 128), bf16), S((2 * hp, rows), f32),
            S(g + (ra, d), bf16), S(g + (r1, d), bf16), S(g + (r2, d), bf16), S((16, d), f32), S((rows, d), f32), S((rows, d), bf16),
            S((rows, d), bf16), S((3, rows, d), bf16), S((tasks, hp, feats, feats, samples, 128), bf16), S((slots, hp, samples, 128), bf16),
            S((rows, d), bf16)]
    return pl.pallas_call(
        body, out_shape=outs, in_specs=[VM, VM, SM, SM] + [VM] * 9, out_specs=[VM if i in (3, 7) else ANY for i in range(len(outs))],
        scratch_shapes=[V(tok.shape, f32), V((slots, samples, d), bf16), V((rows, d), bf16)] + [V(outs[i].shape, outs[i].dtype) for i in (0, 1, 2, 4, 5, 8, 9, 10, 11, 12, 13)] + [V((ra, d), bf16), V((r1, d), bf16), V((r2, d), bf16), V((rows, 128), f32), V((rows, d), bf16), V((128, rows), bf16),
                        V((128, rows), f32), V((16, d), f32), D((10,)), D((tasks,)), D((rows // 512,))] + swap_sems(fs_n) + turn_sems(fs_n, hp) + plane_gather_sems(fs_n) * 3,
        compiler_params=params(1), name="first",
    )(tok, cot, scounts, fcounts, *small_parts, s_qkv, s_out, f_qkv, f_out, m_in, m_out)


def second_kernel(scounts, saved, tasks, rl, fl, fs_n):
    xg, qkv, o, lse, ga, w1, w2, sm, x1, o2, a3, qkv2, p2, back, cot = saved
    slots, samples, d = xg.shape
    feats = slots // tasks
    rows = slots * samples
    hp = d // 128
    z_n = fs_n // 2
    chunks = (w2.shape[3] - fl) // rl
    r1, r2, rs = 16 + 5 * rl, chunks * rl + fl, 16 + 3 * rl
    RB = 256
    per = RB // samples
    bq = 512
    pq = bq // samples

    def body(sc_ref, l_ref, sm_ref, cot_h, w2_h, x1_h, o2_h, a3_h,
             xg_h, qkv_h, o_h, ga_h, w1_h, qkv2_h, p2_h, back_h,
             g1_h, lo_h, dr, out2, out1, outs_,
             g1, lo, cot_ref, w2_ref, x1_ref, o2_ref, a3_ref, o_, w1_, q_, p2_, bk, acc, act, gh, ev, a2, do2, dqkv, G2, G1, GS, do, do1, delta, kt, dqt, kb, gn,
             c2, n2, z2, c1, n1, z1, c0, n0, z0, load_sem, *sems):
        turn_s, back_s = sems[:3], sems[3:6]
        red_s = [sems[6 + 6 * i:12 + 6 * i] for i in range(3)]
        me_f = lax.axis_index("fsdp")
        me_z, me_c = me_f // 2, mod(me_f, 2)
        load = lambda i, src, dst: pltpu.make_async_copy(src, dst, load_sem.at[i])
        get_w1 = load(0, w1_h, w1_)
        get_q2 = load(1, qkv2_h, q_)
        get_p2 = load(2, p2_h, p2_)
        get_bk = load(3, back_h, bk)
        xg_ = a3_ref
        dk, dv = acc.at[:, 0:128], acc.at[:, 128:256]
        get_xg = load(4, xg_h, xg_)
        get_o = load(5, o_h, o_)
        get_q1 = load(6, qkv_h, q_)
        ga_ = w1_.at[:, :, :, 0:rs, :]
        get_ga = load(7, ga_h, ga_)
        heads_in = [load(8 + i, a, b) for i, (a, b) in enumerate([(a3_h, a3_ref), (w2_h, w2_ref), (cot_h, cot_ref), (x1_h, x1_ref), (o2_h, o2_ref)])]
        put_g1 = load(13, g1, g1_h)
        put_lo = load(14, lo, lo_h)
        for c in heads_in + [get_w1, get_q2, get_p2, get_bk, get_o]:
            c.start()
        key_bias(kb, sc_ref, feats)
        gn[...] = jnp.zeros_like(gn)
        for i in range(rows // RB):
            acc[i * RB:(i + 1) * RB, :] = jnp.zeros((RB, d), f32)
            g1[i * RB:(i + 1) * RB, :] = jnp.zeros((RB, d), f32)
        greet(4, fs_n)
        for c in heads_in[:3]:
            c.wait()

        def mat(k):
            return units(w1_, k * rl, rl)

        def in_mat(c):
            return w2_ref[:, :, :, pl.ds(pl.multiple_of(c * rl, rl), rl), :].reshape(d, d)

        def out_mat(c):
            return w2_ref[pl.ds(c, 1), :, :, chunks * rl:, :].reshape(d, d)

        def put(g, start, i, value):
            g[2 * i:2 * i + 2, :, :, :, pl.ds(start, rl), :] = value.reshape(2, z_n // 2, 2, 2, rl, d)

        halves = [(slice(i * 256, i * 256 + 256), i) for i in range(d // 256)]

        def chunk(c, _):
            def part(at):
                hid = dot(a3_ref[at, :], in_mat(c)) + sm_ref[pl.ds(7 + c, 1), :]
                cdf, pdf = gelu_parts(hid)
                al = (hid * cdf).astype(bf16)
                act[at, :] = al
                gl = ((cdf + pdf) * dot(cot_ref[at, :], out_mat(c), NT)).astype(bf16)
                gh[at, :] = gl
                gn[pl.ds(7 + c, 1), :] += jnp.sum(gl.astype(f32), 0, keepdims=True)
                acc[at, :] += dot(al, out_mat(c))
                g1[at, :] += dot(gl, in_mat(c), NT)

            blocks(rows, 512, part)
            for at, i in halves:
                value = dot(act[:, at], cot_ref[...], TN).astype(bf16)
                G2[pl.ds(c, 1), i:i + 1, :, :, chunks * rl:, :] = value.reshape(1, 1, 2, 2, fl, d)
                put(G2, pl.multiple_of(c * rl, rl), i, dot(a3_ref[:, at], gh[...], TN).astype(bf16))
            return 0

        lax.fori_loop(0, chunks, chunk, 0)
        red2 = PlaneReduce(fs_n, G2, (c2, n2, z2), red_s[0])
        red2.start()
        for c in heads_in[3:]:
            c.wait()
        get_w1.wait()

        def third(at):
            x2 = x1_ref[at, :] + dot(o2_ref[at, :], mat(4))
            lo[at, :] = (x2 + acc[at, :] + sm_ref[6:7, :]).astype(bf16)
            u, r = unit(x2)
            y = g1[at, :]
            gn[4:5, :] += jnp.sum(y * u, 0, keepdims=True)
            gn[5:6, :] += jnp.sum(y, 0, keepdims=True)
            cf = cot_ref[at, :].astype(f32)
            gn[6:7, :] += jnp.sum(cf, 0, keepdims=True)
            g2 = cf + unit_back(y, u, r, sm_ref[4:5, :])
            g1[at, :] = g2
            e2 = g2.astype(bf16)
            ev[at, :] = e2
            do2[at, :] = dot(e2, mat(4), NT).astype(bf16)

        blocks(rows, 512, third)
        put_lo.start()
        for at, i in halves:
            put(G1, 16 + 4 * rl, i, dot(o2_ref[:, at], ev[...], TN).astype(bf16))
        red2.every(red2.first)
        get_q2.wait()
        get_p2.wait()
        ones = ones_pairs()

        def unmix(t, _):
            slot = lambda f: rows_at(t * feats + f, samples)
            for p in range(hp):
                lanes = head_pair(p)
                ks = [q_[1, slot(g), lanes].astype(f32) for g in range(feats)]
                vs = [q_[2, slot(g), lanes].astype(f32) for g in range(feats)]
                dks, dvs = [0.0] * feats, [0.0] * feats
                for f in range(feats):
                    q = q_[0, slot(f), lanes].astype(f32)
                    gr = do2[slot(f), lanes].astype(f32)
                    dp = head_sums([gr * v for v in vs], ones)
                    ws = [p2_[t, p, f, g].astype(f32) for g in range(feats)]
                    mean = sum(w * v for w, v in zip(ws, dp))
                    ds = [(w * (v - mean)).astype(bf16).astype(f32) for w, v in zip(ws, dp)]
                    dqkv[0, slot(f), lanes] = (sum(v * k for v, k in zip(ds, ks)) * 0.125).astype(bf16)
                    for g in range(feats):
                        dks[g] += ds[g] * q
                        dvs[g] += ws[g] * gr
                for g in range(feats):
                    dqkv[1, slot(g), lanes] = dks[g].astype(bf16)
                    dqkv[2, slot(g), lanes] = dvs[g].astype(bf16)
            return 0

        lax.fori_loop(0, tasks, unmix, 0)
        get_q1.start()

        def far(i, r):
            return mod(me_z + i, z_n) * 2 + mod(me_c + r, 2)

        me_d = lax.axis_index("dp")
        sends = {}
        for i in range(z_n):
            for r in range(2):
                for p in range(hp):
                    n = (p * z_n + i) * 2 + r
                    to = far(i, r)
                    if i == 0 and r == 0:
                        sends[p, i, r] = pltpu.make_async_copy(do1.at[to, p], do.at[to, p], turn_s[0].at[p])
                    else:
                        sends[p, i, r] = rcopy(do1.at[to, p], do.at[me_f, p], turn_s[1].at[n], turn_s[2].at[n], (me_d, to))
        chips = list(range(1, z_n)) + [0]

        def fourth(i):
            chip = mod(me_z + i, z_n)
            at = rows_at(chip, RB)
            u, r = unit(x1_ref[at, :])
            gain = sm_ref[2:3, :]
            a2[at, :] = (u * gain + sm_ref[3:4, :]).astype(bf16)
            y = dot(dqkv[0, at, :], mat(1), NT) + dot(dqkv[1, at, :], mat(2), NT) + dot(dqkv[2, at, :], mat(3), NT)
            gn[2:3, :] += jnp.sum(y * u, 0, keepdims=True)
            gn[3:4, :] += jnp.sum(y, 0, keepdims=True)
            v = g1[at, :] + unit_back(y, u, r, gain)
            g1[at, :] = v
            e1 = v.astype(bf16)
            ev[at, :] = e1
            g = dot(e1, mat(0), NT).astype(bf16)
            for p in range(hp):
                do1[pl.ds(chip * per, per), p] = g[:, head_pair(p)].reshape(per, samples, 128)
            for r in range(2):
                sends[0, i, r].start()

        for i in chips:
            fourth(i)
        for p in range(1, hp):
            for i in chips:
                for r in range(2):
                    sends[p, i, r].start()
        put_g1.start()
        get_ga.start()

        get_xg.start()
        red2.every(red2.second)
        get_bk.wait()
        for at, i in halves:
            o1 = jnp.concatenate([bk[:, 2 * i].reshape(rows, 128), bk[:, 2 * i + 1].reshape(rows, 128)], 1)
            put(G1, 16, i, dot(o1, ev[...], TN).astype(bf16))
            for j in range(3):
                put(G1, 16 + (1 + j) * rl, i, dot(a2[:, at], dqkv[j], TN).astype(bf16))
        G1[:, :, :, :, 0:16, :] = jnp.broadcast_to(gn[...].astype(bf16), (4, z_n // 2, 2, 2, 16, d))
        red1 = PlaneReduce(fs_n, G1, (c1, n1, z1), red_s[1])
        red1.start()
        red2.every(red2.third)

        lane = lax.broadcasted_iota(jnp.int32, (8, 128), 1) // 64
        pick = (lane == lax.broadcasted_iota(jnp.int32, (8, 128), 0)).astype(f32)
        get_q1.wait()
        get_o.wait()

        def grad_rows(i, p):
            return do[pl.ds(i * pq, pq), p].reshape(bq, 128)

        for p in range(hp):
            at = head_pair(p)
            kt[...] = q_[1, :, at].astype(f32).T.astype(bf16)
            dk[...] = jnp.zeros((rows, 128), f32)
            dv[...] = jnp.zeros((rows, 128), f32)
            for i in range(z_n):
                for r in range(2):
                    if i == 0 and r == 0:
                        sends[p, i, r].wait()
                    else:
                        sends[p, i, r].wait_recv()

            def deltas(i, _):
                qa = rows_at(i, bq)
                prod = grad_rows(i, p).astype(f32) * o_[p, qa, :].astype(f32)
                delta[:, qa] = lax.dot_general(pick, prod, NT, precision=lax.Precision.HIGHEST, preferred_element_type=f32)
                return 0

            lax.fori_loop(0, rows // bq, deltas, 0)
            if p == 0:
                red1.every(red1.first)
            for h in range(2):
                def part(i, _):
                    qa = rows_at(i, bq)
                    mask = head_mask(bq, h)
                    q = q_[0, qa, at]
                    q = jnp.where(mask, q, jnp.zeros_like(q))
                    g = grad_rows(i, p)
                    g = jnp.where(mask, g, jnp.zeros_like(g))
                    s = dot(q_[1, :, at], q, NT) + kb[:, 0:1]
                    e = jnp.exp(s - l_ref[p * 2 + h:p * 2 + h + 1, qa])
                    ds = (e * (dot(q_[2, :, at], g, NT) - delta[h:h + 1, qa])).astype(bf16)
                    dv[...] += dot(e.astype(bf16), g)
                    dk[...] += dot(ds, q)
                    dqt[h * 64:h * 64 + 64, qa] = dot(kt[h * 64:h * 64 + 64, :], ds) * 0.125
                    return 0
                lax.fori_loop(0, rows // bq, part, 0)
            dqkv[0, :, at] = dqt[...].T.astype(bf16)
            dqkv[1, :, at] = dk[...].astype(bf16)
            dqkv[2, :, at] = dv[...].astype(bf16)
            if p == 1:
                red1.every(red1.second)
            if p == 2:
                red1.every(red1.third)

        get_ga.wait()
        get_xg.wait()
        gn[...] = jnp.zeros_like(gn)
        gain, bias = sm_ref[0:1, :], sm_ref[1:2, :]

        backs = {}
        for i in range(z_n):
            for r in range(2):
                to = far(i, r)
                if i == 0 and r == 0:
                    backs[i, r] = pltpu.make_async_copy(xg_.at[rows_at(to, samples)], dr.at[to], back_s[0].at[0])
                else:
                    n = 2 * i + r
                    backs[i, r] = rcopy(xg_.at[rows_at(to, samples)], dr.at[me_f], back_s[1].at[n], back_s[2].at[n], (me_d, to))
        for i in chips:
            chip = mod(me_z + i, z_n)
            at = rows_at(chip, RB)
            u, r = unit(xg_[at, :].astype(f32))
            y = (dot(dqkv[0, at, :], units(ga_, 16, rl), NT) + dot(dqkv[1, at, :], units(ga_, 16 + rl, rl), NT)
                 + dot(dqkv[2, at, :], units(ga_, 16 + 2 * rl, rl), NT))
            gn[0:1, :] += jnp.sum(y * u, 0, keepdims=True)
            gn[1:2, :] += jnp.sum(y, 0, keepdims=True)
            xg_[at, :] = unit_back(y, u, r, gain).astype(bf16)
            ev[at, :] = (u * gain + bias).astype(bf16)
            for r in range(2):
                backs[i, r].start()
        for j in range(3):
            for at, i in halves:
                put(GS, 16 + j * rl, i, dot(ev[:, at], dqkv[j], TN).astype(bf16))
        GS[:, :, :, :, 0:16, :] = jnp.broadcast_to(gn[...].astype(bf16), (4, z_n // 2, 2, 2, 16, d))
        reds = PlaneReduce(fs_n, GS, (c0, n0, z0), red_s[2])
        reds.start()
        red2.finish(out2)
        reds.every(reds.first)
        red1.finish(out1)
        reds.every(reds.second)
        reds.every(reds.third)
        reds.finish(outs_)
        put_g1.wait()
        put_lo.wait()
        for i in range(z_n):
            for r in range(2):
                backs[i, r].wait()
        for key, c in sends.items():
            if key[1:] != (0, 0):
                c.wait_send()

    S, V, D = jax.ShapeDtypeStruct, pltpu.VMEM, pltpu.SemaphoreType.DMA
    SM = pl.BlockSpec(memory_space=pltpu.SMEM)
    g = (4, z_n // 2, 2, 2)
    scratch = [V((rows, d), f32), V((rows, d), bf16), V((rows, d), bf16), V(w2.shape, bf16), V((rows, d), f32), V((rows, d), bf16),
               V((rows, d), bf16)]
    scratch += [V(o.shape, bf16), V(w1.shape, bf16), V(qkv.shape, bf16), V(p2.shape, bf16), V(back.shape, bf16),
               V((rows, d), f32), V((rows, d), bf16), V((rows, d), bf16), V((rows, d), bf16), V((rows, d), bf16), V((rows, d), bf16),
               V((3, rows, d), bf16), V(g + (r2, d), bf16), V(g + (r1, d), bf16), V(g + (rs, d), bf16), V(back.shape, bf16), V(back.shape, bf16), V((8, rows), f32),
               V((128, rows), bf16), V((128, rows), f32), V((rows, 128), f32), V((16, d), f32)]
    scratch += plane_reduce_scratch(fs_n, r2, d) + plane_reduce_scratch(fs_n, r1, d) + plane_reduce_scratch(fs_n, rs, d)
    n = hp * fs_n
    scratch += [D((15,)), D((hp,)), D((n,)), D((n,)), D((1,)), D((fs_n,)), D((fs_n,))] + plane_reduce_sems(fs_n) * 3
    return pl.pallas_call(
        body,
        out_shape=[S((rows, d), f32), S((rows, d), bf16), S((slots, samples, d), bf16), S((r2, d), f32), S((r1, d), f32), S((rs, d), f32)],
        in_specs=[SM, VM, VM] + [ANY] * 13, out_specs=[ANY, ANY, ANY, VM, VM, VM], scratch_shapes=scratch,
        compiler_params=params(2), name="second",
    )(scounts, lse, sm, cot, w2, x1, o2, a3, xg.reshape(rows, d), qkv, o, ga, w1, qkv2, p2, back)


def last_kernel(g1, dr, lo, out2, out1, outs, tasks, rl, fl, fs_n):
    slots, samples, d = dr.shape
    feats = slots // tasks
    part = feats * samples
    wide = d // 128
    chunks = (out2.shape[0] - fl) // rl

    def body(g1_ref, dr_ref, lo_ref, r2, r1, rs, tg, lo_out, gn, gs, gso, gf, gfo, gmi, gib, gmo, gob, low):
        for f in range(feats):
            for i in range(wide):
                at = pl.ds(i * feats + f, samples, stride=feats * wide)
                here = (slice(f * samples, (f + 1) * samples), head_pair(i))
                tg[at, :] = g1_ref[here] + dr_ref[f, :, head_pair(i)].astype(f32)
                low[at, :] = lo_ref[here].astype(f32)
        blocks(part * wide, 512, lambda at: lo_out.__setitem__((at, slice(None)), low[at, :].astype(bf16)))

        @pl.when(pl.program_id(0) == 0)
        def _():
            me = lax.axis_index("dp") * fs_n + lax.axis_index("fsdp")
            for i in range(3):
                gs[i] = rs[16 + i * rl:16 + (i + 1) * rl, :]
                gf[i] = r1[16 + (1 + i) * rl:16 + (2 + i) * rl, :]
            gso[...] = r1[16:16 + rl, :]
            gfo[...] = r1[16 + 4 * rl:16 + 5 * rl, :]
            for c in range(chunks):
                gmi[:, c * d:(c + 1) * d] = r2[c * rl:(c + 1) * rl, :]
            gmo[...] = r2[chunks * rl:, :]
            row = lax.broadcasted_iota(jnp.int32, (16, d), 0)
            both = jnp.where(row < 2, rs[0:16, :], r1[0:16, :])

            def mine(v, n, first):
                hot = lax.broadcasted_iota(jnp.int32, (d, n), 0) == lax.broadcasted_iota(jnp.int32, (d, n), 1) + first
                return lax.dot_general(v, hot.astype(f32), NN, precision=lax.Precision.HIGHEST, preferred_element_type=f32)

            own = mine(both, rl, me * rl)
            gn[...] = own[0:6]
            gob[...] = own[6:7]
            line = jnp.sum(jnp.where(row == 7 + me * fl // d, both, 0.0), 0, keepdims=True)
            gib[...] = mine(jnp.broadcast_to(line, (8, d)), fl, lax.rem(me * fl, d))[0:1]

    S = jax.ShapeDtypeStruct
    shapes = [S((tasks * part * wide, 128), f32), S((tasks * part * wide, 128), bf16), S((6, rl), f32), S((3, rl, d), f32), S((rl, d), f32),
              S((3, rl, d), f32), S((rl, d), f32), S((rl, chunks * d), f32), S((1, fl), f32), S((fl, d), f32), S((1, rl), f32)]
    by_task = lambda *shape: pl.BlockSpec(shape, lambda t: (t,) + (0,) * (len(shape) - 1))
    whole = lambda shape: pl.BlockSpec(shape, lambda t: (0,) * len(shape))
    return pl.pallas_call(
        body, out_shape=shapes, grid=(tasks,),
        in_specs=[by_task(part, d), by_task(feats, samples, d), by_task(part, d)] + [whole(v.shape) for v in (out2, out1, outs)],
        out_specs=[by_task(part * wide, 128), by_task(part * wide, 128)] + [whole(v.shape) for v in shapes[2:]],
        scratch_shapes=[pltpu.VMEM((part * wide, 128), f32)],
        compiler_params=params(), name="last",
    )(g1, dr, lo, out2, out1, outs)


def up16(a):
    rows = a.shape[-2]
    extra = (-rows) % 16
    return a if extra == 0 else jnp.pad(a, [(0, 0)] * (a.ndim - 2) + [(0, extra), (0, 0)])


def local(tokens, sample_counts, feature_counts, norms, sample_qkv, sample_out, feature_qkv, feature_out, mlp_in, mlp_in_bias,
          mlp_out, mlp_out_bias, cotangent):
    dp_n, fs_n = lax.axis_size("dp"), lax.axis_size("fsdp")
    nd = dp_n * fs_n
    me_d, me_f = lax.axis_index("dp"), lax.axis_index("fsdp")
    me = me_d * fs_n + me_f
    tasks, samples, feats, d = tokens.shape
    pairs = tasks * feats
    rep = fs_n // pairs
    dh = d // rep
    hp = dh // 128
    rl = sample_out.shape[0]
    chunks = mlp_in.shape[1] // d
    fl = mlp_out.shape[0]
    total = samples * fs_n
    if rep == 1 and dp_n == 4 and rl % 16 == 0 and fs_n * fl == d and fs_n == 8:
        def pieces(v):
            return v.reshape(tasks, samples, feats, d // 128, 128).transpose(0, 1, 3, 2, 4).reshape(-1, 128)

        saved = first_kernel(pieces(tokens), pieces(cotangent), sample_counts, feature_counts, (norms, mlp_out_bias[None], mlp_in_bias[None]),
                             sample_qkv, sample_out, feature_qkv, feature_out, mlp_in, mlp_out, tasks, samples, fs_n)
        g1, lo, dr, out2, out1, outs = second_kernel(sample_counts, saved, tasks, rl, fl, fs_n)
        tg, low, gn, gs, gso, gf, gfo, gmi, gib, gmo, gob = last_kernel(g1, dr, lo, out2, out1, outs, tasks, rl, fl, fs_n)

        def rows_back(v):
            return v.reshape(tasks, samples, d // 128, feats, 128).transpose(0, 1, 3, 2, 4).reshape(tokens.shape)

        return rows_back(low), rows_back(tg), gn, gs, gso, gf, gfo, gmi, gib[0], gmo, gob[0]


    small = jnp.zeros((16, d), bf16)
    small = lax.dynamic_update_slice(small, norms, (0, me * rl))
    small = lax.dynamic_update_slice(small, mlp_out_bias[None, :], (6, me * rl))
    small = lax.dynamic_update_slice(small, mlp_in_bias[None, :], (7 + (me * fl) // d, lax.rem(me * fl, d)))
    split_in = mlp_in.reshape(rl, chunks, d).transpose(1, 0, 2).reshape(chunks * rl, d)
    pack_a = up16(jnp.concatenate([small, sample_qkv.reshape(3 * rl, d)], 0))
    pack_b = up16(jnp.concatenate([sample_out, feature_qkv.reshape(3 * rl, d), feature_out, split_in, mlp_out], 0))

    xp = tokens.transpose(0, 2, 1, 3).reshape(pairs, samples, d)
    cp = cotangent.transpose(0, 2, 1, 3).reshape(pairs, samples, d)
    my_task = me_f // rep // feats
    count = lax.dynamic_index_in_dim(sample_counts, my_task, keepdims=False)
    keybias = jnp.broadcast_to(jnp.where(jnp.arange(total) < count, 0.0, MASKED).astype(f32)[:, None], (total, 128))
    shown = jnp.arange(feats)[None, :] < feature_counts[:, None]
    fbias = jnp.broadcast_to(jnp.where(shown, 0.0, MASKED).astype(f32).reshape(pairs, 1), (pairs, 128))

    ga, gb = gather_call([pack_a, pack_b], dp_n, fs_n, 3)
    ga, gb = ga.reshape((nd,) + ga.shape[3:]), gb.reshape((nd,) + gb.shape[3:])

    def take(g, start, rows):
        return g[:, start:start + rows].reshape(nd * rows, d)

    smalls = jnp.sum(ga[:, :16].astype(f32), 0)
    w_s = jnp.stack([take(ga, 16 + i * rl, rl) for i in range(3)])
    first = lax.rem(me_f, rep) * dh
    w_mine = lax.dynamic_slice_in_dim(w_s, first, dh, 2)
    w_mid = jnp.concatenate([take(gb, i * rl, rl) for i in range(5 + chunks)] + [take(gb, (5 + chunks) * rl, fl)])[None]
    size = d
    back, xg, o, qkv, lse = forward_kernel(jnp.repeat(xp, rep, 0), [], [w_mine, smalls], keybias, dp_n, fs_n, rl, dh)

    lo, g1, do1, gm = middle_call(xp, back.reshape(pairs, rep * hp, samples, 128), cp, smalls, fbias, w_mid, tasks, chunks, size)
    do1 = do1.reshape(fs_n, hp, samples, 128)
    dxr, gs, gn_s = backward_kernel(do1, xg, qkv, o, lse, w_mine, smalls, keybias, None, None, dp_n, fs_n, rl, dh, tasks, False)
    dxr = jnp.sum(dxr.reshape(pairs, rep, samples, d).astype(f32), 1)
    tokens_grad = (g1.reshape(pairs, samples, d) + dxr).reshape(tasks, feats, samples, d).transpose(0, 2, 1, 3)
    gs = lax.dynamic_update_slice_in_dim(jnp.zeros((3, d, d), bf16), gs, first, 2)

    def give(g, parts):
        return g.reshape(parts, nd, -1, d).transpose(1, 0, 2, 3).reshape(nd, -1, d)

    gm = gm[0]
    mix = jnp.concatenate([gn_s[0:2].astype(bf16), gm[2:16]], 0)
    grads = up16(jnp.concatenate([jnp.broadcast_to(mix[None], (nd, 16, d)), give(gm[16:16 + (5 + chunks) * d], 5 + chunks),
                                  give(gm[16 + (5 + chunks) * d:], 1), give(gs, 3)], 1))
    s = scatter_call(grads.reshape((dp_n, fs_n // 2, 2) + grads.shape[1:]), dp_n, fs_n, 6)
    outs = [s[16 + (5 + chunks) * rl + fl:][:3 * rl]]
    gn = s[0:2]
    gn = jnp.concatenate([gn, s[2:16]], 0)
    layer_output = lo.reshape(tasks, feats, samples, d).transpose(0, 2, 1, 3)

    def piece(start, rows):
        return s[16 + start * rl:16 + start * rl + rows]

    return (
        layer_output,
        tokens_grad,
        lax.dynamic_slice(gn, (0, me * rl), (6, rl)),
        outs[0].reshape(3, rl, d), piece(0, rl), piece(1, 3 * rl).reshape(3, rl, d), piece(4, rl),
        piece(5, chunks * rl).reshape(chunks, rl, d).transpose(1, 0, 2).reshape(rl, chunks * d),
        lax.dynamic_slice(gn[7:7 + chunks].reshape(-1), (me * fl,), (fl,)),
        piece(5 + chunks, fl),
        lax.dynamic_slice(gn[6], (me * rl,), (rl,)),
    )


def solution(mesh):
    rows, whole = ("dp", "fsdp"), P("dp", "fsdp", None, None)
    weights = (P(None, rows), P(None, rows, None), P(rows, None), P(None, rows, None), P(rows, None), P(rows, None), P(rows),
               P(rows, None), P(rows))
    return jax.shard_map(local, mesh=mesh, in_specs=(whole, P("dp"), P("dp")) + weights + (whole,),
                         out_specs=(whole, whole) + weights, check_vma=False)
```
